32 devices in a mesh: ens: 2 (over x), lon: 16 (over z, y, core).
Axes of the slice: x: 2, y: 2, z: 4, core: 2. Of those that a mesh axis runs over, the one named last changes fastest.
Arguments:
- state: bfloat16 [256, 4, 64, 256], P(('ens', 'lon')), parts along dimension 0, may hold values from -24 to 24
- obs_index: int32 [8192], P(('ens', 'lon')), parts along dimension 0, may hold values from 0 to 511
- obs_value: float32 [8192], P(('ens', 'lon')), parts along dimension 0, may hold values from -20 to 20
- obs_var: float32 [8192], P(('ens', 'lon')), parts along dimension 0, may hold values from 0.5 to 2
Outputs:
- analysis: bfloat16 [256, 4, 64, 256], P(('ens', 'lon')), parts along dimension 0
The draws below stay inside these ranges and needn't reach their ends.
There are 2 independent parts, one for each index of `ens`. The reference program is written for one: setup_inputs(seed, part) draws one part's arguments, and reference() takes and returns one part's arrays. A program takes and returns all parts, laid end to end along the dimension named above; each array names one. Nothing has to cross between parts.
Inputs may be any that keep to these rules, and one draw needn't show every extreme that they name: `obs_index`: a column of the device's own strip.
All inputs are finite; a program needn't handle non-finite values.
Results may differ from the reference program's by a relative error of at most 0.0029.
Values may be sent and summed in bfloat16 or wider, within the bound.
No kernel may reach another device: no remote copies, remote signals or barrier semaphores. Data moves between devices by JAX's collectives and lax.ppermute only.
A program may use at most 128 MiB of HBM per device.

```python
import math
import jax
import jax.numpy as jnp
from jax import lax

MEM = 256
VARS = 4
REGION = 8
HALO = 4
SWEEPS = 4
LON_DEV = 8
LAT = 64
OBS_DEV = 256
NLON = 128
NOBS = 4096
N_LON = 16


def draw_state(key, part):
    base = jnp.clip(jax.random.normal(key, (NLON, VARS, LAT, MEM), jnp.float32), -6.0, 6.0)
    return base.astype(jnp.bfloat16)


def draw_obs_value(key, part):
    place = jnp.arange(NOBS) // OBS_DEV
    rise = 1.0 + 2.0 * place.astype(jnp.float32) / max(N_LON - 1, 1)
    base = jnp.clip(jax.random.normal(key, (NOBS,), jnp.float32), -6.0, 6.0)
    return base * rise


def set_ends(values, key, low, top_value):
    longest = values.shape.index(max(values.shape))
    spots = []
    for shift in (0, 1):
        where = [jax.random.randint(jax.random.fold_in(key, axis), (), 0, length) for axis, length in enumerate(values.shape)]
        where[longest] = (where[longest] + shift) % values.shape[longest]
        spots.append(tuple(where))
    return values.at[spots[0]].set(low).at[spots[1]].set(top_value)


def block_levels(rng, extent, pieces, smallest, top_value):
    loudness = 1.0
    for axis_at, shards_of in pieces:
        steps = jax.random.uniform(jax.random.fold_in(jax.random.fold_in(rng, 6), axis_at), (shards_of,), jnp.float32, smallest / len(pieces), top_value / len(pieces))
        loudness = loudness * jnp.repeat(jnp.exp(steps), extent[axis_at] // shards_of).reshape((-1,) + (1,) * (len(extent) - 1 - axis_at))
    return loudness


def setup_inputs(seed: int = 0, part: int = 0) -> dict:
    seeds = jax.random.split(jax.random.key(seed), 5)
    part_splits = jax.random.split(jax.random.fold_in(seeds[4], part), 5)
    state = draw_state(jax.random.fold_in(jax.random.fold_in(seeds[4], part), 71), part)
    obs_index = set_ends(jax.random.randint(part_splits[1], (NOBS,), 0, LON_DEV * LAT), jax.random.fold_in(part_splits[1], 1), 0, (LON_DEV * LAT) - 1).astype(jnp.int32)
    obs_value = draw_obs_value(jax.random.fold_in(jax.random.fold_in(seeds[4], part), 71), part)
    obs_var = jnp.clip(jnp.exp(math.log(2.0) - 1.3862944 * jax.random.uniform(part_splits[3], (NOBS,), jnp.float32) ** block_levels(part_splits[3], (NOBS,), ((0, 16),), -0.2, 0.2)), 0.5, 2.0)
    return {"state": state, "obs_index": obs_index, "obs_value": obs_value, "obs_var": obs_var}


EPS = 0.05


def taper():
    place = jnp.arange(REGION + 2 * HALO)
    dist = jnp.maximum(0, jnp.maximum(HALO - place, place - (HALO + REGION - 1)))
    line = 1.0 - dist.astype(jnp.float32) / (HALO + 1)
    return line[:, None] * line[None, :]


def windows(block):
    lon_len, nvar, lat_len, members = block.shape
    lon_blocks = lon_len // REGION
    lat_blocks = lat_len // REGION
    split = block.reshape(lon_blocks, REGION, nvar, lat_blocks, REGION, members)
    split = jnp.concatenate([split[:-1], split[1:]], axis=1)
    return jnp.concatenate([split[:, :, :, :-1], split[:, :, :, 1:]], axis=4)


def analyse(win, mis_win, beta):
    rho = taper()
    members = win.shape[-1]
    weighted = (win.astype(jnp.float32) * rho[None, :, None, None, :, None]).astype(jnp.bfloat16)
    weighted = lax.optimization_barrier(weighted)
    gram = jnp.einsum("apvbqm,apvbqn->abmn", weighted.astype(jnp.float32), win.astype(jnp.float32), precision=lax.Precision.HIGHEST)
    diag = jnp.diagonal(gram, axis1=2, axis2=3)
    cost = (diag[..., :, None] + diag[..., None, :] - 2.0 * gram) / (win.shape[2] * jnp.sum(rho))
    like = -0.5 * beta * jnp.einsum("apxbqm,pq->abm", mis_win, rho, precision=lax.Precision.HIGHEST)
    logw = like - jax.nn.logsumexp(like, axis=-1, keepdims=True)
    pot_g = jnp.zeros(like.shape, jnp.float32)
    pot_f = pot_g
    for sweep in range(SWEEPS):
        pot_f = EPS * logw - EPS * jax.nn.logsumexp((pot_g[..., None, :] - cost) / EPS, axis=-1)
        pot_g = -EPS * jnp.log(1.0 * members) - EPS * jax.nn.logsumexp((pot_f[..., :, None] - cost) / EPS, axis=-2)
    transport = (members * jnp.exp((pot_f[..., :, None] + pot_g[..., None, :] - cost) / EPS)).astype(jnp.bfloat16)
    own = win[:, HALO:HALO + REGION, :, :, HALO:HALO + REGION, :]
    result = jnp.einsum("apvbqi,abij->apvbqj", own.astype(jnp.float32), transport.astype(jnp.float32), precision=lax.Precision.HIGHEST)
    return result.astype(jnp.bfloat16)


def reference(state, obs_index, obs_value, obs_var):
    nlon, nvar, lat, members = state.shape
    nobs = obs_index.shape[0]
    owner = jnp.arange(nobs, dtype=jnp.int32) // OBS_DEV
    column = ((owner * LON_DEV + obs_index // LAT) * LAT + obs_index % LAT).astype(jnp.int32)
    rows = state[:, 0].reshape(nlon * lat, members)
    seen = jnp.take(rows, column, axis=0).astype(jnp.float32)
    centre = jnp.mean(seen, axis=1)
    spread = jnp.sum((seen - centre[:, None]) ** 2, axis=1) / (members - 1)
    beta = nobs / jnp.sum((obs_value - centre) ** 2 / (obs_var + spread))
    terms = (obs_value[:, None] - seen) ** 2 / obs_var[:, None]
    misfit = jax.ops.segment_sum(terms, column, num_segments=nlon * lat).reshape(nlon, 1, lat, members)
    state_pad = jnp.concatenate([state[-HALO:], state, state[:HALO]], axis=0)
    state_pad = jnp.pad(state_pad, ((0, 0), (0, 0), (HALO, HALO), (0, 0)))
    mis_pad = jnp.concatenate([misfit[-HALO:], misfit, misfit[:HALO]], axis=0)
    mis_pad = jnp.pad(mis_pad, ((0, 0), (0, 0), (HALO, HALO), (0, 0)))

    def one_column(index):
        start = (index * REGION).astype(jnp.int32)
        block = lax.dynamic_slice_in_dim(state_pad, start, REGION + 2 * HALO, 0)
        mblock = lax.dynamic_slice_in_dim(mis_pad, start, REGION + 2 * HALO, 0)
        out = analyse(windows(block), windows(mblock), beta)
        return out.reshape(REGION, nvar, lat, members)

    result = lax.map(one_column, jnp.arange(nlon // REGION, dtype=jnp.int32))
    return result.reshape(nlon, nvar, lat, members)
```

```python
import functools

import jax
import jax.numpy as jnp
from jax import lax
from jax.experimental import pallas as pl
from jax.experimental.pallas import tpu as pltpu
from jax.sharding import PartitionSpec as P

REGION = 8
HALO = 4
SWEEPS = 4
EPS = 0.05
TILE = 8
PAIR = 2
LOG2E = 1.4426950408889634
LIFT = 100.0
ROWS = 32

HIGH = lax.Precision.HIGHEST


def line_weight(place):
    dist = jnp.maximum(0.0, jnp.maximum(HALO - place, place - (HALO + REGION - 1)))
    inside = (place >= 0) & (place < REGION + 2 * HALO)
    return jnp.where(inside, 1.0 - dist / (HALO + 1), 0.0)


def obs_kernel(cells_ref, index_ref, value_ref, var_ref, own_ref, left_ref, right_ref, part_ref):
    lon_dev, _, lat, members = cells_ref.shape
    nobs = index_ref.shape[1]
    rows = cells_ref[:, 0].reshape(lon_dev * lat, members)
    index = index_ref[...]
    sub = lax.broadcasted_iota(jnp.int32, (TILE, nobs), 0)
    table = jnp.where(
        sub == 0,
        index.astype(jnp.float32),
        jnp.where(sub == 1, value_ref[...], var_ref[...]),
    ).T
    index_col = table[:, 0:1].astype(jnp.int32)
    value = table[:, 1:2]
    var = table[:, 2:3]
    pick = index_col == lax.broadcasted_iota(jnp.int32, (nobs, lon_dev * lat), 1)
    pick = jnp.where(pick, 1.0, 0.0).astype(jnp.bfloat16)
    seen = jnp.dot(pick, rows, preferred_element_type=jnp.float32)
    centre = jnp.sum(seen, axis=1, keepdims=True) * (1.0 / members)
    spread = jnp.sum((seen - centre) ** 2, axis=1, keepdims=True) * (1.0 / (members - 1))
    innovation = (value - centre) ** 2 / (var + spread)
    part_ref[...] = jnp.broadcast_to(jnp.sum(innovation, axis=0, keepdims=True), part_ref.shape)
    terms = (value - seen) ** 2 * (1.0 / var)
    lon = (index // lat).astype(jnp.float32)
    along = index.astype(jnp.float32) - lon * lat
    for ref, shift in ((own_ref, HALO), (left_ref, HALO + REGION), (right_ref, HALO - REGION)):
        blocks = ref.shape[0]
        block = lax.broadcasted_iota(jnp.int32, (blocks, nobs), 0).astype(jnp.float32)
        weight = line_weight(lon + shift) * line_weight(along - REGION * block + HALO)
        ref[...] = jnp.dot(weight, terms, precision=HIGH, preferred_element_type=jnp.float32)


def observe(state, obs_index, obs_value, obs_var):
    lon_dev, _, lat, members = state.shape
    nobs = obs_index.shape[0]
    blocks = lat // REGION
    row = pl.BlockSpec((1, nobs), lambda i: (0, 0))
    like = jax.ShapeDtypeStruct((blocks, members), jnp.float32)
    like_spec = pl.BlockSpec((blocks, members), lambda i: (0, 0))
    return pl.pallas_call(
        obs_kernel,
        grid=(1,),
        in_specs=[pl.BlockSpec((lon_dev, 1, lat, members), lambda i: (0, 0, 0, 0)), row, row, row],
        out_specs=[like_spec] * 3 + [pl.BlockSpec((8, 128), lambda i: (0, 0))],
        out_shape=[like] * 3 + [jax.ShapeDtypeStruct((8, 128), jnp.float32)],
        compiler_params=pltpu.CompilerParams(vmem_limit_bytes=32 * 2**20),
        name="observe",
    )(state, obs_index[None], obs_value[None], obs_var[None])


def gram_of(before, here, after, places, step, steps):
    columns, nvar, _, members = here.shape
    wide = here.astype(jnp.float32)
    low, high = wide[:, :, :TILE], wide[:, :, TILE:]
    prev = before[:, :, TILE:].astype(jnp.float32)
    nxt = after[:, :, :TILE].astype(jnp.float32)
    prev = jnp.where(step == 0, 0.0, prev)
    nxt = jnp.where(step == steps - 1, 0.0, nxt)
    row = lax.broadcasted_iota(jnp.int32, (1, 1, TILE, members), 2)
    upper = row < HALO
    rowf = row.astype(jnp.float32)
    edge = line_weight(jnp.where(upper, rowf + (HALO + REGION), rowf - HALO))
    grams = []
    for own, following, preceding in ((low, high, prev), (high, nxt, low)):
        margin = jnp.where(upper, following, preceding)
        win = jnp.concatenate([own, margin], axis=2)
        weighted = []
        for column, place in enumerate(places):
            dist = max(0, HALO - place, place - (HALO + REGION - 1))
            weight = jnp.float32(1.0) - jnp.float32(dist) / jnp.float32(HALO + 1)
            weighted.append(
                jnp.concatenate([own[column] * weight, margin[column] * (edge[0] * weight)], axis=1)
            )
        weighted = jnp.stack(weighted)
        shape = (columns * nvar * 2 * TILE, members)
        grams.append(
            lax.dot_general(
                weighted.astype(jnp.bfloat16).reshape(shape),
                win.astype(jnp.bfloat16).reshape(shape),
                (((0,), (0,)), ((), ())),
                preferred_element_type=jnp.float32,
            )
        )
    return grams


def own_gram_kernel(before_ref, here_ref, after_ref, gram_ref):
    step, steps = pl.program_id(0), pl.num_programs(0)
    places = range(HALO, HALO + here_ref.shape[0])
    grams = gram_of(before_ref[...], here_ref[...], after_ref[...], places, step, steps)
    for region in range(PAIR):
        gram_ref[region] = grams[region]


def lat_specs(columns, nvar, members, steps):
    shape = (columns, nvar, PAIR * TILE, members)
    return [
        pl.BlockSpec(shape, lambda i: (0, 0, jnp.maximum(i - 1, 0), 0)),
        pl.BlockSpec(shape, lambda i: (0, 0, i, 0)),
        pl.BlockSpec(shape, lambda i: (0, 0, jnp.minimum(i + 1, steps - 1), 0)),
    ]


def own_gram(state):
    lon_dev, nvar, lat, members = state.shape
    steps = lat // (PAIR * TILE)
    return pl.pallas_call(
        own_gram_kernel,
        grid=(steps,),
        in_specs=lat_specs(lon_dev, nvar, members, steps),
        out_specs=pl.BlockSpec((PAIR, members, members), lambda i: (i, 0, 0)),
        out_shape=jax.ShapeDtypeStruct((steps * PAIR, members, members), jnp.float32),
        compiler_params=pltpu.CompilerParams(vmem_limit_bytes=48 * 2**20),
        name="own_gram",
    )(state, state, state)


def diagonal(gram_ref, region):
    members = gram_ref.shape[-1]
    across, down = None, []
    for start in range(0, members, ROWS):
        gram = gram_ref[region, start : start + ROWS, :]
        i = lax.broadcasted_iota(jnp.int32, gram.shape, 0) + start
        j = lax.broadcasted_iota(jnp.int32, gram.shape, 1)
        kept = jnp.where(i == j, gram, 0.0)
        down.append(jnp.sum(kept, axis=1, keepdims=True))
        part = jnp.sum(kept.reshape(ROWS // TILE, TILE, members), axis=0)
        across = part if across is None else across + part
    return jnp.sum(across, axis=0, keepdims=True), down


def transport_scaled(gram_ref, plan_ref, out_ref, region, weight, scale):
    members = gram_ref.shape[-1]
    across, down = diagonal(gram_ref, region)
    across = 0.5 * LIFT - across * scale
    starts = range(0, members, ROWS)
    lift = 2.0**LIFT
    factor = None
    least_row = least_col = grown_row = grown_col = None
    grown_rows = [None] * len(starts)
    for sweep in range(SWEEPS):
        total = None
        for at, start in enumerate(starts):
            rows = slice(start, start + ROWS)
            if sweep == 0:
                plan = jnp.exp2(
                    gram_ref[region, rows, :] * (2.0 * scale)
                    + (0.5 * LIFT - down[at] * scale)
                    + across
                )
            else:
                plan = plan_ref[region, rows, :] * factor
            mass = jnp.sum(plan, axis=1, keepdims=True)
            ratio = weight[rows] * (lift / mass)
            plan = plan * ratio
            plan_ref[region, rows, :] = plan
            part = jnp.sum(plan.reshape(ROWS // TILE, TILE, members), axis=0)
            total = part if total is None else total + part
            grow = jnp.maximum(ratio, 1.0)
            grown_rows[at] = grow if sweep == 0 else grown_rows[at] * grow
            least_row = mass if least_row is None else jnp.minimum(least_row, mass)
        total = jnp.sum(total, axis=0, keepdims=True)
        factor = (lift / members) / total
        grow = jnp.maximum(factor, 1.0)
        grown_col = grow if sweep == 0 else grown_col * grow
        least_col = total if sweep == 0 else jnp.minimum(least_col, total)
    final = 1.0 / total
    for start in starts:
        rows = slice(start, start + ROWS)
        out_ref[region, rows, :] = (plan_ref[region, rows, :] * final).astype(jnp.bfloat16)
    for grow in grown_rows:
        grown_row = grow if grown_row is None else jnp.maximum(grown_row, grow)
    least = jnp.minimum(jnp.min(least_row), jnp.min(least_col))
    most = jnp.max(grown_row) * jnp.max(grown_col)
    return least, most * 2.0**-94


def transport_logs(gram_ref, cost_ref, out_ref, region, logw, scale):
    members = gram_ref.shape[-1]
    across, down = diagonal(gram_ref, region)
    starts = range(0, members, ROWS)
    for at, start in enumerate(starts):
        rows = slice(start, start + ROWS)
        cost_ref[region, rows, :] = (
            down[at] * scale + across * scale - gram_ref[region, rows, :] * (2.0 * scale)
        )
    pot_g = jnp.zeros((1, members), jnp.float32)
    cost = cost_ref[region]
    for sweep in range(SWEEPS):
        term = pot_g - cost
        top = jnp.max(term, axis=1, keepdims=True)
        pot_f = logw - top - jnp.log(jnp.sum(jnp.exp2(term - top), axis=1, keepdims=True)) * LOG2E
        term = pot_f - cost
        top = jnp.max(term, axis=0, keepdims=True)
        pot_g = -jnp.log(1.0 * members) * LOG2E - top
        pot_g = pot_g - jnp.log(jnp.sum(jnp.exp2(term - top), axis=0, keepdims=True)) * LOG2E
    plan = members * jnp.exp2(pot_f + pot_g - cost)
    out_ref[region] = plan.astype(jnp.bfloat16)


def analysis_kernel(count, scale, *refs):
    lefts, rights = refs[0:3], refs[3:6]
    own_ref, gram_in_ref, like_refs, total_ref = refs[6], refs[7], refs[8:11], refs[11]
    out_ref, gram_ref, plan_ref, move_ref = refs[12:16]
    step, steps = pl.program_id(0), pl.num_programs(0)
    columns = lefts[0].shape[0]
    left = gram_of(*[r[...] for r in lefts], range(columns), step, steps)
    right = gram_of(
        *[r[...] for r in rights], range(HALO + REGION, HALO + REGION + columns), step, steps
    )
    for region in range(PAIR):
        gram_ref[region] = gram_in_ref[region] + left[region] + right[region]
    beta = count / total_ref[0:1, 0:1]
    like = -0.5 * beta * (like_refs[0][0] + like_refs[1][0] + like_refs[2][0])
    like = like - jnp.max(like, axis=1, keepdims=True)
    weight = jnp.exp(like)
    norm = jnp.sum(weight, axis=1, keepdims=True)
    weight = weight / norm
    logw = (like - jnp.log(norm)) * LOG2E
    pad = jnp.zeros((TILE - 2 * PAIR,) + like.shape[1:], jnp.float32)
    table = jnp.concatenate([weight, logw, pad], axis=0).T
    checks = [
        transport_scaled(gram_ref, plan_ref, move_ref, r, table[:, r : r + 1], scale)
        for r in range(PAIR)
    ]
    for region, (least, most) in enumerate(checks):

        @pl.when(jnp.logical_not(least >= most))
        def _():
            lw = table[:, PAIR + region : PAIR + region + 1]
            transport_logs(gram_ref, plan_ref, move_ref, region, lw, scale)

    lon_dev, nvar, _, members = own_ref.shape
    own = own_ref[...].astype(jnp.float32)
    parts = []
    for region in range(PAIR):
        cells = own[:, :, region * TILE : (region + 1) * TILE].astype(jnp.bfloat16)
        cells = cells.reshape(lon_dev * nvar * TILE, members)
        moved = jnp.dot(cells, move_ref[region], preferred_element_type=jnp.float32)
        parts.append(moved.reshape(lon_dev, nvar, TILE, members))
    out_ref[...] = jnp.concatenate(parts, axis=2).astype(jnp.bfloat16)


def analyse(state, left, right, gram, likes, total, count):
    lon_dev, nvar, lat, members = state.shape
    steps = lat // (PAIR * TILE)
    offsets = range(REGION + 2 * HALO)
    line = [1.0 - max(0, HALO - p, p - (HALO + REGION - 1)) / (HALO + 1) for p in offsets]
    scale = LOG2E / EPS / (nvar * sum(line) ** 2)
    halo_specs = lat_specs(left.shape[0], nvar, members, steps)
    strip = pl.BlockSpec((lon_dev, nvar, PAIR * TILE, members), lambda i: (0, 0, i, 0))
    like_spec = pl.BlockSpec((1, PAIR, members), lambda i: (i, 0, 0))
    return pl.pallas_call(
        functools.partial(analysis_kernel, count, scale),
        grid=(steps,),
        in_specs=halo_specs
        + halo_specs
        + [strip, pl.BlockSpec((PAIR, members, members), lambda i: (i, 0, 0))]
        + [like_spec] * 3
        + [pl.BlockSpec(total.shape, lambda i: (0, 0))],
        out_specs=strip,
        out_shape=jax.ShapeDtypeStruct(state.shape, state.dtype),
        scratch_shapes=[
            pltpu.VMEM((PAIR, members, members), jnp.float32),
            pltpu.VMEM((PAIR, members, members), jnp.float32),
            pltpu.VMEM((PAIR, members, members), jnp.bfloat16),
        ],
        compiler_params=pltpu.CompilerParams(vmem_limit_bytes=48 * 2**20),
        name="analyse",
    )(left, left, left, right, right, right, state, gram,
      *[x.reshape(steps, PAIR, members) for x in likes], total)


def sum_over(value, axis):
    count = lax.axis_size(axis)
    if count & (count - 1):
        return lax.psum(value, axis)
    hop = 1
    while hop < count:
        value = value + lax.ppermute(value, axis, [(i, i ^ hop) for i in range(count)])
        hop *= 2
    return value


def on_device(state, obs_index, obs_value, obs_var):
    lon_dev = state.shape[0]
    count = lax.axis_size("lon")
    to_right = [(i, (i + 1) % count) for i in range(count)]
    to_left = [((i + 1) % count, i) for i in range(count)]
    left = lax.ppermute(state[lon_dev - HALO :], "lon", to_right)
    right = lax.ppermute(state[:HALO], "lon", to_left)
    own, for_left, for_right, part = observe(state, obs_index, obs_value, obs_var)
    total = sum_over(part, "lon")
    from_left = lax.ppermute(for_right, "lon", to_right)
    from_right = lax.ppermute(for_left, "lon", to_left)
    gram = own_gram(state)
    nobs = float(obs_index.shape[0] * count)
    return analyse(state, left, right, gram, (own, from_left, from_right), total, nobs)


def solution(mesh):
    return jax.shard_map(
        on_device,
        mesh=mesh,
        in_specs=(
            P(("ens", "lon"), None, None, None),
            P(("ens", "lon")),
            P(("ens", "lon")),
            P(("ens", "lon")),
        ),
        out_specs=P(("ens", "lon"), None, None, None),
        check_vma=False,
    )
```

```python
import functools
import math

import jax
import jax.numpy as jnp
from jax import lax
from jax.experimental import pallas as pl
from jax.experimental.pallas import tpu as pltpu
from jax.sharding import PartitionSpec as P

REGION = 8
HALO = 4
SWEEPS = 4
EPS = 0.05
TILE = 8
PAIR = 2
LOG2E = 1.4426950408889634
ROWS = 32
GROUP = 4
LIFT, START, MASS = 20, -10, 60

HIGH = lax.Precision.HIGHEST


def line_weight(place):
    dist = jnp.maximum(0.0, jnp.maximum(HALO - place, place - (HALO + REGION - 1)))
    inside = (place >= 0) & (place < REGION + 2 * HALO)
    return jnp.where(inside, 1.0 - dist / (HALO + 1), 0.0)


def obs_kernel(cells_ref, index_ref, value_ref, var_ref, own_ref, left_ref, right_ref, part_ref):
    lon_dev, _, lat, members = cells_ref.shape
    nobs = index_ref.shape[1]
    rows = cells_ref[:, 0].reshape(lon_dev * lat, members)
    index = index_ref[...]
    sub = lax.broadcasted_iota(jnp.int32, (TILE, nobs), 0)
    table = jnp.where(
        sub == 0,
        index.astype(jnp.float32),
        jnp.where(sub == 1, value_ref[...], var_ref[...]),
    ).T
    index_col = table[:, 0:1].astype(jnp.int32)
    value = table[:, 1:2]
    var = table[:, 2:3]
    pick = index_col == lax.broadcasted_iota(jnp.int32, (nobs, lon_dev * lat), 1)
    pick = jnp.where(pick, 1.0, 0.0).astype(jnp.bfloat16)
    seen = jnp.dot(pick, rows, preferred_element_type=jnp.float32)
    centre = jnp.sum(seen, axis=1, keepdims=True) * (1.0 / members)
    spread = jnp.sum((seen - centre) ** 2, axis=1, keepdims=True) * (1.0 / (members - 1))
    innovation = (value - centre) ** 2 / (var + spread)
    part_ref[...] = jnp.broadcast_to(jnp.sum(innovation, axis=0, keepdims=True), part_ref.shape)
    terms = (value - seen) ** 2 * (1.0 / var)
    lon = (index // lat).astype(jnp.float32)
    along = index.astype(jnp.float32) - lon * lat
    for ref, shift in ((own_ref, HALO), (left_ref, HALO + REGION), (right_ref, HALO - REGION)):
        blocks = ref.shape[0]
        block = lax.broadcasted_iota(jnp.int32, (blocks, nobs), 0).astype(jnp.float32)
        weight = line_weight(lon + shift) * line_weight(along - REGION * block + HALO)
        ref[...] = jnp.dot(weight, terms, precision=HIGH, preferred_element_type=jnp.float32)


def observe(state, obs_index, obs_value, obs_var):
    lon_dev, _, lat, members = state.shape
    nobs = obs_index.shape[0]
    blocks = lat // REGION
    row = pl.BlockSpec((1, nobs), lambda i: (0, 0))
    like = jax.ShapeDtypeStruct((blocks, members), jnp.float32)
    like_spec = pl.BlockSpec((blocks, members), lambda i: (0, 0))
    return pl.pallas_call(
        obs_kernel,
        grid=(1,),
        in_specs=[pl.BlockSpec((lon_dev, 1, lat, members), lambda i: (0, 0, 0, 0)), row, row, row],
        out_specs=[like_spec] * 3 + [pl.BlockSpec((8, 128), lambda i: (0, 0))],
        out_shape=[like] * 3 + [jax.ShapeDtypeStruct((8, 128), jnp.float32)],
        compiler_params=pltpu.CompilerParams(vmem_limit_bytes=32 * 2**20),
        name="observe",
    )(state, obs_index[None], obs_value[None], obs_var[None])


def pair_tiles(ref, step, steps):
    size = PAIR * TILE

    def load(at):
        return ref[:, :, pl.ds(pl.multiple_of(at * size, size), size), :].astype(jnp.float32)

    here = load(step)
    before = load(jnp.maximum(step - 1, 0))[:, :, TILE:]
    after = load(jnp.minimum(step + 1, steps - 1))[:, :, :TILE]
    before = jnp.where(step == 0, 0.0, before)
    after = jnp.where(step == steps - 1, 0.0, after)
    return before, here[:, :, :TILE], here[:, :, TILE:], after


def gram_of(tiles, places):
    before, low, high, after = tiles
    columns, nvar, _, members = low.shape
    row = lax.broadcasted_iota(jnp.int32, (1, TILE, members), 1)
    upper = row < HALO
    rowf = row.astype(jnp.float32)
    edge = line_weight(jnp.where(upper, rowf + (HALO + REGION), rowf - HALO))
    grams = []
    for own, following, preceding in ((low, high, before), (high, after, low)):
        margin = jnp.where(upper, following, preceding)
        win = jnp.concatenate([own, margin], axis=2)
        weighted = []
        for column, place in enumerate(places):
            dist = max(0, HALO - place, place - (HALO + REGION - 1))
            if dist:
                weight = jnp.float32(1.0) - jnp.float32(dist) / jnp.float32(HALO + 1)
                parts = [own[column] * weight, margin[column] * (edge * weight)]
            else:
                parts = [own[column], margin[column] * edge]
            weighted.append(jnp.concatenate(parts, axis=1))
        weighted = jnp.stack(weighted)
        shape = (columns * nvar * 2 * TILE, members)
        grams.append(
            lax.dot_general(
                weighted.astype(jnp.bfloat16).reshape(shape),
                win.astype(jnp.bfloat16).reshape(shape),
                (((0,), (0,)), ((), ())),
                preferred_element_type=jnp.float32,
            )
        )
    return grams


def own_gram_kernel(state_ref, gram_ref):
    step, steps = pl.program_id(0), pl.num_programs(0)
    places = range(HALO, HALO + state_ref.shape[0])
    grams = gram_of(pair_tiles(state_ref, step, steps), places)
    for region in range(PAIR):
        gram_ref[region] = grams[region]


def own_gram(state):
    lon_dev, nvar, lat, members = state.shape
    steps = lat // (PAIR * TILE)
    return pl.pallas_call(
        own_gram_kernel,
        grid=(steps,),
        in_specs=[pl.BlockSpec(state.shape, lambda i: (0, 0, 0, 0))],
        out_specs=pl.BlockSpec((PAIR, members, members), lambda i: (i, 0, 0)),
        out_shape=jax.ShapeDtypeStruct((steps * PAIR, members, members), jnp.float32),
        compiler_params=pltpu.CompilerParams(vmem_limit_bytes=48 * 2**20),
        name="own_gram",
    )(state)


def halves(ref, region, rows):
    members = ref.shape[-1]
    return [ref[region, rows, at : at + 128] for at in range(0, members, 128)]


def diagonal(gram_ref, region):
    members = gram_ref.shape[-1]
    across = [None] * (members // 128)
    down = []
    for start in range(0, members, ROWS):
        lane = start // 128
        gram = gram_ref[region, pl.ds(start, ROWS), lane * 128 : lane * 128 + 128]
        i = lax.broadcasted_iota(jnp.int32, gram.shape, 0) + start
        j = lax.broadcasted_iota(jnp.int32, gram.shape, 1) + lane * 128
        kept = jnp.where(i == j, gram, 0.0)
        down.append(jnp.broadcast_to(jnp.sum(kept, axis=1, keepdims=True), gram.shape))
        part = jnp.sum(kept.reshape(ROWS // TILE, TILE, 128), axis=0)
        across[lane] = part if across[lane] is None else across[lane] + part
    return [jnp.sum(x, axis=0, keepdims=True) for x in across], down


def sweep_rows(parts, weight, totals):
    scaled, mass = parts
    mass = jnp.broadcast_to(jnp.sum(mass, axis=1, keepdims=True), weight.shape)
    near = pl.reciprocal(mass, approx=True)
    ratio = weight * (near * (2.0 - mass * near))
    for lane, part in enumerate(scaled):
        part = jnp.sum((part * ratio).reshape(ROWS // TILE, TILE, 128), axis=0)
        totals[lane] = part if totals[lane] is None else totals[lane] + part
    return mass, ratio


def fold(values, op):
    out = values[0]
    for value in values[1:]:
        out = op(out, value)
    return out


def sweeps_scaled(regions, gram_ref, kernel_ref, ratio_ref, weight_ref, scale):
    members = gram_ref.shape[-1]
    starts = range(0, members, ROWS)
    lanes = range(members // 128)
    least_row, most_row, least_col, cols = [], [], [], []
    share = 2.0**MASS / members

    def settle(totals):
        totals = [jnp.sum(x, axis=0, keepdims=True) for x in totals]
        return totals, fold(totals, jnp.minimum)

    for region in regions:
        across, down = diagonal(gram_ref, region)
        across = [0.5 * LIFT - x * scale for x in across]
        totals = [None] * len(lanes)
        masses = []
        for at, start in enumerate(starts):
            rows = pl.ds(start, ROWS)
            base = 0.5 * LIFT - down[at] * scale
            kernel = [
                jnp.exp2(g * (2.0 * scale) + base + x)
                for g, x in zip(halves(gram_ref, region, rows), across)
            ]
            for lane, part in enumerate(kernel):
                kernel_ref[region, rows, lane * 128 : lane * 128 + 128] = part
            mass, _ = sweep_rows(
                (kernel, fold(kernel, jnp.add) * 2.0**START), weight_ref[region, rows, :], totals
            )
            masses.append(mass)
        least_row.append(fold(masses, jnp.minimum))
        most_row.append(fold(masses, jnp.maximum))
        totals, least = settle(totals)
        least_col.append(least)
        cols.append(totals)

    def sweep(last, carry):
        least_row, least_col, cols = carry
        rows_out, least_out, cols_out = [], [], []
        for region, lrow, lcol, col in zip(regions, least_row, least_col, cols):
            factor = [share / x for x in col]
            totals = [None] * len(lanes)
            for start in starts:
                rows = pl.ds(start, ROWS)
                kernel = halves(kernel_ref, region, rows)
                mass = fold([k * f for k, f in zip(kernel, factor)], jnp.add)
                mass, ratio = sweep_rows((kernel, mass), weight_ref[region, rows, :], totals)
                if last:
                    ratio_ref[region, rows, :] = ratio
                lrow = jnp.minimum(lrow, mass)
            totals, least = settle(totals)
            rows_out.append(lrow)
            least_out.append(jnp.minimum(lcol, least))
            cols_out.append(totals)
        return rows_out, least_out, cols_out

    carry = least_row, least_col, cols
    carry = lax.fori_loop(0, SWEEPS - 2, lambda i, c: sweep(False, c), carry)
    least_row, least_col, cols = sweep(True, carry)
    factors = [[1.0 / x for x in col] for col in cols]
    return (
        factors,
        fold(least_row, jnp.minimum),
        fold(least_col, jnp.minimum),
        fold(most_row, jnp.maximum),
    )


def transport_scaled(region, factor, kernel_ref, ratio_ref):
    members = kernel_ref.shape[-1]
    parts = []
    for start in range(0, members, ROWS):
        rows = pl.ds(start, ROWS)
        ratio = ratio_ref[region, rows, :]
        row = [k * ratio * f for k, f in zip(halves(kernel_ref, region, rows), factor)]
        parts.append(jnp.concatenate(row, axis=1).astype(jnp.bfloat16))
    return jnp.concatenate(parts, axis=0)


def transport_logs(region, gram_ref, logw, scale):
    members = gram_ref.shape[-1]
    gram = gram_ref[region]
    i = lax.broadcasted_iota(jnp.int32, gram.shape, 0)
    j = lax.broadcasted_iota(jnp.int32, gram.shape, 1)
    kept = jnp.where(i == j, gram, 0.0)
    down = jnp.sum(kept, axis=1, keepdims=True)
    across = jnp.sum(kept, axis=0, keepdims=True)
    cost = (down + across - 2.0 * gram) * scale
    logw = jnp.sum(jnp.where(i == j, logw, 0.0), axis=1, keepdims=True)
    pot_g = jnp.zeros((1, members), jnp.float32)
    for sweep in range(SWEEPS):
        term = pot_g - cost
        top = jnp.max(term, axis=1, keepdims=True)
        pot_f = logw - top - jnp.log(jnp.sum(jnp.exp2(term - top), axis=1, keepdims=True)) * LOG2E
        term = pot_f - cost
        top = jnp.max(term, axis=0, keepdims=True)
        pot_g = -math.log2(members) - top
        pot_g = pot_g - jnp.log(jnp.sum(jnp.exp2(term - top), axis=0, keepdims=True)) * LOG2E
    return (members * jnp.exp2(pot_f + pot_g - cost)).astype(jnp.bfloat16)


def transform(state_ref, pair, moves):
    lon_dev, nvar, _, members = state_ref.shape
    size = PAIR * TILE
    own = state_ref[:, :, pl.ds(pl.multiple_of(pair * size, size), size), :].astype(jnp.float32)
    parts = []
    for region, move in enumerate(moves):
        cells = own[:, :, region * TILE : (region + 1) * TILE].astype(jnp.bfloat16)
        cells = cells.reshape(lon_dev * nvar * TILE, members)
        moved = jnp.dot(cells, move, preferred_element_type=jnp.float32)
        parts.append(moved.reshape(lon_dev, nvar, TILE, members))
    return jnp.concatenate(parts, axis=2).astype(jnp.bfloat16)


def analysis_kernel(count, scale, *refs):
    left_ref, right_ref, state_ref, gram_in_ref = refs[0:4]
    like_refs, total_ref, out_ref = refs[4:7], refs[7], refs[8]
    gram_ref, kernel_ref, ratio_ref, weight_ref, logw_ref, result_ref, sems = refs[9:]
    columns = left_ref.shape[0]
    regions, members = gram_in_ref.shape[0], gram_in_ref.shape[-1]
    pairs = regions // PAIR
    size = PAIR * TILE

    total = jnp.sum(total_ref[...], axis=0, keepdims=True)[:, 0:1] * (1.0 / TILE)
    like = -0.5 * (count / total) * (like_refs[0][...] + like_refs[1][...] + like_refs[2][...])
    like = like - jnp.max(like, axis=1, keepdims=True)
    logw = (like - jnp.log(jnp.sum(jnp.exp(like), axis=1, keepdims=True))) * LOG2E
    logw_ref[...] = logw
    weight = jnp.exp2(logw + MASS).T
    for region in range(regions):
        weight_ref[region] = jnp.broadcast_to(weight[:, region : region + 1], (members, 128))

    def send(pair):
        at = pl.ds(pl.multiple_of(pair * size, size), size)
        return pltpu.make_async_copy(result_ref.at[pair], out_ref.at[:, :, at, :], sems.at[pair])

    def halo_grams(pair, carry):
        left = pair_tiles(left_ref, pair, pairs)
        right = pair_tiles(right_ref, pair, pairs)
        both = [jnp.concatenate([x, y], axis=0) for x, y in zip(left, right)]
        far = HALO + REGION
        grams = gram_of(both, list(range(columns)) + list(range(far, far + columns)))
        for at in range(PAIR):
            region = pair * PAIR + at
            gram_ref[region] = gram_in_ref[region] + grams[at]
        return carry

    lax.fori_loop(0, pairs, halo_grams, 0)

    def group(at, carry):
        least_row, least_col, most_row = carry
        first = at * GROUP
        factors, row, col, most = sweeps_scaled(
            [first + r for r in range(GROUP)], gram_ref, kernel_ref, ratio_ref, weight_ref, scale
        )
        for pair in range(GROUP // PAIR):
            moves = [
                transport_scaled(first + r, factors[r], kernel_ref, ratio_ref)
                for r in range(pair * PAIR, (pair + 1) * PAIR)
            ]
            where = at * (GROUP // PAIR) + pair
            result_ref[where] = transform(state_ref, where, moves)
            send(where).start()
        return (
            jnp.minimum(least_row, row),
            jnp.minimum(least_col, col),
            jnp.maximum(most_row, most),
        )

    high = jnp.full((ROWS, 128), 1e30, jnp.float32)
    least_row, least_col, most_row = lax.fori_loop(
        0, regions // GROUP, group, (high, high[:1], jnp.zeros((ROWS, 128), jnp.float32))
    )

    def drain(pair, carry):
        send(pair).wait()
        return carry

    lax.fori_loop(0, pairs, drain, 0)
    row, col, most = jnp.min(least_row), jnp.min(least_col), jnp.max(most_row)
    sound = (row >= 2.0**-24) & (col >= 2.0**-30) & (most <= 2.0**20) & (row * col >= 2.0**-34)

    @pl.when(jnp.logical_not(sound))
    def _():
        def again(pair, carry):
            moves = []
            for at in range(PAIR):
                region = pair * PAIR + at
                moves.append(transport_logs(region, gram_ref, logw_ref[pl.ds(region, 1), :], scale))
            result_ref[pair] = transform(state_ref, pair, moves)
            copy = send(pair)
            copy.start()
            copy.wait()
            return carry

        lax.fori_loop(0, pairs, again, 0)


def analyse(state, left, right, gram, likes, total, count):
    lon_dev, nvar, lat, members = state.shape
    regions = lat // REGION
    offsets = range(REGION + 2 * HALO)
    line = [1.0 - max(0, HALO - p, p - (HALO + REGION - 1)) / (HALO + 1) for p in offsets]
    scale = LOG2E / EPS / (nvar * sum(line) ** 2)
    vmem = pl.BlockSpec(memory_space=pltpu.VMEM)
    return pl.pallas_call(
        functools.partial(analysis_kernel, count, scale),
        in_specs=[vmem] * 8,
        out_specs=pl.BlockSpec(memory_space=pl.ANY),
        out_shape=jax.ShapeDtypeStruct(state.shape, state.dtype),
        scratch_shapes=[
            pltpu.VMEM((regions, members, members), jnp.float32),
            pltpu.VMEM((regions, members, members), jnp.float32),
            pltpu.VMEM((regions, members, 128), jnp.float32),
            pltpu.VMEM((regions, members, 128), jnp.float32),
            pltpu.VMEM((regions, members), jnp.float32),
            pltpu.VMEM((regions // PAIR, lon_dev, nvar, PAIR * TILE, members), jnp.bfloat16),
            pltpu.SemaphoreType.DMA((regions // PAIR,)),
        ],
        compiler_params=pltpu.CompilerParams(vmem_limit_bytes=48 * 2**20),
        name="analyse",
    )(left, right, state, gram, *likes, total)


def on_device(state, obs_index, obs_value, obs_var):
    lon_dev = state.shape[0]
    count = lax.axis_size("lon")
    to_right = [(i, (i + 1) % count) for i in range(count)]
    to_left = [((i + 1) % count, i) for i in range(count)]
    left = lax.ppermute(state[lon_dev - HALO :], "lon", to_right)
    right = lax.ppermute(state[:HALO], "lon", to_left)
    own, for_left, for_right, part = observe(state, obs_index, obs_value, obs_var)
    total = lax.all_gather(part, "lon", tiled=True)
    from_left = lax.ppermute(for_right, "lon", to_right)
    from_right = lax.ppermute(for_left, "lon", to_left)
    gram = own_gram(state)
    nobs = float(obs_index.shape[0] * count)
    return analyse(state, left, right, gram, (own, from_left, from_right), total, nobs)


def solution(mesh):
    return jax.shard_map(
        on_device,
        mesh=mesh,
        in_specs=(
            P(("ens", "lon"), None, None, None),
            P(("ens", "lon")),
            P(("ens", "lon")),
            P(("ens", "lon")),
        ),
        out_specs=P(("ens", "lon"), None, None, None),
        check_vma=False,
    )
```

```python
import functools
import math

import jax
import jax.numpy as jnp
from jax import lax
from jax.experimental import pallas as pl
from jax.experimental.pallas import tpu as pltpu
from jax.sharding import PartitionSpec as P

REGION = 8
HALO = 4
SWEEPS = 4
EPS = 0.05
TILE = 8
PAIR = 2
LOG2E = 1.4426950408889634
ROWS = 32
GROUP = 4
LIFT, START, MASS = 20, -10, 60

HIGH = lax.Precision.HIGHEST


def line_weight(place):
    dist = jnp.maximum(0.0, jnp.maximum(HALO - place, place - (HALO + REGION - 1)))
    inside = (place >= 0) & (place < REGION + 2 * HALO)
    return jnp.where(inside, 1.0 - dist / (HALO + 1), 0.0)


def obs_kernel(odd_ref, cells_ref, index_ref, value_ref, var_ref, own_ref, near_ref, far_ref):
    lon_dev, _, lat, members = cells_ref.shape
    nobs = index_ref.shape[1]
    rows = cells_ref[:, 0].reshape(lon_dev * lat, members)
    index = index_ref[...]
    sub = lax.broadcasted_iota(jnp.int32, (TILE, nobs), 0)
    table = jnp.where(
        sub == 0,
        index.astype(jnp.float32),
        jnp.where(sub == 1, value_ref[...], var_ref[...]),
    ).T
    index_col = table[:, 0:1].astype(jnp.int32)
    value = table[:, 1:2]
    var = table[:, 2:3]
    pick = index_col == lax.broadcasted_iota(jnp.int32, (nobs, lon_dev * lat), 1)
    pick = jnp.where(pick, 1.0, 0.0).astype(jnp.bfloat16)
    seen = jnp.dot(pick, rows, preferred_element_type=jnp.float32)
    centre = jnp.sum(seen, axis=1, keepdims=True) * (1.0 / members)
    spread = jnp.sum((seen - centre) ** 2, axis=1, keepdims=True) * (1.0 / (members - 1))
    innovation = (value - centre) ** 2 / (var + spread)
    blocks, members = own_ref.shape
    part = jnp.broadcast_to(jnp.sum(innovation, axis=0, keepdims=True), (TILE, members))
    near_ref[blocks:, :] = part
    terms = (value - seen) ** 2 * (1.0 / var)
    lon = (index // lat).astype(jnp.float32)
    along = index.astype(jnp.float32) - lon * lat
    block = lax.broadcasted_iota(jnp.int32, (blocks, nobs), 0).astype(jnp.float32)
    across = line_weight(along - REGION * block + HALO)
    side = jnp.where(odd_ref[0] == 1, float(REGION), float(-REGION))
    weights = [line_weight(lon + (HALO + shift)) * across for shift in (0.0, side, -side)]
    like = jnp.dot(
        jnp.concatenate(weights, axis=0), terms, precision=HIGH, preferred_element_type=jnp.float32
    )
    own_ref[...] = like[:blocks]
    near_ref[:blocks, :] = like[blocks : 2 * blocks]
    far_ref[...] = like[2 * blocks :]


def observe(odd, state, obs_index, obs_value, obs_var):
    lon_dev, _, lat, members = state.shape
    nobs = obs_index.shape[0]
    blocks = lat // REGION
    row = pl.BlockSpec((1, nobs), lambda i: (0, 0))
    like = jax.ShapeDtypeStruct((blocks, members), jnp.float32)
    like_spec = pl.BlockSpec((blocks, members), lambda i: (0, 0))
    more = jax.ShapeDtypeStruct((blocks + TILE, members), jnp.float32)
    more_spec = pl.BlockSpec((blocks + TILE, members), lambda i: (0, 0))
    return pl.pallas_call(
        obs_kernel,
        grid=(1,),
        in_specs=[
            pl.BlockSpec(memory_space=pltpu.SMEM),
            pl.BlockSpec((lon_dev, 1, lat, members), lambda i: (0, 0, 0, 0)),
            row,
            row,
            row,
        ],
        out_specs=[like_spec, more_spec, like_spec],
        out_shape=[like, more, like],
        compiler_params=pltpu.CompilerParams(vmem_limit_bytes=32 * 2**20),
        name="observe",
    )(odd, state, obs_index[None], obs_value[None], obs_var[None])


def pair_tiles(ref, step, steps):
    size = PAIR * TILE

    def load(at):
        return ref[:, :, pl.ds(pl.multiple_of(at * size, size), size), :].astype(jnp.float32)

    here = load(step)
    before = load(jnp.maximum(step - 1, 0))[:, :, TILE:]
    after = load(jnp.minimum(step + 1, steps - 1))[:, :, :TILE]
    before = jnp.where(step == 0, 0.0, before)
    after = jnp.where(step == steps - 1, 0.0, after)
    return before, here[:, :, :TILE], here[:, :, TILE:], after


def halo_weights(to_left):
    steps = [jnp.float32(1.0) - jnp.float32(d) / jnp.float32(HALO + 1) for d in range(HALO, 0, -1)]
    return [jnp.where(to_left, x, y) for x, y in zip(steps, steps[::-1])]


def gram_of(tiles, weights):
    before, low, high, after = tiles
    columns, nvar, _, members = low.shape
    row = lax.broadcasted_iota(jnp.int32, (1, TILE, members), 1)
    upper = row < HALO
    rowf = row.astype(jnp.float32)
    edge = line_weight(jnp.where(upper, rowf + (HALO + REGION), rowf - HALO))
    grams = []
    for own, following, preceding in ((low, high, before), (high, after, low)):
        margin = jnp.where(upper, following, preceding)
        win = jnp.concatenate([own, margin], axis=2)
        weighted = []
        for column, weight in enumerate(weights):
            if weight is None:
                parts = [own[column], margin[column] * edge]
            else:
                parts = [own[column] * weight, margin[column] * (edge * weight)]
            weighted.append(jnp.concatenate(parts, axis=1))
        weighted = jnp.stack(weighted)
        shape = (columns * nvar * 2 * TILE, members)
        grams.append(
            lax.dot_general(
                weighted.astype(jnp.bfloat16).reshape(shape),
                win.astype(jnp.bfloat16).reshape(shape),
                (((0,), (0,)), ((), ())),
                preferred_element_type=jnp.float32,
            )
        )
    return grams


def own_gram_kernel(odd_ref, state_ref, near_ref, gram_ref):
    step, steps = pl.program_id(0), pl.num_programs(0)
    tiles = zip(pair_tiles(state_ref, step, steps), pair_tiles(near_ref, step, steps))
    tiles = [jnp.concatenate([x, y], axis=0) for x, y in tiles]
    grams = gram_of(tiles, [None] * state_ref.shape[0] + halo_weights(odd_ref[0] == 1))
    for region in range(PAIR):
        gram_ref[region] = grams[region]


def own_gram(odd, state, near):
    lon_dev, nvar, lat, members = state.shape
    steps = lat // (PAIR * TILE)
    return pl.pallas_call(
        own_gram_kernel,
        grid=(steps,),
        in_specs=[
            pl.BlockSpec(memory_space=pltpu.SMEM),
            pl.BlockSpec(state.shape, lambda i: (0, 0, 0, 0)),
            pl.BlockSpec(near.shape, lambda i: (0, 0, 0, 0)),
        ],
        out_specs=pl.BlockSpec((PAIR, members, members), lambda i: (i, 0, 0)),
        out_shape=jax.ShapeDtypeStruct((steps * PAIR, members, members), jnp.float32),
        compiler_params=pltpu.CompilerParams(vmem_limit_bytes=48 * 2**20),
        name="own_gram",
    )(odd, state, near)


def halves(ref, region, rows):
    members = ref.shape[-1]
    return [ref[region, rows, at : at + 128] for at in range(0, members, 128)]


def diagonal(gram_ref, region):
    members = gram_ref.shape[-1]
    across = [None] * (members // 128)
    down = []
    for start in range(0, members, ROWS):
        lane = start // 128
        gram = gram_ref[region, pl.ds(start, ROWS), lane * 128 : lane * 128 + 128]
        i = lax.broadcasted_iota(jnp.int32, gram.shape, 0) + start
        j = lax.broadcasted_iota(jnp.int32, gram.shape, 1) + lane * 128
        kept = jnp.where(i == j, gram, 0.0)
        down.append(jnp.broadcast_to(jnp.sum(kept, axis=1, keepdims=True), gram.shape))
        part = jnp.sum(kept.reshape(ROWS // TILE, TILE, 128), axis=0)
        across[lane] = part if across[lane] is None else across[lane] + part
    return [jnp.sum(x, axis=0, keepdims=True) for x in across], down


def sweep_rows(parts, weight, totals):
    scaled, mass = parts
    mass = jnp.broadcast_to(jnp.sum(mass, axis=1, keepdims=True), weight.shape)
    near = pl.reciprocal(mass, approx=True)
    ratio = weight * (near * (2.0 - mass * near))
    for lane, part in enumerate(scaled):
        part = jnp.sum((part * ratio).reshape(ROWS // TILE, TILE, 128), axis=0)
        totals[lane] = part if totals[lane] is None else totals[lane] + part
    return mass, ratio


def fold(values, op):
    out = values[0]
    for value in values[1:]:
        out = op(out, value)
    return out


def sweeps_scaled(regions, gram_ref, kernel_ref, ratio_ref, weight_ref, scale):
    members = gram_ref.shape[-1]
    starts = range(0, members, ROWS)
    lanes = range(members // 128)
    least_row, most_row, least_col, cols = [], [], [], []
    share = 2.0**MASS / members

    def settle(totals):
        totals = [jnp.sum(x, axis=0, keepdims=True) for x in totals]
        return totals, fold(totals, jnp.minimum)

    for region in regions:
        across, down = diagonal(gram_ref, region)
        across = [0.5 * LIFT - x * scale for x in across]
        totals = [None] * len(lanes)
        masses = []
        for at, start in enumerate(starts):
            rows = pl.ds(start, ROWS)
            base = 0.5 * LIFT - down[at] * scale
            kernel = [
                jnp.exp2(g * (2.0 * scale) + base + x)
                for g, x in zip(halves(gram_ref, region, rows), across)
            ]
            for lane, part in enumerate(kernel):
                kernel_ref[region, rows, lane * 128 : lane * 128 + 128] = part
            mass, _ = sweep_rows(
                (kernel, fold(kernel, jnp.add) * 2.0**START), weight_ref[region, rows, :], totals
            )
            masses.append(mass)
        least_row.append(fold(masses, jnp.minimum))
        most_row.append(fold(masses, jnp.maximum))
        totals, least = settle(totals)
        least_col.append(least)
        cols.append(totals)

    def sweep(last, carry):
        least_row, least_col, cols = carry
        rows_out, least_out, cols_out = [], [], []
        for region, lrow, lcol, col in zip(regions, least_row, least_col, cols):
            factor = [share / x for x in col]
            totals = [None] * len(lanes)
            for start in starts:
                rows = pl.ds(start, ROWS)
                kernel = halves(kernel_ref, region, rows)
                mass = fold([k * f for k, f in zip(kernel, factor)], jnp.add)
                mass, ratio = sweep_rows((kernel, mass), weight_ref[region, rows, :], totals)
                if last:
                    ratio_ref[region, rows, :] = ratio
                lrow = jnp.minimum(lrow, mass)
            totals, least = settle(totals)
            rows_out.append(lrow)
            least_out.append(jnp.minimum(lcol, least))
            cols_out.append(totals)
        return rows_out, least_out, cols_out

    carry = least_row, least_col, cols
    carry = lax.fori_loop(0, SWEEPS - 2, lambda i, c: sweep(False, c), carry)
    least_row, least_col, cols = sweep(True, carry)
    factors = [[1.0 / x for x in col] for col in cols]
    return (
        factors,
        fold(least_row, jnp.minimum),
        fold(least_col, jnp.minimum),
        fold(most_row, jnp.maximum),
    )


def transport_scaled(region, factor, kernel_ref, ratio_ref):
    members = kernel_ref.shape[-1]
    parts = []
    for start in range(0, members, ROWS):
        rows = pl.ds(start, ROWS)
        ratio = ratio_ref[region, rows, :]
        row = [k * ratio * f for k, f in zip(halves(kernel_ref, region, rows), factor)]
        parts.append(jnp.concatenate(row, axis=1).astype(jnp.bfloat16))
    return jnp.concatenate(parts, axis=0)


def transport_logs(region, gram_ref, logw, scale):
    members = gram_ref.shape[-1]
    gram = gram_ref[region]
    i = lax.broadcasted_iota(jnp.int32, gram.shape, 0)
    j = lax.broadcasted_iota(jnp.int32, gram.shape, 1)
    kept = jnp.where(i == j, gram, 0.0)
    down = jnp.sum(kept, axis=1, keepdims=True)
    across = jnp.sum(kept, axis=0, keepdims=True)
    cost = (down + across - 2.0 * gram) * scale
    logw = jnp.sum(jnp.where(i == j, logw, 0.0), axis=1, keepdims=True)
    pot_g = jnp.zeros((1, members), jnp.float32)
    for sweep in range(SWEEPS):
        term = pot_g - cost
        top = jnp.max(term, axis=1, keepdims=True)
        pot_f = logw - top - jnp.log(jnp.sum(jnp.exp2(term - top), axis=1, keepdims=True)) * LOG2E
        term = pot_f - cost
        top = jnp.max(term, axis=0, keepdims=True)
        pot_g = -math.log2(members) - top
        pot_g = pot_g - jnp.log(jnp.sum(jnp.exp2(term - top), axis=0, keepdims=True)) * LOG2E
    return (members * jnp.exp2(pot_f + pot_g - cost)).astype(jnp.bfloat16)


def transform(state_ref, pair, moves):
    lon_dev, nvar, _, members = state_ref.shape
    size = PAIR * TILE
    own = state_ref[:, :, pl.ds(pl.multiple_of(pair * size, size), size), :].astype(jnp.float32)
    parts = []
    for region, move in enumerate(moves):
        cells = own[:, :, region * TILE : (region + 1) * TILE].astype(jnp.bfloat16)
        cells = cells.reshape(lon_dev * nvar * TILE, members)
        moved = jnp.dot(cells, move, preferred_element_type=jnp.float32)
        parts.append(moved.reshape(lon_dev, nvar, TILE, members))
    return jnp.concatenate(parts, axis=2).astype(jnp.bfloat16)


def analysis_kernel(count, scale, *refs):
    odd_ref, halo_ref, state_ref, gram_in_ref = refs[0:4]
    own_ref, near_ref, far_ref, sum_ref, out_ref = refs[4:9]
    gram_ref, kernel_ref, ratio_ref, weight_ref, logw_ref, result_ref, sems = refs[9:]
    regions, members = gram_in_ref.shape[0], gram_in_ref.shape[-1]
    pairs = regions // PAIR
    size = PAIR * TILE

    total = sum_ref[0:1, 0:1] + far_ref[regions : regions + 1, 0:1]
    like = own_ref[...] + near_ref[:regions, :] + far_ref[:regions, :]
    like = -0.5 * (count / total) * like
    like = like - jnp.max(like, axis=1, keepdims=True)
    logw = (like - jnp.log(jnp.sum(jnp.exp(like), axis=1, keepdims=True))) * LOG2E
    logw_ref[...] = logw
    weight = jnp.exp2(logw + MASS).T
    for region in range(regions):
        weight_ref[region] = jnp.broadcast_to(weight[:, region : region + 1], (members, 128))

    def send(pair):
        at = pl.ds(pl.multiple_of(pair * size, size), size)
        return pltpu.make_async_copy(result_ref.at[pair], out_ref.at[:, :, at, :], sems.at[pair])

    def halo_grams(pair, carry):
        grams = gram_of(pair_tiles(halo_ref, pair, pairs), halo_weights(odd_ref[0] == 0))
        for at in range(PAIR):
            region = pair * PAIR + at
            gram_ref[region] = gram_in_ref[region] + grams[at]
        return carry

    lax.fori_loop(0, pairs, halo_grams, 0)

    def group(at, carry):
        least_row, least_col, most_row = carry
        first = at * GROUP
        factors, row, col, most = sweeps_scaled(
            [first + r for r in range(GROUP)], gram_ref, kernel_ref, ratio_ref, weight_ref, scale
        )
        for pair in range(GROUP // PAIR):
            moves = [
                transport_scaled(first + r, factors[r], kernel_ref, ratio_ref)
                for r in range(pair * PAIR, (pair + 1) * PAIR)
            ]
            where = at * (GROUP // PAIR) + pair
            result_ref[where] = transform(state_ref, where, moves)
            send(where).start()
        return (
            jnp.minimum(least_row, row),
            jnp.minimum(least_col, col),
            jnp.maximum(most_row, most),
        )

    high = jnp.full((ROWS, 128), 1e30, jnp.float32)
    least_row, least_col, most_row = lax.fori_loop(
        0, regions // GROUP, group, (high, high[:1], jnp.zeros((ROWS, 128), jnp.float32))
    )

    def drain(pair, carry):
        send(pair).wait()
        return carry

    lax.fori_loop(0, pairs, drain, 0)
    row, col, most = jnp.min(least_row), jnp.min(least_col), jnp.max(most_row)
    sound = (row >= 2.0**-24) & (col >= 2.0**-30) & (most <= 2.0**20) & (row * col >= 2.0**-34)

    @pl.when(jnp.logical_not(sound))
    def _():
        def again(pair, carry):
            moves = []
            for at in range(PAIR):
                region = pair * PAIR + at
                moves.append(transport_logs(region, gram_ref, logw_ref[pl.ds(region, 1), :], scale))
            result_ref[pair] = transform(state_ref, pair, moves)
            copy = send(pair)
            copy.start()
            copy.wait()
            return carry

        lax.fori_loop(0, pairs, again, 0)


def analyse(odd, halo, state, gram, own, near, far, total, count):
    lon_dev, nvar, lat, members = state.shape
    regions = lat // REGION
    offsets = range(REGION + 2 * HALO)
    line = [1.0 - max(0, HALO - p, p - (HALO + REGION - 1)) / (HALO + 1) for p in offsets]
    scale = LOG2E / EPS / (nvar * sum(line) ** 2)
    vmem = pl.BlockSpec(memory_space=pltpu.VMEM)
    return pl.pallas_call(
        functools.partial(analysis_kernel, count, scale),
        in_specs=[pl.BlockSpec(memory_space=pltpu.SMEM)] + [vmem] * 7,
        out_specs=pl.BlockSpec(memory_space=pl.ANY),
        out_shape=jax.ShapeDtypeStruct(state.shape, state.dtype),
        scratch_shapes=[
            pltpu.VMEM((regions, members, members), jnp.float32),
            pltpu.VMEM((regions, members, members), jnp.float32),
            pltpu.VMEM((regions, members, 128), jnp.float32),
            pltpu.VMEM((regions, members, 128), jnp.float32),
            pltpu.VMEM((regions, members), jnp.float32),
            pltpu.VMEM((regions // PAIR, lon_dev, nvar, PAIR * TILE, members), jnp.bfloat16),
            pltpu.SemaphoreType.DMA((regions // PAIR,)),
        ],
        compiler_params=pltpu.CompilerParams(vmem_limit_bytes=48 * 2**20),
        name="analyse",
    )(odd, halo, state, gram, own, near, far, total)


def on_device(state, obs_index, obs_value, obs_var):
    lon_dev = state.shape[0]
    count = lax.axis_size("lon")
    odd = lax.axis_index("lon") % 2
    near_pairs = [(i, i ^ 1) for i in range(count)]
    far_pairs = [(i, (i + 1 if i % 2 else i - 1) % count) for i in range(count)]
    for_far = lax.dynamic_slice_in_dim(state, odd * (lon_dev - HALO), HALO, axis=0)
    for_near = lax.dynamic_slice_in_dim(state, (1 - odd) * (lon_dev - HALO), HALO, axis=0)
    far = lax.ppermute(for_far, "lon", far_pairs)
    near = lax.ppermute(for_near, "lon", near_pairs)
    odd = odd.astype(jnp.int32).reshape(1)
    own_like, near_like, far_like = observe(odd, state, obs_index, obs_value, obs_var)
    blocks = own_like.shape[0]
    got_near = lax.ppermute(near_like, "lon", near_pairs)
    total = near_like[blocks:] + got_near[blocks:]
    hop = 4
    while hop < count:
        total = total + lax.ppermute(total, "lon", [(i, i ^ hop) for i in range(count)])
        hop *= 2
    got_far = lax.ppermute(jnp.concatenate([far_like, total], axis=0), "lon", far_pairs)
    gram = own_gram(odd, state, near)
    nobs = float(obs_index.shape[0] * count)
    return analyse(odd, far, state, gram, own_like, got_near, got_far, total, nobs)


def solution(mesh):
    return jax.shard_map(
        on_device,
        mesh=mesh,
        in_specs=(
            P(("ens", "lon"), None, None, None),
            P(("ens", "lon")),
            P(("ens", "lon")),
            P(("ens", "lon")),
        ),
        out_specs=P(("ens", "lon"), None, None, None),
        check_vma=False,
    )
```

```python
import functools
import math

import jax
import jax.numpy as jnp
from jax import lax
from jax.experimental import pallas as pl
from jax.experimental.pallas import tpu as pltpu
from jax.sharding import PartitionSpec as P

REGION = 8
HALO = 4
SWEEPS = 4
EPS = 0.05
TILE = 8
PAIR = 2
LOG2E = 1.4426950408889634
ROWS = 32
GROUP = 4
LIFT, START, MASS = 20, -10, 60

HIGH = lax.Precision.HIGHEST


def line_weight(place):
    dist = jnp.maximum(0.0, jnp.maximum(HALO - place, place - (HALO + REGION - 1)))
    inside = (place >= 0) & (place < REGION + 2 * HALO)
    return jnp.where(inside, 1.0 - dist / (HALO + 1), 0.0)


def observe_kernel(*refs):
    odd_ref, state_ref, index_ref, value_ref, var_ref = refs[:5]
    own_ref, near_ref, far_ref, near_edge_ref, far_edge_ref, cells_ref, sems = refs[5:]
    lon_dev, lat, members = cells_ref.shape
    nobs = index_ref.shape[1]
    last = lon_dev - HALO
    far_at = odd_ref[0] * last
    copies = [
        pltpu.make_async_copy(state_ref.at[:, 0], cells_ref, sems.at[0]),
        pltpu.make_async_copy(state_ref.at[pl.ds(far_at, HALO)], far_edge_ref, sems.at[1]),
        pltpu.make_async_copy(state_ref.at[pl.ds(last - far_at, HALO)], near_edge_ref, sems.at[2]),
    ]
    for copy in copies:
        copy.start()
    copies[0].wait()
    rows = cells_ref[...].reshape(lon_dev * lat, members)
    index = index_ref[...]
    sub = lax.broadcasted_iota(jnp.int32, (TILE, nobs), 0)
    table = jnp.where(
        sub == 0,
        index.astype(jnp.float32),
        jnp.where(sub == 1, value_ref[...], var_ref[...]),
    ).T
    index_col = table[:, 0:1].astype(jnp.int32)
    value = table[:, 1:2]
    var = table[:, 2:3]
    pick = index_col == lax.broadcasted_iota(jnp.int32, (nobs, lon_dev * lat), 1)
    pick = jnp.where(pick, 1.0, 0.0).astype(jnp.bfloat16)
    seen = jnp.dot(pick, rows, preferred_element_type=jnp.float32)
    centre = jnp.sum(seen, axis=1, keepdims=True) * (1.0 / members)
    spread = jnp.sum((seen - centre) ** 2, axis=1, keepdims=True) * (1.0 / (members - 1))
    innovation = (value - centre) ** 2 / (var + spread)
    blocks, members = own_ref.shape
    part = jnp.broadcast_to(jnp.sum(innovation, axis=0, keepdims=True), (TILE, members))
    near_ref[blocks:, :] = part
    terms = (value - seen) ** 2 * (1.0 / var)
    lon = (index // lat).astype(jnp.float32)
    along = index.astype(jnp.float32) - lon * lat
    block = lax.broadcasted_iota(jnp.int32, (blocks, nobs), 0).astype(jnp.float32)
    across = line_weight(along - REGION * block + HALO)
    side = jnp.where(odd_ref[0] == 1, float(REGION), float(-REGION))
    weights = [line_weight(lon + (HALO + shift)) * across for shift in (0.0, side, -side)]
    like = jnp.dot(
        jnp.concatenate(weights, axis=0), terms, precision=HIGH, preferred_element_type=jnp.float32
    )
    own_ref[...] = like[:blocks]
    near_ref[:blocks, :] = like[blocks : 2 * blocks]
    far_ref[...] = like[2 * blocks :]
    for copy in copies[1:]:
        copy.wait()


def observe(odd, state, obs_index, obs_value, obs_var):
    lon_dev, nvar, lat, members = state.shape
    blocks = lat // REGION
    like = jax.ShapeDtypeStruct((blocks, members), jnp.float32)
    more = jax.ShapeDtypeStruct((blocks + TILE, members), jnp.float32)
    edge = jax.ShapeDtypeStruct((HALO, nvar, lat, members), state.dtype)
    vmem = pl.BlockSpec(memory_space=pltpu.VMEM)
    return pl.pallas_call(
        observe_kernel,
        in_specs=[
            pl.BlockSpec(memory_space=pltpu.SMEM),
            pl.BlockSpec(memory_space=pltpu.HBM),
            vmem,
            vmem,
            vmem,
        ],
        out_specs=[vmem] * 5,
        out_shape=[like, more, like, edge, edge],
        scratch_shapes=[
            pltpu.VMEM((lon_dev, lat, members), state.dtype),
            pltpu.SemaphoreType.DMA((3,)),
        ],
        compiler_params=pltpu.CompilerParams(vmem_limit_bytes=24 * 2**20),
        name="observe",
    )(odd, state, obs_index[None], obs_value[None], obs_var[None])


def pair_tiles(ref, step, steps):
    size = PAIR * TILE

    def load(at):
        return ref[:, :, pl.ds(pl.multiple_of(at * size, size), size), :].astype(jnp.float32)

    here = load(step)
    before = load(jnp.maximum(step - 1, 0))[:, :, TILE:]
    after = load(jnp.minimum(step + 1, steps - 1))[:, :, :TILE]
    before = jnp.where(step == 0, 0.0, before)
    after = jnp.where(step == steps - 1, 0.0, after)
    return before, here[:, :, :TILE], here[:, :, TILE:], after


def halo_weights(to_left):
    steps = [jnp.float32(1.0) - jnp.float32(d) / jnp.float32(HALO + 1) for d in range(HALO, 0, -1)]
    return [jnp.where(to_left, x, y) for x, y in zip(steps, steps[::-1])]


def gram_of(tiles, weights):
    before, low, high, after = tiles
    columns, nvar, _, members = low.shape
    row = lax.broadcasted_iota(jnp.int32, (1, TILE, members), 1)
    upper = row < HALO
    rowf = row.astype(jnp.float32)
    edge = line_weight(jnp.where(upper, rowf + (HALO + REGION), rowf - HALO))
    grams = []
    for own, following, preceding in ((low, high, before), (high, after, low)):
        margin = jnp.where(upper, following, preceding)
        win = jnp.concatenate([own, margin], axis=2)
        weighted = []
        for column, weight in enumerate(weights):
            if weight is None:
                parts = [own[column], margin[column] * edge]
            else:
                parts = [own[column] * weight, margin[column] * (edge * weight)]
            weighted.append(jnp.concatenate(parts, axis=1))
        weighted = jnp.stack(weighted)
        shape = (columns * nvar * 2 * TILE, members)
        grams.append(
            lax.dot_general(
                weighted.astype(jnp.bfloat16).reshape(shape),
                win.astype(jnp.bfloat16).reshape(shape),
                (((0,), (0,)), ((), ())),
                preferred_element_type=jnp.float32,
            )
        )
    return grams


def own_gram_kernel(odd_ref, state_ref, near_ref, gram_ref):
    step, steps = pl.program_id(0), pl.num_programs(0)
    tiles = zip(pair_tiles(state_ref, step, steps), pair_tiles(near_ref, step, steps))
    tiles = [jnp.concatenate([x, y], axis=0) for x, y in tiles]
    grams = gram_of(tiles, [None] * state_ref.shape[0] + halo_weights(odd_ref[0] == 1))
    for region in range(PAIR):
        gram_ref[region] = grams[region]


def own_gram(odd, state, near):
    lon_dev, nvar, lat, members = state.shape
    steps = lat // (PAIR * TILE)
    return pl.pallas_call(
        own_gram_kernel,
        grid=(steps,),
        in_specs=[
            pl.BlockSpec(memory_space=pltpu.SMEM),
            pl.BlockSpec(state.shape, lambda i: (0, 0, 0, 0)),
            pl.BlockSpec(near.shape, lambda i: (0, 0, 0, 0)),
        ],
        out_specs=pl.BlockSpec((PAIR, members, members), lambda i: (i, 0, 0)),
        out_shape=jax.ShapeDtypeStruct((steps * PAIR, members, members), jnp.float32),
        compiler_params=pltpu.CompilerParams(vmem_limit_bytes=24 * 2**20),
        cost_estimate=pl.CostEstimate(
            flops=2 * (lon_dev + HALO) * nvar * 2 * lat * members**2,
            bytes_accessed=2 * (state.size + near.size) + 4 * lat // REGION * members**2,
            transcendentals=0,
        ),
        name="own_gram",
    )(odd, state, near)


def halves(ref, region, rows):
    members = ref.shape[-1]
    return [ref[region, rows, at : at + 128] for at in range(0, members, 128)]


def diagonal(gram_ref, region):
    members = gram_ref.shape[-1]
    across = [None] * (members // 128)
    down = []
    for start in range(0, members, ROWS):
        lane = start // 128
        gram = gram_ref[region, pl.ds(start, ROWS), lane * 128 : lane * 128 + 128]
        i = lax.broadcasted_iota(jnp.int32, gram.shape, 0) + start
        j = lax.broadcasted_iota(jnp.int32, gram.shape, 1) + lane * 128
        kept = jnp.where(i == j, gram, 0.0)
        down.append(jnp.broadcast_to(jnp.sum(kept, axis=1, keepdims=True), gram.shape))
        part = jnp.sum(kept.reshape(ROWS // TILE, TILE, 128), axis=0)
        across[lane] = part if across[lane] is None else across[lane] + part
    return [jnp.sum(x, axis=0, keepdims=True) for x in across], down


def prepare_kernel(scale, odd_ref, halo_ref, gram_in_ref, gram_ref, kernel_ref, most_ref):
    step, steps = pl.program_id(0), pl.num_programs(0)
    members = gram_ref.shape[-1]
    grams = gram_of(pair_tiles(halo_ref, step, steps), halo_weights(odd_ref[0] == 0))
    most = None
    for region in range(PAIR):
        gram_ref[region] = gram_in_ref[region] + grams[region]
    for region in range(PAIR):
        across, down = diagonal(gram_ref, region)
        across = [0.5 * LIFT - x * scale for x in across]
        for at, start in enumerate(range(0, members, ROWS)):
            rows = pl.ds(start, ROWS)
            base = 0.5 * LIFT - down[at] * scale
            for lane, (gram, x) in enumerate(zip(halves(gram_ref, region, rows), across)):
                part = jnp.exp2(gram * (2.0 * scale) + base + x)
                kernel_ref[region, rows, lane * 128 : lane * 128 + 128] = part
                most = part if most is None else jnp.maximum(most, part)
    most_ref[0] = jnp.max(most.reshape(ROWS // TILE, TILE, 128), axis=0)


def prepare(odd, halo, gram, scale):
    regions, members, _ = gram.shape
    steps = regions // PAIR
    matrices = pl.BlockSpec((PAIR, members, members), lambda i: (i, 0, 0))
    return pl.pallas_call(
        functools.partial(prepare_kernel, scale),
        grid=(steps,),
        in_specs=[
            pl.BlockSpec(memory_space=pltpu.SMEM),
            pl.BlockSpec(halo.shape, lambda i: (0, 0, 0, 0)),
            matrices,
        ],
        out_specs=[matrices, matrices, pl.BlockSpec((1, TILE, 128), lambda i: (i, 0, 0))],
        out_shape=[
            jax.ShapeDtypeStruct(gram.shape, jnp.float32),
            jax.ShapeDtypeStruct(gram.shape, jnp.float32),
            jax.ShapeDtypeStruct((steps, TILE, 128), jnp.float32),
        ],
        input_output_aliases={2: 0},
        compiler_params=pltpu.CompilerParams(vmem_limit_bytes=24 * 2**20),
        cost_estimate=pl.CostEstimate(
            flops=2 * halo.size * 2 * members + 10 * gram.size,
            bytes_accessed=2 * halo.size + 12 * gram.size,
            transcendentals=gram.size,
        ),
        name="prepare",
    )(odd, halo, gram)


def fold(values, op):
    out = values[0]
    for value in values[1:]:
        out = op(out, value)
    return out


def sweeps_scaled(regions, kernel_ref, ratio_ref, weight_ref):
    members = kernel_ref.shape[-1]
    starts = range(0, members, ROWS)
    lanes = range(members // 128)
    share = 2.0**MASS / members

    def sweep(last, carry):
        least_row, least_col, factors = carry
        rows_out, least_out, factors_out = [], [], []
        for region, lrow, lcol, factor in zip(regions, least_row, least_col, factors):
            totals = [None for _ in lanes]
            for start in starts:
                rows = pl.ds(start, ROWS)
                kernel = halves(kernel_ref, region, rows)
                mass = fold([k * f for k, f in zip(kernel, factor)], jnp.add)
                mass = jnp.broadcast_to(jnp.sum(mass, axis=1, keepdims=True), (ROWS, 128))
                near = pl.reciprocal(mass, approx=True)
                ratio = weight_ref[region, rows, :] * (near * (2.0 - mass * near))
                for lane, part in enumerate(kernel):
                    part = jnp.sum((part * ratio).reshape(ROWS // TILE, TILE, 128), axis=0)
                    totals[lane] = part if totals[lane] is None else totals[lane] + part
                if last:
                    ratio_ref[region, rows, :] = ratio
                lrow = jnp.minimum(lrow, mass)
            totals = [jnp.sum(x, axis=0, keepdims=True) for x in totals]
            rows_out.append(lrow)
            least_out.append(jnp.minimum(lcol, fold(totals, jnp.minimum)))
            factors_out.append([(1.0 if last else share) / x for x in totals])
        return rows_out, least_out, factors_out

    high = jnp.full((ROWS, 128), 1e30, jnp.float32)
    first = jnp.full((1, 128), 2.0**START, jnp.float32)
    carry = [high for _ in regions], [high[:1] for _ in regions], [[first] * len(lanes) for _ in regions]
    carry = lax.fori_loop(0, SWEEPS - 1, lambda i, c: sweep(False, c), carry)
    least_row, least_col, factors = sweep(True, carry)
    return factors, fold(least_row, jnp.minimum), fold(least_col, jnp.minimum)


def transport_scaled(region, factor, kernel_ref, ratio_ref):
    members = kernel_ref.shape[-1]
    parts = []
    for start in range(0, members, ROWS):
        rows = pl.ds(start, ROWS)
        ratio = ratio_ref[region, rows, :]
        row = [k * ratio * f for k, f in zip(halves(kernel_ref, region, rows), factor)]
        parts.append(jnp.concatenate(row, axis=1).astype(jnp.bfloat16))
    return jnp.concatenate(parts, axis=0)


def transport_logs(region, gram_ref, logw, scale):
    members = gram_ref.shape[-1]
    gram = gram_ref[region]
    i = lax.broadcasted_iota(jnp.int32, gram.shape, 0)
    j = lax.broadcasted_iota(jnp.int32, gram.shape, 1)
    kept = jnp.where(i == j, gram, 0.0)
    down = jnp.sum(kept, axis=1, keepdims=True)
    across = jnp.sum(kept, axis=0, keepdims=True)
    cost = (down + across - 2.0 * gram) * scale
    logw = jnp.sum(jnp.where(i == j, logw, 0.0), axis=1, keepdims=True)
    pot_g = jnp.zeros((1, members), jnp.float32)
    for sweep in range(SWEEPS):
        term = pot_g - cost
        top = jnp.max(term, axis=1, keepdims=True)
        pot_f = logw - top - jnp.log(jnp.sum(jnp.exp2(term - top), axis=1, keepdims=True)) * LOG2E
        term = pot_f - cost
        top = jnp.max(term, axis=0, keepdims=True)
        pot_g = -math.log2(members) - top
        pot_g = pot_g - jnp.log(jnp.sum(jnp.exp2(term - top), axis=0, keepdims=True)) * LOG2E
    return (members * jnp.exp2(pot_f + pot_g - cost)).astype(jnp.bfloat16)


def transform(state_ref, pair, moves):
    lon_dev, nvar, _, members = state_ref.shape
    size = PAIR * TILE
    own = state_ref[:, :, pl.ds(pl.multiple_of(pair * size, size), size), :].astype(jnp.float32)
    parts = []
    for region, move in enumerate(moves):
        cells = own[:, :, region * TILE : (region + 1) * TILE].astype(jnp.bfloat16)
        cells = cells.reshape(lon_dev * nvar * TILE, members)
        moved = jnp.dot(cells, move, preferred_element_type=jnp.float32)
        parts.append(moved.reshape(lon_dev, nvar, TILE, members))
    return jnp.concatenate(parts, axis=2).astype(jnp.bfloat16)


def finish_kernel(count, scale, *refs):
    state_ref, gram_ref, kernel_ref, most_ref = refs[0:4]
    own_ref, near_ref, far_ref, total_ref, handed_ref, out_ref = refs[4:10]
    ratio_ref, weight_ref, logw_ref, result_ref, sems = refs[10:]
    regions, members = gram_ref.shape[0], gram_ref.shape[-1]
    pairs = regions // PAIR
    size = PAIR * TILE

    like = own_ref[...] + near_ref[:regions, :] + far_ref[:regions, :]
    like = -0.5 * (count / (total_ref[0:1, 0:1] + handed_ref[0:1, 0:1])) * like
    like = like - jnp.max(like, axis=1, keepdims=True)
    logw = (like - jnp.log(jnp.sum(jnp.exp(like), axis=1, keepdims=True))) * LOG2E
    logw_ref[...] = logw
    weight = jnp.exp2(logw + MASS).T
    for region in range(regions):
        weight_ref[region] = jnp.broadcast_to(weight[:, region : region + 1], (members, 128))

    def send(pair):
        at = pl.ds(pl.multiple_of(pair * size, size), size)
        return pltpu.make_async_copy(result_ref.at[pair], out_ref.at[:, :, at, :], sems.at[pair])

    def group(at, carry):
        first = at * GROUP
        factors, row, col = sweeps_scaled(
            [first + r for r in range(GROUP)], kernel_ref, ratio_ref, weight_ref
        )
        for pair in range(GROUP // PAIR):
            moves = [
                transport_scaled(first + r, factors[r], kernel_ref, ratio_ref)
                for r in range(pair * PAIR, (pair + 1) * PAIR)
            ]
            where = at * (GROUP // PAIR) + pair
            result_ref[where] = transform(state_ref, where, moves)
            send(where).start()
        return jnp.minimum(carry[0], row), jnp.minimum(carry[1], col)

    high = jnp.full((ROWS, 128), 1e30, jnp.float32)
    least_row, least_col = lax.fori_loop(0, regions // GROUP, group, (high, high[:1]))

    def drain(pair, carry):
        send(pair).wait()
        return carry

    lax.fori_loop(0, pairs, drain, 0)
    row, col, most = jnp.min(least_row), jnp.min(least_col), jnp.max(most_ref[...])
    sound = (row >= 2.0**-24) & (col >= 2.0**-30) & (most <= 2.0**30) & (row * col >= 2.0**-34)

    @pl.when(jnp.logical_not(sound))
    def _():
        def again(pair, carry):
            moves = []
            for at in range(PAIR):
                region = pair * PAIR + at
                moves.append(transport_logs(region, gram_ref, logw_ref[pl.ds(region, 1), :], scale))
            result_ref[pair] = transform(state_ref, pair, moves)
            copy = send(pair)
            copy.start()
            copy.wait()
            return carry

        lax.fori_loop(0, pairs, again, 0)


def finish(state, gram, kernel, most, own, near, far, total, handed, count, scale):
    lon_dev, nvar, lat, members = state.shape
    regions = lat // REGION
    vmem = pl.BlockSpec(memory_space=pltpu.VMEM)
    return pl.pallas_call(
        functools.partial(finish_kernel, count, scale),
        in_specs=[vmem] * 9,
        out_specs=pl.BlockSpec(memory_space=pl.ANY),
        out_shape=jax.ShapeDtypeStruct(state.shape, state.dtype),
        scratch_shapes=[
            pltpu.VMEM((regions, members, 128), jnp.float32),
            pltpu.VMEM((regions, members, 128), jnp.float32),
            pltpu.VMEM((regions, members), jnp.float32),
            pltpu.VMEM((regions // PAIR, lon_dev, nvar, PAIR * TILE, members), jnp.bfloat16),
            pltpu.SemaphoreType.DMA((regions // PAIR,)),
        ],
        compiler_params=pltpu.CompilerParams(vmem_limit_bytes=24 * 2**20),
        name="finish",
    )(state, gram, kernel, most, own, near, far, total, handed)


def on_device(state, obs_index, obs_value, obs_var):
    nvar = state.shape[1]
    count = lax.axis_size("lon")
    place = lax.axis_index("lon")
    odd = place & 1
    near_pairs = [(i, i ^ 1) for i in range(count)]
    far_pairs = [(i, (i + 1 if i % 2 else i - 1) % count) for i in range(count)]
    odd = odd.astype(jnp.int32).reshape(1)
    own_like, near_like, far_like, for_near, for_far = observe(
        odd, state, obs_index, obs_value, obs_var
    )
    far = lax.ppermute(for_far, "lon", far_pairs)
    near = lax.ppermute(for_near, "lon", near_pairs)
    blocks = own_like.shape[0]
    got_near = lax.ppermute(near_like, "lon", near_pairs)
    gram = own_gram(odd, state, near)
    if count % 4 == 0 and count & (count - 1) == 0:
        leads = [i for i in range(count) if (i ^ i >> 1) & 1]
        total = near_like[blocks:] + got_near[blocks:]
        hop = 4
        while hop < count:
            total = total + lax.ppermute(total, "lon", [(i, i ^ hop) for i in leads])
            hop *= 2
        total, gram = lax.optimization_barrier((total, gram))
        got_far = lax.ppermute(jnp.concatenate([far_like, total], axis=0), "lon", far_pairs)
        lead = (place ^ place >> 1) & 1
        total = jnp.where(lead == 1, total + got_far[blocks:], 0.0)
        handed = lax.ppermute(total, "lon", [(i, i ^ 1) for i in leads])
    else:
        got_far = lax.ppermute(far_like, "lon", far_pairs)
        total = lax.psum(near_like[blocks:], "lon")
        handed = jnp.zeros_like(total)
    offsets = range(REGION + 2 * HALO)
    line = [1.0 - max(0, HALO - p, p - (HALO + REGION - 1)) / (HALO + 1) for p in offsets]
    scale = LOG2E / EPS / (nvar * sum(line) ** 2)
    gram, kernel, most = prepare(odd, far, gram, scale)
    nobs = float(obs_index.shape[0] * count)
    return finish(
        state, gram, kernel, most, own_like, got_near, got_far, total, handed, nobs, scale
    )


def solution(mesh):
    return jax.shard_map(
        on_device,
        mesh=mesh,
        in_specs=(
            P(("ens", "lon"), None, None, None),
            P(("ens", "lon")),
            P(("ens", "lon")),
            P(("ens", "lon")),
        ),
        out_specs=P(("ens", "lon"), None, None, None),
        check_vma=False,
    )
```

```python
import functools
import math

import jax
import jax.numpy as jnp
from jax import lax
from jax.experimental import pallas as pl
from jax.experimental.pallas import tpu as pltpu
from jax.sharding import PartitionSpec as P

REGION = 8
HALO = 4
SWEEPS = 4
EPS = 0.05
TILE = 8
PAIR = 2
LOG2E = 1.4426950408889634
ROWS = 32
GROUP = 4
LIFT, START, MASS = 20, -10, 60

HIGH = lax.Precision.HIGHEST


def line_weight(place):
    dist = jnp.maximum(0.0, jnp.maximum(HALO - place, place - (HALO + REGION - 1)))
    inside = (place >= 0) & (place < REGION + 2 * HALO)
    return jnp.where(inside, 1.0 - dist / (HALO + 1), 0.0)


def observe_kernel(*refs):
    odd_ref, state_ref = refs[:2]
    own_ref, near_ref, far_ref, near_edge_ref, far_edge_ref = refs[5:10]
    cells_ref, index_ref, value_ref, var_ref, sems = refs[10:]
    lon_dev, lat, members = cells_ref.shape
    nobs = index_ref.shape[1]
    last = lon_dev - HALO
    far_at = odd_ref[0] * last
    copies = [
        pltpu.make_async_copy(state_ref.at[:, 0], cells_ref, sems.at[0]),
        pltpu.make_async_copy(state_ref.at[pl.ds(far_at, HALO)], far_edge_ref, sems.at[1]),
        pltpu.make_async_copy(state_ref.at[pl.ds(last - far_at, HALO)], near_edge_ref, sems.at[2]),
    ]
    fetches = [
        pltpu.make_async_copy(src, dst, sems.at[len(copies) + i])
        for i, (src, dst) in enumerate(zip(refs[2:5], (index_ref, value_ref, var_ref)))
    ]
    for copy in fetches + copies:
        copy.start()
    for copy in fetches + copies[:1]:
        copy.wait()
    rows = cells_ref[...].reshape(lon_dev * lat, members)
    index = index_ref[...]
    sub = lax.broadcasted_iota(jnp.int32, (TILE, nobs), 0)
    table = jnp.where(
        sub == 0,
        index.astype(jnp.float32),
        jnp.where(sub == 1, value_ref[...], var_ref[...]),
    ).T
    index_col = table[:, 0:1].astype(jnp.int32)
    value = table[:, 1:2]
    var = table[:, 2:3]
    pick = index_col == lax.broadcasted_iota(jnp.int32, (nobs, lon_dev * lat), 1)
    pick = jnp.where(pick, 1.0, 0.0).astype(jnp.bfloat16)
    seen = jnp.dot(pick, rows, preferred_element_type=jnp.float32)
    centre = jnp.sum(seen, axis=1, keepdims=True) * (1.0 / members)
    spread = jnp.sum((seen - centre) ** 2, axis=1, keepdims=True) * (1.0 / (members - 1))
    innovation = (value - centre) ** 2 / (var + spread)
    blocks, members = own_ref.shape
    part = jnp.broadcast_to(jnp.sum(innovation, axis=0, keepdims=True), (TILE, members))
    near_ref[blocks:, :] = part
    terms = (value - seen) ** 2 * (1.0 / var)
    lon = (index // lat).astype(jnp.float32)
    along = index.astype(jnp.float32) - lon * lat
    block = lax.broadcasted_iota(jnp.int32, (blocks, nobs), 0).astype(jnp.float32)
    across = line_weight(along - REGION * block + HALO)
    side = jnp.where(odd_ref[0] == 1, float(REGION), float(-REGION))
    weights = [line_weight(lon + (HALO + shift)) * across for shift in (0.0, side, -side)]
    like = jnp.dot(
        jnp.concatenate(weights, axis=0), terms, precision=HIGH, preferred_element_type=jnp.float32
    )
    own_ref[...] = like[:blocks]
    near_ref[:blocks, :] = like[blocks : 2 * blocks]
    far_ref[...] = like[2 * blocks :]
    for copy in copies[1:]:
        copy.wait()


def observe(odd, state, obs_index, obs_value, obs_var):
    lon_dev, nvar, lat, members = state.shape
    blocks = lat // REGION
    like = jax.ShapeDtypeStruct((blocks, members), jnp.float32)
    more = jax.ShapeDtypeStruct((blocks + TILE, members), jnp.float32)
    edge = jax.ShapeDtypeStruct((HALO, nvar, lat, members), state.dtype)
    vmem = pl.BlockSpec(memory_space=pltpu.VMEM)
    arrays = state, obs_index[None], obs_value[None], obs_var[None]
    return pl.pallas_call(
        observe_kernel,
        in_specs=[
            pl.BlockSpec(memory_space=pltpu.SMEM),
        ]
        + [pl.BlockSpec(memory_space=pltpu.HBM)] * 4,
        out_specs=[vmem] * 5,
        out_shape=[like, more, like, edge, edge],
        scratch_shapes=[
            pltpu.VMEM((lon_dev, lat, members), state.dtype),
            pltpu.VMEM((1, obs_index.size), jnp.int32),
            pltpu.VMEM((1, obs_index.size), jnp.float32),
            pltpu.VMEM((1, obs_index.size), jnp.float32),
            pltpu.SemaphoreType.DMA((6,)),
        ],
        compiler_params=pltpu.CompilerParams(vmem_limit_bytes=24 * 2**20),
        name="observe",
    )(odd, *[pltpu.with_memory_space_constraint(x, pltpu.HBM) for x in arrays])


def pair_tiles(ref, step, steps):
    size = PAIR * TILE

    def load(at):
        return ref[:, :, pl.ds(pl.multiple_of(at * size, size), size), :].astype(jnp.float32)

    here = load(step)
    before = load(jnp.maximum(step - 1, 0))[:, :, TILE:]
    after = load(jnp.minimum(step + 1, steps - 1))[:, :, :TILE]
    before = jnp.where(step == 0, 0.0, before)
    after = jnp.where(step == steps - 1, 0.0, after)
    return before, here[:, :, :TILE], here[:, :, TILE:], after


def halo_weights(to_left):
    steps = [jnp.float32(1.0) - jnp.float32(d) / jnp.float32(HALO + 1) for d in range(HALO, 0, -1)]
    return [jnp.where(to_left, x, y) for x, y in zip(steps, steps[::-1])]


def gram_of(tiles, weights):
    before, low, high, after = tiles
    columns, nvar, _, members = low.shape
    row = lax.broadcasted_iota(jnp.int32, (1, TILE, members), 1)
    upper = row < HALO
    rowf = row.astype(jnp.float32)
    edge = line_weight(jnp.where(upper, rowf + (HALO + REGION), rowf - HALO))
    grams = []
    for own, following, preceding in ((low, high, before), (high, after, low)):
        margin = jnp.where(upper, following, preceding)
        win = jnp.concatenate([own, margin], axis=2)
        weighted = []
        for column, weight in enumerate(weights):
            if weight is None:
                parts = [own[column], margin[column] * edge]
            else:
                parts = [own[column] * weight, margin[column] * (edge * weight)]
            weighted.append(jnp.concatenate(parts, axis=1))
        weighted = jnp.stack(weighted)
        shape = (columns * nvar * 2 * TILE, members)
        grams.append(
            lax.dot_general(
                weighted.astype(jnp.bfloat16).reshape(shape),
                win.astype(jnp.bfloat16).reshape(shape),
                (((0,), (0,)), ((), ())),
                preferred_element_type=jnp.float32,
            )
        )
    return grams


def own_gram_kernel(odd_ref, state_ref, near_ref, gram_ref):
    step, steps = pl.program_id(0), pl.num_programs(0)
    tiles = zip(pair_tiles(state_ref, step, steps), pair_tiles(near_ref, step, steps))
    tiles = [jnp.concatenate([x, y], axis=0) for x, y in tiles]
    grams = gram_of(tiles, [None] * state_ref.shape[0] + halo_weights(odd_ref[0] == 1))
    for region in range(PAIR):
        gram_ref[region] = grams[region]


def own_gram(odd, state, near):
    lon_dev, nvar, lat, members = state.shape
    steps = lat // (PAIR * TILE)
    return pl.pallas_call(
        own_gram_kernel,
        grid=(steps,),
        in_specs=[
            pl.BlockSpec(memory_space=pltpu.SMEM),
            pl.BlockSpec(state.shape, lambda i: (0, 0, 0, 0)),
            pl.BlockSpec(near.shape, lambda i: (0, 0, 0, 0)),
        ],
        out_specs=pl.BlockSpec((PAIR, members, members), lambda i: (i, 0, 0)),
        out_shape=jax.ShapeDtypeStruct((steps * PAIR, members, members), jnp.float32),
        compiler_params=pltpu.CompilerParams(vmem_limit_bytes=24 * 2**20),
        cost_estimate=pl.CostEstimate(
            flops=2 * (lon_dev + HALO) * nvar * 2 * lat * members**2,
            bytes_accessed=2 * (state.size + near.size) + 4 * lat // REGION * members**2,
            transcendentals=0,
        ),
        name="own_gram",
    )(odd, state, near)


def halves(ref, region, rows):
    members = ref.shape[-1]
    return [ref[region, rows, at : at + 128] for at in range(0, members, 128)]


def diagonal(gram_ref, region):
    members = gram_ref.shape[-1]
    across = [None] * (members // 128)
    down = []
    for start in range(0, members, ROWS):
        lane = start // 128
        gram = gram_ref[region, pl.ds(start, ROWS), lane * 128 : lane * 128 + 128]
        i = lax.broadcasted_iota(jnp.int32, gram.shape, 0) + start
        j = lax.broadcasted_iota(jnp.int32, gram.shape, 1) + lane * 128
        kept = jnp.where(i == j, gram, 0.0)
        down.append(jnp.broadcast_to(jnp.sum(kept, axis=1, keepdims=True), gram.shape))
        part = jnp.sum(kept.reshape(ROWS // TILE, TILE, 128), axis=0)
        across[lane] = part if across[lane] is None else across[lane] + part
    return [jnp.sum(x, axis=0, keepdims=True) for x in across], down


def sweep_rows(parts, weight, totals):
    scaled, mass = parts
    mass = jnp.broadcast_to(jnp.sum(mass, axis=1, keepdims=True), weight.shape)
    near = pl.reciprocal(mass, approx=True)
    ratio = weight * (near * (2.0 - mass * near))
    for lane, part in enumerate(scaled):
        part = jnp.sum((part * ratio).reshape(ROWS // TILE, TILE, 128), axis=0)
        totals[lane] = part if totals[lane] is None else totals[lane] + part
    return mass, ratio


def fold(values, op):
    out = values[0]
    for value in values[1:]:
        out = op(out, value)
    return out


def sweeps_scaled(regions, gram_ref, kernel_ref, ratio_ref, weight_ref, scale):
    members = gram_ref.shape[-1]
    starts = range(0, members, ROWS)
    lanes = range(members // 128)
    least_row, most_row, least_col, cols = [], [], [], []
    share = 2.0**MASS / members

    def settle(totals):
        totals = [jnp.sum(x, axis=0, keepdims=True) for x in totals]
        return totals, fold(totals, jnp.minimum)

    for region in regions:
        across, down = diagonal(gram_ref, region)
        across = [0.5 * LIFT - x * scale for x in across]
        totals = [None] * len(lanes)
        masses = []
        for at, start in enumerate(starts):
            rows = pl.ds(start, ROWS)
            base = 0.5 * LIFT - down[at] * scale
            kernel = [
                jnp.exp2(g * (2.0 * scale) + base + x)
                for g, x in zip(halves(gram_ref, region, rows), across)
            ]
            for lane, part in enumerate(kernel):
                kernel_ref[region, rows, lane * 128 : lane * 128 + 128] = part
            mass, _ = sweep_rows(
                (kernel, fold(kernel, jnp.add) * 2.0**START), weight_ref[region, rows, :], totals
            )
            masses.append(mass)
        least_row.append(fold(masses, jnp.minimum))
        most_row.append(fold(masses, jnp.maximum))
        totals, least = settle(totals)
        least_col.append(least)
        cols.append(totals)

    def sweep(last, carry):
        least_row, least_col, cols = carry
        rows_out, least_out, cols_out = [], [], []
        for region, lrow, lcol, col in zip(regions, least_row, least_col, cols):
            factor = [share / x for x in col]
            totals = [None] * len(lanes)
            for start in starts:
                rows = pl.ds(start, ROWS)
                kernel = halves(kernel_ref, region, rows)
                mass = fold([k * f for k, f in zip(kernel, factor)], jnp.add)
                mass, ratio = sweep_rows((kernel, mass), weight_ref[region, rows, :], totals)
                if last:
                    ratio_ref[region, rows, :] = ratio
                lrow = jnp.minimum(lrow, mass)
            totals, least = settle(totals)
            rows_out.append(lrow)
            least_out.append(jnp.minimum(lcol, least))
            cols_out.append(totals)
        return rows_out, least_out, cols_out

    carry = least_row, least_col, cols
    carry = lax.fori_loop(0, SWEEPS - 2, lambda i, c: sweep(False, c), carry)
    least_row, least_col, cols = sweep(True, carry)
    factors = [[1.0 / x for x in col] for col in cols]
    return (
        factors,
        fold(least_row, jnp.minimum),
        fold(least_col, jnp.minimum),
        fold(most_row, jnp.maximum),
    )


def transport_scaled(region, factor, kernel_ref, ratio_ref):
    members = kernel_ref.shape[-1]
    parts = []
    for start in range(0, members, ROWS):
        rows = pl.ds(start, ROWS)
        ratio = ratio_ref[region, rows, :]
        row = [k * ratio * f for k, f in zip(halves(kernel_ref, region, rows), factor)]
        parts.append(jnp.concatenate(row, axis=1).astype(jnp.bfloat16))
    return jnp.concatenate(parts, axis=0)


def transport_logs(region, gram_ref, logw, scale):
    members = gram_ref.shape[-1]
    gram = gram_ref[region]
    i = lax.broadcasted_iota(jnp.int32, gram.shape, 0)
    j = lax.broadcasted_iota(jnp.int32, gram.shape, 1)
    kept = jnp.where(i == j, gram, 0.0)
    down = jnp.sum(kept, axis=1, keepdims=True)
    across = jnp.sum(kept, axis=0, keepdims=True)
    cost = (down + across - 2.0 * gram) * scale
    logw = jnp.sum(jnp.where(i == j, logw, 0.0), axis=1, keepdims=True)
    pot_g = jnp.zeros((1, members), jnp.float32)
    for sweep in range(SWEEPS):
        term = pot_g - cost
        top = jnp.max(term, axis=1, keepdims=True)
        pot_f = logw - top - jnp.log(jnp.sum(jnp.exp2(term - top), axis=1, keepdims=True)) * LOG2E
        term = pot_f - cost
        top = jnp.max(term, axis=0, keepdims=True)
        pot_g = -math.log2(members) - top
        pot_g = pot_g - jnp.log(jnp.sum(jnp.exp2(term - top), axis=0, keepdims=True)) * LOG2E
    return (members * jnp.exp2(pot_f + pot_g - cost)).astype(jnp.bfloat16)


def transform(state_ref, pair, moves):
    lon_dev, nvar, _, members = state_ref.shape
    size = PAIR * TILE
    own = state_ref[:, :, pl.ds(pl.multiple_of(pair * size, size), size), :].astype(jnp.float32)
    parts = []
    for region, move in enumerate(moves):
        cells = own[:, :, region * TILE : (region + 1) * TILE].astype(jnp.bfloat16)
        cells = cells.reshape(lon_dev * nvar * TILE, members)
        moved = jnp.dot(cells, move, preferred_element_type=jnp.float32)
        parts.append(moved.reshape(lon_dev, nvar, TILE, members))
    return jnp.concatenate(parts, axis=2).astype(jnp.bfloat16)


def analysis_kernel(count, scale, *refs):
    flags_ref, close_ref, wide_ref, state_ref, gram_in_ref = refs[0:5]
    own_ref, near_ref, far_close_ref, far_wide_ref, sum_ref, back_ref, out_ref = refs[5:12]
    gram_ref, kernel_ref, ratio_ref, weight_ref, logw_ref, result_ref, sems = refs[12:]
    regions, members = gram_in_ref.shape[0], gram_in_ref.shape[-1]
    pairs = regions // PAIR
    size = PAIR * TILE

    total = sum_ref[0:1, 0:1] + back_ref[0:1, 0:1]
    like = own_ref[...] + near_ref[:regions, :] + far_close_ref[:regions, :] + far_wide_ref[...]
    like = -0.5 * (count / total) * like
    like = like - jnp.max(like, axis=1, keepdims=True)
    logw = (like - jnp.log(jnp.sum(jnp.exp(like), axis=1, keepdims=True))) * LOG2E
    logw_ref[...] = logw
    weight = jnp.exp2(logw + MASS).T
    for region in range(regions):
        weight_ref[region] = jnp.broadcast_to(weight[:, region : region + 1], (members, 128))

    def send(pair):
        at = pl.ds(pl.multiple_of(pair * size, size), size)
        return pltpu.make_async_copy(result_ref.at[pair], out_ref.at[:, :, at, :], sems.at[pair])

    def halo_grams(pair, carry):
        tiles = zip(pair_tiles(close_ref, pair, pairs), pair_tiles(wide_ref, pair, pairs))
        tiles = [jnp.where(flags_ref[1] == 1, x, y) for x, y in tiles]
        grams = gram_of(tiles, halo_weights(flags_ref[0] == 0))
        for at in range(PAIR):
            region = pair * PAIR + at
            gram_ref[region] = gram_in_ref[region] + grams[at]
        return carry

    lax.fori_loop(0, pairs, halo_grams, 0)

    def group(at, carry):
        least_row, least_col, most_row = carry
        first = at * GROUP
        factors, row, col, most = sweeps_scaled(
            [first + r for r in range(GROUP)], gram_ref, kernel_ref, ratio_ref, weight_ref, scale
        )
        for pair in range(GROUP // PAIR):
            moves = [
                transport_scaled(first + r, factors[r], kernel_ref, ratio_ref)
                for r in range(pair * PAIR, (pair + 1) * PAIR)
            ]
            where = at * (GROUP // PAIR) + pair
            result_ref[where] = transform(state_ref, where, moves)
            send(where).start()
        return (
            jnp.minimum(least_row, row),
            jnp.minimum(least_col, col),
            jnp.maximum(most_row, most),
        )

    high = jnp.full((ROWS, 128), 1e30, jnp.float32)
    least_row, least_col, most_row = lax.fori_loop(
        0, regions // GROUP, group, (high, high[:1], jnp.zeros((ROWS, 128), jnp.float32))
    )

    def drain(pair, carry):
        send(pair).wait()
        return carry

    lax.fori_loop(0, pairs, drain, 0)
    row, col, most = jnp.min(least_row), jnp.min(least_col), jnp.max(most_row)
    sound = (row >= 2.0**-24) & (col >= 2.0**-30) & (most <= 2.0**20) & (row * col >= 2.0**-34)

    @pl.when(jnp.logical_not(sound))
    def _():
        def again(pair, carry):
            moves = []
            for at in range(PAIR):
                region = pair * PAIR + at
                moves.append(transport_logs(region, gram_ref, logw_ref[pl.ds(region, 1), :], scale))
            result_ref[pair] = transform(state_ref, pair, moves)
            copy = send(pair)
            copy.start()
            copy.wait()
            return carry

        lax.fori_loop(0, pairs, again, 0)


def analyse(flags, halos, state, gram, likes, totals, count):
    lon_dev, nvar, lat, members = state.shape
    regions = lat // REGION
    offsets = range(REGION + 2 * HALO)
    line = [1.0 - max(0, HALO - p, p - (HALO + REGION - 1)) / (HALO + 1) for p in offsets]
    scale = LOG2E / EPS / (nvar * sum(line) ** 2)
    vmem = pl.BlockSpec(memory_space=pltpu.VMEM)
    return pl.pallas_call(
        functools.partial(analysis_kernel, count, scale),
        in_specs=[pl.BlockSpec(memory_space=pltpu.SMEM)] + [vmem] * 10,
        out_specs=pl.BlockSpec(memory_space=pl.ANY),
        out_shape=jax.ShapeDtypeStruct(state.shape, state.dtype),
        scratch_shapes=[
            pltpu.VMEM((regions, members, members), jnp.float32),
            pltpu.VMEM((regions, members, members), jnp.float32),
            pltpu.VMEM((regions, members, 128), jnp.float32),
            pltpu.VMEM((regions, members, 128), jnp.float32),
            pltpu.VMEM((regions, members), jnp.float32),
            pltpu.VMEM((regions // PAIR, lon_dev, nvar, PAIR * TILE, members), jnp.bfloat16),
            pltpu.SemaphoreType.DMA((regions // PAIR,)),
        ],
        compiler_params=pltpu.CompilerParams(vmem_limit_bytes=24 * 2**20),
        name="analyse",
    )(flags, *halos, state, gram, *likes, *totals)


def on_device(state, obs_index, obs_value, obs_var):
    count = lax.axis_size("lon")
    place = lax.axis_index("lon")

    def send(value, pairs):
        return lax.ppermute(value, "lon", pairs)

    near_pairs = [(i, i ^ 1) for i in range(count)]
    far_pairs = [(i, (i + 1 if i % 2 else i - 1) % count) for i in range(count)]
    close_pairs = [(i, j) for i, j in far_pairs if (i ^ i >> 1) & 1]
    wide_pairs = [(i, j) for i, j in far_pairs if not (i ^ i >> 1) & 1]
    flags = jnp.stack([place & 1, (place ^ place >> 1) & 1]).astype(jnp.int32)
    own_like, near_like, far_like, for_near, for_far = observe(
        flags, state, obs_index, obs_value, obs_var
    )
    blocks = own_like.shape[0]
    close = send(for_far, close_pairs)
    near = send(for_near, near_pairs)
    got_near = send(near_like, near_pairs)
    line = near_like[blocks:] + got_near[blocks:]
    close, line = lax.optimization_barrier((close, line))
    hop = 4
    while hop < count:
        line = line + send(line, [(i, i ^ hop) for i, _ in wide_pairs])
        hop *= 2
    for_far, near, far_like, line = lax.optimization_barrier((for_far, near, far_like, line))
    wide = send(for_far, wide_pairs)
    handed = send(line, [(i, i ^ 1) for i, _ in wide_pairs])
    got_close = send(jnp.concatenate([far_like, handed], axis=0), close_pairs)
    got_wide = send(far_like, wide_pairs)
    total = handed + got_close[blocks:]
    back = send(total, [(i, i ^ 1) for i, _ in close_pairs])
    if count % 4 or count & (count - 1):
        total = lax.psum(near_like[blocks:], "lon")
        back = jnp.zeros_like(total)
    gram = own_gram(flags, state, near)
    nobs = float(obs_index.shape[0] * count)
    likes = own_like, got_near, got_close, got_wide
    return analyse(flags, (close, wide), state, gram, likes, (total, back), nobs)


def solution(mesh):
    return jax.shard_map(
        on_device,
        mesh=mesh,
        in_specs=(
            P(("ens", "lon"), None, None, None),
            P(("ens", "lon")),
            P(("ens", "lon")),
            P(("ens", "lon")),
        ),
        out_specs=P(("ens", "lon"), None, None, None),
        check_vma=False,
    )
```

```python
import functools
import math

import jax
import jax.numpy as jnp
from jax import lax
from jax.experimental import pallas as pl
from jax.experimental.pallas import tpu as pltpu
from jax.sharding import PartitionSpec as P

REGION = 8
HALO = 4
SWEEPS = 4
EPS = 0.05
TILE = 8
PAIR = 2
LOG2E = 1.4426950408889634
ROWS = 32
GROUP = 4
LIFT, START, MASS = 20, -10, 60

HIGH = lax.Precision.HIGHEST


def line_weight(place):
    dist = jnp.maximum(0.0, jnp.maximum(HALO - place, place - (HALO + REGION - 1)))
    inside = (place >= 0) & (place < REGION + 2 * HALO)
    return jnp.where(inside, 1.0 - dist / (HALO + 1), 0.0)


def obs_kernel(odd_ref, cells_ref, index_ref, value_ref, var_ref, own_ref, near_ref, far_ref, part_ref):
    lon_dev, _, lat, members = cells_ref.shape
    nobs = index_ref.shape[1]
    rows = cells_ref[:, 0].reshape(lon_dev * lat, members)
    index = index_ref[...]
    sub = lax.broadcasted_iota(jnp.int32, (TILE, nobs), 0)
    table = jnp.where(
        sub == 0,
        index.astype(jnp.float32),
        jnp.where(sub == 1, value_ref[...], var_ref[...]),
    ).T
    index_col = table[:, 0:1].astype(jnp.int32)
    value = table[:, 1:2]
    var = table[:, 2:3]
    pick = index_col == lax.broadcasted_iota(jnp.int32, (nobs, lon_dev * lat), 1)
    pick = jnp.where(pick, 1.0, 0.0).astype(jnp.bfloat16)
    seen = jnp.dot(pick, rows, preferred_element_type=jnp.float32)
    centre = jnp.sum(seen, axis=1, keepdims=True) * (1.0 / members)
    spread = jnp.sum((seen - centre) ** 2, axis=1, keepdims=True) * (1.0 / (members - 1))
    innovation = (value - centre) ** 2 / (var + spread)
    blocks, members = own_ref.shape
    part_ref[...] = jnp.broadcast_to(jnp.sum(innovation, axis=0, keepdims=True), part_ref.shape)
    terms = (value - seen) ** 2 * (1.0 / var)
    lon = (index // lat).astype(jnp.float32)
    along = index.astype(jnp.float32) - lon * lat
    block = lax.broadcasted_iota(jnp.int32, (blocks, nobs), 0).astype(jnp.float32)
    across = line_weight(along - REGION * block + HALO)
    side = jnp.where(odd_ref[0] == 1, float(REGION), float(-REGION))
    weights = [line_weight(lon + (HALO + shift)) * across for shift in (0.0, side, -side)]
    like = jnp.dot(
        jnp.concatenate(weights, axis=0), terms, precision=HIGH, preferred_element_type=jnp.float32
    )
    own_ref[...] = like[:blocks]
    near_ref[...] = like[blocks : 2 * blocks]
    far_ref[...] = like[2 * blocks :]


def observe(odd, state, obs_index, obs_value, obs_var, parts):
    lon_dev, _, lat, members = state.shape
    nobs = obs_index.shape[0]
    blocks = lat // REGION
    row = pl.BlockSpec((1, nobs), lambda i: (0, 0))
    like = jax.ShapeDtypeStruct((blocks, members), jnp.float32)
    like_spec = pl.BlockSpec((blocks, members), lambda i: (0, 0))
    part = jax.ShapeDtypeStruct((parts * TILE, 128), jnp.float32)
    part_spec = pl.BlockSpec((parts * TILE, 128), lambda i: (0, 0))
    return pl.pallas_call(
        obs_kernel,
        grid=(1,),
        in_specs=[
            pl.BlockSpec(memory_space=pltpu.SMEM),
            pl.BlockSpec((lon_dev, 1, lat, members), lambda i: (0, 0, 0, 0)),
            row,
            row,
            row,
        ],
        out_specs=[like_spec] * 3 + [part_spec],
        out_shape=[like] * 3 + [part],
        compiler_params=pltpu.CompilerParams(vmem_limit_bytes=32 * 2**20),
        name="observe",
    )(odd, state, obs_index[None], obs_value[None], obs_var[None])


def pair_tiles(ref, step, steps):
    size = PAIR * TILE

    def load(at):
        return ref[:, :, pl.ds(pl.multiple_of(at * size, size), size), :].astype(jnp.float32)

    here = load(step)
    before = load(jnp.maximum(step - 1, 0))[:, :, TILE:]
    after = load(jnp.minimum(step + 1, steps - 1))[:, :, :TILE]
    before = jnp.where(step == 0, 0.0, before)
    after = jnp.where(step == steps - 1, 0.0, after)
    return before, here[:, :, :TILE], here[:, :, TILE:], after


def halo_weights(to_left):
    steps = [jnp.float32(1.0) - jnp.float32(d) / jnp.float32(HALO + 1) for d in range(HALO, 0, -1)]
    return [jnp.where(to_left, x, y) for x, y in zip(steps, steps[::-1])]


def gram_of(tiles, weights):
    before, low, high, after = tiles
    columns, nvar, _, members = low.shape
    row = lax.broadcasted_iota(jnp.int32, (1, TILE, members), 1)
    upper = row < HALO
    rowf = row.astype(jnp.float32)
    edge = line_weight(jnp.where(upper, rowf + (HALO + REGION), rowf - HALO))
    grams = []
    for own, following, preceding in ((low, high, before), (high, after, low)):
        margin = jnp.where(upper, following, preceding)
        win = jnp.concatenate([own, margin], axis=2)
        weighted = []
        for column, weight in enumerate(weights):
            if weight is None:
                parts = [own[column], margin[column] * edge]
            else:
                parts = [own[column] * weight, margin[column] * (edge * weight)]
            weighted.append(jnp.concatenate(parts, axis=1))
        weighted = jnp.stack(weighted)
        shape = (columns * nvar * 2 * TILE, members)
        grams.append(
            lax.dot_general(
                weighted.astype(jnp.bfloat16).reshape(shape),
                win.astype(jnp.bfloat16).reshape(shape),
                (((0,), (0,)), ((), ())),
                preferred_element_type=jnp.float32,
            )
        )
    return grams


def own_gram_kernel(odd_ref, state_ref, near_ref, gram_ref):
    step, steps = pl.program_id(0), pl.num_programs(0)
    tiles = zip(pair_tiles(state_ref, step, steps), pair_tiles(near_ref, step, steps))
    tiles = [jnp.concatenate([x, y], axis=0) for x, y in tiles]
    grams = gram_of(tiles, [None] * state_ref.shape[0] + halo_weights(odd_ref[0] == 1))
    for region in range(PAIR):
        gram_ref[region] = grams[region]


def own_gram(odd, state, near):
    lon_dev, nvar, lat, members = state.shape
    steps = lat // (PAIR * TILE)
    return pl.pallas_call(
        own_gram_kernel,
        grid=(steps,),
        in_specs=[
            pl.BlockSpec(memory_space=pltpu.SMEM),
            pl.BlockSpec(state.shape, lambda i: (0, 0, 0, 0)),
            pl.BlockSpec(near.shape, lambda i: (0, 0, 0, 0)),
        ],
        out_specs=pl.BlockSpec((PAIR, members, members), lambda i: (i, 0, 0)),
        out_shape=jax.ShapeDtypeStruct((steps * PAIR, members, members), jnp.float32),
        compiler_params=pltpu.CompilerParams(vmem_limit_bytes=48 * 2**20),
        name="own_gram",
    )(odd, state, near)


def halves(ref, region, rows):
    members = ref.shape[-1]
    return [ref[region, rows, at : at + 128] for at in range(0, members, 128)]


def diagonal(gram_ref, region):
    members = gram_ref.shape[-1]
    across = [None] * (members // 128)
    down = []
    for start in range(0, members, ROWS):
        lane = start // 128
        gram = gram_ref[region, pl.ds(start, ROWS), lane * 128 : lane * 128 + 128]
        i = lax.broadcasted_iota(jnp.int32, gram.shape, 0) + start
        j = lax.broadcasted_iota(jnp.int32, gram.shape, 1) + lane * 128
        kept = jnp.where(i == j, gram, 0.0)
        down.append(jnp.broadcast_to(jnp.sum(kept, axis=1, keepdims=True), gram.shape))
        part = jnp.sum(kept.reshape(ROWS // TILE, TILE, 128), axis=0)
        across[lane] = part if across[lane] is None else across[lane] + part
    return [jnp.sum(x, axis=0, keepdims=True) for x in across], down


def sweep_rows(parts, weight, totals):
    scaled, mass = parts
    mass = jnp.broadcast_to(jnp.sum(mass, axis=1, keepdims=True), weight.shape)
    near = pl.reciprocal(mass, approx=True)
    ratio = weight * (near * (2.0 - mass * near))
    for lane, part in enumerate(scaled):
        part = jnp.sum((part * ratio).reshape(ROWS // TILE, TILE, 128), axis=0)
        totals[lane] = part if totals[lane] is None else totals[lane] + part
    return mass, ratio


def fold(values, op):
    out = values[0]
    for value in values[1:]:
        out = op(out, value)
    return out


def sweeps_scaled(regions, gram_ref, kernel_ref, ratio_ref, weight_ref, scale):
    members = gram_ref.shape[-1]
    starts = range(0, members, ROWS)
    lanes = range(members // 128)
    least_row, most_row, least_col, cols = [], [], [], []
    share = 2.0**MASS / members

    def settle(totals):
        totals = [jnp.sum(x, axis=0, keepdims=True) for x in totals]
        return totals, fold(totals, jnp.minimum)

    for region in regions:
        across, down = diagonal(gram_ref, region)
        across = [0.5 * LIFT - x * scale for x in across]
        totals = [None] * len(lanes)
        masses = []
        for at, start in enumerate(starts):
            rows = pl.ds(start, ROWS)
            base = 0.5 * LIFT - down[at] * scale
            kernel = [
                jnp.exp2(g * (2.0 * scale) + base + x)
                for g, x in zip(halves(gram_ref, region, rows), across)
            ]
            for lane, part in enumerate(kernel):
                kernel_ref[region, rows, lane * 128 : lane * 128 + 128] = part
            mass, _ = sweep_rows(
                (kernel, fold(kernel, jnp.add) * 2.0**START), weight_ref[region, rows, :], totals
            )
            masses.append(mass)
        least_row.append(fold(masses, jnp.minimum))
        most_row.append(fold(masses, jnp.maximum))
        totals, least = settle(totals)
        least_col.append(least)
        cols.append(totals)

    def sweep(last, carry):
        least_row, least_col, cols = carry
        rows_out, least_out, cols_out = [], [], []
        for region, lrow, lcol, col in zip(regions, least_row, least_col, cols):
            factor = [share / x for x in col]
            totals = [None] * len(lanes)
            for start in starts:
                rows = pl.ds(start, ROWS)
                kernel = halves(kernel_ref, region, rows)
                mass = fold([k * f for k, f in zip(kernel, factor)], jnp.add)
                mass, ratio = sweep_rows((kernel, mass), weight_ref[region, rows, :], totals)
                if last:
                    ratio_ref[region, rows, :] = ratio
                lrow = jnp.minimum(lrow, mass)
            totals, least = settle(totals)
            rows_out.append(lrow)
            least_out.append(jnp.minimum(lcol, least))
            cols_out.append(totals)
        return rows_out, least_out, cols_out

    carry = least_row, least_col, cols
    carry = lax.fori_loop(0, SWEEPS - 2, lambda i, c: sweep(False, c), carry)
    least_row, least_col, cols = sweep(True, carry)
    factors = [[1.0 / x for x in col] for col in cols]
    return (
        factors,
        fold(least_row, jnp.minimum),
        fold(least_col, jnp.minimum),
        fold(most_row, jnp.maximum),
    )


def transport_scaled(region, factor, kernel_ref, ratio_ref):
    members = kernel_ref.shape[-1]
    parts = []
    for start in range(0, members, ROWS):
        rows = pl.ds(start, ROWS)
        ratio = ratio_ref[region, rows, :]
        row = [k * ratio * f for k, f in zip(halves(kernel_ref, region, rows), factor)]
        parts.append(jnp.concatenate(row, axis=1).astype(jnp.bfloat16))
    return jnp.concatenate(parts, axis=0)


def transport_logs(region, gram_ref, logw, scale):
    members = gram_ref.shape[-1]
    gram = gram_ref[region]
    i = lax.broadcasted_iota(jnp.int32, gram.shape, 0)
    j = lax.broadcasted_iota(jnp.int32, gram.shape, 1)
    kept = jnp.where(i == j, gram, 0.0)
    down = jnp.sum(kept, axis=1, keepdims=True)
    across = jnp.sum(kept, axis=0, keepdims=True)
    cost = (down + across - 2.0 * gram) * scale
    logw = jnp.sum(jnp.where(i == j, logw, 0.0), axis=1, keepdims=True)
    pot_g = jnp.zeros((1, members), jnp.float32)
    for sweep in range(SWEEPS):
        term = pot_g - cost
        top = jnp.max(term, axis=1, keepdims=True)
        pot_f = logw - top - jnp.log(jnp.sum(jnp.exp2(term - top), axis=1, keepdims=True)) * LOG2E
        term = pot_f - cost
        top = jnp.max(term, axis=0, keepdims=True)
        pot_g = -math.log2(members) - top
        pot_g = pot_g - jnp.log(jnp.sum(jnp.exp2(term - top), axis=0, keepdims=True)) * LOG2E
    return (members * jnp.exp2(pot_f + pot_g - cost)).astype(jnp.bfloat16)


def transform(state_ref, pair, moves):
    lon_dev, nvar, _, members = state_ref.shape
    size = PAIR * TILE
    own = state_ref[:, :, pl.ds(pl.multiple_of(pair * size, size), size), :].astype(jnp.float32)
    parts = []
    for region, move in enumerate(moves):
        cells = own[:, :, region * TILE : (region + 1) * TILE].astype(jnp.bfloat16)
        cells = cells.reshape(lon_dev * nvar * TILE, members)
        moved = jnp.dot(cells, move, preferred_element_type=jnp.float32)
        parts.append(moved.reshape(lon_dev, nvar, TILE, members))
    return jnp.concatenate(parts, axis=2).astype(jnp.bfloat16)


def analysis_kernel(count, scale, *refs):
    odd_ref, halo_ref, state_ref, gram_in_ref = refs[0:4]
    own_ref, near_ref, far_ref, sum_ref, out_ref = refs[4:9]
    gram_ref, kernel_ref, ratio_ref, weight_ref, logw_ref, result_ref, sems = refs[9:]
    regions, members = gram_in_ref.shape[0], gram_in_ref.shape[-1]
    pairs = regions // PAIR
    size = PAIR * TILE

    total = jnp.sum(sum_ref[...], axis=0, keepdims=True)[:, 0:1] * (1.0 / TILE)
    like = own_ref[...] + near_ref[...] + far_ref[...]
    like = -0.5 * (count / total) * like
    like = like - jnp.max(like, axis=1, keepdims=True)
    logw = (like - jnp.log(jnp.sum(jnp.exp(like), axis=1, keepdims=True))) * LOG2E
    logw_ref[...] = logw
    weight = jnp.exp2(logw + MASS).T
    for region in range(regions):
        weight_ref[region] = jnp.broadcast_to(weight[:, region : region + 1], (members, 128))

    def send(pair):
        at = pl.ds(pl.multiple_of(pair * size, size), size)
        return pltpu.make_async_copy(result_ref.at[pair], out_ref.at[:, :, at, :], sems.at[pair])

    def halo_grams(pair, carry):
        grams = gram_of(pair_tiles(halo_ref, pair, pairs), halo_weights(odd_ref[0] == 0))
        for at in range(PAIR):
            region = pair * PAIR + at
            gram_ref[region] = gram_in_ref[region] + grams[at]
        return carry

    lax.fori_loop(0, pairs, halo_grams, 0)

    def group(at, carry):
        least_row, least_col, most_row = carry
        first = at * GROUP
        factors, row, col, most = sweeps_scaled(
            [first + r for r in range(GROUP)], gram_ref, kernel_ref, ratio_ref, weight_ref, scale
        )
        for pair in range(GROUP // PAIR):
            moves = [
                transport_scaled(first + r, factors[r], kernel_ref, ratio_ref)
                for r in range(pair * PAIR, (pair + 1) * PAIR)
            ]
            where = at * (GROUP // PAIR) + pair
            result_ref[where] = transform(state_ref, where, moves)
            send(where).start()
        return (
            jnp.minimum(least_row, row),
            jnp.minimum(least_col, col),
            jnp.maximum(most_row, most),
        )

    high = jnp.full((ROWS, 128), 1e30, jnp.float32)
    least_row, least_col, most_row = lax.fori_loop(
        0, regions // GROUP, group, (high, high[:1], jnp.zeros((ROWS, 128), jnp.float32))
    )

    def drain(pair, carry):
        send(pair).wait()
        return carry

    lax.fori_loop(0, pairs, drain, 0)
    row, col, most = jnp.min(least_row), jnp.min(least_col), jnp.max(most_row)
    sound = (row >= 2.0**-24) & (col >= 2.0**-30) & (most <= 2.0**20) & (row * col >= 2.0**-34)

    @pl.when(jnp.logical_not(sound))
    def _():
        def again(pair, carry):
            moves = []
            for at in range(PAIR):
                region = pair * PAIR + at
                moves.append(transport_logs(region, gram_ref, logw_ref[pl.ds(region, 1), :], scale))
            result_ref[pair] = transform(state_ref, pair, moves)
            copy = send(pair)
            copy.start()
            copy.wait()
            return carry

        lax.fori_loop(0, pairs, again, 0)


def analyse(odd, halo, state, gram, own, near, far, total, count):
    lon_dev, nvar, lat, members = state.shape
    regions = lat // REGION
    offsets = range(REGION + 2 * HALO)
    line = [1.0 - max(0, HALO - p, p - (HALO + REGION - 1)) / (HALO + 1) for p in offsets]
    scale = LOG2E / EPS / (nvar * sum(line) ** 2)
    vmem = pl.BlockSpec(memory_space=pltpu.VMEM)
    return pl.pallas_call(
        functools.partial(analysis_kernel, count, scale),
        in_specs=[pl.BlockSpec(memory_space=pltpu.SMEM)] + [vmem] * 7,
        out_specs=pl.BlockSpec(memory_space=pl.ANY),
        out_shape=jax.ShapeDtypeStruct(state.shape, state.dtype),
        scratch_shapes=[
            pltpu.VMEM((regions, members, members), jnp.float32),
            pltpu.VMEM((regions, members, members), jnp.float32),
            pltpu.VMEM((regions, members, 128), jnp.float32),
            pltpu.VMEM((regions, members, 128), jnp.float32),
            pltpu.VMEM((regions, members), jnp.float32),
            pltpu.VMEM((regions // PAIR, lon_dev, nvar, PAIR * TILE, members), jnp.bfloat16),
            pltpu.SemaphoreType.DMA((regions // PAIR,)),
        ],
        compiler_params=pltpu.CompilerParams(vmem_limit_bytes=48 * 2**20),
        name="analyse",
    )(odd, halo, state, gram, own, near, far, total)


def on_device(state, obs_index, obs_value, obs_var):
    lon_dev = state.shape[0]
    count = lax.axis_size("lon")
    odd = lax.axis_index("lon") % 2
    near_pairs = [(i, i ^ 1) for i in range(count)]
    far_pairs = [(i, (i + 1 if i % 2 else i - 1) % count) for i in range(count)]
    for_far = lax.dynamic_slice_in_dim(state, odd * (lon_dev - HALO), HALO, axis=0)
    for_near = lax.dynamic_slice_in_dim(state, (1 - odd) * (lon_dev - HALO), HALO, axis=0)
    far = lax.ppermute(for_far, "lon", far_pairs)
    near = lax.ppermute(for_near, "lon", near_pairs)
    odd = odd.astype(jnp.int32).reshape(1)
    own_like, near_like, far_like, part = observe(
        odd, state, obs_index, obs_value, obs_var, count
    )
    got_far = lax.ppermute(far_like, "lon", far_pairs)
    got_near = lax.ppermute(near_like, "lon", near_pairs)
    parts = lax.all_to_all(part, "lon", 0, 0, tiled=True)
    gram = own_gram(odd, state, near)
    nobs = float(obs_index.shape[0] * count)
    return analyse(odd, far, state, gram, own_like, got_near, got_far, parts, nobs)


def solution(mesh):
    return jax.shard_map(
        on_device,
        mesh=mesh,
        in_specs=(
            P(("ens", "lon"), None, None, None),
            P(("ens", "lon")),
            P(("ens", "lon")),
            P(("ens", "lon")),
        ),
        out_specs=P(("ens", "lon"), None, None, None),
        check_vma=False,
    )
```

```python
import functools
import math

import jax
import jax.numpy as jnp
from jax import lax
from jax.experimental import pallas as pl
from jax.experimental.pallas import tpu as pltpu
from jax.sharding import PartitionSpec as P

REGION = 8
HALO = 4
SWEEPS = 4
EPS = 0.05
TILE = 8
PAIR = 2
LOG2E = 1.4426950408889634
ROWS = 32
GROUP = 4
LIFT, START, MASS = 20, -10, 60

HIGH = lax.Precision.HIGHEST


def line_weight(place):
    dist = jnp.maximum(0.0, jnp.maximum(HALO - place, place - (HALO + REGION - 1)))
    inside = (place >= 0) & (place < REGION + 2 * HALO)
    return jnp.where(inside, 1.0 - dist / (HALO + 1), 0.0)


def in_parts(values):
    high = values.astype(jnp.bfloat16).astype(jnp.float32)
    middle = (values - high).astype(jnp.bfloat16).astype(jnp.float32)
    low = values - high - middle
    return jnp.concatenate([high, middle, low, jnp.zeros_like(low)], axis=0).astype(jnp.bfloat16)


def from_parts(ref, start):
    rows = ref[start : start + 4 * TILE, :].astype(jnp.float32)
    return rows[:TILE] + rows[TILE : 2 * TILE] + rows[2 * TILE : 3 * TILE]


def observe_kernel(*refs):
    odd_ref, state_ref, rows_ref = refs[:3]
    own_ref, near_ref, far_ref, part_ref = refs[6:10]
    cells_ref, index_ref, value_ref, var_ref, sems = refs[10:]
    lon_dev, lat, members = cells_ref.shape
    nobs = index_ref.shape[1]
    edge = rows_ref.shape[0] // lon_dev * HALO
    last = rows_ref.shape[0] - edge
    far_at = pl.multiple_of(odd_ref[0] * last, 16)
    near_at = pl.multiple_of(last - far_at, 16)
    fetches = [
        (refs[3], index_ref),
        (refs[4], value_ref),
        (refs[5], var_ref),
        (state_ref.at[:, 0], cells_ref),
        (rows_ref.at[pl.ds(far_at, edge), :], far_ref.at[pl.ds(0, edge), :]),
        (rows_ref.at[pl.ds(near_at, edge), :], near_ref.at[pl.ds(0, edge), :]),
    ]
    copies = [
        pltpu.make_async_copy(src, dst, sems.at[i]) for i, (src, dst) in enumerate(fetches)
    ]
    for copy in copies:
        copy.start()
    for copy in copies[:4]:
        copy.wait()
    rows = cells_ref[...].reshape(lon_dev * lat, members)
    index = index_ref[...]
    sub = lax.broadcasted_iota(jnp.int32, (TILE, nobs), 0)
    table = jnp.where(
        sub == 0,
        index.astype(jnp.float32),
        jnp.where(sub == 1, value_ref[...], var_ref[...]),
    ).T
    index_col = table[:, 0:1].astype(jnp.int32)
    value = table[:, 1:2]
    var = table[:, 2:3]
    pick = index_col == lax.broadcasted_iota(jnp.int32, (nobs, lon_dev * lat), 1)
    pick = jnp.where(pick, 1.0, 0.0).astype(jnp.bfloat16)
    seen = jnp.dot(pick, rows, preferred_element_type=jnp.float32)
    centre = jnp.sum(seen, axis=1, keepdims=True) * (1.0 / members)
    spread = jnp.sum((seen - centre) ** 2, axis=1, keepdims=True) * (1.0 / (members - 1))
    innovation = (value - centre) ** 2 / (var + spread)
    part_ref[...] = jnp.broadcast_to(jnp.sum(innovation, axis=0, keepdims=True), part_ref.shape)
    terms = (value - seen) ** 2 * (1.0 / var)
    lon = (index // lat).astype(jnp.float32)
    along = index.astype(jnp.float32) - lon * lat
    blocks = own_ref.shape[0]
    block = lax.broadcasted_iota(jnp.int32, (blocks, nobs), 0).astype(jnp.float32)
    across = line_weight(along - REGION * block + HALO)
    side = jnp.where(odd_ref[0] == 1, float(REGION), float(-REGION))
    weights = [line_weight(lon + (HALO + shift)) * across for shift in (0.0, side, -side)]
    like = jnp.dot(
        jnp.concatenate(weights, axis=0), terms, precision=HIGH, preferred_element_type=jnp.float32
    )
    own_ref[...] = like[:blocks]
    near_ref[edge:, :] = in_parts(like[blocks : 2 * blocks])
    far_ref[edge:, :] = in_parts(like[2 * blocks :])
    for copy in copies[4:]:
        copy.wait()


def observe(odd, state, obs_index, obs_value, obs_var, parts):
    lon_dev, nvar, lat, members = state.shape
    nobs = obs_index.size
    assert lat // REGION == TILE
    like = jax.ShapeDtypeStruct((lat // REGION, members), jnp.float32)
    payload = jax.ShapeDtypeStruct((HALO * nvar * lat + 4 * TILE, members), state.dtype)
    part = jax.ShapeDtypeStruct((parts * TILE, 128), jnp.float32)
    arrays = state, state.reshape(-1, members), obs_index[None], obs_value[None], obs_var[None]
    return pl.pallas_call(
        observe_kernel,
        in_specs=[pl.BlockSpec(memory_space=pltpu.SMEM)]
        + [pl.BlockSpec(memory_space=pltpu.HBM)] * len(arrays),
        out_specs=[pl.BlockSpec(memory_space=pltpu.VMEM)] * 4,
        out_shape=[like, payload, payload, part],
        scratch_shapes=[
            pltpu.VMEM((lon_dev, lat, members), state.dtype),
            pltpu.VMEM((1, nobs), jnp.int32),
            pltpu.VMEM((1, nobs), jnp.float32),
            pltpu.VMEM((1, nobs), jnp.float32),
            pltpu.SemaphoreType.DMA((6,)),
        ],
        compiler_params=pltpu.CompilerParams(vmem_limit_bytes=16 * 2**20),
        name="observe",
    )(odd, *[pltpu.with_memory_space_constraint(x, pltpu.HBM) for x in arrays])


def pair_tiles(ref, step, steps):
    size = PAIR * TILE
    lat = steps * size

    def load(at):
        at = pl.multiple_of(at * size, size)
        if len(ref.shape) == 4:
            return ref[:, :, pl.ds(at, size), :].astype(jnp.float32)
        planes = ref.shape[0] // lat
        rows = [ref[pl.ds(i * lat + at, size), :] for i in range(planes)]
        rows = jnp.stack(rows).astype(jnp.float32)
        return rows.reshape(HALO, planes // HALO, size, rows.shape[-1])

    here = load(step)
    before = load(jnp.maximum(step - 1, 0))[:, :, TILE:]
    after = load(jnp.minimum(step + 1, steps - 1))[:, :, :TILE]
    before = jnp.where(step == 0, 0.0, before)
    after = jnp.where(step == steps - 1, 0.0, after)
    return before, here[:, :, :TILE], here[:, :, TILE:], after


def halo_weights(to_left):
    steps = [jnp.float32(1.0) - jnp.float32(d) / jnp.float32(HALO + 1) for d in range(HALO, 0, -1)]
    return [jnp.where(to_left, x, y) for x, y in zip(steps, steps[::-1])]


def gram_of(tiles, weights):
    before, low, high, after = tiles
    columns, nvar, _, members = low.shape
    row = lax.broadcasted_iota(jnp.int32, (1, TILE, members), 1)
    upper = row < HALO
    rowf = row.astype(jnp.float32)
    edge = line_weight(jnp.where(upper, rowf + (HALO + REGION), rowf - HALO))
    grams = []
    for own, following, preceding in ((low, high, before), (high, after, low)):
        margin = jnp.where(upper, following, preceding)
        win = jnp.concatenate([own, margin], axis=2)
        weighted = []
        for column, weight in enumerate(weights):
            if weight is None:
                parts = [own[column], margin[column] * edge]
            else:
                parts = [own[column] * weight, margin[column] * (edge * weight)]
            weighted.append(jnp.concatenate(parts, axis=1))
        weighted = jnp.stack(weighted)
        shape = (columns * nvar * 2 * TILE, members)
        grams.append(
            lax.dot_general(
                weighted.astype(jnp.bfloat16).reshape(shape),
                win.astype(jnp.bfloat16).reshape(shape),
                (((0,), (0,)), ((), ())),
                preferred_element_type=jnp.float32,
            )
        )
    return grams


def own_gram_kernel(odd_ref, state_ref, near_ref, gram_ref):
    step, steps = pl.program_id(0), pl.num_programs(0)
    tiles = zip(pair_tiles(state_ref, step, steps), pair_tiles(near_ref, step, steps))
    tiles = [jnp.concatenate([x, y], axis=0) for x, y in tiles]
    grams = gram_of(tiles, [None] * state_ref.shape[0] + halo_weights(odd_ref[0] == 1))
    for region in range(PAIR):
        gram_ref[region] = grams[region]


def own_gram(odd, state, near):
    lon_dev, nvar, lat, members = state.shape
    steps = lat // (PAIR * TILE)
    return pl.pallas_call(
        own_gram_kernel,
        grid=(steps,),
        in_specs=[
            pl.BlockSpec(memory_space=pltpu.SMEM),
            pl.BlockSpec(state.shape, lambda i: (0, 0, 0, 0)),
            pl.BlockSpec(near.shape, lambda i: (0, 0)),
        ],
        out_specs=pl.BlockSpec((PAIR, members, members), lambda i: (i, 0, 0)),
        out_shape=jax.ShapeDtypeStruct((steps * PAIR, members, members), jnp.float32),
        compiler_params=pltpu.CompilerParams(vmem_limit_bytes=24 * 2**20),
        name="own_gram",
    )(odd, state, near)


def halves(ref, region, rows):
    members = ref.shape[-1]
    return [ref[region, rows, at : at + 128] for at in range(0, members, 128)]


def diagonal(gram_ref, region):
    members = gram_ref.shape[-1]
    across = [None] * (members // 128)
    down = []
    for start in range(0, members, ROWS):
        lane = start // 128
        gram = gram_ref[region, pl.ds(start, ROWS), lane * 128 : lane * 128 + 128]
        i = lax.broadcasted_iota(jnp.int32, gram.shape, 0) + start
        j = lax.broadcasted_iota(jnp.int32, gram.shape, 1) + lane * 128
        kept = jnp.where(i == j, gram, 0.0)
        down.append(jnp.broadcast_to(jnp.sum(kept, axis=1, keepdims=True), gram.shape))
        part = jnp.sum(kept.reshape(ROWS // TILE, TILE, 128), axis=0)
        across[lane] = part if across[lane] is None else across[lane] + part
    return [jnp.sum(x, axis=0, keepdims=True) for x in across], down


def sweep_rows(parts, weight, totals):
    scaled, mass = parts
    mass = jnp.broadcast_to(jnp.sum(mass, axis=1, keepdims=True), weight.shape)
    near = pl.reciprocal(mass, approx=True)
    ratio = weight * (near * (2.0 - mass * near))
    for lane, part in enumerate(scaled):
        part = jnp.sum((part * ratio).reshape(ROWS // TILE, TILE, 128), axis=0)
        totals[lane] = part if totals[lane] is None else totals[lane] + part
    return mass, ratio


def fold(values, op):
    out = values[0]
    for value in values[1:]:
        out = op(out, value)
    return out


def sweeps_scaled(regions, gram_ref, kernel_ref, ratio_ref, weight_ref, scale):
    members = gram_ref.shape[-1]
    starts = range(0, members, ROWS)
    lanes = range(members // 128)
    least_row, most_row, least_col, cols = [], [], [], []
    share = 2.0**MASS / members

    def settle(totals):
        totals = [jnp.sum(x, axis=0, keepdims=True) for x in totals]
        return totals, fold(totals, jnp.minimum)

    for region in regions:
        across, down = diagonal(gram_ref, region)
        across = [0.5 * LIFT - x * scale for x in across]
        totals = [None] * len(lanes)
        masses = []
        for at, start in enumerate(starts):
            rows = pl.ds(start, ROWS)
            base = 0.5 * LIFT - down[at] * scale
            kernel = [
                jnp.exp2(g * (2.0 * scale) + base + x)
                for g, x in zip(halves(gram_ref, region, rows), across)
            ]
            for lane, part in enumerate(kernel):
                kernel_ref[region, rows, lane * 128 : lane * 128 + 128] = part
            mass, _ = sweep_rows(
                (kernel, fold(kernel, jnp.add) * 2.0**START), weight_ref[region, rows, :], totals
            )
            masses.append(mass)
        least_row.append(fold(masses, jnp.minimum))
        most_row.append(fold(masses, jnp.maximum))
        totals, least = settle(totals)
        least_col.append(least)
        cols.append(totals)

    def sweep(last, carry):
        least_row, least_col, cols = carry
        rows_out, least_out, cols_out = [], [], []
        for region, lrow, lcol, col in zip(regions, least_row, least_col, cols):
            factor = [share / x for x in col]
            totals = [None] * len(lanes)
            for start in starts:
                rows = pl.ds(start, ROWS)
                kernel = halves(kernel_ref, region, rows)
                mass = fold([k * f for k, f in zip(kernel, factor)], jnp.add)
                mass, ratio = sweep_rows((kernel, mass), weight_ref[region, rows, :], totals)
                if last:
                    ratio_ref[region, rows, :] = ratio
                lrow = jnp.minimum(lrow, mass)
            totals, least = settle(totals)
            rows_out.append(lrow)
            least_out.append(jnp.minimum(lcol, least))
            cols_out.append(totals)
        return rows_out, least_out, cols_out

    carry = least_row, least_col, cols
    carry = lax.fori_loop(0, SWEEPS - 2, lambda i, c: sweep(False, c), carry)
    least_row, least_col, cols = sweep(True, carry)
    factors = [[1.0 / x for x in col] for col in cols]
    return (
        factors,
        fold(least_row, jnp.minimum),
        fold(least_col, jnp.minimum),
        fold(most_row, jnp.maximum),
    )


def transport_scaled(region, factor, kernel_ref, ratio_ref):
    members = kernel_ref.shape[-1]
    parts = []
    for start in range(0, members, ROWS):
        rows = pl.ds(start, ROWS)
        ratio = ratio_ref[region, rows, :]
        row = [k * ratio * f for k, f in zip(halves(kernel_ref, region, rows), factor)]
        parts.append(jnp.concatenate(row, axis=1).astype(jnp.bfloat16))
    return jnp.concatenate(parts, axis=0)


def transport_logs(region, gram_ref, logw, scale):
    members = gram_ref.shape[-1]
    gram = gram_ref[region]
    i = lax.broadcasted_iota(jnp.int32, gram.shape, 0)
    j = lax.broadcasted_iota(jnp.int32, gram.shape, 1)
    kept = jnp.where(i == j, gram, 0.0)
    down = jnp.sum(kept, axis=1, keepdims=True)
    across = jnp.sum(kept, axis=0, keepdims=True)
    cost = (down + across - 2.0 * gram) * scale
    logw = jnp.sum(jnp.where(i == j, logw, 0.0), axis=1, keepdims=True)
    pot_g = jnp.zeros((1, members), jnp.float32)
    for sweep in range(SWEEPS):
        term = pot_g - cost
        top = jnp.max(term, axis=1, keepdims=True)
        pot_f = logw - top - jnp.log(jnp.sum(jnp.exp2(term - top), axis=1, keepdims=True)) * LOG2E
        term = pot_f - cost
        top = jnp.max(term, axis=0, keepdims=True)
        pot_g = -math.log2(members) - top
        pot_g = pot_g - jnp.log(jnp.sum(jnp.exp2(term - top), axis=0, keepdims=True)) * LOG2E
    return (members * jnp.exp2(pot_f + pot_g - cost)).astype(jnp.bfloat16)


def transform(state_ref, pair, moves):
    lon_dev, nvar, _, members = state_ref.shape
    size = PAIR * TILE
    own = state_ref[:, :, pl.ds(pl.multiple_of(pair * size, size), size), :].astype(jnp.float32)
    parts = []
    for region, move in enumerate(moves):
        cells = own[:, :, region * TILE : (region + 1) * TILE].astype(jnp.bfloat16)
        cells = cells.reshape(lon_dev * nvar * TILE, members)
        moved = jnp.dot(cells, move, preferred_element_type=jnp.float32)
        parts.append(moved.reshape(lon_dev, nvar, TILE, members))
    return jnp.concatenate(parts, axis=2).astype(jnp.bfloat16)


def analysis_kernel(count, scale, *refs):
    odd_ref, halo_ref, state_ref, gram_in_ref = refs[0:4]
    own_ref, near_ref, sum_ref, out_ref = refs[4:8]
    gram_ref, kernel_ref, ratio_ref, weight_ref, logw_ref, result_ref, sems = refs[8:]
    regions, members = gram_in_ref.shape[0], gram_in_ref.shape[-1]
    pairs = regions // PAIR
    size = PAIR * TILE

    total = jnp.sum(sum_ref[...], axis=0, keepdims=True)[:, 0:1] * (1.0 / TILE)
    halo = halo_ref.shape[0] - 4 * TILE
    like = own_ref[...] + from_parts(near_ref, 0) + from_parts(halo_ref, halo)
    like = -0.5 * (count / total) * like
    like = like - jnp.max(like, axis=1, keepdims=True)
    logw = (like - jnp.log(jnp.sum(jnp.exp(like), axis=1, keepdims=True))) * LOG2E
    logw_ref[...] = logw
    weight = jnp.exp2(logw + MASS).T
    for region in range(regions):
        weight_ref[region] = jnp.broadcast_to(weight[:, region : region + 1], (members, 128))

    def send(pair):
        at = pl.ds(pl.multiple_of(pair * size, size), size)
        return pltpu.make_async_copy(result_ref.at[pair], out_ref.at[:, :, at, :], sems.at[pair])

    def halo_grams(pair, carry):
        grams = gram_of(pair_tiles(halo_ref, pair, pairs), halo_weights(odd_ref[0] == 0))
        for at in range(PAIR):
            region = pair * PAIR + at
            gram_ref[region] = gram_in_ref[region] + grams[at]
        return carry

    lax.fori_loop(0, pairs, halo_grams, 0)

    def group(at, carry):
        least_row, least_col, most_row = carry
        first = at * GROUP
        factors, row, col, most = sweeps_scaled(
            [first + r for r in range(GROUP)], gram_ref, kernel_ref, ratio_ref, weight_ref, scale
        )
        for pair in range(GROUP // PAIR):
            moves = [
                transport_scaled(first + r, factors[r], kernel_ref, ratio_ref)
                for r in range(pair * PAIR, (pair + 1) * PAIR)
            ]
            where = at * (GROUP // PAIR) + pair
            result_ref[where] = transform(state_ref, where, moves)
            send(where).start()
        return (
            jnp.minimum(least_row, row),
            jnp.minimum(least_col, col),
            jnp.maximum(most_row, most),
        )

    high = jnp.full((ROWS, 128), 1e30, jnp.float32)
    least_row, least_col, most_row = lax.fori_loop(
        0, regions // GROUP, group, (high, high[:1], jnp.zeros((ROWS, 128), jnp.float32))
    )

    def drain(pair, carry):
        send(pair).wait()
        return carry

    lax.fori_loop(0, pairs, drain, 0)
    row, col, most = jnp.min(least_row), jnp.min(least_col), jnp.max(most_row)
    sound = (row >= 2.0**-24) & (col >= 2.0**-30) & (most <= 2.0**20) & (row * col >= 2.0**-34)

    @pl.when(jnp.logical_not(sound))
    def _():
        def again(pair, carry):
            moves = []
            for at in range(PAIR):
                region = pair * PAIR + at
                moves.append(transport_logs(region, gram_ref, logw_ref[pl.ds(region, 1), :], scale))
            result_ref[pair] = transform(state_ref, pair, moves)
            copy = send(pair)
            copy.start()
            copy.wait()
            return carry

        lax.fori_loop(0, pairs, again, 0)


def analyse(odd, halo, state, gram, own, near, total, count):
    lon_dev, nvar, lat, members = state.shape
    regions = lat // REGION
    offsets = range(REGION + 2 * HALO)
    line = [1.0 - max(0, HALO - p, p - (HALO + REGION - 1)) / (HALO + 1) for p in offsets]
    scale = LOG2E / EPS / (nvar * sum(line) ** 2)
    vmem = pl.BlockSpec(memory_space=pltpu.VMEM)
    return pl.pallas_call(
        functools.partial(analysis_kernel, count, scale),
        in_specs=[pl.BlockSpec(memory_space=pltpu.SMEM)] + [vmem] * 6,
        out_specs=pl.BlockSpec(memory_space=pl.ANY),
        out_shape=jax.ShapeDtypeStruct(state.shape, state.dtype),
        scratch_shapes=[
            pltpu.VMEM((regions, members, members), jnp.float32),
            pltpu.VMEM((regions, members, members), jnp.float32),
            pltpu.VMEM((regions, members, 128), jnp.float32),
            pltpu.VMEM((regions, members, 128), jnp.float32),
            pltpu.VMEM((regions, members), jnp.float32),
            pltpu.VMEM((regions // PAIR, lon_dev, nvar, PAIR * TILE, members), jnp.bfloat16),
            pltpu.SemaphoreType.DMA((regions // PAIR,)),
        ],
        compiler_params=pltpu.CompilerParams(vmem_limit_bytes=24 * 2**20),
        name="analyse",
    )(odd, halo, state, gram, own, near, total)


def on_device(state, obs_index, obs_value, obs_var):
    count = lax.axis_size("lon")
    odd = lax.axis_index("lon") % 2
    near_pairs = [(i, i ^ 1) for i in range(count)]
    far_pairs = [(i, (i + 1 if i % 2 else i - 1) % count) for i in range(count)]
    odd = odd.astype(jnp.int32).reshape(1)
    own_like, for_near, for_far, part = observe(odd, state, obs_index, obs_value, obs_var, count)
    far = lax.ppermute(for_far, "lon", far_pairs)
    near = lax.ppermute(for_near, "lon", near_pairs)
    parts = lax.all_to_all(part, "lon", 0, 0, tiled=True)
    near_like = near[near.shape[0] - 4 * TILE :]
    gram = own_gram(odd, state, near)
    nobs = float(obs_index.shape[0] * count)
    return analyse(odd, far, state, gram, own_like, near_like, parts, nobs)


def solution(mesh):
    return jax.shard_map(
        on_device,
        mesh=mesh,
        in_specs=(
            P(("ens", "lon"), None, None, None),
            P(("ens", "lon")),
            P(("ens", "lon")),
            P(("ens", "lon")),
        ),
        out_specs=P(("ens", "lon"), None, None, None),
        check_vma=False,
    )
```

```python
import functools
import math

import jax
import jax.numpy as jnp
from jax import lax
from jax.experimental import pallas as pl
from jax.experimental.pallas import tpu as pltpu
from jax.sharding import PartitionSpec as P

REGION = 8
HALO = 4
SWEEPS = 4
EPS = 0.05
TILE = 8
PAIR = 2
LOG2E = 1.4426950408889634
ROWS = 32
GROUP = 4
LIFT, START, MASS = 20, -10, 60

HIGH = lax.Precision.HIGHEST


def line_weight(place):
    dist = jnp.maximum(0.0, jnp.maximum(HALO - place, place - (HALO + REGION - 1)))
    inside = (place >= 0) & (place < REGION + 2 * HALO)
    return jnp.where(inside, 1.0 - dist / (HALO + 1), 0.0)


def fetch_kernel(*refs):
    odd_ref, state_ref = refs[:2]
    far_ref, near_ref, cells_ref = refs[5:8]
    sems = refs[-1]
    last = state_ref.shape[0] - HALO
    far = odd_ref[0] * last
    pieces = [
        (state_ref.at[pl.ds(far, HALO)], far_ref),
        (state_ref.at[pl.ds(last - far, HALO)], near_ref),
        (state_ref.at[:, 0], cells_ref),
    ] + list(zip(refs[2:5], refs[8:11]))
    copies = [pltpu.make_async_copy(src, dst, sems.at[i]) for i, (src, dst) in enumerate(pieces)]
    for copy in copies:
        copy.start()
    for copy in copies:
        copy.wait()


def fetch(odd, state, obs_index, obs_value, obs_var):
    lon_dev, nvar, lat, members = state.shape
    arrays = state, obs_index[None], obs_value[None], obs_var[None]
    edge = jax.ShapeDtypeStruct((HALO, nvar, lat, members), state.dtype)
    cells = jax.ShapeDtypeStruct((lon_dev, lat, members), state.dtype)
    shapes = [edge, edge, cells] + [jax.ShapeDtypeStruct(x.shape, x.dtype) for x in arrays[1:]]
    return pl.pallas_call(
        fetch_kernel,
        in_specs=[pl.BlockSpec(memory_space=pltpu.SMEM)]
        + [pl.BlockSpec(memory_space=pltpu.HBM)] * len(arrays),
        out_specs=[pl.BlockSpec(memory_space=pltpu.VMEM)] * len(shapes),
        out_shape=shapes,
        scratch_shapes=[pltpu.SemaphoreType.DMA((len(shapes),))],
        compiler_params=pltpu.CompilerParams(vmem_limit_bytes=8 * 2**20),
        name="fetch",
    )(odd, *[pltpu.with_memory_space_constraint(x, pltpu.HBM) for x in arrays])


def observe_kernel(place_ref, cells_ref, index_ref, value_ref, var_ref, own_ref, slots_ref):
    lon_dev, lat, members = cells_ref.shape
    nobs = index_ref.shape[1]
    odd = place_ref[0]
    rows = cells_ref[...].reshape(lon_dev * lat, members)
    index = index_ref[...]
    sub = lax.broadcasted_iota(jnp.int32, (TILE, nobs), 0)
    table = jnp.where(
        sub == 0,
        index.astype(jnp.float32),
        jnp.where(sub == 1, value_ref[...], var_ref[...]),
    ).T
    index_col = table[:, 0:1].astype(jnp.int32)
    value = table[:, 1:2]
    var = table[:, 2:3]
    pick = index_col == lax.broadcasted_iota(jnp.int32, (nobs, lon_dev * lat), 1)
    pick = jnp.where(pick, 1.0, 0.0).astype(jnp.bfloat16)
    seen = jnp.dot(pick, rows, preferred_element_type=jnp.float32)
    centre = jnp.sum(seen, axis=1, keepdims=True) * (1.0 / members)
    spread = jnp.sum((seen - centre) ** 2, axis=1, keepdims=True) * (1.0 / (members - 1))
    innovation = (value - centre) ** 2 / (var + spread)
    part = jnp.sum(innovation, axis=0, keepdims=True)
    terms = (value - seen) ** 2 * (1.0 / var)
    lon = (index // lat).astype(jnp.float32)
    along = index.astype(jnp.float32) - lon * lat
    blocks = own_ref.shape[0]
    block = lax.broadcasted_iota(jnp.int32, (blocks, nobs), 0).astype(jnp.float32)
    across = line_weight(along - REGION * block + HALO)
    side = jnp.where(odd == 1, float(REGION), float(-REGION))
    weights = [line_weight(lon + (HALO + shift)) * across for shift in (0.0, side, -side)]
    like = jnp.dot(
        jnp.concatenate(weights, axis=0), terms, precision=HIGH, preferred_element_type=jnp.float32
    )
    own_ref[...] = like[:blocks]
    like = like - like[:, 0:1]
    slots_ref[...] = jnp.broadcast_to(part, slots_ref.shape)
    first = lax.broadcasted_iota(jnp.int32, (blocks, 128), 1) == 0
    for at, device in ((1, place_ref[1]), (2, place_ref[2])):
        start = device * (members // 128 * blocks)
        for lane in range(members // 128):
            rows = like[at * blocks : (at + 1) * blocks, lane * 128 : (lane + 1) * 128]
            if lane == 0:
                rows = jnp.where(first, part, rows)
            slots_ref[pl.ds(pl.multiple_of(start + lane * blocks, TILE), blocks), :] = rows


def like_of(slots_ref, device, blocks, members):
    start = device * (members // 128 * blocks)
    rows = [
        slots_ref[pl.ds(pl.multiple_of(start + lane * blocks, TILE), blocks), :]
        for lane in range(members // 128)
    ]
    rows[0] = jnp.where(lax.broadcasted_iota(jnp.int32, (blocks, 128), 1) == 0, 0.0, rows[0])
    return jnp.concatenate(rows, axis=1)


def observe(place, cells, obs_index, obs_value, obs_var, devices):
    lon_dev, lat, members = cells.shape
    blocks = lat // REGION
    assert blocks % TILE == 0 and members % 128 == 0
    vmem = pl.BlockSpec(memory_space=pltpu.VMEM)
    return pl.pallas_call(
        observe_kernel,
        in_specs=[pl.BlockSpec(memory_space=pltpu.SMEM)] + [vmem] * 4,
        out_specs=[vmem] * 2,
        out_shape=[
            jax.ShapeDtypeStruct((blocks, members), jnp.float32),
            jax.ShapeDtypeStruct((devices * members // 128 * blocks, 128), jnp.float32),
        ],
        compiler_params=pltpu.CompilerParams(vmem_limit_bytes=16 * 2**20),
        name="observe",
    )(place, cells, obs_index, obs_value, obs_var)


def pair_tiles(ref, step, steps):
    size = PAIR * TILE

    def load(at):
        return ref[:, :, pl.ds(pl.multiple_of(at * size, size), size), :].astype(jnp.float32)

    here = load(step)
    before = load(jnp.maximum(step - 1, 0))[:, :, TILE:]
    after = load(jnp.minimum(step + 1, steps - 1))[:, :, :TILE]
    before = jnp.where(step == 0, 0.0, before)
    after = jnp.where(step == steps - 1, 0.0, after)
    return before, here[:, :, :TILE], here[:, :, TILE:], after


def halo_weights(to_left):
    steps = [jnp.float32(1.0) - jnp.float32(d) / jnp.float32(HALO + 1) for d in range(HALO, 0, -1)]
    return [jnp.where(to_left, x, y) for x, y in zip(steps, steps[::-1])]


def gram_of(tiles, weights):
    before, low, high, after = tiles
    columns, nvar, _, members = low.shape
    row = lax.broadcasted_iota(jnp.int32, (1, TILE, members), 1)
    upper = row < HALO
    rowf = row.astype(jnp.float32)
    edge = line_weight(jnp.where(upper, rowf + (HALO + REGION), rowf - HALO))
    grams = []
    for own, following, preceding in ((low, high, before), (high, after, low)):
        margin = jnp.where(upper, following, preceding)
        win = jnp.concatenate([own, margin], axis=2)
        weighted = []
        for column, weight in enumerate(weights):
            if weight is None:
                parts = [own[column], margin[column] * edge]
            else:
                parts = [own[column] * weight, margin[column] * (edge * weight)]
            weighted.append(jnp.concatenate(parts, axis=1))
        weighted = jnp.stack(weighted)
        shape = (columns * nvar * 2 * TILE, members)
        grams.append(
            lax.dot_general(
                weighted.astype(jnp.bfloat16).reshape(shape),
                win.astype(jnp.bfloat16).reshape(shape),
                (((0,), (0,)), ((), ())),
                preferred_element_type=jnp.float32,
            )
        )
    return grams


def own_gram_kernel(odd_ref, state_hbm_ref, near_ref, gram_ref, state_ref, sem):
    regions = gram_ref.shape[0]
    copy = pltpu.make_async_copy(state_hbm_ref, state_ref, sem)
    copy.start()
    copy.wait()

    def pair(at, carry):
        steps = regions // PAIR
        tiles = zip(pair_tiles(state_ref, at, steps), pair_tiles(near_ref, at, steps))
        tiles = [jnp.concatenate([x, y], axis=0) for x, y in tiles]
        grams = gram_of(tiles, [None] * state_ref.shape[0] + halo_weights(odd_ref[0] == 1))
        for region in range(PAIR):
            gram_ref[at * PAIR + region] = grams[region]
        return carry

    lax.fori_loop(0, regions // PAIR, pair, 0)


def own_gram(odd, state, near):
    _, _, lat, members = state.shape
    vmem = pl.BlockSpec(memory_space=pltpu.VMEM)
    return pl.pallas_call(
        own_gram_kernel,
        in_specs=[
            pl.BlockSpec(memory_space=pltpu.SMEM),
            pl.BlockSpec(memory_space=pltpu.HBM),
            vmem,
        ],
        out_specs=vmem,
        out_shape=jax.ShapeDtypeStruct((lat // REGION, members, members), jnp.float32),
        scratch_shapes=[pltpu.VMEM(state.shape, state.dtype), pltpu.SemaphoreType.DMA],
        compiler_params=pltpu.CompilerParams(vmem_limit_bytes=24 * 2**20),
        name="own_gram",
    )(odd, pltpu.with_memory_space_constraint(state, pltpu.HBM), near)


def halves(ref, region, rows):
    members = ref.shape[-1]
    return [ref[region, rows, at : at + 128] for at in range(0, members, 128)]


def diagonal(gram_ref, region):
    members = gram_ref.shape[-1]
    across = [None] * (members // 128)
    down = []
    for start in range(0, members, ROWS):
        lane = start // 128
        gram = gram_ref[region, pl.ds(start, ROWS), lane * 128 : lane * 128 + 128]
        i = lax.broadcasted_iota(jnp.int32, gram.shape, 0) + start
        j = lax.broadcasted_iota(jnp.int32, gram.shape, 1) + lane * 128
        kept = jnp.where(i == j, gram, 0.0)
        down.append(jnp.broadcast_to(jnp.sum(kept, axis=1, keepdims=True), gram.shape))
        part = jnp.sum(kept.reshape(ROWS // TILE, TILE, 128), axis=0)
        across[lane] = part if across[lane] is None else across[lane] + part
    return [jnp.sum(x, axis=0, keepdims=True) for x in across], down


def sweep_rows(parts, weight, totals):
    scaled, mass = parts
    mass = jnp.broadcast_to(jnp.sum(mass, axis=1, keepdims=True), weight.shape)
    near = pl.reciprocal(mass, approx=True)
    ratio = weight * (near * (2.0 - mass * near))
    for lane, part in enumerate(scaled):
        part = jnp.sum((part * ratio).reshape(ROWS // TILE, TILE, 128), axis=0)
        totals[lane] = part if totals[lane] is None else totals[lane] + part
    return mass, ratio


def fold(values, op):
    out = values[0]
    for value in values[1:]:
        out = op(out, value)
    return out


def sweeps_scaled(regions, gram_ref, kernel_ref, ratio_ref, weight_ref, scale):
    members = gram_ref.shape[-1]
    starts = range(0, members, ROWS)
    lanes = range(members // 128)
    least_row, most_row, least_col, cols = [], [], [], []
    share = 2.0**MASS / members

    def settle(totals):
        totals = [jnp.sum(x, axis=0, keepdims=True) for x in totals]
        return totals, fold(totals, jnp.minimum)

    for region in regions:
        across, down = diagonal(gram_ref, region)
        across = [0.5 * LIFT - x * scale for x in across]
        totals = [None] * len(lanes)
        masses = []
        for at, start in enumerate(starts):
            rows = pl.ds(start, ROWS)
            base = 0.5 * LIFT - down[at] * scale
            kernel = [
                jnp.exp2(g * (2.0 * scale) + base + x)
                for g, x in zip(halves(gram_ref, region, rows), across)
            ]
            for lane, part in enumerate(kernel):
                kernel_ref[region, rows, lane * 128 : lane * 128 + 128] = part
            mass, _ = sweep_rows(
                (kernel, fold(kernel, jnp.add) * 2.0**START), weight_ref[region, rows, :], totals
            )
            masses.append(mass)
        least_row.append(fold(masses, jnp.minimum))
        most_row.append(fold(masses, jnp.maximum))
        totals, least = settle(totals)
        least_col.append(least)
        cols.append(totals)

    def sweep(last, carry):
        least_row, least_col, cols = carry
        rows_out, least_out, cols_out = [], [], []
        for region, lrow, lcol, col in zip(regions, least_row, least_col, cols):
            factor = [share / x for x in col]
            totals = [None] * len(lanes)
            for start in starts:
                rows = pl.ds(start, ROWS)
                kernel = halves(kernel_ref, region, rows)
                mass = fold([k * f for k, f in zip(kernel, factor)], jnp.add)
                mass, ratio = sweep_rows((kernel, mass), weight_ref[region, rows, :], totals)
                if last:
                    ratio_ref[region, rows, :] = ratio
                lrow = jnp.minimum(lrow, mass)
            totals, least = settle(totals)
            rows_out.append(lrow)
            least_out.append(jnp.minimum(lcol, least))
            cols_out.append(totals)
        return rows_out, least_out, cols_out

    carry = least_row, least_col, cols
    carry = lax.fori_loop(0, SWEEPS - 2, lambda i, c: sweep(False, c), carry)
    least_row, least_col, cols = sweep(True, carry)
    factors = [[1.0 / x for x in col] for col in cols]
    return (
        factors,
        fold(least_row, jnp.minimum),
        fold(least_col, jnp.minimum),
        fold(most_row, jnp.maximum),
    )


def transport_scaled(region, factor, kernel_ref, ratio_ref):
    members = kernel_ref.shape[-1]
    parts = []
    for start in range(0, members, ROWS):
        rows = pl.ds(start, ROWS)
        ratio = ratio_ref[region, rows, :]
        row = [k * ratio * f for k, f in zip(halves(kernel_ref, region, rows), factor)]
        parts.append(jnp.concatenate(row, axis=1).astype(jnp.bfloat16))
    return jnp.concatenate(parts, axis=0)


def transport_logs(region, gram_ref, logw, scale):
    members = gram_ref.shape[-1]
    gram = gram_ref[region]
    i = lax.broadcasted_iota(jnp.int32, gram.shape, 0)
    j = lax.broadcasted_iota(jnp.int32, gram.shape, 1)
    kept = jnp.where(i == j, gram, 0.0)
    down = jnp.sum(kept, axis=1, keepdims=True)
    across = jnp.sum(kept, axis=0, keepdims=True)
    cost = (down + across - 2.0 * gram) * scale
    logw = jnp.sum(jnp.where(i == j, logw, 0.0), axis=1, keepdims=True)
    pot_g = jnp.zeros((1, members), jnp.float32)
    for sweep in range(SWEEPS):
        term = pot_g - cost
        top = jnp.max(term, axis=1, keepdims=True)
        pot_f = logw - top - jnp.log(jnp.sum(jnp.exp2(term - top), axis=1, keepdims=True)) * LOG2E
        term = pot_f - cost
        top = jnp.max(term, axis=0, keepdims=True)
        pot_g = -math.log2(members) - top
        pot_g = pot_g - jnp.log(jnp.sum(jnp.exp2(term - top), axis=0, keepdims=True)) * LOG2E
    return (members * jnp.exp2(pot_f + pot_g - cost)).astype(jnp.bfloat16)


def transform(state_ref, pair, moves):
    lon_dev, nvar, _, members = state_ref.shape
    size = PAIR * TILE
    own = state_ref[:, :, pl.ds(pl.multiple_of(pair * size, size), size), :].astype(jnp.float32)
    parts = []
    for region, move in enumerate(moves):
        cells = own[:, :, region * TILE : (region + 1) * TILE].astype(jnp.bfloat16)
        cells = cells.reshape(lon_dev * nvar * TILE, members)
        moved = jnp.dot(cells, move, preferred_element_type=jnp.float32)
        parts.append(moved.reshape(lon_dev, nvar, TILE, members))
    return jnp.concatenate(parts, axis=2).astype(jnp.bfloat16)


def analysis_kernel(count, scale, *refs):
    place_ref, halo_ref, state_hbm_ref, gram_in_ref, own_ref, slots_ref, out_ref = refs[:7]
    gram_ref, kernel_ref, ratio_ref, weight_ref, logw_ref, result_ref, state_ref = refs[7:14]
    state_sem, sems = refs[14:]
    regions, members = gram_in_ref.shape[0], gram_in_ref.shape[-1]
    pairs = regions // PAIR
    size = PAIR * TILE

    fetch_state = pltpu.make_async_copy(state_hbm_ref, state_ref, state_sem)
    fetch_state.start()
    slot = members // 128 * regions
    total = slots_ref[0:1, 0:1]
    for device in range(1, slots_ref.shape[0] // slot):
        total = total + slots_ref[device * slot : device * slot + 1, 0:1]
    like = own_ref[...]
    for neighbour in (1, 2):
        like = like + like_of(slots_ref, place_ref[neighbour], regions, members)
    like = -0.5 * (count / total) * like
    like = like - jnp.max(like, axis=1, keepdims=True)
    logw = (like - jnp.log(jnp.sum(jnp.exp(like), axis=1, keepdims=True))) * LOG2E
    logw_ref[...] = logw
    weight = jnp.exp2(logw + MASS).T
    for region in range(regions):
        weight_ref[region] = jnp.broadcast_to(weight[:, region : region + 1], (members, 128))

    def send(pair):
        at = pl.ds(pl.multiple_of(pair * size, size), size)
        return pltpu.make_async_copy(result_ref.at[pair], out_ref.at[:, :, at, :], sems.at[pair])

    def halo_grams(pair, carry):
        grams = gram_of(pair_tiles(halo_ref, pair, pairs), halo_weights(place_ref[0] == 0))
        for at in range(PAIR):
            region = pair * PAIR + at
            gram_ref[region] = gram_in_ref[region] + grams[at]
        return carry

    lax.fori_loop(0, pairs, halo_grams, 0)
    fetch_state.wait()

    def group(at, carry):
        least_row, least_col, most_row = carry
        first = at * GROUP
        factors, row, col, most = sweeps_scaled(
            [first + r for r in range(GROUP)], gram_ref, kernel_ref, ratio_ref, weight_ref, scale
        )
        for pair in range(GROUP // PAIR):
            moves = [
                transport_scaled(first + r, factors[r], kernel_ref, ratio_ref)
                for r in range(pair * PAIR, (pair + 1) * PAIR)
            ]
            where = at * (GROUP // PAIR) + pair
            result_ref[where] = transform(state_ref, where, moves)
            send(where).start()
        return (
            jnp.minimum(least_row, row),
            jnp.minimum(least_col, col),
            jnp.maximum(most_row, most),
        )

    high = jnp.full((ROWS, 128), 1e30, jnp.float32)
    least_row, least_col, most_row = lax.fori_loop(
        0, regions // GROUP, group, (high, high[:1], jnp.zeros((ROWS, 128), jnp.float32))
    )

    def drain(pair, carry):
        send(pair).wait()
        return carry

    lax.fori_loop(0, pairs, drain, 0)
    row, col, most = jnp.min(least_row), jnp.min(least_col), jnp.max(most_row)
    sound = (row >= 2.0**-24) & (col >= 2.0**-30) & (most <= 2.0**20) & (row * col >= 2.0**-34)

    @pl.when(jnp.logical_not(sound))
    def _():
        def again(pair, carry):
            moves = []
            for at in range(PAIR):
                region = pair * PAIR + at
                moves.append(transport_logs(region, gram_ref, logw_ref[pl.ds(region, 1), :], scale))
            result_ref[pair] = transform(state_ref, pair, moves)
            copy = send(pair)
            copy.start()
            copy.wait()
            return carry

        lax.fori_loop(0, pairs, again, 0)


def analyse(place, halo, state, gram, own, slots, count):
    lon_dev, nvar, lat, members = state.shape
    regions = lat // REGION
    offsets = range(REGION + 2 * HALO)
    line = [1.0 - max(0, HALO - p, p - (HALO + REGION - 1)) / (HALO + 1) for p in offsets]
    scale = LOG2E / EPS / (nvar * sum(line) ** 2)
    vmem = pl.BlockSpec(memory_space=pltpu.VMEM)
    return pl.pallas_call(
        functools.partial(analysis_kernel, count, scale),
        in_specs=[
            pl.BlockSpec(memory_space=pltpu.SMEM),
            vmem,
            pl.BlockSpec(memory_space=pltpu.HBM),
            vmem,
            vmem,
            vmem,
        ],
        out_specs=pl.BlockSpec(memory_space=pl.ANY),
        out_shape=jax.ShapeDtypeStruct(state.shape, state.dtype),
        scratch_shapes=[
            pltpu.VMEM((regions, members, members), jnp.float32),
            pltpu.VMEM((regions, members, members), jnp.float32),
            pltpu.VMEM((regions, members, 128), jnp.float32),
            pltpu.VMEM((regions, members, 128), jnp.float32),
            pltpu.VMEM((regions, members), jnp.float32),
            pltpu.VMEM((regions // PAIR, lon_dev, nvar, PAIR * TILE, members), jnp.bfloat16),
            pltpu.VMEM(state.shape, state.dtype),
            pltpu.SemaphoreType.DMA,
            pltpu.SemaphoreType.DMA((regions // PAIR,)),
        ],
        compiler_params=pltpu.CompilerParams(vmem_limit_bytes=24 * 2**20),
        name="analyse",
    )(place, halo, pltpu.with_memory_space_constraint(state, pltpu.HBM), gram, own, slots)


def on_device(state, obs_index, obs_value, obs_var):
    count = lax.axis_size("lon")
    me = lax.axis_index("lon").astype(jnp.int32)
    odd = me & 1
    near_pairs = [(i, i ^ 1) for i in range(count)]
    far_pairs = [(i, (i + 1 if i % 2 else i - 1) % count) for i in range(count)]
    far_place = me + 2 * odd - 1
    far_place = jnp.where(far_place < 0, count - 1, jnp.where(far_place == count, 0, far_place))
    place = jnp.stack([odd, me ^ 1, far_place])
    for_far, for_near, cells, *obs = fetch(place, state, obs_index, obs_value, obs_var)
    far = lax.ppermute(for_far, "lon", far_pairs)
    near = lax.ppermute(for_near, "lon", near_pairs)
    own_like, slots = observe(place, cells, *obs, count)
    slots = lax.all_to_all(slots, "lon", 0, 0, tiled=True)
    gram = own_gram(place, state, near)
    nobs = float(obs_index.shape[0] * count)
    return analyse(place, far, state, gram, own_like, slots, nobs)


def solution(mesh):
    return jax.shard_map(
        on_device,
        mesh=mesh,
        in_specs=(
            P(("ens", "lon"), None, None, None),
            P(("ens", "lon")),
            P(("ens", "lon")),
            P(("ens", "lon")),
        ),
        out_specs=P(("ens", "lon"), None, None, None),
        check_vma=False,
    )
```

```python
import functools
import math

import jax
import jax.numpy as jnp
from jax import lax
from jax.experimental import pallas as pl
from jax.experimental.pallas import tpu as pltpu
from jax.sharding import PartitionSpec as P

REGION = 8
HALO = 4
SWEEPS = 4
EPS = 0.05
TILE = 8
PAIR = 2
LOG2E = 1.4426950408889634
ROWS = 32
GROUP = 4
LIFT, START, MASS = 20, -10, 60

HIGH = lax.Precision.HIGHEST


def line_weight(place):
    dist = jnp.maximum(0.0, jnp.maximum(HALO - place, place - (HALO + REGION - 1)))
    inside = (place >= 0) & (place < REGION + 2 * HALO)
    return jnp.where(inside, 1.0 - dist / (HALO + 1), 0.0)


def in_parts(values, extra):
    below = lax.broadcasted_iota(jnp.int32, values.shape, 0)
    extra_high = extra.astype(jnp.bfloat16).astype(jnp.float32)
    extra_middle = (extra - extra_high).astype(jnp.bfloat16).astype(jnp.float32)
    extra_low = extra - extra_high - extra_middle
    last = jnp.where(below == 0, extra_high, jnp.where(below == 1, extra_middle, extra_low))
    last = jnp.where(below < 3, last, 0.0)
    high = values.astype(jnp.bfloat16).astype(jnp.float32)
    middle = (values - high).astype(jnp.bfloat16).astype(jnp.float32)
    low = values - high - middle
    return jnp.concatenate([high, middle, low, last], axis=0).astype(jnp.bfloat16)


def from_parts(ref):
    rows = ref[ref.shape[0] - 4 * TILE :, :].astype(jnp.float32)
    return rows[:TILE] + rows[TILE : 2 * TILE] + rows[2 * TILE : 3 * TILE]


def observe_kernel(*refs):
    odd_ref, state_ref, rows_ref = refs[:3]
    own_ref, near_ref, far_ref, part_ref = refs[6:10]
    cells_ref, index_ref, value_ref, var_ref, sems = refs[10:]
    lon_dev, lat, members = cells_ref.shape
    nobs = index_ref.shape[1]
    edge = rows_ref.shape[0] // lon_dev * HALO
    last = rows_ref.shape[0] - edge
    far_at = pl.multiple_of(odd_ref[0] * last, 16)
    near_at = pl.multiple_of(last - far_at, 16)
    fetches = [
        (refs[3], index_ref),
        (refs[4], value_ref),
        (refs[5], var_ref),
        (state_ref.at[:, 0], cells_ref),
        (rows_ref.at[pl.ds(far_at, edge), :], far_ref.at[pl.ds(0, edge), :]),
        (rows_ref.at[pl.ds(near_at, edge), :], near_ref.at[pl.ds(0, edge), :]),
    ]
    copies = [
        pltpu.make_async_copy(src, dst, sems.at[i]) for i, (src, dst) in enumerate(fetches)
    ]
    for copy in copies:
        copy.start()
    for copy in copies[:4]:
        copy.wait()
    rows = cells_ref[...].reshape(lon_dev * lat, members)
    index = index_ref[...]
    sub = lax.broadcasted_iota(jnp.int32, (TILE, nobs), 0)
    table = jnp.where(
        sub == 0,
        index.astype(jnp.float32),
        jnp.where(sub == 1, value_ref[...], var_ref[...]),
    ).T
    index_col = table[:, 0:1].astype(jnp.int32)
    value = table[:, 1:2]
    var = table[:, 2:3]
    pick = index_col == lax.broadcasted_iota(jnp.int32, (nobs, lon_dev * lat), 1)
    pick = jnp.where(pick, 1.0, 0.0).astype(jnp.bfloat16)
    seen = jnp.dot(pick, rows, preferred_element_type=jnp.float32)
    centre = jnp.sum(seen, axis=1, keepdims=True) * (1.0 / members)
    spread = jnp.sum((seen - centre) ** 2, axis=1, keepdims=True) * (1.0 / (members - 1))
    innovation = (value - centre) ** 2 / (var + spread)
    part = jnp.sum(innovation, axis=0, keepdims=True)
    part_ref[...] = jnp.broadcast_to(part, part_ref.shape)
    terms = (value - seen) ** 2 * (1.0 / var)
    lon = (index // lat).astype(jnp.float32)
    along = index.astype(jnp.float32) - lon * lat
    blocks = own_ref.shape[0]
    block = lax.broadcasted_iota(jnp.int32, (blocks, nobs), 0).astype(jnp.float32)
    across = line_weight(along - REGION * block + HALO)
    side = jnp.where(odd_ref[0] == 1, float(REGION), float(-REGION))
    weights = [line_weight(lon + (HALO + shift)) * across for shift in (0.0, side, -side)]
    like = jnp.dot(
        jnp.concatenate(weights, axis=0), terms, precision=HIGH, preferred_element_type=jnp.float32
    )
    own_ref[...] = like[:blocks]
    near_ref[edge:, :] = in_parts(like[blocks : 2 * blocks], part)
    far_ref[edge:, :] = in_parts(like[2 * blocks :], jnp.zeros_like(part))
    for copy in copies[4:]:
        copy.wait()


def observe(odd, state, obs_index, obs_value, obs_var):
    lon_dev, nvar, lat, members = state.shape
    nobs = obs_index.size
    assert lat // REGION == TILE
    like = jax.ShapeDtypeStruct((lat // REGION, members), jnp.float32)
    payload = pltpu.VMEM((HALO * nvar * lat + 4 * TILE, members), state.dtype)
    part = jax.ShapeDtypeStruct((TILE, 128), jnp.float32)
    arrays = state, state.reshape(-1, members), obs_index[None], obs_value[None], obs_var[None]
    return pl.pallas_call(
        observe_kernel,
        in_specs=[pl.BlockSpec(memory_space=pltpu.SMEM)]
        + [pl.BlockSpec(memory_space=pltpu.HBM)] * len(arrays),
        out_specs=[pl.BlockSpec(memory_space=pltpu.VMEM)] * 4,
        out_shape=[like, payload, payload, part],
        scratch_shapes=[
            pltpu.VMEM((lon_dev, lat, members), state.dtype),
            pltpu.VMEM((1, nobs), jnp.int32),
            pltpu.VMEM((1, nobs), jnp.float32),
            pltpu.VMEM((1, nobs), jnp.float32),
            pltpu.SemaphoreType.DMA((6,)),
        ],
        compiler_params=pltpu.CompilerParams(vmem_limit_bytes=16 * 2**20),
        name="observe",
    )(odd, *[pltpu.with_memory_space_constraint(x, pltpu.HBM) for x in arrays])


def pair_tiles(ref, step, steps):
    size = PAIR * TILE
    lat = steps * size

    def load(at):
        at = pl.multiple_of(at * size, size)
        if len(ref.shape) == 4:
            return ref[:, :, pl.ds(at, size), :].astype(jnp.float32)
        planes = ref.shape[0] // lat
        rows = [ref[pl.ds(i * lat + at, size), :] for i in range(planes)]
        rows = jnp.stack(rows).astype(jnp.float32)
        return rows.reshape(HALO, planes // HALO, size, rows.shape[-1])

    here = load(step)
    before = load(jnp.maximum(step - 1, 0))[:, :, TILE:]
    after = load(jnp.minimum(step + 1, steps - 1))[:, :, :TILE]
    before = jnp.where(step == 0, 0.0, before)
    after = jnp.where(step == steps - 1, 0.0, after)
    return before, here[:, :, :TILE], here[:, :, TILE:], after


def halo_weights(to_left):
    steps = [jnp.float32(1.0) - jnp.float32(d) / jnp.float32(HALO + 1) for d in range(HALO, 0, -1)]
    return [jnp.where(to_left, x, y) for x, y in zip(steps, steps[::-1])]


def gram_of(tiles, weights):
    before, low, high, after = tiles
    columns, nvar, _, members = low.shape
    row = lax.broadcasted_iota(jnp.int32, (1, TILE, members), 1)
    upper = row < HALO
    rowf = row.astype(jnp.float32)
    edge = line_weight(jnp.where(upper, rowf + (HALO + REGION), rowf - HALO))
    grams = []
    for own, following, preceding in ((low, high, before), (high, after, low)):
        margin = jnp.where(upper, following, preceding)
        win = jnp.concatenate([own, margin], axis=2)
        weighted = []
        for column, weight in enumerate(weights):
            if weight is None:
                parts = [own[column], margin[column] * edge]
            else:
                parts = [own[column] * weight, margin[column] * (edge * weight)]
            weighted.append(jnp.concatenate(parts, axis=1))
        weighted = jnp.stack(weighted)
        shape = (columns * nvar * 2 * TILE, members)
        grams.append(
            lax.dot_general(
                weighted.astype(jnp.bfloat16).reshape(shape),
                win.astype(jnp.bfloat16).reshape(shape),
                (((0,), (0,)), ((), ())),
                preferred_element_type=jnp.float32,
            )
        )
    return grams


def slab_copies(src_ref, dst_ref, sems):
    size = PAIR * TILE
    return [
        pltpu.make_async_copy(
            src_ref.at[:, :, pl.ds(i * size, size), :], dst_ref.at[:, :, pl.ds(i * size, size), :], sems.at[i]
        )
        for i in range(src_ref.shape[2] // size)
    ]


def own_gram_kernel(odd_ref, state_hbm_ref, near_ref, own_ref, gram_ref, like_ref, state_ref, sems):
    steps = gram_ref.shape[0] // PAIR
    copies = slab_copies(state_hbm_ref, state_ref, sems)
    for copy in copies:
        copy.start()
    like_ref[...] = own_ref[...] + from_parts(near_ref)
    copies[0].wait()
    for step in range(steps):
        if step + 1 < steps:
            copies[step + 1].wait()
        tiles = zip(pair_tiles(state_ref, step, steps), pair_tiles(near_ref, step, steps))
        tiles = [jnp.concatenate([x, y], axis=0) for x, y in tiles]
        grams = gram_of(tiles, [None] * state_ref.shape[0] + halo_weights(odd_ref[0] == 1))
        for region in range(PAIR):
            gram_ref[step * PAIR + region] = grams[region]


def own_gram(odd, state, near, own):
    _, _, lat, members = state.shape
    vmem = pl.BlockSpec(memory_space=pltpu.VMEM)
    return pl.pallas_call(
        own_gram_kernel,
        in_specs=[
            pl.BlockSpec(memory_space=pltpu.SMEM),
            pl.BlockSpec(memory_space=pltpu.HBM),
            vmem,
            vmem,
        ],
        out_specs=[vmem, vmem],
        out_shape=[
            jax.ShapeDtypeStruct((lat // REGION, members, members), jnp.float32),
            jax.ShapeDtypeStruct(own.shape, jnp.float32),
        ],
        scratch_shapes=[
            pltpu.VMEM(state.shape, state.dtype),
            pltpu.SemaphoreType.DMA((lat // (PAIR * TILE),)),
        ],
        compiler_params=pltpu.CompilerParams(vmem_limit_bytes=16 * 2**20),
        name="own_gram",
    )(odd, pltpu.with_memory_space_constraint(state, pltpu.HBM), near, own)


def halves(ref, region, rows):
    members = ref.shape[-1]
    return [ref[region, rows, at : at + 128] for at in range(0, members, 128)]


def diagonal(gram_ref, region):
    members = gram_ref.shape[-1]
    across = [None] * (members // 128)
    down = []
    for start in range(0, members, ROWS):
        lane = start // 128
        gram = gram_ref[region, pl.ds(start, ROWS), lane * 128 : lane * 128 + 128]
        i = lax.broadcasted_iota(jnp.int32, gram.shape, 0) + start
        j = lax.broadcasted_iota(jnp.int32, gram.shape, 1) + lane * 128
        kept = jnp.where(i == j, gram, 0.0)
        down.append(jnp.broadcast_to(jnp.sum(kept, axis=1, keepdims=True), gram.shape))
        part = jnp.sum(kept.reshape(ROWS // TILE, TILE, 128), axis=0)
        across[lane] = part if across[lane] is None else across[lane] + part
    return [jnp.sum(x, axis=0, keepdims=True) for x in across], down


def prepare_kernel(scale, *refs):
    odd_ref, halo_ref, gram_in_ref, like_in_ref = refs[:4]
    gram_hbm_ref, kernel_ref, most_ref, like_ref, gram_ref, sems = refs[4:]
    regions, members, _ = gram_ref.shape
    steps = regions // PAIR
    like_ref[...] = like_in_ref[...] + from_parts(halo_ref)

    def keep(step):
        part = pl.ds(step * PAIR, PAIR)
        return pltpu.make_async_copy(gram_ref.at[part], gram_hbm_ref.at[part], sems.at[step])

    def pair(step, most):
        grams = gram_of(pair_tiles(halo_ref, step, steps), halo_weights(odd_ref[0] == 0))
        for at in range(PAIR):
            region = step * PAIR + at
            gram_ref[region] = gram_in_ref[region] + grams[at]
        keep(step).start()
        for at in range(PAIR):
            region = step * PAIR + at
            across, down = diagonal(gram_ref, region)
            across = [0.5 * LIFT - x * scale for x in across]
            for i, start in enumerate(range(0, members, ROWS)):
                rows = pl.ds(start, ROWS)
                base = 0.5 * LIFT - down[i] * scale
                for lane, (gram, x) in enumerate(zip(halves(gram_ref, region, rows), across)):
                    part = jnp.exp2(gram * (2.0 * scale) + base + x)
                    kernel_ref[region, rows, lane * 128 : lane * 128 + 128] = part
                    most = jnp.maximum(most, part)
        return most

    most = lax.fori_loop(0, steps, pair, jnp.zeros((ROWS, 128), jnp.float32))
    most_ref[...] = jnp.max(most.reshape(ROWS // TILE, TILE, 128), axis=0)

    def drain(step, carry):
        keep(step).wait()
        return carry

    lax.fori_loop(0, steps, drain, 0)


def prepare(odd, halo, gram, like, scale):
    regions = gram.shape[0]
    vmem = pl.BlockSpec(memory_space=pltpu.VMEM)
    return pl.pallas_call(
        functools.partial(prepare_kernel, scale),
        in_specs=[pl.BlockSpec(memory_space=pltpu.SMEM)] + [vmem] * 3,
        out_specs=[pl.BlockSpec(memory_space=pltpu.HBM)] + [vmem] * 3,
        out_shape=[
            pltpu.HBM(gram.shape, jnp.float32),
            jax.ShapeDtypeStruct(gram.shape, jnp.float32),
            jax.ShapeDtypeStruct((TILE, 128), jnp.float32),
            jax.ShapeDtypeStruct(like.shape, jnp.float32),
        ],
        scratch_shapes=[
            pltpu.VMEM(gram.shape, jnp.float32),
            pltpu.SemaphoreType.DMA((regions // PAIR,)),
        ],
        compiler_params=pltpu.CompilerParams(vmem_limit_bytes=16 * 2**20),
        name="prepare",
    )(odd, halo, gram, like)


def fold(values, op):
    out = values[0]
    for value in values[1:]:
        out = op(out, value)
    return out


def sweeps_scaled(regions, kernel_ref, ratio_ref, weight_ref):
    members = kernel_ref.shape[-1]
    starts = range(0, members, ROWS)
    lanes = range(members // 128)
    share = 2.0**MASS / members

    def sweep(last, carry):
        least_row, least_col, factors = carry
        rows_out, least_out, factors_out = [], [], []
        for region, lrow, lcol, factor in zip(regions, least_row, least_col, factors):
            totals = [None for _ in lanes]
            for start in starts:
                rows = pl.ds(start, ROWS)
                kernel = halves(kernel_ref, region, rows)
                mass = fold([k * f for k, f in zip(kernel, factor)], jnp.add)
                mass = jnp.broadcast_to(jnp.sum(mass, axis=1, keepdims=True), (ROWS, 128))
                near = pl.reciprocal(mass, approx=True)
                ratio = weight_ref[region, rows, :] * (near * (2.0 - mass * near))
                for lane, part in enumerate(kernel):
                    part = jnp.sum((part * ratio).reshape(ROWS // TILE, TILE, 128), axis=0)
                    totals[lane] = part if totals[lane] is None else totals[lane] + part
                if last:
                    ratio_ref[region, rows, :] = ratio
                lrow = jnp.minimum(lrow, mass)
            totals = [jnp.sum(x, axis=0, keepdims=True) for x in totals]
            rows_out.append(lrow)
            least_out.append(jnp.minimum(lcol, fold(totals, jnp.minimum)))
            factors_out.append([(1.0 if last else share) / x for x in totals])
        return rows_out, least_out, factors_out

    high = jnp.full((ROWS, 128), 1e30, jnp.float32)
    first = jnp.full((1, 128), 2.0**START, jnp.float32)
    carry = [high for _ in regions], [high[:1] for _ in regions], [[first] * len(lanes) for _ in regions]
    carry = lax.fori_loop(0, SWEEPS - 1, lambda i, c: sweep(False, c), carry)
    least_row, least_col, factors = sweep(True, carry)
    return factors, fold(least_row, jnp.minimum), fold(least_col, jnp.minimum)


def transport_scaled(region, factor, kernel_ref, ratio_ref):
    members = kernel_ref.shape[-1]
    parts = []
    for start in range(0, members, ROWS):
        rows = pl.ds(start, ROWS)
        ratio = ratio_ref[region, rows, :]
        row = [k * ratio * f for k, f in zip(halves(kernel_ref, region, rows), factor)]
        parts.append(jnp.concatenate(row, axis=1).astype(jnp.bfloat16))
    return jnp.concatenate(parts, axis=0)


def transport_logs(region, gram_ref, logw, scale):
    members = gram_ref.shape[-1]
    gram = gram_ref[region]
    i = lax.broadcasted_iota(jnp.int32, gram.shape, 0)
    j = lax.broadcasted_iota(jnp.int32, gram.shape, 1)
    kept = jnp.where(i == j, gram, 0.0)
    down = jnp.sum(kept, axis=1, keepdims=True)
    across = jnp.sum(kept, axis=0, keepdims=True)
    cost = (down + across - 2.0 * gram) * scale
    logw = jnp.sum(jnp.where(i == j, logw, 0.0), axis=1, keepdims=True)
    pot_g = jnp.zeros((1, members), jnp.float32)
    for sweep in range(SWEEPS):
        term = pot_g - cost
        top = jnp.max(term, axis=1, keepdims=True)
        pot_f = logw - top - jnp.log(jnp.sum(jnp.exp2(term - top), axis=1, keepdims=True)) * LOG2E
        term = pot_f - cost
        top = jnp.max(term, axis=0, keepdims=True)
        pot_g = -math.log2(members) - top
        pot_g = pot_g - jnp.log(jnp.sum(jnp.exp2(term - top), axis=0, keepdims=True)) * LOG2E
    return (members * jnp.exp2(pot_f + pot_g - cost)).astype(jnp.bfloat16)


def transform(state_ref, pair, moves):
    lon_dev, nvar, _, members = state_ref.shape
    size = PAIR * TILE
    own = state_ref[:, :, pl.ds(pl.multiple_of(pair * size, size), size), :].astype(jnp.float32)
    parts = []
    for region, move in enumerate(moves):
        cells = own[:, :, region * TILE : (region + 1) * TILE].astype(jnp.bfloat16)
        cells = cells.reshape(lon_dev * nvar * TILE, members)
        moved = jnp.dot(cells, move, preferred_element_type=jnp.float32)
        parts.append(moved.reshape(lon_dev, nvar, TILE, members))
    return jnp.concatenate(parts, axis=2).astype(jnp.bfloat16)


def finish_kernel(count, scale, *refs):
    state_hbm_ref, gram_hbm_ref, kernel_ref, most_ref, like_ref, sums_ref, out_ref = refs[:7]
    ratio_ref, weight_ref, logw_ref, result_ref, state_ref, gram_ref = refs[7:13]
    sems, state_sems = refs[13:]
    regions, members = kernel_ref.shape[0], kernel_ref.shape[-1]
    pairs = regions // PAIR
    size = PAIR * TILE
    fetches = slab_copies(state_hbm_ref, state_ref, state_sems)
    for copy in fetches:
        copy.start()

    total = jnp.sum(sums_ref[...], axis=0, keepdims=True)[:, 0:1] * (1.0 / TILE)
    like = -0.5 * (count / total) * like_ref[...]
    like = like - jnp.max(like, axis=1, keepdims=True)
    logw = (like - jnp.log(jnp.sum(jnp.exp(like), axis=1, keepdims=True))) * LOG2E
    logw_ref[...] = logw
    weight = jnp.exp2(logw + MASS).T
    for region in range(regions):
        weight_ref[region] = jnp.broadcast_to(weight[:, region : region + 1], (members, 128))

    def send(pair):
        at = pl.ds(pl.multiple_of(pair * size, size), size)
        return pltpu.make_async_copy(result_ref.at[pair], out_ref.at[:, :, at, :], sems.at[pair])

    for copy in fetches:
        copy.wait()

    def group(at, carry):
        first = at * GROUP
        factors, row, col = sweeps_scaled(
            [first + r for r in range(GROUP)], kernel_ref, ratio_ref, weight_ref
        )
        for pair in range(GROUP // PAIR):
            moves = [
                transport_scaled(first + r, factors[r], kernel_ref, ratio_ref)
                for r in range(pair * PAIR, (pair + 1) * PAIR)
            ]
            where = at * (GROUP // PAIR) + pair
            result_ref[where] = transform(state_ref, where, moves)
            send(where).start()
        return jnp.minimum(carry[0], row), jnp.minimum(carry[1], col)

    high = jnp.full((ROWS, 128), 1e30, jnp.float32)
    least_row, least_col = lax.fori_loop(0, regions // GROUP, group, (high, high[:1]))

    def drain(pair, carry):
        send(pair).wait()
        return carry

    lax.fori_loop(0, pairs, drain, 0)
    row, col, most = jnp.min(least_row), jnp.min(least_col), jnp.max(most_ref[...])
    sound = (row >= 2.0**-24) & (col >= 2.0**-30) & (most <= 2.0**30) & (row * col >= 2.0**-34)

    @pl.when(jnp.logical_not(sound))
    def _():
        def again(pair, carry):
            moves = []
            for at in range(PAIR):
                region = pair * PAIR + at
                copy = pltpu.make_async_copy(gram_hbm_ref.at[region], gram_ref.at[at], state_sems.at[0])
                copy.start()
                copy.wait()
                logw = logw_ref[pl.ds(region, 1), :]
                moves.append(transport_logs(at, gram_ref, logw, scale))
            result_ref[pair] = transform(state_ref, pair, moves)
            copy = send(pair)
            copy.start()
            copy.wait()
            return carry

        lax.fori_loop(0, pairs, again, 0)


def finish(state, gram, kernel, most, like, sums, count, scale):
    lon_dev, nvar, lat, members = state.shape
    regions = lat // REGION
    vmem = pl.BlockSpec(memory_space=pltpu.VMEM)
    hbm = pl.BlockSpec(memory_space=pltpu.HBM)
    return pl.pallas_call(
        functools.partial(finish_kernel, count, scale),
        in_specs=[hbm, hbm] + [vmem] * 4,
        out_specs=pl.BlockSpec(memory_space=pl.ANY),
        out_shape=jax.ShapeDtypeStruct(state.shape, state.dtype),
        scratch_shapes=[
            pltpu.VMEM((regions, members, 128), jnp.float32),
            pltpu.VMEM((regions, members, 128), jnp.float32),
            pltpu.VMEM((regions, members), jnp.float32),
            pltpu.VMEM((regions // PAIR, lon_dev, nvar, PAIR * TILE, members), jnp.bfloat16),
            pltpu.VMEM(state.shape, state.dtype),
            pltpu.VMEM((PAIR, members, members), jnp.float32),
            pltpu.SemaphoreType.DMA((regions // PAIR,)),
            pltpu.SemaphoreType.DMA((regions // PAIR,)),
        ],
        compiler_params=pltpu.CompilerParams(vmem_limit_bytes=24 * 2**20),
        name="finish",
    )(*[pltpu.with_memory_space_constraint(x, pltpu.HBM) for x in (state, gram)], kernel, most, like, sums)


def on_device(state, obs_index, obs_value, obs_var):
    nvar = state.shape[1]
    count = lax.axis_size("lon")
    odd = (lax.axis_index("lon") & 1).astype(jnp.int32).reshape(1)
    near_pairs = [(i, i ^ 1) for i in range(count)]
    far_pairs = [(i, (i + 1 if i % 2 else i - 1) % count) for i in range(count)]
    own_like, for_near, for_far, part = observe(odd, state, obs_index, obs_value, obs_var)
    far = lax.ppermute(for_far, "lon", far_pairs)
    near = lax.ppermute(for_near, "lon", near_pairs)
    start = near.shape[0] - TILE
    part = part[0] + jnp.sum(near[start : start + 3, :128].astype(jnp.float32), axis=0)
    sums = lax.all_to_all(
        jnp.broadcast_to(part, (count // 2 * TILE, 128)),
        "lon",
        0,
        0,
        axis_index_groups=[list(range(core, count, 2)) for core in range(2)],
        tiled=True,
    )
    offsets = range(REGION + 2 * HALO)
    line = [1.0 - max(0, HALO - p, p - (HALO + REGION - 1)) / (HALO + 1) for p in offsets]
    scale = LOG2E / EPS / (nvar * sum(line) ** 2)
    gram, like = own_gram(odd, state, near, own_like)
    gram, kernel, most, like = prepare(odd, far, gram, like, scale)
    nobs = float(obs_index.shape[0] * count)
    return finish(state, gram, kernel, most, like, sums, nobs, scale)


def solution(mesh):
    return jax.shard_map(
        on_device,
        mesh=mesh,
        in_specs=(
            P(("ens", "lon"), None, None, None),
            P(("ens", "lon")),
            P(("ens", "lon")),
            P(("ens", "lon")),
        ),
        out_specs=P(("ens", "lon"), None, None, None),
        check_vma=False,
    )
```

```python
import functools
import math

import jax
import jax.numpy as jnp
from jax import lax
from jax.experimental import pallas as pl
from jax.experimental.pallas import tpu as pltpu
from jax.sharding import PartitionSpec as P

REGION = 8
HALO = 4
SWEEPS = 4
EPS = 0.05
TILE = 8
PAIR = 2
LOG2E = 1.4426950408889634
ROWS = 32
GROUP = 4
LIFT, START, MASS = 20, -10, 60

HIGH = lax.Precision.HIGHEST


def line_weight(place):
    dist = jnp.maximum(0.0, jnp.maximum(HALO - place, place - (HALO + REGION - 1)))
    inside = (place >= 0) & (place < REGION + 2 * HALO)
    return jnp.where(inside, 1.0 - dist / (HALO + 1), 0.0)


def in_parts(values, extra):
    below = lax.broadcasted_iota(jnp.int32, values.shape, 0)
    extra_high = extra.astype(jnp.bfloat16).astype(jnp.float32)
    extra_middle = (extra - extra_high).astype(jnp.bfloat16).astype(jnp.float32)
    extra_low = extra - extra_high - extra_middle
    last = jnp.where(below == 0, extra_high, jnp.where(below == 1, extra_middle, extra_low))
    last = jnp.where(below < 3, last, 0.0)
    high = values.astype(jnp.bfloat16).astype(jnp.float32)
    middle = (values - high).astype(jnp.bfloat16).astype(jnp.float32)
    low = values - high - middle
    return jnp.concatenate([high, middle, low, last], axis=0).astype(jnp.bfloat16)


def from_parts(ref):
    rows = ref[ref.shape[0] - 4 * TILE :, :].astype(jnp.float32)
    return rows[:TILE] + rows[TILE : 2 * TILE] + rows[2 * TILE : 3 * TILE]


def observe_kernel(*refs):
    odd_ref, state_ref, rows_ref = refs[:3]
    own_ref, near_ref, far_ref, part_ref = refs[6:10]
    cells_ref, index_ref, value_ref, var_ref, sems = refs[10:]
    lon_dev, lat, members = cells_ref.shape
    nobs = index_ref.shape[1]
    edge = rows_ref.shape[0] // lon_dev * HALO
    last = rows_ref.shape[0] - edge
    far_at = pl.multiple_of(odd_ref[0] * last, 16)
    near_at = pl.multiple_of(last - far_at, 16)
    fetches = [
        (refs[3], index_ref),
        (refs[4], value_ref),
        (refs[5], var_ref),
        (state_ref.at[:, 0], cells_ref),
        (rows_ref.at[pl.ds(far_at, edge), :], far_ref.at[pl.ds(0, edge), :]),
        (rows_ref.at[pl.ds(near_at, edge), :], near_ref.at[pl.ds(0, edge), :]),
    ]
    copies = [
        pltpu.make_async_copy(src, dst, sems.at[i]) for i, (src, dst) in enumerate(fetches)
    ]
    for copy in copies:
        copy.start()
    for copy in copies[:4]:
        copy.wait()
    rows = cells_ref[...].reshape(lon_dev * lat, members)
    index = index_ref[...]
    sub = lax.broadcasted_iota(jnp.int32, (TILE, nobs), 0)
    table = jnp.where(
        sub == 0,
        index.astype(jnp.float32),
        jnp.where(sub == 1, value_ref[...], var_ref[...]),
    ).T
    index_col = table[:, 0:1].astype(jnp.int32)
    value = table[:, 1:2]
    var = table[:, 2:3]
    pick = index_col == lax.broadcasted_iota(jnp.int32, (nobs, lon_dev * lat), 1)
    pick = jnp.where(pick, 1.0, 0.0).astype(jnp.bfloat16)
    seen = jnp.dot(pick, rows, preferred_element_type=jnp.float32)
    centre = jnp.sum(seen, axis=1, keepdims=True) * (1.0 / members)
    spread = jnp.sum((seen - centre) ** 2, axis=1, keepdims=True) * (1.0 / (members - 1))
    innovation = (value - centre) ** 2 / (var + spread)
    part = jnp.sum(innovation, axis=0, keepdims=True)
    part_ref[...] = jnp.broadcast_to(part, part_ref.shape)
    terms = (value - seen) ** 2 * (1.0 / var)
    lon = (index // lat).astype(jnp.float32)
    along = index.astype(jnp.float32) - lon * lat
    blocks = own_ref.shape[0]
    block = lax.broadcasted_iota(jnp.int32, (blocks, nobs), 0).astype(jnp.float32)
    across = line_weight(along - REGION * block + HALO)
    side = jnp.where(odd_ref[0] == 1, float(REGION), float(-REGION))
    weights = [line_weight(lon + (HALO + shift)) * across for shift in (0.0, side, -side)]
    like = jnp.dot(
        jnp.concatenate(weights, axis=0), terms, precision=HIGH, preferred_element_type=jnp.float32
    )
    own_ref[...] = like[:blocks]
    near_ref[edge:, :] = in_parts(like[blocks : 2 * blocks], part)
    far_ref[edge:, :] = in_parts(like[2 * blocks :], jnp.zeros_like(part))
    for copy in copies[4:]:
        copy.wait()


def observe(odd, state, obs_index, obs_value, obs_var):
    lon_dev, nvar, lat, members = state.shape
    nobs = obs_index.size
    assert lat // REGION == TILE
    like = jax.ShapeDtypeStruct((lat // REGION, members), jnp.float32)
    payload = pltpu.VMEM((HALO * nvar * lat + 4 * TILE, members), state.dtype)
    part = jax.ShapeDtypeStruct((TILE, 128), jnp.float32)
    arrays = state, state.reshape(-1, members), obs_index[None], obs_value[None], obs_var[None]
    return pl.pallas_call(
        observe_kernel,
        in_specs=[pl.BlockSpec(memory_space=pltpu.SMEM)]
        + [pl.BlockSpec(memory_space=pltpu.HBM)] * len(arrays),
        out_specs=[pl.BlockSpec(memory_space=pltpu.VMEM)] * 4,
        out_shape=[like, payload, payload, part],
        scratch_shapes=[
            pltpu.VMEM((lon_dev, lat, members), state.dtype),
            pltpu.VMEM((1, nobs), jnp.int32),
            pltpu.VMEM((1, nobs), jnp.float32),
            pltpu.VMEM((1, nobs), jnp.float32),
            pltpu.SemaphoreType.DMA((6,)),
        ],
        compiler_params=pltpu.CompilerParams(vmem_limit_bytes=16 * 2**20),
        name="observe",
    )(odd, *[pltpu.with_memory_space_constraint(x, pltpu.HBM) for x in arrays])


def pair_tiles(ref, step, steps):
    size = PAIR * TILE
    lat = steps * size

    def load(at):
        at = pl.multiple_of(at * size, size)
        if len(ref.shape) == 4:
            return ref[:, :, pl.ds(at, size), :].astype(jnp.float32)
        planes = ref.shape[0] // lat
        rows = [ref[pl.ds(i * lat + at, size), :] for i in range(planes)]
        rows = jnp.stack(rows).astype(jnp.float32)
        return rows.reshape(HALO, planes // HALO, size, rows.shape[-1])

    here = load(step)
    before = load(jnp.maximum(step - 1, 0))[:, :, TILE:]
    after = load(jnp.minimum(step + 1, steps - 1))[:, :, :TILE]
    before = jnp.where(step == 0, 0.0, before)
    after = jnp.where(step == steps - 1, 0.0, after)
    return before, here[:, :, :TILE], here[:, :, TILE:], after


def halo_weights(to_left):
    steps = [jnp.float32(1.0) - jnp.float32(d) / jnp.float32(HALO + 1) for d in range(HALO, 0, -1)]
    return [jnp.where(to_left, x, y) for x, y in zip(steps, steps[::-1])]


def turn_tiles(low, high, turned_ref, step):
    for at, tile in enumerate((low, high)):
        flat = tile.reshape(-1, tile.shape[-1]).astype(jnp.bfloat16)
        turned_ref[step * PAIR + at] = flat.T


def gram_of(tiles, turned_ref, weights, step, steps):
    before, low, high, after = tiles
    columns, nvar, _, members = low.shape
    depth = columns * nvar * TILE
    row = lax.broadcasted_iota(jnp.int32, (1, TILE, members), 1)
    upper = row < HALO
    rowf = row.astype(jnp.float32)
    edge = line_weight(jnp.where(upper, rowf + (HALO + REGION), rowf - HALO))
    lane = lax.broadcasted_iota(jnp.int32, (1, depth), 1) & (TILE - 1)
    grams = []
    for at, (own, following, preceding) in enumerate(((low, high, before), (high, after, low))):
        region = step * PAIR + at
        margin = jnp.where(upper, following, preceding)
        main_rows, margin_rows = [], []
        for column, weight in enumerate(weights):
            main_rows.append(own[column] if weight is None else own[column] * weight)
            scale = edge if weight is None else edge * weight
            margin_rows.append(margin[column] * scale)
        weighted = jnp.concatenate([jnp.stack(main_rows), jnp.stack(margin_rows)], axis=0)
        weighted = weighted.reshape(2 * depth, members).astype(jnp.bfloat16)
        has_next = jnp.where(region + 1 < steps * PAIR, 1.0, 0.0)
        has_prev = jnp.where(region > 0, 1.0, 0.0)
        take_next = jnp.where(lane < HALO, has_next, 0.0).astype(jnp.bfloat16)
        take_prev = jnp.where(lane < HALO, 0.0, has_prev).astype(jnp.bfloat16)
        turned = (
            turned_ref[jnp.minimum(region + 1, steps * PAIR - 1)] * take_next
            + turned_ref[jnp.maximum(region - 1, 0)] * take_prev
        )
        turned = jnp.concatenate([turned_ref[region], turned], axis=1)
        grams.append(jnp.dot(turned, weighted, preferred_element_type=jnp.float32))
    return grams


def slab_copies(src_ref, dst_ref, sems):
    size = PAIR * TILE
    return [
        pltpu.make_async_copy(
            src_ref.at[:, :, pl.ds(i * size, size), :], dst_ref.at[:, :, pl.ds(i * size, size), :], sems.at[i]
        )
        for i in range(src_ref.shape[2] // size)
    ]


def own_gram_kernel(odd_ref, state_hbm_ref, near_ref, own_ref, gram_ref, like_ref, *scratch):
    state_ref, turned_ref, sems = scratch
    steps = gram_ref.shape[0] // PAIR
    copies = slab_copies(state_hbm_ref, state_ref, sems)
    for copy in copies:
        copy.start()
    like_ref[...] = own_ref[...] + from_parts(near_ref)
    pairs = []
    for step in range(steps):
        copies[step].wait()
    for step in range(steps):
        tiles = zip(pair_tiles(state_ref, step, steps), pair_tiles(near_ref, step, steps))
        pairs.append([jnp.concatenate([x, y], axis=0) for x, y in tiles])
        turn_tiles(pairs[-1][1], pairs[-1][2], turned_ref, step)
    weights = [None] * state_ref.shape[0] + halo_weights(odd_ref[0] == 1)
    for step in range(steps):
        grams = gram_of(pairs[step], turned_ref, weights, step, steps)
        for at in range(PAIR):
            gram_ref[step * PAIR + at] = grams[at]


def own_gram(odd, state, near, own):
    lon_dev, nvar, lat, members = state.shape
    depth = (lon_dev + HALO) * nvar * TILE
    vmem = pl.BlockSpec(memory_space=pltpu.VMEM)
    return pl.pallas_call(
        own_gram_kernel,
        in_specs=[
            pl.BlockSpec(memory_space=pltpu.SMEM),
            pl.BlockSpec(memory_space=pltpu.HBM),
            vmem,
            vmem,
        ],
        out_specs=[vmem, vmem],
        out_shape=[
            jax.ShapeDtypeStruct((lat // REGION, members, members), jnp.float32),
            jax.ShapeDtypeStruct(own.shape, jnp.float32),
        ],
        scratch_shapes=[
            pltpu.VMEM(state.shape, state.dtype),
            pltpu.VMEM((lat // TILE, members, depth), state.dtype),
            pltpu.SemaphoreType.DMA((lat // (PAIR * TILE),)),
        ],
        compiler_params=pltpu.CompilerParams(vmem_limit_bytes=16 * 2**20),
        name="own_gram",
    )(odd, pltpu.with_memory_space_constraint(state, pltpu.HBM), near, own)


def halves(ref, region, rows):
    members = ref.shape[-1]
    return [ref[region, rows, at : at + 128] for at in range(0, members, 128)]


def diagonal(gram_ref, region):
    members = gram_ref.shape[-1]
    across = [None] * (members // 128)
    down = []
    for start in range(0, members, ROWS):
        lane = start // 128
        gram = gram_ref[region, pl.ds(start, ROWS), lane * 128 : lane * 128 + 128]
        i = lax.broadcasted_iota(jnp.int32, gram.shape, 0) + start
        j = lax.broadcasted_iota(jnp.int32, gram.shape, 1) + lane * 128
        kept = jnp.where(i == j, gram, 0.0)
        down.append(jnp.broadcast_to(jnp.sum(kept, axis=1, keepdims=True), gram.shape))
        part = jnp.sum(kept.reshape(ROWS // TILE, TILE, 128), axis=0)
        across[lane] = part if across[lane] is None else across[lane] + part
    return [jnp.sum(x, axis=0, keepdims=True) for x in across], down


def prepare_kernel(scale, *refs):
    odd_ref, halo_ref, gram_in_ref, like_in_ref = refs[:4]
    gram_hbm_ref, kernel_ref, mass_ref, most_ref, like_ref, gram_ref, turned_ref, sems = refs[4:]
    regions, members, _ = gram_ref.shape
    steps = regions // PAIR
    like_ref[...] = like_in_ref[...] + from_parts(halo_ref)

    def keep(step):
        part = pl.ds(step * PAIR, PAIR)
        return pltpu.make_async_copy(gram_ref.at[part], gram_hbm_ref.at[part], sems.at[step])

    def turn(step, carry):
        tiles = pair_tiles(halo_ref, step, steps)
        turn_tiles(tiles[1], tiles[2], turned_ref, step)
        return carry

    lax.fori_loop(0, steps, turn, 0)

    def pair(step, most):
        weights = halo_weights(odd_ref[0] == 0)
        grams = gram_of(pair_tiles(halo_ref, step, steps), turned_ref, weights, step, steps)
        for at in range(PAIR):
            region = step * PAIR + at
            gram_ref[region] = gram_in_ref[region] + grams[at]
        keep(step).start()
        for at in range(PAIR):
            region = step * PAIR + at
            across, down = diagonal(gram_ref, region)
            across = [0.5 * LIFT - x * scale for x in across]
            masses = [0.0 for _ in across]
            for i, start in enumerate(range(0, members, ROWS)):
                rows = pl.ds(start, ROWS)
                base = 0.5 * LIFT - down[i] * scale
                for lane, (gram, x) in enumerate(zip(halves(gram_ref, region, rows), across)):
                    part = jnp.exp2(gram * (2.0 * scale) + base + x)
                    kernel_ref[region, rows, lane * 128 : lane * 128 + 128] = part
                    most = jnp.maximum(most, part)
                    part = jnp.sum(part.reshape(ROWS // TILE, TILE, 128), axis=0)
                    masses[lane] = masses[lane] + part
            masses = [jnp.sum(x, axis=0, keepdims=True) for x in masses]
            mass_ref[region] = jnp.concatenate(masses, axis=1)
        return most

    most = lax.fori_loop(0, steps, pair, jnp.zeros((ROWS, 128), jnp.float32))
    most_ref[...] = jnp.max(most.reshape(ROWS // TILE, TILE, 128), axis=0)

    def drain(step, carry):
        keep(step).wait()
        return carry

    lax.fori_loop(0, steps, drain, 0)


def prepare(odd, halo, gram, like, scale):
    regions = gram.shape[0]
    halo_depth = (halo.shape[0] - 4 * TILE) // regions
    vmem = pl.BlockSpec(memory_space=pltpu.VMEM)
    return pl.pallas_call(
        functools.partial(prepare_kernel, scale),
        in_specs=[pl.BlockSpec(memory_space=pltpu.SMEM)] + [vmem] * 3,
        out_specs=[pl.BlockSpec(memory_space=pltpu.HBM)] + [vmem] * 4,
        out_shape=[
            pltpu.HBM(gram.shape, jnp.float32),
            jax.ShapeDtypeStruct(gram.shape, jnp.float32),
            jax.ShapeDtypeStruct((regions, 1, like.shape[1]), jnp.float32),
            jax.ShapeDtypeStruct((TILE, 128), jnp.float32),
            jax.ShapeDtypeStruct(like.shape, jnp.float32),
        ],
        scratch_shapes=[
            pltpu.VMEM(gram.shape, jnp.float32),
            pltpu.VMEM((regions, gram.shape[1], halo_depth), halo.dtype),
            pltpu.SemaphoreType.DMA((regions // PAIR,)),
        ],
        compiler_params=pltpu.CompilerParams(vmem_limit_bytes=16 * 2**20),
        name="prepare",
    )(odd, halo, gram, like)


def fold(values, op):
    out = values[0]
    for value in values[1:]:
        out = op(out, value)
    return out


def transports_scaled(regions, kernel_ref, weight_ref, mass_ref):
    members = kernel_ref.shape[-1]
    starts = range(0, members, ROWS)
    lanes = range(members // 128)
    share = 2.0**MASS / members

    def lane_parts(ref, region):
        row = ref[region]
        return [row[:, lane * 128 : lane * 128 + 128] for lane in lanes]

    def settle(totals, region):
        return [w / x for w, x in zip(lane_parts(weight_ref, region), totals)]

    def masses_of(region, rows, factor):
        parts = [k * f for k, f in zip(halves(kernel_ref, region, rows), factor)]
        mass = jnp.sum(fold(parts, jnp.add), axis=1, keepdims=True)
        mass = jnp.broadcast_to(mass, (ROWS, 128))
        near = pl.reciprocal(mass, approx=True)
        return parts, mass, near * (2.0 - mass * near)

    def sweep(_, carry):
        least_i, least_j, factors = carry
        next_i, next_j, next_factors = [], [], []
        for region, low_i, low_j, factor in zip(regions, least_i, least_j, factors):
            totals = [None for _ in lanes]
            for start in starts:
                rows = pl.ds(start, ROWS)
                _, mass, ratio = masses_of(region, rows, factor)
                low_j = jnp.minimum(low_j, mass)
                for lane, kernel in enumerate(halves(kernel_ref, region, rows)):
                    part = jnp.sum((kernel * ratio).reshape(ROWS // TILE, TILE, 128), axis=0)
                    totals[lane] = part if totals[lane] is None else totals[lane] + part
            totals = [jnp.sum(x, axis=0, keepdims=True) * share for x in totals]
            next_i.append(jnp.minimum(low_i, fold(totals, jnp.minimum)))
            next_j.append(low_j)
            next_factors.append(settle(totals, region))
        return next_i, next_j, next_factors

    totals = [[x * 2.0**START for x in lane_parts(mass_ref, region)] for region in regions]
    least_i = [fold(x, jnp.minimum) for x in totals]
    least_j = [jnp.full((ROWS, 128), 1e30, jnp.float32) for _ in regions]
    factors = [settle(x, region) for x, region in zip(totals, regions)]
    carry = lax.fori_loop(0, SWEEPS - 1, sweep, (least_i, least_j, factors))
    least_i, least_j, factors = carry
    moves, last_j = [], []
    for region, low_j, factor in zip(regions, least_j, factors):
        blocks = []
        for start in starts:
            parts, mass, ratio = masses_of(region, pl.ds(start, ROWS), factor)
            low_j = jnp.minimum(low_j, mass)
            blocks.append(jnp.concatenate([x * ratio for x in parts], axis=1).astype(jnp.bfloat16))
        moves.append(jnp.concatenate(blocks, axis=0))
        last_j.append(low_j)
    return moves, fold(least_i, jnp.minimum), fold(last_j, jnp.minimum)


def transport_logs(gram, logw, scale):
    members = gram.shape[-1]
    j = lax.broadcasted_iota(jnp.int32, gram.shape, 0)
    i = lax.broadcasted_iota(jnp.int32, gram.shape, 1)
    kept = jnp.where(i == j, gram, 0.0)
    down = jnp.sum(kept, axis=1, keepdims=True)
    across = jnp.sum(kept, axis=0, keepdims=True)
    cost = (down + across - 2.0 * gram) * scale
    pot_g = jnp.zeros((members, 1), jnp.float32)
    for sweep in range(SWEEPS):
        term = pot_g - cost
        top = jnp.max(term, axis=0, keepdims=True)
        pot_f = logw - top - jnp.log(jnp.sum(jnp.exp2(term - top), axis=0, keepdims=True)) * LOG2E
        term = pot_f - cost
        top = jnp.max(term, axis=1, keepdims=True)
        pot_g = -math.log2(members) - top
        pot_g = pot_g - jnp.log(jnp.sum(jnp.exp2(term - top), axis=1, keepdims=True)) * LOG2E
    return (members * jnp.exp2(pot_f + pot_g - cost)).astype(jnp.bfloat16)


def transform(state_ref, pair, moves):
    lon_dev, nvar, _, members = state_ref.shape
    size = PAIR * TILE
    own = state_ref[:, :, pl.ds(pl.multiple_of(pair * size, size), size), :].astype(jnp.float32)
    parts = []
    for region, move in enumerate(moves):
        cells = own[:, :, region * TILE : (region + 1) * TILE].astype(jnp.bfloat16)
        cells = cells.reshape(lon_dev * nvar * TILE, members)
        moved = lax.dot_general(
            cells, move, (((1,), (1,)), ((), ())), preferred_element_type=jnp.float32
        )
        parts.append(moved.reshape(lon_dev, nvar, TILE, members))
    return jnp.concatenate(parts, axis=2).astype(jnp.bfloat16)


def finish_kernel(count, scale, *refs):
    state_hbm_ref, gram_hbm_ref, kernel_ref, mass_ref, most_ref, like_ref, sums_ref = refs[:7]
    out_ref, weight_ref, logw_ref, result_ref, state_ref, gram_ref, sems, state_sems = refs[7:]
    regions, members = kernel_ref.shape[0], kernel_ref.shape[-1]
    pairs = regions // PAIR
    size = PAIR * TILE
    fetches = slab_copies(state_hbm_ref, state_ref, state_sems)
    for copy in fetches:
        copy.start()

    total = jnp.sum(sums_ref[...], axis=0, keepdims=True)[:, 0:1] * (1.0 / TILE)
    like = -0.5 * (count / total) * like_ref[...]
    like = like - jnp.max(like, axis=1, keepdims=True)
    logw = (like - jnp.log(jnp.sum(jnp.exp(like), axis=1, keepdims=True))) * LOG2E
    weight = jnp.exp2(logw + MASS)
    for region in range(regions):
        weight_ref[region] = weight[region : region + 1]
        logw_ref[region] = logw[region : region + 1]

    def send(pair):
        at = pl.ds(pl.multiple_of(pair * size, size), size)
        return pltpu.make_async_copy(result_ref.at[pair], out_ref.at[:, :, at, :], sems.at[pair])

    for copy in fetches:
        copy.wait()

    def group(at, carry):
        first = at * GROUP
        moves, least_i, least_j = transports_scaled(
            [first + r for r in range(GROUP)], kernel_ref, weight_ref, mass_ref
        )
        for pair in range(GROUP // PAIR):
            where = at * (GROUP // PAIR) + pair
            result_ref[where] = transform(state_ref, where, moves[pair * PAIR : (pair + 1) * PAIR])
            send(where).start()
        return jnp.minimum(carry[0], least_i), jnp.minimum(carry[1], least_j)

    high = jnp.full((ROWS, 128), 1e30, jnp.float32)
    least_i, least_j = lax.fori_loop(0, regions // GROUP, group, (high[:1], high))

    def drain(pair, carry):
        send(pair).wait()
        return carry

    lax.fori_loop(0, pairs, drain, 0)
    row, col, most = jnp.min(least_i), jnp.min(least_j), jnp.max(most_ref[...])
    sound = (row >= 2.0**-24) & (col >= 2.0**-30) & (most <= 2.0**30) & (row * col >= 2.0**-34)

    @pl.when(jnp.logical_not(sound))
    def _():
        def again(pair, carry):
            moves = []
            for at in range(PAIR):
                region = pair * PAIR + at
                copy = pltpu.make_async_copy(gram_hbm_ref.at[region], gram_ref.at[at], state_sems.at[0])
                copy.start()
                copy.wait()
                moves.append(transport_logs(gram_ref[at], logw_ref[region], scale))
            result_ref[pair] = transform(state_ref, pair, moves)
            copy = send(pair)
            copy.start()
            copy.wait()
            return carry

        lax.fori_loop(0, pairs, again, 0)


def finish(state, gram, kernel, mass, most, like, sums, count, scale):
    lon_dev, nvar, lat, members = state.shape
    regions = lat // REGION
    vmem = pl.BlockSpec(memory_space=pltpu.VMEM)
    hbm = pl.BlockSpec(memory_space=pltpu.HBM)
    return pl.pallas_call(
        functools.partial(finish_kernel, count, scale),
        in_specs=[hbm, hbm] + [vmem] * 5,
        out_specs=pl.BlockSpec(memory_space=pl.ANY),
        out_shape=jax.ShapeDtypeStruct(state.shape, state.dtype),
        scratch_shapes=[
            pltpu.VMEM((regions, 1, members), jnp.float32),
            pltpu.VMEM((regions, 1, members), jnp.float32),
            pltpu.VMEM((regions // PAIR, lon_dev, nvar, PAIR * TILE, members), jnp.bfloat16),
            pltpu.VMEM(state.shape, state.dtype),
            pltpu.VMEM((PAIR, members, members), jnp.float32),
            pltpu.SemaphoreType.DMA((regions // PAIR,)),
            pltpu.SemaphoreType.DMA((regions // PAIR,)),
        ],
        compiler_params=pltpu.CompilerParams(vmem_limit_bytes=24 * 2**20),
        name="finish",
    )(
        *[pltpu.with_memory_space_constraint(x, pltpu.HBM) for x in (state, gram)],
        kernel,
        mass,
        most,
        like,
        sums,
    )


def on_device(state, obs_index, obs_value, obs_var):
    nvar = state.shape[1]
    count = lax.axis_size("lon")
    odd = (lax.axis_index("lon") & 1).astype(jnp.int32).reshape(1)
    near_pairs = [(i, i ^ 1) for i in range(count)]
    far_pairs = [(i, (i + 1 if i % 2 else i - 1) % count) for i in range(count)]
    own_like, for_near, for_far, part = observe(odd, state, obs_index, obs_value, obs_var)
    far = lax.ppermute(for_far, "lon", far_pairs)
    near = lax.ppermute(for_near, "lon", near_pairs)
    start = near.shape[0] - TILE
    part = part[0] + jnp.sum(near[start : start + 3, :128].astype(jnp.float32), axis=0)
    sums = lax.all_to_all(
        jnp.broadcast_to(part, (count // 2 * TILE, 128)),
        "lon",
        0,
        0,
        axis_index_groups=[list(range(core, count, 2)) for core in range(2)],
        tiled=True,
    )
    offsets = range(REGION + 2 * HALO)
    line = [1.0 - max(0, HALO - p, p - (HALO + REGION - 1)) / (HALO + 1) for p in offsets]
    scale = LOG2E / EPS / (nvar * sum(line) ** 2)
    gram, like = own_gram(odd, state, near, own_like)
    gram, kernel, mass, most, like = prepare(odd, far, gram, like, scale)
    nobs = float(obs_index.shape[0] * count)
    return finish(state, gram, kernel, mass, most, like, sums, nobs, scale)


def solution(mesh):
    return jax.shard_map(
        on_device,
        mesh=mesh,
        in_specs=(
            P(("ens", "lon"), None, None, None),
            P(("ens", "lon")),
            P(("ens", "lon")),
            P(("ens", "lon")),
        ),
        out_specs=P(("ens", "lon"), None, None, None),
        check_vma=False,
    )
```

```python
import functools
import math

import jax
import jax.numpy as jnp
from jax import lax
from jax.experimental import pallas as pl
from jax.experimental.pallas import tpu as pltpu
from jax.sharding import PartitionSpec as P

REGION = 8
HALO = 4
SWEEPS = 4
EPS = 0.05
TILE = 8
PAIR = 2
LOG2E = 1.4426950408889634
ROWS = 32
GROUP = 4
LIFT, START, MASS = 20, -10, 60

HIGH = lax.Precision.HIGHEST


def line_weight(place):
    dist = jnp.maximum(0.0, jnp.maximum(HALO - place, place - (HALO + REGION - 1)))
    inside = (place >= 0) & (place < REGION + 2 * HALO)
    return jnp.where(inside, 1.0 - dist / (HALO + 1), 0.0)


def in_parts(values, extra):
    below = lax.broadcasted_iota(jnp.int32, values.shape, 0)
    extra_high = extra.astype(jnp.bfloat16).astype(jnp.float32)
    extra_middle = (extra - extra_high).astype(jnp.bfloat16).astype(jnp.float32)
    extra_low = extra - extra_high - extra_middle
    last = jnp.where(below == 0, extra_high, jnp.where(below == 1, extra_middle, extra_low))
    last = jnp.where(below < 3, last, 0.0)
    high = values.astype(jnp.bfloat16).astype(jnp.float32)
    middle = (values - high).astype(jnp.bfloat16).astype(jnp.float32)
    low = values - high - middle
    return jnp.concatenate([high, middle, low, last], axis=0).astype(jnp.bfloat16)


def from_parts(ref):
    rows = ref[ref.shape[0] - 4 * TILE :, :].astype(jnp.float32)
    return rows[:TILE] + rows[TILE : 2 * TILE] + rows[2 * TILE : 3 * TILE]


def observe_kernel(*refs):
    odd_ref, state_ref, rows_ref = refs[:3]
    own_ref, near_ref, far_ref, part_ref = refs[6:10]
    cells_ref, index_ref, value_ref, var_ref, sems = refs[10:]
    lon_dev, lat, members = cells_ref.shape
    nobs = index_ref.shape[1]
    edge = rows_ref.shape[0] // lon_dev * HALO
    last = rows_ref.shape[0] - edge
    far_at = pl.multiple_of(odd_ref[0] * last, 16)
    near_at = pl.multiple_of(last - far_at, 16)
    fetches = [
        (refs[3], index_ref),
        (refs[4], value_ref),
        (refs[5], var_ref),
        (state_ref.at[:, 0], cells_ref),
        (rows_ref.at[pl.ds(far_at, edge), :], far_ref.at[pl.ds(0, edge), :]),
        (rows_ref.at[pl.ds(near_at, edge), :], near_ref.at[pl.ds(0, edge), :]),
    ]
    copies = [
        pltpu.make_async_copy(src, dst, sems.at[i]) for i, (src, dst) in enumerate(fetches)
    ]
    for copy in copies:
        copy.start()
    for copy in copies[:4]:
        copy.wait()
    rows = cells_ref[...].reshape(lon_dev * lat, members)
    index = index_ref[...]
    sub = lax.broadcasted_iota(jnp.int32, (TILE, nobs), 0)
    table = jnp.where(
        sub == 0,
        index.astype(jnp.float32),
        jnp.where(sub == 1, value_ref[...], var_ref[...]),
    ).T
    index_col = table[:, 0:1].astype(jnp.int32)
    value = table[:, 1:2]
    var = table[:, 2:3]
    pick = index_col == lax.broadcasted_iota(jnp.int32, (nobs, lon_dev * lat), 1)
    pick = jnp.where(pick, 1.0, 0.0).astype(jnp.bfloat16)
    seen = jnp.dot(pick, rows, preferred_element_type=jnp.float32)
    centre = jnp.sum(seen, axis=1, keepdims=True) * (1.0 / members)
    spread = jnp.sum((seen - centre) ** 2, axis=1, keepdims=True) * (1.0 / (members - 1))
    innovation = (value - centre) ** 2 / (var + spread)
    part = jnp.sum(innovation, axis=0, keepdims=True)
    part_ref[...] = jnp.broadcast_to(part, part_ref.shape)
    terms = (value - seen) ** 2 * (1.0 / var)
    lon = (index // lat).astype(jnp.float32)
    along = index.astype(jnp.float32) - lon * lat
    blocks = own_ref.shape[0]
    block = lax.broadcasted_iota(jnp.int32, (blocks, nobs), 0).astype(jnp.float32)
    across = line_weight(along - REGION * block + HALO)
    side = jnp.where(odd_ref[0] == 1, float(REGION), float(-REGION))
    weights = [line_weight(lon + (HALO + shift)) * across for shift in (0.0, side, -side)]
    like = jnp.dot(
        jnp.concatenate(weights, axis=0), terms, precision=HIGH, preferred_element_type=jnp.float32
    )
    own_ref[...] = like[:blocks]
    near_ref[edge:, :] = in_parts(like[blocks : 2 * blocks], part)
    far_ref[edge:, :] = in_parts(like[2 * blocks :], jnp.zeros_like(part))
    for copy in copies[4:]:
        copy.wait()


def observe(odd, state, obs_index, obs_value, obs_var):
    lon_dev, nvar, lat, members = state.shape
    nobs = obs_index.size
    assert lat // REGION == TILE
    like = jax.ShapeDtypeStruct((lat // REGION, members), jnp.float32)
    payload = pltpu.VMEM((HALO * nvar * lat + 4 * TILE, members), state.dtype)
    part = jax.ShapeDtypeStruct((TILE, 128), jnp.float32)
    arrays = state, state.reshape(-1, members), obs_index[None], obs_value[None], obs_var[None]
    return pl.pallas_call(
        observe_kernel,
        in_specs=[pl.BlockSpec(memory_space=pltpu.SMEM)]
        + [pl.BlockSpec(memory_space=pltpu.HBM)] * len(arrays),
        out_specs=[pl.BlockSpec(memory_space=pltpu.VMEM)] * 4,
        out_shape=[like, payload, payload, part],
        scratch_shapes=[
            pltpu.VMEM((lon_dev, lat, members), state.dtype),
            pltpu.VMEM((1, nobs), jnp.int32),
            pltpu.VMEM((1, nobs), jnp.float32),
            pltpu.VMEM((1, nobs), jnp.float32),
            pltpu.SemaphoreType.DMA((6,)),
        ],
        compiler_params=pltpu.CompilerParams(vmem_limit_bytes=16 * 2**20),
        name="observe",
    )(odd, *[pltpu.with_memory_space_constraint(x, pltpu.HBM) for x in arrays])


def pair_tiles(ref, step, steps):
    size = PAIR * TILE
    lat = steps * size

    def load(at):
        at = pl.multiple_of(at * size, size)
        if len(ref.shape) == 4:
            return ref[:, :, pl.ds(at, size), :].astype(jnp.float32)
        planes = ref.shape[0] // lat
        rows = [ref[pl.ds(i * lat + at, size), :] for i in range(planes)]
        rows = jnp.stack(rows).astype(jnp.float32)
        return rows.reshape(HALO, planes // HALO, size, rows.shape[-1])

    here = load(step)
    before = load(jnp.maximum(step - 1, 0))[:, :, TILE:]
    after = load(jnp.minimum(step + 1, steps - 1))[:, :, :TILE]
    before = jnp.where(step == 0, 0.0, before)
    after = jnp.where(step == steps - 1, 0.0, after)
    return before, here[:, :, :TILE], here[:, :, TILE:], after


def halo_weights(to_left):
    steps = [jnp.float32(1.0) - jnp.float32(d) / jnp.float32(HALO + 1) for d in range(HALO, 0, -1)]
    return [jnp.where(to_left, x, y) for x, y in zip(steps, steps[::-1])]


def turn_tiles(low, high, turned_ref, step):
    for at, tile in enumerate((low, high)):
        flat = tile.reshape(-1, tile.shape[-1]).astype(jnp.bfloat16)
        turned_ref[step * PAIR + at] = flat.T


def gram_of(tiles, turned_ref, weights, step, steps):
    before, low, high, after = tiles
    columns, nvar, _, members = low.shape
    depth = columns * nvar * TILE
    row = lax.broadcasted_iota(jnp.int32, (1, TILE, members), 1)
    upper = row < HALO
    rowf = row.astype(jnp.float32)
    edge = line_weight(jnp.where(upper, rowf + (HALO + REGION), rowf - HALO))
    lane = lax.broadcasted_iota(jnp.int32, (1, depth), 1) & (TILE - 1)
    grams = []
    for at, (own, following, preceding) in enumerate(((low, high, before), (high, after, low))):
        region = step * PAIR + at
        margin = jnp.where(upper, following, preceding)
        main_rows, margin_rows = [], []
        for column, weight in enumerate(weights):
            main_rows.append(own[column] if weight is None else own[column] * weight)
            scale = edge if weight is None else edge * weight
            margin_rows.append(margin[column] * scale)
        weighted = jnp.concatenate([jnp.stack(main_rows), jnp.stack(margin_rows)], axis=0)
        weighted = weighted.reshape(2 * depth, members).astype(jnp.bfloat16)
        has_next = jnp.where(region + 1 < steps * PAIR, 1.0, 0.0)
        has_prev = jnp.where(region > 0, 1.0, 0.0)
        take_next = jnp.where(lane < HALO, has_next, 0.0).astype(jnp.bfloat16)
        take_prev = jnp.where(lane < HALO, 0.0, has_prev).astype(jnp.bfloat16)
        turned = (
            turned_ref[jnp.minimum(region + 1, steps * PAIR - 1)] * take_next
            + turned_ref[jnp.maximum(region - 1, 0)] * take_prev
        )
        turned = jnp.concatenate([turned_ref[region], turned], axis=1)
        grams.append(jnp.dot(turned, weighted, preferred_element_type=jnp.float32))
    return grams


def slab_copies(src_ref, dst_ref, sems, only=None):
    size = PAIR * TILE

    def slab(at):
        rows = pl.ds(pl.multiple_of(at * size, size), size)
        return pltpu.make_async_copy(
            src_ref.at[:, :, rows, :], dst_ref.at[:, :, rows, :], sems.at[at]
        )

    return slab(only) if only is not None else [slab(i) for i in range(src_ref.shape[2] // size)]


def own_gram_kernel(odd_ref, state_hbm_ref, near_ref, own_ref, gram_ref, like_ref, *scratch):
    state_ref, near_turned_ref, turned_ref, sems = scratch
    steps = gram_ref.shape[0] // PAIR
    copies = slab_copies(state_hbm_ref, state_ref, sems)
    for copy in copies:
        copy.start()
    like_ref[...] = own_ref[...] + from_parts(near_ref)

    def add_strip(ref, turned_ref, weights, first):
        def turn(step, carry):
            tiles = pair_tiles(ref, step, steps)
            turn_tiles(tiles[1], tiles[2], turned_ref, step)
            return carry

        def pair(step, carry):
            grams = gram_of(pair_tiles(ref, step, steps), turned_ref, weights, step, steps)
            for at in range(PAIR):
                region = step * PAIR + at
                gram_ref[region] = grams[at] if first else gram_ref[region] + grams[at]
            return carry

        lax.fori_loop(0, steps, turn, 0)
        lax.fori_loop(0, steps, pair, 0)

    add_strip(near_ref, near_turned_ref, halo_weights(odd_ref[0] == 1), True)
    for copy in copies:
        copy.wait()
    add_strip(state_ref, turned_ref, [None] * state_ref.shape[0], False)


def own_gram(odd, state, near, own):
    lon_dev, nvar, lat, members = state.shape
    tiles = lat // TILE
    vmem = pl.BlockSpec(memory_space=pltpu.VMEM)
    return pl.pallas_call(
        own_gram_kernel,
        in_specs=[
            pl.BlockSpec(memory_space=pltpu.SMEM),
            pl.BlockSpec(memory_space=pltpu.HBM),
            vmem,
            vmem,
        ],
        out_specs=[vmem, vmem],
        out_shape=[
            jax.ShapeDtypeStruct((lat // REGION, members, members), jnp.float32),
            jax.ShapeDtypeStruct(own.shape, jnp.float32),
        ],
        scratch_shapes=[
            pltpu.VMEM(state.shape, state.dtype),
            pltpu.VMEM((tiles, members, HALO * nvar * TILE), state.dtype),
            pltpu.VMEM((tiles, members, lon_dev * nvar * TILE), state.dtype),
            pltpu.SemaphoreType.DMA((lat // (PAIR * TILE),)),
        ],
        compiler_params=pltpu.CompilerParams(vmem_limit_bytes=16 * 2**20),
        name="own_gram",
    )(odd, pltpu.with_memory_space_constraint(state, pltpu.HBM), near, own)


def halves(ref, region, rows):
    members = ref.shape[-1]
    return [ref[region, rows, at : at + 128] for at in range(0, members, 128)]


def diagonal(gram_ref, region):
    members = gram_ref.shape[-1]
    across = [None] * (members // 128)
    down = []
    for start in range(0, members, ROWS):
        lane = start // 128
        gram = gram_ref[region, pl.ds(start, ROWS), lane * 128 : lane * 128 + 128]
        i = lax.broadcasted_iota(jnp.int32, gram.shape, 0) + start
        j = lax.broadcasted_iota(jnp.int32, gram.shape, 1) + lane * 128
        kept = jnp.where(i == j, gram, 0.0)
        down.append(jnp.broadcast_to(jnp.sum(kept, axis=1, keepdims=True), gram.shape))
        part = jnp.sum(kept.reshape(ROWS // TILE, TILE, 128), axis=0)
        across[lane] = part if across[lane] is None else across[lane] + part
    return [jnp.sum(x, axis=0, keepdims=True) for x in across], down


def prepare_kernel(scale, *refs):
    odd_ref, halo_ref, gram_in_ref, like_in_ref = refs[:4]
    gram_hbm_ref, kernel_ref, mass_ref, most_ref, like_ref, gram_ref, turned_ref, sems = refs[4:]
    regions, members, _ = gram_ref.shape
    steps = regions // PAIR
    like_ref[...] = like_in_ref[...] + from_parts(halo_ref)

    def keep(step):
        part = pl.ds(step * PAIR, PAIR)
        return pltpu.make_async_copy(gram_ref.at[part], gram_hbm_ref.at[part], sems.at[step])

    def turn(step, carry):
        tiles = pair_tiles(halo_ref, step, steps)
        turn_tiles(tiles[1], tiles[2], turned_ref, step)
        return carry

    lax.fori_loop(0, steps, turn, 0)

    def pair(step, carry):
        weights = halo_weights(odd_ref[0] == 0)
        grams = gram_of(pair_tiles(halo_ref, step, steps), turned_ref, weights, step, steps)
        for at in range(PAIR):
            region = step * PAIR + at
            gram_ref[region] = gram_in_ref[region] + grams[at]
        keep(step).start()
        return carry

    lax.fori_loop(0, steps, pair, 0)

    def exponentials(step, most):
        for at in range(PAIR):
            region = step * PAIR + at
            across, down = diagonal(gram_ref, region)
            across = [0.5 * LIFT - x * scale for x in across]
            masses = [0.0 for _ in across]
            for i, start in enumerate(range(0, members, ROWS)):
                rows = pl.ds(start, ROWS)
                base = 0.5 * LIFT - down[i] * scale
                for lane, (gram, x) in enumerate(zip(halves(gram_ref, region, rows), across)):
                    part = jnp.exp2(gram * (2.0 * scale) + base + x)
                    kernel_ref[region, rows, lane * 128 : lane * 128 + 128] = part
                    most = jnp.maximum(most, part)
                    part = jnp.sum(part.reshape(ROWS // TILE, TILE, 128), axis=0)
                    masses[lane] = masses[lane] + part
            masses = [jnp.sum(x, axis=0, keepdims=True) for x in masses]
            mass_ref[region] = jnp.concatenate(masses, axis=1)
        return most

    most = lax.fori_loop(0, steps, exponentials, jnp.zeros((ROWS, 128), jnp.float32))
    most_ref[...] = jnp.max(most.reshape(ROWS // TILE, TILE, 128), axis=0)

    def drain(step, carry):
        keep(step).wait()
        return carry

    lax.fori_loop(0, steps, drain, 0)


def prepare(odd, halo, gram, like, scale):
    regions = gram.shape[0]
    halo_depth = (halo.shape[0] - 4 * TILE) // regions
    vmem = pl.BlockSpec(memory_space=pltpu.VMEM)
    return pl.pallas_call(
        functools.partial(prepare_kernel, scale),
        in_specs=[pl.BlockSpec(memory_space=pltpu.SMEM)] + [vmem] * 3,
        out_specs=[pl.BlockSpec(memory_space=pltpu.HBM)] + [vmem] * 4,
        out_shape=[
            pltpu.HBM(gram.shape, jnp.float32),
            jax.ShapeDtypeStruct(gram.shape, jnp.float32),
            jax.ShapeDtypeStruct((regions, 1, like.shape[1]), jnp.float32),
            jax.ShapeDtypeStruct((TILE, 128), jnp.float32),
            jax.ShapeDtypeStruct(like.shape, jnp.float32),
        ],
        scratch_shapes=[
            pltpu.VMEM(gram.shape, jnp.float32),
            pltpu.VMEM((regions, gram.shape[1], halo_depth), halo.dtype),
            pltpu.SemaphoreType.DMA((regions // PAIR,)),
        ],
        compiler_params=pltpu.CompilerParams(vmem_limit_bytes=16 * 2**20),
        name="prepare",
    )(odd, halo, gram, like)


def fold(values, op):
    out = values[0]
    for value in values[1:]:
        out = op(out, value)
    return out


def transports_scaled(regions, kernel_ref, weight_ref, mass_ref):
    members = kernel_ref.shape[-1]
    starts = range(0, members, ROWS)
    lanes = range(members // 128)
    share = 2.0**MASS / members

    def lane_parts(ref, region):
        row = ref[region]
        return [row[:, lane * 128 : lane * 128 + 128] for lane in lanes]

    def settle(totals, region):
        return [w / x for w, x in zip(lane_parts(weight_ref, region), totals)]

    def masses_of(region, rows, factor):
        parts = [k * f for k, f in zip(halves(kernel_ref, region, rows), factor)]
        mass = jnp.sum(fold(parts, jnp.add), axis=1, keepdims=True)
        mass = jnp.broadcast_to(mass, (ROWS, 128))
        near = pl.reciprocal(mass, approx=True)
        return parts, mass, near * (2.0 - mass * near)

    def sweep(_, carry):
        least_i, least_j, factors = carry
        next_i, next_j, next_factors = [], [], []
        for region, low_i, low_j, factor in zip(regions, least_i, least_j, factors):
            totals = [None for _ in lanes]
            for start in starts:
                rows = pl.ds(start, ROWS)
                _, mass, ratio = masses_of(region, rows, factor)
                low_j = jnp.minimum(low_j, mass)
                for lane, kernel in enumerate(halves(kernel_ref, region, rows)):
                    part = jnp.sum((kernel * ratio).reshape(ROWS // TILE, TILE, 128), axis=0)
                    totals[lane] = part if totals[lane] is None else totals[lane] + part
            totals = [jnp.sum(x, axis=0, keepdims=True) * share for x in totals]
            next_i.append(jnp.minimum(low_i, fold(totals, jnp.minimum)))
            next_j.append(low_j)
            next_factors.append(settle(totals, region))
        return next_i, next_j, next_factors

    totals = [[x * 2.0**START for x in lane_parts(mass_ref, region)] for region in regions]
    least_i = [fold(x, jnp.minimum) for x in totals]
    least_j = [jnp.full((ROWS, 128), 1e30, jnp.float32) for _ in regions]
    factors = [settle(x, region) for x, region in zip(totals, regions)]
    carry = lax.fori_loop(0, SWEEPS - 1, sweep, (least_i, least_j, factors))
    least_i, least_j, factors = carry
    moves, last_j = [], []
    for region, low_j, factor in zip(regions, least_j, factors):
        blocks = []
        for start in starts:
            parts, mass, ratio = masses_of(region, pl.ds(start, ROWS), factor)
            low_j = jnp.minimum(low_j, mass)
            blocks.append(jnp.concatenate([x * ratio for x in parts], axis=1).astype(jnp.bfloat16))
        moves.append(jnp.concatenate(blocks, axis=0))
        last_j.append(low_j)
    return moves, fold(least_i, jnp.minimum), fold(last_j, jnp.minimum)


def transport_logs(gram, logw, scale):
    members = gram.shape[-1]
    j = lax.broadcasted_iota(jnp.int32, gram.shape, 0)
    i = lax.broadcasted_iota(jnp.int32, gram.shape, 1)
    kept = jnp.where(i == j, gram, 0.0)
    down = jnp.sum(kept, axis=1, keepdims=True)
    across = jnp.sum(kept, axis=0, keepdims=True)
    cost = (down + across - 2.0 * gram) * scale
    pot_g = jnp.zeros((members, 1), jnp.float32)
    for sweep in range(SWEEPS):
        term = pot_g - cost
        top = jnp.max(term, axis=0, keepdims=True)
        pot_f = logw - top - jnp.log(jnp.sum(jnp.exp2(term - top), axis=0, keepdims=True)) * LOG2E
        term = pot_f - cost
        top = jnp.max(term, axis=1, keepdims=True)
        pot_g = -math.log2(members) - top
        pot_g = pot_g - jnp.log(jnp.sum(jnp.exp2(term - top), axis=1, keepdims=True)) * LOG2E
    return (members * jnp.exp2(pot_f + pot_g - cost)).astype(jnp.bfloat16)


def transform(state_ref, pair, moves):
    lon_dev, nvar, _, members = state_ref.shape
    size = PAIR * TILE
    own = state_ref[:, :, pl.ds(pl.multiple_of(pair * size, size), size), :].astype(jnp.float32)
    parts = []
    for region, move in enumerate(moves):
        cells = own[:, :, region * TILE : (region + 1) * TILE].astype(jnp.bfloat16)
        cells = cells.reshape(lon_dev * nvar * TILE, members)
        moved = lax.dot_general(
            cells, move, (((1,), (1,)), ((), ())), preferred_element_type=jnp.float32
        )
        parts.append(moved.reshape(lon_dev, nvar, TILE, members))
    return jnp.concatenate(parts, axis=2).astype(jnp.bfloat16)


def finish_kernel(count, scale, *refs):
    state_hbm_ref, gram_hbm_ref, kernel_ref, mass_ref, most_ref, like_ref, sums_ref = refs[:7]
    out_ref, weight_ref, logw_ref, result_ref, state_ref, gram_ref, sems, state_sems = refs[7:]
    regions, members = kernel_ref.shape[0], kernel_ref.shape[-1]
    pairs = regions // PAIR
    size = PAIR * TILE
    fetches = slab_copies(state_hbm_ref, state_ref, state_sems)
    for copy in fetches:
        copy.start()

    total = jnp.sum(sums_ref[...], axis=0, keepdims=True)[:, 0:1] * (1.0 / TILE)
    like = -0.5 * (count / total) * like_ref[...]
    like = like - jnp.max(like, axis=1, keepdims=True)
    logw = (like - jnp.log(jnp.sum(jnp.exp(like), axis=1, keepdims=True))) * LOG2E
    weight = jnp.exp2(logw + MASS)
    for region in range(regions):
        weight_ref[region] = weight[region : region + 1]
        logw_ref[region] = logw[region : region + 1]

    def send(pair):
        at = pl.ds(pl.multiple_of(pair * size, size), size)
        return pltpu.make_async_copy(result_ref.at[pair], out_ref.at[:, :, at, :], sems.at[pair])

    def group(at, carry):
        first = at * GROUP
        moves, least_i, least_j = transports_scaled(
            [first + r for r in range(GROUP)], kernel_ref, weight_ref, mass_ref
        )
        for pair in range(GROUP // PAIR):
            where = at * (GROUP // PAIR) + pair
            slab_copies(state_hbm_ref, state_ref, state_sems, where).wait()
            result_ref[where] = transform(state_ref, where, moves[pair * PAIR : (pair + 1) * PAIR])
            send(where).start()
        return jnp.minimum(carry[0], least_i), jnp.minimum(carry[1], least_j)

    high = jnp.full((ROWS, 128), 1e30, jnp.float32)
    least_i, least_j = lax.fori_loop(0, regions // GROUP, group, (high[:1], high))

    def drain(pair, carry):
        send(pair).wait()
        return carry

    lax.fori_loop(0, pairs, drain, 0)
    row, col, most = jnp.min(least_i), jnp.min(least_j), jnp.max(most_ref[...])
    sound = (row >= 2.0**-24) & (col >= 2.0**-30) & (most <= 2.0**30) & (row * col >= 2.0**-34)

    @pl.when(jnp.logical_not(sound))
    def _():
        def again(pair, carry):
            moves = []
            for at in range(PAIR):
                region = pair * PAIR + at
                copy = pltpu.make_async_copy(gram_hbm_ref.at[region], gram_ref.at[at], state_sems.at[0])
                copy.start()
                copy.wait()
                moves.append(transport_logs(gram_ref[at], logw_ref[region], scale))
            result_ref[pair] = transform(state_ref, pair, moves)
            copy = send(pair)
            copy.start()
            copy.wait()
            return carry

        lax.fori_loop(0, pairs, again, 0)


def finish(state, gram, kernel, mass, most, like, sums, count, scale):
    lon_dev, nvar, lat, members = state.shape
    regions = lat // REGION
    vmem = pl.BlockSpec(memory_space=pltpu.VMEM)
    hbm = pl.BlockSpec(memory_space=pltpu.HBM)
    return pl.pallas_call(
        functools.partial(finish_kernel, count, scale),
        in_specs=[hbm, hbm] + [vmem] * 5,
        out_specs=pl.BlockSpec(memory_space=pl.ANY),
        out_shape=jax.ShapeDtypeStruct(state.shape, state.dtype),
        scratch_shapes=[
            pltpu.VMEM((regions, 1, members), jnp.float32),
            pltpu.VMEM((regions, 1, members), jnp.float32),
            pltpu.VMEM((regions // PAIR, lon_dev, nvar, PAIR * TILE, members), jnp.bfloat16),
            pltpu.VMEM(state.shape, state.dtype),
            pltpu.VMEM((PAIR, members, members), jnp.float32),
            pltpu.SemaphoreType.DMA((regions // PAIR,)),
            pltpu.SemaphoreType.DMA((regions // PAIR,)),
        ],
        compiler_params=pltpu.CompilerParams(vmem_limit_bytes=24 * 2**20),
        name="finish",
    )(
        *[pltpu.with_memory_space_constraint(x, pltpu.HBM) for x in (state, gram)],
        kernel,
        mass,
        most,
        like,
        sums,
    )


def on_device(state, obs_index, obs_value, obs_var):
    nvar = state.shape[1]
    count = lax.axis_size("lon")
    odd = (lax.axis_index("lon") & 1).astype(jnp.int32).reshape(1)
    near_pairs = [(i, i ^ 1) for i in range(count)]
    far_pairs = [(i, (i + 1 if i % 2 else i - 1) % count) for i in range(count)]
    own_like, for_near, for_far, part = observe(odd, state, obs_index, obs_value, obs_var)
    far = lax.ppermute(for_far, "lon", far_pairs)
    near = lax.ppermute(for_near, "lon", near_pairs)
    start = near.shape[0] - TILE
    part = part[0] + jnp.sum(near[start : start + 3, :128].astype(jnp.float32), axis=0)
    sums = lax.all_to_all(
        jnp.broadcast_to(part, (count // 2 * TILE, 128)),
        "lon",
        0,
        0,
        axis_index_groups=[list(range(core, count, 2)) for core in range(2)],
        tiled=True,
    )
    offsets = range(REGION + 2 * HALO)
    line = [1.0 - max(0, HALO - p, p - (HALO + REGION - 1)) / (HALO + 1) for p in offsets]
    scale = LOG2E / EPS / (nvar * sum(line) ** 2)
    gram, like = own_gram(odd, state, near, own_like)
    gram, kernel, mass, most, like = prepare(odd, far, gram, like, scale)
    nobs = float(obs_index.shape[0] * count)
    return finish(state, gram, kernel, mass, most, like, sums, nobs, scale)


def solution(mesh):
    return jax.shard_map(
        on_device,
        mesh=mesh,
        in_specs=(
            P(("ens", "lon"), None, None, None),
            P(("ens", "lon")),
            P(("ens", "lon")),
            P(("ens", "lon")),
        ),
        out_specs=P(("ens", "lon"), None, None, None),
        check_vma=False,
    )
```

```python
import functools
import math

import jax
import jax.numpy as jnp
from jax import lax
from jax.experimental import pallas as pl
from jax.experimental.pallas import tpu as pltpu
from jax.sharding import PartitionSpec as P

REGION = 8
HALO = 4
SWEEPS = 4
EPS = 0.05
TILE = 8
PAIR = 2
LOG2E = 1.4426950408889634
ROWS = 32
FIRST = 3
LIFT, START, MASS = 20, -10, 60

HIGH = lax.Precision.HIGHEST


def line_weight(place):
    dist = jnp.maximum(0.0, jnp.maximum(HALO - place, place - (HALO + REGION - 1)))
    inside = (place >= 0) & (place < REGION + 2 * HALO)
    return jnp.where(inside, 1.0 - dist / (HALO + 1), 0.0)


def like_rows(rows):
    rows = rows.astype(jnp.float32)
    return rows[:TILE] + rows[TILE : 2 * TILE] + rows[2 * TILE : 3 * TILE]


def in_parts(values, extra):
    below = lax.broadcasted_iota(jnp.int32, values.shape, 0)
    extra_high = extra.astype(jnp.bfloat16).astype(jnp.float32)
    extra_middle = (extra - extra_high).astype(jnp.bfloat16).astype(jnp.float32)
    extra_low = extra - extra_high - extra_middle
    last = jnp.where(below == 0, extra_high, jnp.where(below == 1, extra_middle, extra_low))
    last = jnp.where(below < 3, last, 0.0)
    high = values.astype(jnp.bfloat16).astype(jnp.float32)
    middle = (values - high).astype(jnp.bfloat16).astype(jnp.float32)
    low = values - high - middle
    return jnp.concatenate([high, middle, low, last], axis=0).astype(jnp.bfloat16)


def observe_kernel(*refs):
    odd_ref, state_ref, planes_ref = refs[:3]
    own_ref, near_ref, far_ref, far_last_ref, part_ref = refs[6:11]
    cells_ref, index_ref, value_ref, var_ref, sems = refs[11:]
    lon_dev, lat, members = cells_ref.shape
    nobs = index_ref.shape[1]
    edge = planes_ref.shape[0] // lon_dev * HALO
    last = planes_ref.shape[0] - edge
    far_at = odd_ref[0] * last
    cut = far_ref.shape[1]
    far_planes = planes_ref.at[pl.ds(far_at, edge)]
    fetches = [
        (refs[3], index_ref),
        (refs[4], value_ref),
        (refs[5], var_ref),
        (state_ref.at[:, 0], cells_ref),
        (far_planes.at[:, pl.ds(0, cut), :], far_ref.at[pl.ds(0, edge)]),
        (planes_ref.at[pl.ds(last - far_at, edge)], near_ref.at[pl.ds(0, edge)]),
        (far_planes.at[:, pl.ds(cut, lat - cut), :], far_last_ref),
    ]
    copies = [
        pltpu.make_async_copy(src, dst, sems.at[i]) for i, (src, dst) in enumerate(fetches)
    ]
    for copy in copies:
        copy.start()
    for copy in copies[:4]:
        copy.wait()
    rows = cells_ref[...].reshape(lon_dev * lat, members)
    index = index_ref[...]
    sub = lax.broadcasted_iota(jnp.int32, (TILE, nobs), 0)
    table = jnp.where(
        sub == 0,
        index.astype(jnp.float32),
        jnp.where(sub == 1, value_ref[...], var_ref[...]),
    ).T
    index_col = table[:, 0:1].astype(jnp.int32)
    value = table[:, 1:2]
    var = table[:, 2:3]
    pick = index_col == lax.broadcasted_iota(jnp.int32, (nobs, lon_dev * lat), 1)
    pick = jnp.where(pick, 1.0, 0.0).astype(jnp.bfloat16)
    seen = jnp.dot(pick, rows, preferred_element_type=jnp.float32)
    centre = jnp.sum(seen, axis=1, keepdims=True) * (1.0 / members)
    spread = jnp.sum((seen - centre) ** 2, axis=1, keepdims=True) * (1.0 / (members - 1))
    innovation = (value - centre) ** 2 / (var + spread)
    part = jnp.sum(innovation, axis=0, keepdims=True)
    part_ref[...] = jnp.broadcast_to(part, part_ref.shape)
    terms = (value - seen) ** 2 * (1.0 / var)
    lon = (index // lat).astype(jnp.float32)
    along = index.astype(jnp.float32) - lon * lat
    blocks = own_ref.shape[0]
    block = lax.broadcasted_iota(jnp.int32, (blocks, nobs), 0).astype(jnp.float32)
    across = line_weight(along - REGION * block + HALO)
    side = jnp.where(odd_ref[0] == 1, float(REGION), float(-REGION))
    weights = [line_weight(lon + (HALO + shift)) * across for shift in (0.0, side, -side)]
    like = jnp.dot(
        jnp.concatenate(weights, axis=0), terms, precision=HIGH, preferred_element_type=jnp.float32
    )
    own_ref[...] = like[:blocks]
    near_ref[edge, : 4 * TILE, :] = in_parts(like[blocks : 2 * blocks], part)
    far_ref[edge, : 4 * TILE, :] = in_parts(like[2 * blocks :], jnp.zeros_like(part))
    for copy in copies[4:]:
        copy.wait()


def observe(odd, state, obs_index, obs_value, obs_var):
    lon_dev, nvar, lat, members = state.shape
    nobs = obs_index.size
    assert lat // REGION == TILE
    like = jax.ShapeDtypeStruct((lat // REGION, members), jnp.float32)
    planes = HALO * nvar
    cut = FIRST * PAIR * TILE
    near = pltpu.VMEM((planes + 1, lat, members), state.dtype)
    far = pltpu.VMEM((planes + 1, cut, members), state.dtype)
    far_last = pltpu.VMEM((planes, lat - cut, members), state.dtype)
    part = jax.ShapeDtypeStruct((TILE, 128), jnp.float32)
    arrays = state, state.reshape(-1, lat, members), obs_index[None], obs_value[None], obs_var[None]
    return pl.pallas_call(
        observe_kernel,
        in_specs=[pl.BlockSpec(memory_space=pltpu.SMEM)]
        + [pl.BlockSpec(memory_space=pltpu.HBM)] * len(arrays),
        out_specs=[pl.BlockSpec(memory_space=pltpu.VMEM)] * 5,
        out_shape=[like, near, far, far_last, part],
        scratch_shapes=[
            pltpu.VMEM((lon_dev, lat, members), state.dtype),
            pltpu.VMEM((1, nobs), jnp.int32),
            pltpu.VMEM((1, nobs), jnp.float32),
            pltpu.VMEM((1, nobs), jnp.float32),
            pltpu.SemaphoreType.DMA((7,)),
        ],
        compiler_params=pltpu.CompilerParams(vmem_limit_bytes=16 * 2**20),
        name="observe",
    )(odd, *[pltpu.with_memory_space_constraint(x, pltpu.HBM) for x in arrays])


def slab_of(refs, planes, at):
    size = PAIR * TILE
    for ref in refs:
        if at * size < ref.shape[1]:
            return ref[:planes, at * size : (at + 1) * size, :].astype(jnp.float32)
        at -= ref.shape[1] // size


def pair_tiles(load, step, steps):
    here = load(step)
    none = jnp.zeros_like(here[:, :TILE])
    before = load(step - 1)[:, TILE:] if step else none
    after = load(step + 1)[:, :TILE] if step + 1 < steps else none
    return before, here[:, :TILE], here[:, TILE:], after


def halo_weights(to_left):
    steps = [jnp.float32(1.0) - jnp.float32(d) / jnp.float32(HALO + 1) for d in range(HALO, 0, -1)]
    return [jnp.where(to_left, x, y) for x, y in zip(steps, steps[::-1])]


def turn(tile):
    return tile.reshape(-1, tile.shape[-1]).astype(jnp.bfloat16).T


def gram_of(tiles, turned, weights):
    planes, _, members = tiles[0].shape
    depth = planes * TILE
    row = lax.broadcasted_iota(jnp.int32, (TILE, members), 0)
    upper = row < HALO
    rowf = row.astype(jnp.float32)
    edge = line_weight(jnp.where(upper, rowf + (HALO + REGION), rowf - HALO))
    lane = lax.broadcasted_iota(jnp.int32, (1, depth), 1) & (TILE - 1)
    take_next = jnp.where(lane < HALO, 1.0, 0.0).astype(jnp.bfloat16)
    take_prev = jnp.where(lane < HALO, 0.0, 1.0).astype(jnp.bfloat16)
    grams = []
    for at in (1, 2):
        margin = jnp.where(upper, tiles[at + 1], tiles[at - 1])
        main_rows, margin_rows = [], []
        for plane, weight in enumerate(weights):
            own = tiles[at][plane]
            main_rows.append(own if weight is None else own * weight)
            margin_rows.append(margin[plane] * (edge if weight is None else edge * weight))
        weighted = jnp.stack(main_rows + margin_rows)
        weighted = weighted.reshape(2 * depth, members).astype(jnp.bfloat16)
        margin = turned[at + 1] * take_next + turned[at - 1] * take_prev
        both = jnp.concatenate([turned[at], margin], axis=1)
        grams.append(jnp.dot(both, weighted, preferred_element_type=jnp.float32))
    return grams


def slab_copies(src_ref, dst_ref, sems, only=None):
    size = PAIR * TILE

    def slab(at):
        rows = pl.ds(pl.multiple_of(at * size, size), size)
        return pltpu.make_async_copy(
            src_ref.at[:, :, rows, :], dst_ref.at[:, :, rows, :], sems.at[at]
        )

    return slab(only) if only is not None else [slab(i) for i in range(src_ref.shape[2] // size)]


def own_gram_kernel(odd_ref, state_hbm_ref, near_ref, own_ref, *refs):
    gram_refs, like_ref, state_ref, sems = refs[:-3], refs[-3], refs[-2], refs[-1]
    near_planes = near_ref.shape[0] - 1
    nvar = near_planes // HALO
    lon_dev = state_ref.shape[0]
    steps = state_ref.shape[2] // (PAIR * TILE)
    copies = slab_copies(state_hbm_ref, state_ref, sems)
    for copy in copies:
        copy.start()
    like_ref[...] = own_ref[...] + like_rows(near_ref[near_planes, : 4 * TILE, :])
    size = PAIR * TILE

    def load(step):
        own = state_ref[:, :, step * size : (step + 1) * size, :].astype(jnp.float32)
        own = own.reshape(lon_dev * nvar, size, own.shape[-1])
        return jnp.concatenate([own, slab_of([near_ref], near_planes, step)], axis=0)

    weights = [None] * (lon_dev * nvar)
    weights += [w for w in halo_weights(odd_ref[0] == 1) for _ in range(nvar)]
    for copy in copies:
        copy.wait()
    slabs = [load(step) for step in range(steps)]
    add_grams(slabs, weights, range(steps), None, gram_refs)


def add_grams(slabs, weights, pairs, old_refs, new_refs):
    steps = len(slabs)
    none = jnp.zeros_like(slabs[pairs[0]][:, :TILE])
    turned_none = jnp.zeros((none.shape[-1], none.shape[0] * TILE), jnp.bfloat16)
    tiles, turned = {}, {}
    for at in range(pairs[0] * PAIR - 1, pairs[-1] * PAIR + PAIR + 1):
        if 0 <= at < steps * PAIR:
            half = at % PAIR
            tiles[at] = slabs[at // PAIR][:, half * TILE : (half + 1) * TILE]
            turned[at] = turn(tiles[at])
        else:
            tiles[at], turned[at] = none, turned_none
    for index, pair in enumerate(pairs):
        window = range(pair * PAIR - 1, pair * PAIR + PAIR + 1)
        grams = gram_of([tiles[i] for i in window], [turned[i] for i in window], weights)
        for half in range(PAIR):
            per = new_refs[0].shape[0]
            ref, region = divmod(index * PAIR + half, per)
            gram = grams[half]
            new_refs[ref][region] = gram if old_refs is None else old_refs[ref][region] + gram


def own_gram(odd, state, near, own):
    _, _, lat, members = state.shape
    vmem = pl.BlockSpec(memory_space=pltpu.VMEM)
    half = jax.ShapeDtypeStruct((lat // REGION // 2, members, members), jnp.float32)
    return pl.pallas_call(
        own_gram_kernel,
        in_specs=[
            pl.BlockSpec(memory_space=pltpu.SMEM),
            pl.BlockSpec(memory_space=pltpu.HBM),
            vmem,
            vmem,
        ],
        out_specs=[vmem] * 3,
        out_shape=[half, half, jax.ShapeDtypeStruct(own.shape, jnp.float32)],
        scratch_shapes=[
            pltpu.VMEM(state.shape, state.dtype),
            pltpu.SemaphoreType.DMA((lat // (PAIR * TILE),)),
        ],
        compiler_params=pltpu.CompilerParams(vmem_limit_bytes=24 * 2**20),
        name="own_gram",
    )(odd, pltpu.with_memory_space_constraint(state, pltpu.HBM), near, own)


def halves(ref, region, rows):
    members = ref.shape[-1]
    return [ref[region, rows, at : at + 128] for at in range(0, members, 128)]


def diagonal(gram_ref, region):
    members = gram_ref.shape[-1]
    across = [None] * (members // 128)
    down = []
    for start in range(0, members, ROWS):
        lane = start // 128
        gram = gram_ref[region, pl.ds(start, ROWS), lane * 128 : lane * 128 + 128]
        i = lax.broadcasted_iota(jnp.int32, gram.shape, 0) + start
        j = lax.broadcasted_iota(jnp.int32, gram.shape, 1) + lane * 128
        kept = jnp.where(i == j, gram, 0.0)
        down.append(jnp.broadcast_to(jnp.sum(kept, axis=1, keepdims=True), gram.shape))
        part = jnp.sum(kept.reshape(ROWS // TILE, TILE, 128), axis=0)
        across[lane] = part if across[lane] is None else across[lane] + part
    return [jnp.sum(x, axis=0, keepdims=True) for x in across], down


def kernel_matrices(gram_ref, kernel_ref, mass_ref, scale):
    members = gram_ref.shape[-1]
    most = None
    for region in range(gram_ref.shape[0]):
        across, down = diagonal(gram_ref, region)
        across = [0.5 * LIFT - x * scale for x in across]
        masses = [0.0 for _ in across]
        for i, start in enumerate(range(0, members, ROWS)):
            rows = pl.ds(start, ROWS)
            base = 0.5 * LIFT - down[i] * scale
            for lane, (gram, x) in enumerate(zip(halves(gram_ref, region, rows), across)):
                part = jnp.exp2(gram * (2.0 * scale) + base + x)
                kernel_ref[region, rows, lane * 128 : lane * 128 + 128] = part
                most = part if most is None else jnp.maximum(most, part)
                part = jnp.sum(part.reshape(ROWS // TILE, TILE, 128), axis=0)
                masses[lane] = masses[lane] + part
        masses = [jnp.sum(x, axis=0, keepdims=True) for x in masses]
        mass_ref[region] = jnp.concatenate(masses, axis=1)
    return jnp.max(most.reshape(ROWS // TILE, TILE, 128), axis=0)


def far_grams(odd_ref, halo_refs, lat, pairs, old_ref, new_ref):
    planes = halo_refs[0].shape[0] - 1
    slabs = [None] * (lat // (PAIR * TILE))
    for at in range(max(pairs[0] - 1, 0), min(pairs[-1] + 2, len(slabs))):
        slabs[at] = slab_of(halo_refs, planes, at)
    weights = [w for w in halo_weights(odd_ref[0] == 0) for _ in range(planes // HALO)]
    add_grams(slabs, weights, pairs, [old_ref], [new_ref])


def prepare_kernel(scale, lat, *refs):
    odd_ref, halo_ref, old_ref, like_in_ref = refs[:4]
    gram_hbm_ref, kernel_ref, mass_ref, most_ref, like_ref, gram_ref, sem = refs[4:]
    like_ref[...] = like_in_ref[...] + like_rows(halo_ref[halo_ref.shape[0] - 1, : 4 * TILE, :])
    far_grams(odd_ref, [halo_ref], lat, range(gram_ref.shape[0] // PAIR), old_ref, gram_ref)
    keep = pltpu.make_async_copy(gram_ref, gram_hbm_ref, sem)
    keep.start()
    most_ref[...] = kernel_matrices(gram_ref, kernel_ref, mass_ref, scale)
    keep.wait()


def prepare(odd, halo, gram, like, lat, scale):
    vmem = pl.BlockSpec(memory_space=pltpu.VMEM)
    return pl.pallas_call(
        functools.partial(prepare_kernel, scale, lat),
        in_specs=[pl.BlockSpec(memory_space=pltpu.SMEM)] + [vmem] * 3,
        out_specs=[pl.BlockSpec(memory_space=pltpu.HBM)] + [vmem] * 4,
        out_shape=[
            pltpu.HBM(gram.shape, jnp.float32),
            jax.ShapeDtypeStruct(gram.shape, jnp.float32),
            jax.ShapeDtypeStruct((gram.shape[0], 1, like.shape[1]), jnp.float32),
            jax.ShapeDtypeStruct((TILE, 128), jnp.float32),
            jax.ShapeDtypeStruct(like.shape, jnp.float32),
        ],
        scratch_shapes=[pltpu.VMEM(gram.shape, jnp.float32), pltpu.SemaphoreType.DMA],
        compiler_params=pltpu.CompilerParams(vmem_limit_bytes=24 * 2**20),
        name="prepare",
    )(odd, halo, gram, like)


def fold(values, op):
    out = values[0]
    for value in values[1:]:
        out = op(out, value)
    return out


def transports_scaled(kernel_ref, weights, mass_ref):
    regions = range(kernel_ref.shape[0])
    members = kernel_ref.shape[-1]
    starts = range(0, members, ROWS)
    lanes = range(members // 128)
    share = 2.0**MASS / members

    def lane_parts(row):
        return [row[:, lane * 128 : lane * 128 + 128] for lane in lanes]

    def settle(totals, region):
        return [w / x for w, x in zip(lane_parts(weights[region : region + 1]), totals)]

    def masses_of(region, rows, factor):
        parts = [k * f for k, f in zip(halves(kernel_ref, region, rows), factor)]
        mass = jnp.sum(fold(parts, jnp.add), axis=1, keepdims=True)
        mass = jnp.broadcast_to(mass, (ROWS, 128))
        near = pl.reciprocal(mass, approx=True)
        return parts, mass, near * (2.0 - mass * near)

    def sweep(_, carry):
        least_i, least_j, factors = carry
        next_i, next_j, next_factors = [], [], []
        for region, low_i, low_j, factor in zip(regions, least_i, least_j, factors):
            totals = [None for _ in lanes]
            for start in starts:
                rows = pl.ds(start, ROWS)
                _, mass, ratio = masses_of(region, rows, factor)
                low_j = jnp.minimum(low_j, mass)
                for lane, kernel in enumerate(halves(kernel_ref, region, rows)):
                    part = jnp.sum((kernel * ratio).reshape(ROWS // TILE, TILE, 128), axis=0)
                    totals[lane] = part if totals[lane] is None else totals[lane] + part
            totals = [jnp.sum(x, axis=0, keepdims=True) * share for x in totals]
            next_i.append(jnp.minimum(low_i, fold(totals, jnp.minimum)))
            next_j.append(low_j)
            next_factors.append(settle(totals, region))
        return next_i, next_j, next_factors

    totals = [[x * 2.0**START for x in lane_parts(mass_ref[region])] for region in regions]
    least_i = [fold(x, jnp.minimum) for x in totals]
    least_j = [jnp.full((ROWS, 128), 1e30, jnp.float32) for _ in regions]
    factors = [settle(x, region) for x, region in zip(totals, regions)]
    carry = lax.fori_loop(0, SWEEPS - 1, sweep, (least_i, least_j, factors))
    least_i, least_j, factors = carry
    moves, last_j = [], []
    for region, low_j, factor in zip(regions, least_j, factors):
        blocks = []
        for start in starts:
            parts, mass, ratio = masses_of(region, pl.ds(start, ROWS), factor)
            low_j = jnp.minimum(low_j, mass)
            blocks.append(jnp.concatenate([x * ratio for x in parts], axis=1).astype(jnp.bfloat16))
        moves.append(jnp.concatenate(blocks, axis=0))
        last_j.append(low_j)
    return moves, fold(least_i, jnp.minimum), fold(last_j, jnp.minimum)


def transport_logs(gram, logw, scale):
    members = gram.shape[-1]
    j = lax.broadcasted_iota(jnp.int32, gram.shape, 0)
    i = lax.broadcasted_iota(jnp.int32, gram.shape, 1)
    kept = jnp.where(i == j, gram, 0.0)
    down = jnp.sum(kept, axis=1, keepdims=True)
    across = jnp.sum(kept, axis=0, keepdims=True)
    cost = (down + across - 2.0 * gram) * scale
    pot_g = jnp.zeros((members, 1), jnp.float32)
    for sweep in range(SWEEPS):
        term = pot_g - cost
        top = jnp.max(term, axis=0, keepdims=True)
        pot_f = logw - top - jnp.log(jnp.sum(jnp.exp2(term - top), axis=0, keepdims=True)) * LOG2E
        term = pot_f - cost
        top = jnp.max(term, axis=1, keepdims=True)
        pot_g = -math.log2(members) - top
        pot_g = pot_g - jnp.log(jnp.sum(jnp.exp2(term - top), axis=1, keepdims=True)) * LOG2E
    return (members * jnp.exp2(pot_f + pot_g - cost)).astype(jnp.bfloat16)


def transform(state_ref, pair, moves):
    lon_dev, nvar, _, members = state_ref.shape
    size = PAIR * TILE
    own = state_ref[:, :, pair * size : (pair + 1) * size, :].astype(jnp.float32)
    parts = []
    for region, move in enumerate(moves):
        cells = own[:, :, region * TILE : (region + 1) * TILE].astype(jnp.bfloat16)
        cells = cells.reshape(lon_dev * nvar * TILE, members)
        moved = lax.dot_general(
            cells, move, (((1,), (1,)), ((), ())), preferred_element_type=jnp.float32
        )
        parts.append(moved.reshape(lon_dev, nvar, TILE, members))
    return jnp.concatenate(parts, axis=2).astype(jnp.bfloat16)


def analyse_half(half, count, scale, like_ref, sums_ref, kernel_ref, mass_ref, most, gram, state, out):
    regions = kernel_ref.shape[0]
    pairs = regions // PAIR
    size = PAIR * TILE
    state_hbm_ref, state_ref, state_sems = state
    out_ref, result_ref, out_sems = out
    first = half * pairs

    def fetch(pair):
        rows = pl.ds((first + pair) * size, size)
        return pltpu.make_async_copy(
            state_hbm_ref.at[:, :, rows, :],
            state_ref.at[:, :, pl.ds(pair * size, size), :],
            state_sems.at[pair],
        )

    def send(pair):
        rows = pl.ds((first + pair) * size, size)
        return pltpu.make_async_copy(
            result_ref.at[pair], out_ref.at[:, :, rows, :], out_sems.at[pair]
        )

    total = jnp.sum(sums_ref[...], axis=0, keepdims=True)[:, 0:1] * (1.0 / TILE)
    like = like_ref[half * regions : (half + 1) * regions, :]
    like = -0.5 * (count / total) * like
    like = like - jnp.max(like, axis=1, keepdims=True)
    logw = (like - jnp.log(jnp.sum(jnp.exp(like), axis=1, keepdims=True))) * LOG2E
    moves, least_i, least_j = transports_scaled(kernel_ref, jnp.exp2(logw + MASS), mass_ref)
    for pair in range(pairs):
        fetch(pair).wait()
        result_ref[pair] = transform(state_ref, pair, moves[pair * PAIR : (pair + 1) * PAIR])
        send(pair).start()
    row, col, most = jnp.min(least_i), jnp.min(least_j), jnp.max(most)
    sound = (row >= 2.0**-24) & (col >= 2.0**-30) & (most <= 2.0**30) & (row * col >= 2.0**-34)
    for pair in range(pairs):
        send(pair).wait()

    @pl.when(jnp.logical_not(sound))
    def _():
        for pair in range(pairs):
            again = [
                transport_logs(gram(region), logw[region : region + 1], scale)
                for region in range(pair * PAIR, (pair + 1) * PAIR)
            ]
            result_ref[pair] = transform(state_ref, pair, again)
            send(pair).start()
            send(pair).wait()


def start_fetches(half, pairs, state):
    state_hbm_ref, state_ref, state_sems = state
    size = PAIR * TILE
    for pair in range(pairs):
        rows = pl.ds((half * pairs + pair) * size, size)
        pltpu.make_async_copy(
            state_hbm_ref.at[:, :, rows, :],
            state_ref.at[:, :, pl.ds(pair * size, size), :],
            state_sems.at[pair],
        ).start()


def first_kernel(count, scale, *refs):
    state_hbm_ref, gram_hbm_ref, kernel_ref, mass_ref, most_ref, like_ref, sums_ref = refs[:7]
    out_ref, result_ref, state_ref, gram_ref, out_sems, state_sems, sem = refs[7:]
    state = state_hbm_ref, state_ref, state_sems
    start_fetches(0, kernel_ref.shape[0] // PAIR, state)

    def gram(region):
        copy = pltpu.make_async_copy(gram_hbm_ref.at[region], gram_ref, sem)
        copy.start()
        copy.wait()
        return gram_ref[...]

    out = out_ref, result_ref, out_sems
    analyse_half(
        0, count, scale, like_ref, sums_ref, kernel_ref, mass_ref, most_ref[...], gram, state, out
    )


def last_kernel(count, scale, *refs):
    odd_ref, halo_ref, halo_last_ref, old_ref, state_hbm_ref, like_ref, sums_ref = refs[:7]
    out_ref, result_ref, state_ref, gram_ref, kernel_ref, mass_ref, out_sems, state_sems = refs[8:]
    state = state_hbm_ref, state_ref, state_sems
    pairs = gram_ref.shape[0] // PAIR
    start_fetches(1, pairs, state)
    halos = [halo_ref, halo_last_ref]
    far_grams(odd_ref, halos, 2 * pairs * PAIR * TILE, range(pairs, 2 * pairs), old_ref, gram_ref)
    most = kernel_matrices(gram_ref, kernel_ref, mass_ref, scale)
    out = out_ref, result_ref, out_sems
    analyse_half(
        1,
        count,
        scale,
        like_ref,
        sums_ref,
        kernel_ref,
        mass_ref,
        most,
        lambda region: gram_ref[region],
        state,
        out,
    )


def half_buffers(state):
    lon_dev, nvar, lat, members = state.shape
    pairs = lat // (PAIR * TILE) // 2
    return [
        pltpu.VMEM((pairs, lon_dev, nvar, PAIR * TILE, members), state.dtype),
        pltpu.VMEM((lon_dev, nvar, lat // 2, members), state.dtype),
    ], [pltpu.SemaphoreType.DMA((pairs,)), pltpu.SemaphoreType.DMA((pairs,))]


def analyse_first(state, gram, kernel, mass, most, like, sums, count, scale):
    members = state.shape[-1]
    vmem = pl.BlockSpec(memory_space=pltpu.VMEM)
    hbm = pl.BlockSpec(memory_space=pltpu.HBM)
    buffers, sems = half_buffers(state)
    return pl.pallas_call(
        functools.partial(first_kernel, count, scale),
        in_specs=[hbm, hbm] + [vmem] * 5,
        out_specs=pl.BlockSpec(memory_space=pl.ANY),
        out_shape=jax.ShapeDtypeStruct(state.shape, state.dtype),
        scratch_shapes=buffers
        + [pltpu.VMEM((members, members), jnp.float32)]
        + sems
        + [pltpu.SemaphoreType.DMA],
        compiler_params=pltpu.CompilerParams(vmem_limit_bytes=24 * 2**20),
        name="analyse_first",
    )(
        *[pltpu.with_memory_space_constraint(x, pltpu.HBM) for x in (state, gram)],
        kernel,
        mass,
        most,
        like,
        sums,
    )


def analyse_last(odd, halo, halo_last, gram, state, like, sums, out, count, scale):
    vmem = pl.BlockSpec(memory_space=pltpu.VMEM)
    hbm = pl.BlockSpec(memory_space=pltpu.HBM)
    buffers, sems = half_buffers(state)
    return pl.pallas_call(
        functools.partial(last_kernel, count, scale),
        in_specs=[pl.BlockSpec(memory_space=pltpu.SMEM)]
        + [vmem] * 3
        + [hbm, vmem, vmem, pl.BlockSpec(memory_space=pl.ANY)],
        out_specs=pl.BlockSpec(memory_space=pl.ANY),
        out_shape=jax.ShapeDtypeStruct(state.shape, state.dtype),
        input_output_aliases={7: 0},
        scratch_shapes=buffers
        + [pltpu.VMEM(gram.shape, jnp.float32)] * 2
        + [pltpu.VMEM((gram.shape[0], 1, gram.shape[2]), jnp.float32)]
        + sems,
        compiler_params=pltpu.CompilerParams(vmem_limit_bytes=24 * 2**20),
        name="analyse_last",
    )(
        odd,
        halo,
        halo_last,
        gram,
        pltpu.with_memory_space_constraint(state, pltpu.HBM),
        like,
        sums,
        out,
    )


def on_device(state, obs_index, obs_value, obs_var):
    nvar = state.shape[1]
    count = lax.axis_size("lon")
    odd = (lax.axis_index("lon") & 1).astype(jnp.int32).reshape(1)
    near_pairs = [(i, i ^ 1) for i in range(count)]
    far_pairs = [(i, (i + 1 if i % 2 else i - 1) % count) for i in range(count)]
    own_like, for_near, for_far, for_far_last, part = observe(
        odd, state, obs_index, obs_value, obs_var
    )
    far = lax.ppermute(for_far, "lon", far_pairs)
    near = lax.ppermute(for_near, "lon", near_pairs)
    sums = near[HALO * nvar, 3 * TILE : 3 * TILE + 3, :128].astype(jnp.float32)
    sums = jnp.broadcast_to(part[0] + jnp.sum(sums, axis=0), (count // 2 * TILE, 128))
    sums, for_far_last = lax.optimization_barrier((sums, for_far_last))
    sums = lax.all_to_all(
        sums,
        "lon",
        0,
        0,
        axis_index_groups=[list(range(core, count, 2)) for core in range(2)],
        tiled=True,
    )
    far_last = lax.ppermute(for_far_last, "lon", far_pairs)
    offsets = range(REGION + 2 * HALO)
    line = [1.0 - max(0, HALO - p, p - (HALO + REGION - 1)) / (HALO + 1) for p in offsets]
    scale = LOG2E / EPS / (nvar * sum(line) ** 2)
    gram_first, gram_last, like = own_gram(odd, state, near, own_like)
    gram, kernel, mass, most, like = prepare(odd, far, gram_first, like, state.shape[2], scale)
    nobs = float(obs_index.shape[0] * count)
    out = analyse_first(state, gram, kernel, mass, most, like, sums, nobs, scale)
    return analyse_last(odd, far, far_last, gram_last, state, like, sums, out, nobs, scale)


def solution(mesh):
    return jax.shard_map(
        on_device,
        mesh=mesh,
        in_specs=(
            P(("ens", "lon"), None, None, None),
            P(("ens", "lon")),
            P(("ens", "lon")),
            P(("ens", "lon")),
        ),
        out_specs=P(("ens", "lon"), None, None, None),
        check_vma=False,
    )
```

```python
import functools
import math

import jax
import jax.numpy as jnp
from jax import lax
from jax.experimental import pallas as pl
from jax.experimental.pallas import tpu as pltpu
from jax.sharding import PartitionSpec as P

REGION = 8
HALO = 4
SWEEPS = 4
EPS = 0.05
TILE = 8
PAIR = 2
LOG2E = 1.4426950408889634
ROWS = 32
LIFT, START, MASS = 20, -10, 60

HIGH = lax.Precision.HIGHEST


def line_weight(place):
    dist = jnp.maximum(0.0, jnp.maximum(HALO - place, place - (HALO + REGION - 1)))
    inside = (place >= 0) & (place < REGION + 2 * HALO)
    return jnp.where(inside, 1.0 - dist / (HALO + 1), 0.0)


def like_rows(rows):
    rows = rows.astype(jnp.float32)
    return rows[:TILE] + rows[TILE : 2 * TILE] + rows[2 * TILE : 3 * TILE]


def in_parts(values, extra):
    below = lax.broadcasted_iota(jnp.int32, values.shape, 0)
    extra_high = extra.astype(jnp.bfloat16).astype(jnp.float32)
    extra_middle = (extra - extra_high).astype(jnp.bfloat16).astype(jnp.float32)
    extra_low = extra - extra_high - extra_middle
    last = jnp.where(below == 0, extra_high, jnp.where(below == 1, extra_middle, extra_low))
    last = jnp.where(below < 3, last, 0.0)
    high = values.astype(jnp.bfloat16).astype(jnp.float32)
    middle = (values - high).astype(jnp.bfloat16).astype(jnp.float32)
    low = values - high - middle
    return jnp.concatenate([high, middle, low, last], axis=0).astype(jnp.bfloat16)


def observe_kernel(*refs):
    odd_ref, state_ref, rows_ref = refs[:3]
    own_ref, near_ref, far_ref, part_ref = refs[6:10]
    cells_ref, index_ref, value_ref, var_ref, sems = refs[10:]
    lon_dev, lat, members = cells_ref.shape
    nobs = index_ref.shape[1]
    edge = rows_ref.shape[0] // lon_dev * HALO
    last = rows_ref.shape[0] - edge
    far_at = pl.multiple_of(odd_ref[0] * last, 16)
    near_at = pl.multiple_of(last - far_at, 16)
    fetches = [
        (refs[3], index_ref),
        (refs[4], value_ref),
        (refs[5], var_ref),
        (state_ref.at[:, 0], cells_ref),
        (rows_ref.at[pl.ds(far_at, edge), :], far_ref.at[pl.ds(0, edge), :]),
        (rows_ref.at[pl.ds(near_at, edge), :], near_ref.at[pl.ds(0, edge), :]),
    ]
    copies = [
        pltpu.make_async_copy(src, dst, sems.at[i]) for i, (src, dst) in enumerate(fetches)
    ]
    for copy in copies:
        copy.start()
    for copy in copies[:4]:
        copy.wait()
    rows = cells_ref[...].reshape(lon_dev * lat, members)
    index = index_ref[...]
    sub = lax.broadcasted_iota(jnp.int32, (TILE, nobs), 0)
    table = jnp.where(
        sub == 0,
        index.astype(jnp.float32),
        jnp.where(sub == 1, value_ref[...], var_ref[...]),
    ).T
    index_col = table[:, 0:1].astype(jnp.int32)
    value = table[:, 1:2]
    var = table[:, 2:3]
    pick = index_col == lax.broadcasted_iota(jnp.int32, (nobs, lon_dev * lat), 1)
    pick = jnp.where(pick, 1.0, 0.0).astype(jnp.bfloat16)
    seen = jnp.dot(pick, rows, preferred_element_type=jnp.float32)
    centre = jnp.sum(seen, axis=1, keepdims=True) * (1.0 / members)
    spread = jnp.sum((seen - centre) ** 2, axis=1, keepdims=True) * (1.0 / (members - 1))
    innovation = (value - centre) ** 2 / (var + spread)
    part = jnp.sum(innovation, axis=0, keepdims=True)
    part_ref[...] = jnp.broadcast_to(part, part_ref.shape)
    terms = (value - seen) ** 2 * (1.0 / var)
    lon = (index // lat).astype(jnp.float32)
    along = index.astype(jnp.float32) - lon * lat
    blocks = own_ref.shape[0]
    block = lax.broadcasted_iota(jnp.int32, (blocks, nobs), 0).astype(jnp.float32)
    across = line_weight(along - REGION * block + HALO)
    side = jnp.where(odd_ref[0] == 1, float(REGION), float(-REGION))
    weights = [line_weight(lon + (HALO + shift)) * across for shift in (0.0, side, -side)]
    like = jnp.dot(
        jnp.concatenate(weights, axis=0), terms, precision=HIGH, preferred_element_type=jnp.float32
    )
    own_ref[...] = like[:blocks]
    near_ref[edge:, :] = in_parts(like[blocks : 2 * blocks], part)
    far_ref[edge:, :] = in_parts(like[2 * blocks :], jnp.zeros_like(part))
    for copy in copies[4:]:
        copy.wait()


def observe(odd, state, obs_index, obs_value, obs_var):
    lon_dev, nvar, lat, members = state.shape
    nobs = obs_index.size
    assert lat // REGION == TILE
    like = jax.ShapeDtypeStruct((lat // REGION, members), jnp.float32)
    payload = pltpu.VMEM((HALO * nvar * lat + 4 * TILE, members), state.dtype)
    part = jax.ShapeDtypeStruct((TILE, 128), jnp.float32)
    arrays = state, state.reshape(-1, members), obs_index[None], obs_value[None], obs_var[None]
    return pl.pallas_call(
        observe_kernel,
        in_specs=[pl.BlockSpec(memory_space=pltpu.SMEM)]
        + [pl.BlockSpec(memory_space=pltpu.HBM)] * len(arrays),
        out_specs=[pl.BlockSpec(memory_space=pltpu.VMEM)] * 4,
        out_shape=[like, payload, payload, part],
        scratch_shapes=[
            pltpu.VMEM((lon_dev, lat, members), state.dtype),
            pltpu.VMEM((1, nobs), jnp.int32),
            pltpu.VMEM((1, nobs), jnp.float32),
            pltpu.VMEM((1, nobs), jnp.float32),
            pltpu.SemaphoreType.DMA((6,)),
        ],
        compiler_params=pltpu.CompilerParams(vmem_limit_bytes=16 * 2**20),
        name="observe",
    )(odd, *[pltpu.with_memory_space_constraint(x, pltpu.HBM) for x in arrays])


def slab_of(ref, lat, at):
    size = PAIR * TILE
    planes = ref.shape[0] // lat
    rows = [ref[i * lat + at * size : i * lat + (at + 1) * size, :] for i in range(planes)]
    return jnp.stack(rows).astype(jnp.float32)


def pair_tiles(load, step, steps):
    here = load(step)
    none = jnp.zeros_like(here[:, :TILE])
    before = load(step - 1)[:, TILE:] if step else none
    after = load(step + 1)[:, :TILE] if step + 1 < steps else none
    return before, here[:, :TILE], here[:, TILE:], after


def halo_weights(to_left):
    steps = [jnp.float32(1.0) - jnp.float32(d) / jnp.float32(HALO + 1) for d in range(HALO, 0, -1)]
    return [jnp.where(to_left, x, y) for x, y in zip(steps, steps[::-1])]


def turn(tile):
    return tile.reshape(-1, tile.shape[-1]).astype(jnp.bfloat16).T


def gram_of(tiles, turned, weights):
    planes, _, members = tiles[0].shape
    depth = planes * TILE
    row = lax.broadcasted_iota(jnp.int32, (TILE, members), 0)
    upper = row < HALO
    rowf = row.astype(jnp.float32)
    edge = line_weight(jnp.where(upper, rowf + (HALO + REGION), rowf - HALO))
    lane = lax.broadcasted_iota(jnp.int32, (1, depth), 1) & (TILE - 1)
    take_next = jnp.where(lane < HALO, 1.0, 0.0).astype(jnp.bfloat16)
    take_prev = jnp.where(lane < HALO, 0.0, 1.0).astype(jnp.bfloat16)
    grams = []
    for at in (1, 2):
        margin = jnp.where(upper, tiles[at + 1], tiles[at - 1])
        main_rows, margin_rows = [], []
        for plane, weight in enumerate(weights):
            own = tiles[at][plane]
            main_rows.append(own if weight is None else own * weight)
            margin_rows.append(margin[plane] * (edge if weight is None else edge * weight))
        weighted = jnp.stack(main_rows + margin_rows)
        weighted = weighted.reshape(2 * depth, members).astype(jnp.bfloat16)
        margin = turned[at + 1] * take_next + turned[at - 1] * take_prev
        both = jnp.concatenate([turned[at], margin], axis=1)
        grams.append(jnp.dot(both, weighted, preferred_element_type=jnp.float32))
    return grams


def slab_copies(src_ref, dst_ref, sems, only=None):
    size = PAIR * TILE

    def slab(at):
        rows = pl.ds(pl.multiple_of(at * size, size), size)
        return pltpu.make_async_copy(
            src_ref.at[:, :, rows, :], dst_ref.at[:, :, rows, :], sems.at[at]
        )

    return slab(only) if only is not None else [slab(i) for i in range(src_ref.shape[2] // size)]


def own_gram_kernel(odd_ref, state_hbm_ref, near_ref, own_ref, *refs):
    gram_ref, like_ref, state_ref, sems = refs
    lon_dev, nvar, lat, members = state_ref.shape
    steps = lat // (PAIR * TILE)
    copies = slab_copies(state_hbm_ref, state_ref, sems)
    for copy in copies:
        copy.start()
    like_ref[...] = own_ref[...] + like_rows(near_ref[near_ref.shape[0] - 4 * TILE :, :])
    size = PAIR * TILE

    def load(step):
        own = state_ref[:, :, step * size : (step + 1) * size, :].astype(jnp.float32)
        own = own.reshape(lon_dev * nvar, size, members)
        return jnp.concatenate([own, slab_of(near_ref, lat, step)], axis=0)

    weights = [None] * (lon_dev * nvar)
    weights += [w for w in halo_weights(odd_ref[0] == 1) for _ in range(nvar)]
    for copy in copies:
        copy.wait()
    slabs = [load(step) for step in range(steps)]
    add_grams(slabs, weights, None, gram_ref)


def add_grams(slabs, weights, old_ref, new_ref):
    none = jnp.zeros_like(slabs[0][:, :TILE])
    tiles = [none]
    for slab in slabs:
        tiles += [slab[:, :TILE], slab[:, TILE:]]
    tiles.append(none)
    turned = [turn(tile) for tile in tiles[1:-1]]
    turned = [jnp.zeros_like(turned[0])] + turned + [jnp.zeros_like(turned[0])]
    for pair in range(len(slabs)):
        window = slice(pair * PAIR, pair * PAIR + PAIR + 2)
        grams = gram_of(tiles[window], turned[window], weights)
        for at, gram in enumerate(grams):
            region = pair * PAIR + at
            new_ref[region] = gram if old_ref is None else old_ref[region] + gram


def own_gram(odd, state, near, own):
    _, _, lat, members = state.shape
    vmem = pl.BlockSpec(memory_space=pltpu.VMEM)
    return pl.pallas_call(
        own_gram_kernel,
        in_specs=[
            pl.BlockSpec(memory_space=pltpu.SMEM),
            pl.BlockSpec(memory_space=pltpu.HBM),
            vmem,
            vmem,
        ],
        out_specs=[vmem] * 2,
        out_shape=[
            jax.ShapeDtypeStruct((lat // REGION, members, members), jnp.float32),
            jax.ShapeDtypeStruct(own.shape, jnp.float32),
        ],
        scratch_shapes=[
            pltpu.VMEM(state.shape, state.dtype),
            pltpu.SemaphoreType.DMA((lat // (PAIR * TILE),)),
        ],
        compiler_params=pltpu.CompilerParams(vmem_limit_bytes=24 * 2**20),
        name="own_gram",
    )(odd, pltpu.with_memory_space_constraint(state, pltpu.HBM), near, own)


def halves(ref, region, rows):
    members = ref.shape[-1]
    return [ref[region, rows, at : at + 128] for at in range(0, members, 128)]


def diagonal(gram_ref, region):
    members = gram_ref.shape[-1]
    across = [None] * (members // 128)
    down = []
    for start in range(0, members, ROWS):
        lane = start // 128
        gram = gram_ref[region, pl.ds(start, ROWS), lane * 128 : lane * 128 + 128]
        i = lax.broadcasted_iota(jnp.int32, gram.shape, 0) + start
        j = lax.broadcasted_iota(jnp.int32, gram.shape, 1) + lane * 128
        kept = jnp.where(i == j, gram, 0.0)
        down.append(jnp.broadcast_to(jnp.sum(kept, axis=1, keepdims=True), gram.shape))
        part = jnp.sum(kept.reshape(ROWS // TILE, TILE, 128), axis=0)
        across[lane] = part if across[lane] is None else across[lane] + part
    return [jnp.sum(x, axis=0, keepdims=True) for x in across], down


def kernel_matrices(gram_ref, kernel_ref, mass_ref, scale):
    members = gram_ref.shape[-1]
    most = None
    for region in range(gram_ref.shape[0]):
        across, down = diagonal(gram_ref, region)
        across = [0.5 * LIFT - x * scale for x in across]
        masses = [0.0 for _ in across]
        for i, start in enumerate(range(0, members, ROWS)):
            rows = pl.ds(start, ROWS)
            base = 0.5 * LIFT - down[i] * scale
            for lane, (gram, x) in enumerate(zip(halves(gram_ref, region, rows), across)):
                part = jnp.exp2(gram * (2.0 * scale) + base + x)
                kernel_ref[region, rows, lane * 128 : lane * 128 + 128] = part
                most = part if most is None else jnp.maximum(most, part)
                part = jnp.sum(part.reshape(ROWS // TILE, TILE, 128), axis=0)
                masses[lane] = masses[lane] + part
        masses = [jnp.sum(x, axis=0, keepdims=True) for x in masses]
        mass_ref[region] = jnp.concatenate(masses, axis=1)
    return jnp.max(most.reshape(ROWS // TILE, TILE, 128), axis=0)


def prepare_kernel(scale, *refs):
    odd_ref, halo_ref, old_ref, like_in_ref = refs[:4]
    gram_hbm_ref, kernel_ref, mass_ref, most_ref, like_ref, gram_ref, sem = refs[4:]
    like_ref[...] = like_in_ref[...] + like_rows(halo_ref[halo_ref.shape[0] - 4 * TILE :, :])
    lat = gram_ref.shape[0] * REGION
    planes = halo_ref.shape[0] // lat
    weights = [w for w in halo_weights(odd_ref[0] == 0) for _ in range(planes // HALO)]
    slabs = [slab_of(halo_ref, lat, at) for at in range(lat // (PAIR * TILE))]
    add_grams(slabs, weights, old_ref, gram_ref)
    keep = pltpu.make_async_copy(gram_ref, gram_hbm_ref, sem)
    keep.start()
    most_ref[...] = kernel_matrices(gram_ref, kernel_ref, mass_ref, scale)
    keep.wait()


def prepare(odd, halo, gram, like, scale):
    vmem = pl.BlockSpec(memory_space=pltpu.VMEM)
    return pl.pallas_call(
        functools.partial(prepare_kernel, scale),
        in_specs=[pl.BlockSpec(memory_space=pltpu.SMEM)] + [vmem] * 3,
        out_specs=[pl.BlockSpec(memory_space=pltpu.HBM)] + [vmem] * 4,
        out_shape=[
            pltpu.HBM(gram.shape, jnp.float32),
            jax.ShapeDtypeStruct(gram.shape, jnp.float32),
            jax.ShapeDtypeStruct((gram.shape[0], 1, like.shape[1]), jnp.float32),
            jax.ShapeDtypeStruct((TILE, 128), jnp.float32),
            jax.ShapeDtypeStruct(like.shape, jnp.float32),
        ],
        scratch_shapes=[pltpu.VMEM(gram.shape, jnp.float32), pltpu.SemaphoreType.DMA],
        compiler_params=pltpu.CompilerParams(vmem_limit_bytes=24 * 2**20),
        name="prepare",
    )(odd, halo, gram, like)


def fold(values, op):
    out = values[0]
    for value in values[1:]:
        out = op(out, value)
    return out


def transports_scaled(kernel_ref, weights, mass_ref):
    regions = range(kernel_ref.shape[0])
    members = kernel_ref.shape[-1]
    starts = range(0, members, ROWS)
    lanes = range(members // 128)
    share = 2.0**MASS / members

    def lane_parts(row):
        return [row[:, lane * 128 : lane * 128 + 128] for lane in lanes]

    def settle(totals, region):
        return [w / x for w, x in zip(lane_parts(weights[region : region + 1]), totals)]

    def masses_of(region, rows, factor):
        parts = [k * f for k, f in zip(halves(kernel_ref, region, rows), factor)]
        mass = jnp.sum(fold(parts, jnp.add), axis=1, keepdims=True)
        mass = jnp.broadcast_to(mass, (ROWS, 128))
        near = pl.reciprocal(mass, approx=True)
        return parts, mass, near * (2.0 - mass * near)

    def sweep(_, carry):
        least_i, least_j, factors = carry
        next_i, next_j, next_factors = [], [], []
        for region, low_i, low_j, factor in zip(regions, least_i, least_j, factors):
            totals = [None for _ in lanes]
            for start in starts:
                rows = pl.ds(start, ROWS)
                _, mass, ratio = masses_of(region, rows, factor)
                low_j = jnp.minimum(low_j, mass)
                for lane, kernel in enumerate(halves(kernel_ref, region, rows)):
                    part = jnp.sum((kernel * ratio).reshape(ROWS // TILE, TILE, 128), axis=0)
                    totals[lane] = part if totals[lane] is None else totals[lane] + part
            totals = [jnp.sum(x, axis=0, keepdims=True) * share for x in totals]
            next_i.append(jnp.minimum(low_i, fold(totals, jnp.minimum)))
            next_j.append(low_j)
            next_factors.append(settle(totals, region))
        return next_i, next_j, next_factors

    totals = [[x * 2.0**START for x in lane_parts(mass_ref[region])] for region in regions]
    least_i = [fold(x, jnp.minimum) for x in totals]
    least_j = [jnp.full((ROWS, 128), 1e30, jnp.float32) for _ in regions]
    factors = [settle(x, region) for x, region in zip(totals, regions)]
    carry = lax.fori_loop(0, SWEEPS - 1, sweep, (least_i, least_j, factors))
    least_i, least_j, factors = carry
    moves, last_j = [], []
    for region, low_j, factor in zip(regions, least_j, factors):
        blocks = []
        for start in starts:
            parts, mass, ratio = masses_of(region, pl.ds(start, ROWS), factor)
            low_j = jnp.minimum(low_j, mass)
            blocks.append(jnp.concatenate([x * ratio for x in parts], axis=1).astype(jnp.bfloat16))
        moves.append(jnp.concatenate(blocks, axis=0))
        last_j.append(low_j)
    return moves, fold(least_i, jnp.minimum), fold(last_j, jnp.minimum)


def transport_logs(gram, logw, scale):
    members = gram.shape[-1]
    j = lax.broadcasted_iota(jnp.int32, gram.shape, 0)
    i = lax.broadcasted_iota(jnp.int32, gram.shape, 1)
    kept = jnp.where(i == j, gram, 0.0)
    down = jnp.sum(kept, axis=1, keepdims=True)
    across = jnp.sum(kept, axis=0, keepdims=True)
    cost = (down + across - 2.0 * gram) * scale
    pot_g = jnp.zeros((members, 1), jnp.float32)
    for sweep in range(SWEEPS):
        term = pot_g - cost
        top = jnp.max(term, axis=0, keepdims=True)
        pot_f = logw - top - jnp.log(jnp.sum(jnp.exp2(term - top), axis=0, keepdims=True)) * LOG2E
        term = pot_f - cost
        top = jnp.max(term, axis=1, keepdims=True)
        pot_g = -math.log2(members) - top
        pot_g = pot_g - jnp.log(jnp.sum(jnp.exp2(term - top), axis=1, keepdims=True)) * LOG2E
    return (members * jnp.exp2(pot_f + pot_g - cost)).astype(jnp.bfloat16)


def transform(state_ref, pair, moves):
    lon_dev, nvar, _, members = state_ref.shape
    size = PAIR * TILE
    own = state_ref[:, :, pair * size : (pair + 1) * size, :].astype(jnp.float32)
    parts = []
    for region, move in enumerate(moves):
        cells = own[:, :, region * TILE : (region + 1) * TILE].astype(jnp.bfloat16)
        cells = cells.reshape(lon_dev * nvar * TILE, members)
        moved = lax.dot_general(
            cells, move, (((1,), (1,)), ((), ())), preferred_element_type=jnp.float32
        )
        parts.append(moved.reshape(lon_dev, nvar, TILE, members))
    return jnp.concatenate(parts, axis=2).astype(jnp.bfloat16)


def finish_kernel(count, scale, *refs):
    state_hbm_ref, gram_hbm_ref, kernel_ref, mass_ref, most_ref, like_ref, sums_ref = refs[:7]
    out_ref, result_ref, state_ref, gram_ref, out_sems, state_sems, sem = refs[7:]
    pairs = kernel_ref.shape[0] // PAIR
    size = PAIR * TILE
    fetches = slab_copies(state_hbm_ref, state_ref, state_sems)
    for copy in fetches:
        copy.start()

    def send(pair):
        rows = pl.ds(pair * size, size)
        return pltpu.make_async_copy(
            result_ref.at[pair], out_ref.at[:, :, rows, :], out_sems.at[pair]
        )

    total = jnp.sum(sums_ref[...], axis=0, keepdims=True)[:, 0:1] * (1.0 / TILE)
    like = -0.5 * (count / total) * like_ref[...]
    like = like - jnp.max(like, axis=1, keepdims=True)
    logw = (like - jnp.log(jnp.sum(jnp.exp(like), axis=1, keepdims=True))) * LOG2E
    moves, least_i, least_j = transports_scaled(kernel_ref, jnp.exp2(logw + MASS), mass_ref)
    for pair in range(pairs):
        fetches[pair].wait()
        result_ref[pair] = transform(state_ref, pair, moves[pair * PAIR : (pair + 1) * PAIR])
        send(pair).start()
    row, col, most = jnp.min(least_i), jnp.min(least_j), jnp.max(most_ref[...])
    sound = (row >= 2.0**-24) & (col >= 2.0**-30) & (most <= 2.0**30) & (row * col >= 2.0**-34)
    for pair in range(pairs):
        send(pair).wait()

    @pl.when(jnp.logical_not(sound))
    def _():
        for pair in range(pairs):
            again = []
            for region in range(pair * PAIR, (pair + 1) * PAIR):
                copy = pltpu.make_async_copy(gram_hbm_ref.at[region], gram_ref, sem)
                copy.start()
                copy.wait()
                again.append(transport_logs(gram_ref[...], logw[region : region + 1], scale))
            result_ref[pair] = transform(state_ref, pair, again)
            send(pair).start()
            send(pair).wait()


def finish(state, gram, kernel, mass, most, like, sums, count, scale):
    lon_dev, nvar, lat, members = state.shape
    pairs = lat // (PAIR * TILE)
    vmem = pl.BlockSpec(memory_space=pltpu.VMEM)
    hbm = pl.BlockSpec(memory_space=pltpu.HBM)
    return pl.pallas_call(
        functools.partial(finish_kernel, count, scale),
        in_specs=[hbm, hbm] + [vmem] * 5,
        out_specs=pl.BlockSpec(memory_space=pl.ANY),
        out_shape=jax.ShapeDtypeStruct(state.shape, state.dtype),
        scratch_shapes=[
            pltpu.VMEM((pairs, lon_dev, nvar, PAIR * TILE, members), state.dtype),
            pltpu.VMEM(state.shape, state.dtype),
            pltpu.VMEM((members, members), jnp.float32),
            pltpu.SemaphoreType.DMA((pairs,)),
            pltpu.SemaphoreType.DMA((pairs,)),
            pltpu.SemaphoreType.DMA,
        ],
        compiler_params=pltpu.CompilerParams(vmem_limit_bytes=24 * 2**20),
        name="finish",
    )(
        *[pltpu.with_memory_space_constraint(x, pltpu.HBM) for x in (state, gram)],
        kernel,
        mass,
        most,
        like,
        sums,
    )


def on_device(state, obs_index, obs_value, obs_var):
    nvar = state.shape[1]
    count = lax.axis_size("lon")
    odd = (lax.axis_index("lon") & 1).astype(jnp.int32).reshape(1)
    near_pairs = [(i, i ^ 1) for i in range(count)]
    far_pairs = [(i, (i + 1 if i % 2 else i - 1) % count) for i in range(count)]
    own_like, for_near, for_far, part = observe(odd, state, obs_index, obs_value, obs_var)
    far = lax.ppermute(for_far, "lon", far_pairs)
    near = lax.ppermute(for_near, "lon", near_pairs)
    start = near.shape[0] - TILE
    part = part[0] + jnp.sum(near[start : start + 3, :128].astype(jnp.float32), axis=0)
    sums = lax.all_to_all(
        jnp.broadcast_to(part, (count // 2 * TILE, 128)),
        "lon",
        0,
        0,
        axis_index_groups=[list(range(core, count, 2)) for core in range(2)],
        tiled=True,
    )
    offsets = range(REGION + 2 * HALO)
    line = [1.0 - max(0, HALO - p, p - (HALO + REGION - 1)) / (HALO + 1) for p in offsets]
    scale = LOG2E / EPS / (nvar * sum(line) ** 2)
    gram, like = own_gram(odd, state, near, own_like)
    gram, kernel, mass, most, like = prepare(odd, far, gram, like, scale)
    nobs = float(obs_index.shape[0] * count)
    return finish(state, gram, kernel, mass, most, like, sums, nobs, scale)


def solution(mesh):
    return jax.shard_map(
        on_device,
        mesh=mesh,
        in_specs=(
            P(("ens", "lon"), None, None, None),
            P(("ens", "lon")),
            P(("ens", "lon")),
            P(("ens", "lon")),
        ),
        out_specs=P(("ens", "lon"), None, None, None),
        check_vma=False,
    )
```

```python
import functools
import math

import jax
import jax.numpy as jnp
from jax import lax
from jax.experimental import pallas as pl
from jax.experimental.pallas import tpu as pltpu
from jax.sharding import PartitionSpec as P

REGION = 8
HALO = 4
SWEEPS = 4
EPS = 0.05
TILE = 8
PAIR = 2
LOG2E = 1.4426950408889634
ROWS = 32
LIFT, START, MASS = 20, -10, 60

HIGH = lax.Precision.HIGHEST


def line_weight(place):
    dist = jnp.maximum(0.0, jnp.maximum(HALO - place, place - (HALO + REGION - 1)))
    inside = (place >= 0) & (place < REGION + 2 * HALO)
    return jnp.where(inside, 1.0 - dist / (HALO + 1), 0.0)


def like_rows(rows):
    rows = rows.astype(jnp.float32)
    return rows[:TILE] + rows[TILE : 2 * TILE] + rows[2 * TILE : 3 * TILE]


def in_parts(values, extra):
    below = lax.broadcasted_iota(jnp.int32, values.shape, 0)
    extra_high = extra.astype(jnp.bfloat16).astype(jnp.float32)
    extra_middle = (extra - extra_high).astype(jnp.bfloat16).astype(jnp.float32)
    extra_low = extra - extra_high - extra_middle
    last = jnp.where(below == 0, extra_high, jnp.where(below == 1, extra_middle, extra_low))
    last = jnp.where(below < 3, last, 0.0)
    high = values.astype(jnp.bfloat16).astype(jnp.float32)
    middle = (values - high).astype(jnp.bfloat16).astype(jnp.float32)
    low = values - high - middle
    return jnp.concatenate([high, middle, low, last], axis=0).astype(jnp.bfloat16)


def observe_kernel(*refs):
    odd_ref, state_ref, rows_ref = refs[:3]
    own_ref, near_ref, far_ref, part_ref = refs[6:10]
    cells_ref, index_ref, value_ref, var_ref, sems = refs[10:]
    lon_dev, lat, members = cells_ref.shape
    nobs = index_ref.shape[1]
    edge = rows_ref.shape[0] // lon_dev * HALO
    last = rows_ref.shape[0] - edge
    far_at = pl.multiple_of(odd_ref[0] * last, 16)
    near_at = pl.multiple_of(last - far_at, 16)
    fetches = [
        (refs[3], index_ref),
        (refs[4], value_ref),
        (refs[5], var_ref),
        (state_ref.at[:, 0], cells_ref),
        (rows_ref.at[pl.ds(far_at, edge), :], far_ref.at[pl.ds(0, edge), :]),
        (rows_ref.at[pl.ds(near_at, edge), :], near_ref.at[pl.ds(0, edge), :]),
    ]
    copies = [
        pltpu.make_async_copy(src, dst, sems.at[i]) for i, (src, dst) in enumerate(fetches)
    ]
    for copy in copies:
        copy.start()
    for copy in copies[:3]:
        copy.wait()
    index = index_ref[...]
    sub = lax.broadcasted_iota(jnp.int32, (TILE, nobs), 0)
    table = jnp.where(
        sub == 0,
        index.astype(jnp.float32),
        jnp.where(sub == 1, value_ref[...], var_ref[...]),
    ).T
    index_col = table[:, 0:1].astype(jnp.int32)
    value = table[:, 1:2]
    var = table[:, 2:3]
    pick = index_col == lax.broadcasted_iota(jnp.int32, (nobs, lon_dev * lat), 1)
    pick = jnp.where(pick, 1.0, 0.0).astype(jnp.bfloat16)
    lon = (index // lat).astype(jnp.float32)
    along = index.astype(jnp.float32) - lon * lat
    blocks = own_ref.shape[0]
    block = lax.broadcasted_iota(jnp.int32, (blocks, nobs), 0).astype(jnp.float32)
    across = line_weight(along - REGION * block + HALO)
    side = jnp.where(odd_ref[0] == 1, float(REGION), float(-REGION))
    weights = [line_weight(lon + (HALO + shift)) * across for shift in (0.0, side, -side)]
    weights = jnp.concatenate(weights, axis=0)
    inverse = 1.0 / var
    copies[3].wait()
    rows = cells_ref[...].reshape(lon_dev * lat, members)
    seen = jnp.dot(pick, rows, preferred_element_type=jnp.float32)
    terms = (value - seen) ** 2 * inverse
    like = jnp.dot(weights, terms, precision=HIGH, preferred_element_type=jnp.float32)
    centre = jnp.sum(seen, axis=1, keepdims=True) * (1.0 / members)
    spread = jnp.sum((seen - centre) ** 2, axis=1, keepdims=True) * (1.0 / (members - 1))
    innovation = (value - centre) ** 2 / (var + spread)
    part = jnp.sum(innovation, axis=0, keepdims=True)
    part_ref[...] = jnp.broadcast_to(part, part_ref.shape)
    own_ref[...] = like[:blocks]
    near_ref[edge:, :] = in_parts(like[blocks : 2 * blocks], part)
    far_ref[edge:, :] = in_parts(like[2 * blocks :], jnp.zeros_like(part))
    for copy in copies[4:]:
        copy.wait()


def observe(odd, state, obs_index, obs_value, obs_var):
    lon_dev, nvar, lat, members = state.shape
    nobs = obs_index.size
    assert lat // REGION == TILE
    like = jax.ShapeDtypeStruct((lat // REGION, members), jnp.float32)
    payload = pltpu.VMEM((HALO * nvar * lat + 4 * TILE, members), state.dtype)
    part = jax.ShapeDtypeStruct((TILE, 128), jnp.float32)
    arrays = state, state.reshape(-1, members), obs_index[None], obs_value[None], obs_var[None]
    return pl.pallas_call(
        observe_kernel,
        in_specs=[pl.BlockSpec(memory_space=pltpu.SMEM)]
        + [pl.BlockSpec(memory_space=pltpu.HBM)] * len(arrays),
        out_specs=[pl.BlockSpec(memory_space=pltpu.VMEM)] * 4,
        out_shape=[like, payload, payload, part],
        scratch_shapes=[
            pltpu.VMEM((lon_dev, lat, members), state.dtype),
            pltpu.VMEM((1, nobs), jnp.int32),
            pltpu.VMEM((1, nobs), jnp.float32),
            pltpu.VMEM((1, nobs), jnp.float32),
            pltpu.SemaphoreType.DMA((6,)),
        ],
        compiler_params=pltpu.CompilerParams(vmem_limit_bytes=16 * 2**20),
        name="observe",
    )(odd, *[pltpu.with_memory_space_constraint(x, pltpu.HBM) for x in arrays])


def slab_of(ref, lat, at):
    size = PAIR * TILE
    planes = ref.shape[0] // lat
    rows = [ref[i * lat + at * size : i * lat + (at + 1) * size, :] for i in range(planes)]
    return jnp.stack(rows).astype(jnp.float32)


def pair_tiles(load, step, steps):
    here = load(step)
    none = jnp.zeros_like(here[:, :TILE])
    before = load(step - 1)[:, TILE:] if step else none
    after = load(step + 1)[:, :TILE] if step + 1 < steps else none
    return before, here[:, :TILE], here[:, TILE:], after


def halo_weights(to_left):
    steps = [jnp.float32(1.0) - jnp.float32(d) / jnp.float32(HALO + 1) for d in range(HALO, 0, -1)]
    return [jnp.where(to_left, x, y) for x, y in zip(steps, steps[::-1])]


def turn(tile):
    return tile.reshape(-1, tile.shape[-1]).astype(jnp.bfloat16).T


def gram_of(tiles, turned, weights):
    planes, _, members = tiles[0].shape
    depth = planes * TILE
    row = lax.broadcasted_iota(jnp.int32, (TILE, members), 0)
    upper = row < HALO
    rowf = row.astype(jnp.float32)
    edge = line_weight(jnp.where(upper, rowf + (HALO + REGION), rowf - HALO))
    lane = lax.broadcasted_iota(jnp.int32, (1, depth), 1) & (TILE - 1)
    take_next = jnp.where(lane < HALO, 1.0, 0.0).astype(jnp.bfloat16)
    take_prev = jnp.where(lane < HALO, 0.0, 1.0).astype(jnp.bfloat16)
    grams = []
    for at in (1, 2):
        margin = jnp.where(upper, tiles[at + 1], tiles[at - 1])
        main_rows, margin_rows = [], []
        for plane, weight in enumerate(weights):
            own = tiles[at][plane]
            main_rows.append(own if weight is None else own * weight)
            margin_rows.append(margin[plane] * (edge if weight is None else edge * weight))
        weighted = jnp.stack(main_rows + margin_rows)
        weighted = weighted.reshape(2 * depth, members).astype(jnp.bfloat16)
        margin = turned[at + 1] * take_next + turned[at - 1] * take_prev
        both = jnp.concatenate([turned[at], margin], axis=1)
        grams.append(jnp.dot(both, weighted, preferred_element_type=jnp.float32))
    return grams


def slab_copies(src_ref, dst_ref, sems, only=None):
    size = PAIR * TILE

    def slab(at):
        rows = pl.ds(pl.multiple_of(at * size, size), size)
        return pltpu.make_async_copy(
            src_ref.at[:, :, rows, :], dst_ref.at[:, :, rows, :], sems.at[at]
        )

    return slab(only) if only is not None else [slab(i) for i in range(src_ref.shape[2] // size)]


def own_gram_kernel(odd_ref, state_hbm_ref, near_ref, own_ref, *refs):
    gram_ref, like_ref, state_ref, sems = refs
    lon_dev, nvar, lat, members = state_ref.shape
    steps = lat // (PAIR * TILE)
    copies = slab_copies(state_hbm_ref, state_ref, sems)
    for copy in copies:
        copy.start()
    like_ref[...] = own_ref[...] + like_rows(near_ref[near_ref.shape[0] - 4 * TILE :, :])
    size = PAIR * TILE

    def load(step):
        own = state_ref[:, :, step * size : (step + 1) * size, :].astype(jnp.float32)
        own = own.reshape(lon_dev * nvar, size, members)
        return jnp.concatenate([own, slab_of(near_ref, lat, step)], axis=0)

    weights = [None] * (lon_dev * nvar)
    weights += [w for w in halo_weights(odd_ref[0] == 1) for _ in range(nvar)]
    for copy in copies:
        copy.wait()
    slabs = [load(step) for step in range(steps)]
    add_grams(slabs, weights, None, gram_ref)


def add_grams(slabs, weights, old_ref, new_ref, done=None):
    none = jnp.zeros_like(slabs[0][:, :TILE])
    tiles = [none]
    for slab in slabs:
        tiles += [slab[:, :TILE], slab[:, TILE:]]
    tiles.append(none)
    turned = [turn(tile) for tile in tiles[1:-1]]
    turned = [jnp.zeros_like(turned[0])] + turned + [jnp.zeros_like(turned[0])]
    for pair in range(len(slabs)):
        window = slice(pair * PAIR, pair * PAIR + PAIR + 2)
        grams = gram_of(tiles[window], turned[window], weights)
        for at, gram in enumerate(grams):
            region = pair * PAIR + at
            new_ref[region] = gram if old_ref is None else old_ref[region] + gram
        if done is not None:
            done(pair)


def own_gram(odd, state, near, own):
    _, _, lat, members = state.shape
    vmem = pl.BlockSpec(memory_space=pltpu.VMEM)
    return pl.pallas_call(
        own_gram_kernel,
        in_specs=[
            pl.BlockSpec(memory_space=pltpu.SMEM),
            pl.BlockSpec(memory_space=pltpu.HBM),
            vmem,
            vmem,
        ],
        out_specs=[vmem] * 2,
        out_shape=[
            jax.ShapeDtypeStruct((lat // REGION, members, members), jnp.float32),
            jax.ShapeDtypeStruct(own.shape, jnp.float32),
        ],
        scratch_shapes=[
            pltpu.VMEM(state.shape, state.dtype),
            pltpu.SemaphoreType.DMA((lat // (PAIR * TILE),)),
        ],
        compiler_params=pltpu.CompilerParams(vmem_limit_bytes=24 * 2**20),
        name="own_gram",
    )(odd, pltpu.with_memory_space_constraint(state, pltpu.HBM), near, own)


def halves(ref, region, rows):
    members = ref.shape[-1]
    return [ref[region, rows, at : at + 128] for at in range(0, members, 128)]


def diagonal(gram_ref, region):
    members = gram_ref.shape[-1]
    across = [None] * (members // 128)
    down = []
    for start in range(0, members, ROWS):
        lane = start // 128
        gram = gram_ref[region, pl.ds(start, ROWS), lane * 128 : lane * 128 + 128]
        i = lax.broadcasted_iota(jnp.int32, gram.shape, 0) + start
        j = lax.broadcasted_iota(jnp.int32, gram.shape, 1) + lane * 128
        kept = jnp.where(i == j, gram, 0.0)
        down.append(jnp.broadcast_to(jnp.sum(kept, axis=1, keepdims=True), gram.shape))
        part = jnp.sum(kept.reshape(ROWS // TILE, TILE, 128), axis=0)
        across[lane] = part if across[lane] is None else across[lane] + part
    return [jnp.sum(x, axis=0, keepdims=True) for x in across], down


def kernel_matrices(gram_ref, kernel_ref, mass_ref, scale):
    members = gram_ref.shape[-1]
    for region in range(gram_ref.shape[0]):
        across, down = diagonal(gram_ref, region)
        across = [0.5 * LIFT - x * scale for x in across]
        masses = [0.0 for _ in across]
        for i, start in enumerate(range(0, members, ROWS)):
            rows = pl.ds(start, ROWS)
            base = 0.5 * LIFT - down[i] * scale
            for lane, (gram, x) in enumerate(zip(halves(gram_ref, region, rows), across)):
                part = jnp.exp2(gram * (2.0 * scale) + base + x)
                kernel_ref[region, rows, lane * 128 : lane * 128 + 128] = part
                part = jnp.sum(part.reshape(ROWS // TILE, TILE, 128), axis=0)
                masses[lane] = masses[lane] + part
        masses = [jnp.sum(x, axis=0, keepdims=True) for x in masses]
        mass_ref[region] = jnp.concatenate(masses, axis=1)


def prepare_kernel(scale, *refs):
    odd_ref, halo_ref, old_ref, like_in_ref = refs[:4]
    gram_hbm_ref, kernel_ref, mass_ref, like_ref, gram_ref, sems = refs[4:]
    like_ref[...] = like_in_ref[...] + like_rows(halo_ref[halo_ref.shape[0] - 4 * TILE :, :])
    lat = gram_ref.shape[0] * REGION
    planes = halo_ref.shape[0] // lat
    weights = [w for w in halo_weights(odd_ref[0] == 0) for _ in range(planes // HALO)]
    slabs = [slab_of(halo_ref, lat, at) for at in range(lat // (PAIR * TILE))]

    def keep(pair):
        part = pl.ds(pair * PAIR, PAIR)
        return pltpu.make_async_copy(gram_ref.at[part], gram_hbm_ref.at[part], sems.at[pair])

    add_grams(slabs, weights, old_ref, gram_ref, lambda pair: keep(pair).start())
    kernel_matrices(gram_ref, kernel_ref, mass_ref, scale)
    for pair in range(len(slabs)):
        keep(pair).wait()


def prepare(odd, halo, gram, like, scale):
    vmem = pl.BlockSpec(memory_space=pltpu.VMEM)
    return pl.pallas_call(
        functools.partial(prepare_kernel, scale),
        in_specs=[pl.BlockSpec(memory_space=pltpu.SMEM)] + [vmem] * 3,
        out_specs=[pl.BlockSpec(memory_space=pltpu.HBM)] + [vmem] * 3,
        out_shape=[
            pltpu.HBM(gram.shape, jnp.float32),
            jax.ShapeDtypeStruct(gram.shape, jnp.float32),
            jax.ShapeDtypeStruct((gram.shape[0], 1, like.shape[1]), jnp.float32),
            jax.ShapeDtypeStruct(like.shape, jnp.float32),
        ],
        scratch_shapes=[
            pltpu.VMEM(gram.shape, jnp.float32),
            pltpu.SemaphoreType.DMA((gram.shape[0] // PAIR,)),
        ],
        compiler_params=pltpu.CompilerParams(vmem_limit_bytes=24 * 2**20),
        name="prepare",
    )(odd, halo, gram, like)


def fold(values, op):
    out = values[0]
    for value in values[1:]:
        out = op(out, value)
    return out


def transports_scaled(kernel_ref, weights, mass_ref, use):
    regions = range(kernel_ref.shape[0])
    members = kernel_ref.shape[-1]
    starts = range(0, members, ROWS)
    lanes = range(members // 128)
    share = 2.0**MASS / members

    def lane_parts(row):
        return [row[:, lane * 128 : lane * 128 + 128] for lane in lanes]

    def settle(totals, region):
        return [w / x for w, x in zip(lane_parts(weights[region : region + 1]), totals)]

    def masses_of(region, rows, factor):
        parts = [k * f for k, f in zip(halves(kernel_ref, region, rows), factor)]
        mass = jnp.sum(fold(parts, jnp.add), axis=1, keepdims=True)
        mass = jnp.broadcast_to(mass, (ROWS, 128))
        return parts, mass, pl.reciprocal(mass, approx=True)

    def sweep(_, carry):
        least_i, least_j, factors = carry
        next_i, next_j, next_factors = [], [], []
        for region, low_i, low_j, factor in zip(regions, least_i, least_j, factors):
            totals = [None for _ in lanes]
            for start in starts:
                rows = pl.ds(start, ROWS)
                _, mass, ratio = masses_of(region, rows, factor)
                low_j = jnp.minimum(low_j, mass)
                for lane, kernel in enumerate(halves(kernel_ref, region, rows)):
                    part = jnp.sum((kernel * ratio).reshape(ROWS // TILE, TILE, 128), axis=0)
                    totals[lane] = part if totals[lane] is None else totals[lane] + part
            totals = [jnp.sum(x, axis=0, keepdims=True) * share for x in totals]
            next_i.append(jnp.minimum(low_i, fold(totals, jnp.minimum)))
            next_j.append(low_j)
            next_factors.append(settle(totals, region))
        return next_i, next_j, next_factors

    masses = [lane_parts(mass_ref[region]) for region in regions]
    most = fold([fold(x, jnp.maximum) for x in masses], jnp.maximum)
    totals = [[x * 2.0**START for x in mass] for mass in masses]
    least_i = [fold(x, jnp.minimum) for x in totals]
    least_j = [jnp.full((ROWS, 128), 1e30, jnp.float32) for _ in regions]
    factors = [settle(x, region) for x, region in zip(totals, regions)]
    carry = lax.fori_loop(0, SWEEPS - 1, sweep, (least_i, least_j, factors))
    least_i, least_j, factors = carry
    moves, last_j = [], []
    for region, low_j, factor in zip(regions, least_j, factors):
        blocks = []
        for start in starts:
            parts, mass, ratio = masses_of(region, pl.ds(start, ROWS), factor)
            low_j = jnp.minimum(low_j, mass)
            blocks.append(jnp.concatenate([x * ratio for x in parts], axis=1).astype(jnp.bfloat16))
        moves.append(jnp.concatenate(blocks, axis=0))
        last_j.append(low_j)
        if len(moves) == PAIR:
            use(region // PAIR, moves)
            moves = []
    least_i = fold(least_i, jnp.minimum)
    return jnp.min(least_i), jnp.min(fold(last_j, jnp.minimum)), jnp.max(most)


def transport_logs(gram, logw, scale):
    members = gram.shape[-1]
    j = lax.broadcasted_iota(jnp.int32, gram.shape, 0)
    i = lax.broadcasted_iota(jnp.int32, gram.shape, 1)
    kept = jnp.where(i == j, gram, 0.0)
    down = jnp.sum(kept, axis=1, keepdims=True)
    across = jnp.sum(kept, axis=0, keepdims=True)
    cost = (down + across - 2.0 * gram) * scale
    pot_g = jnp.zeros((members, 1), jnp.float32)
    for sweep in range(SWEEPS):
        term = pot_g - cost
        top = jnp.max(term, axis=0, keepdims=True)
        pot_f = logw - top - jnp.log(jnp.sum(jnp.exp2(term - top), axis=0, keepdims=True)) * LOG2E
        term = pot_f - cost
        top = jnp.max(term, axis=1, keepdims=True)
        pot_g = -math.log2(members) - top
        pot_g = pot_g - jnp.log(jnp.sum(jnp.exp2(term - top), axis=1, keepdims=True)) * LOG2E
    return (members * jnp.exp2(pot_f + pot_g - cost)).astype(jnp.bfloat16)


def transform(state_ref, pair, moves):
    lon_dev, nvar, _, members = state_ref.shape
    size = PAIR * TILE
    own = state_ref[:, :, pair * size : (pair + 1) * size, :].astype(jnp.float32)
    parts = []
    for region, move in enumerate(moves):
        cells = own[:, :, region * TILE : (region + 1) * TILE].astype(jnp.bfloat16)
        cells = cells.reshape(lon_dev * nvar * TILE, members)
        moved = lax.dot_general(
            cells, move, (((1,), (1,)), ((), ())), preferred_element_type=jnp.float32
        )
        parts.append(moved.reshape(lon_dev, nvar, TILE, members))
    return jnp.concatenate(parts, axis=2).astype(jnp.bfloat16)


def finish_kernel(count, scale, *refs):
    state_hbm_ref, gram_hbm_ref, kernel_ref, mass_ref, like_ref, sums_ref = refs[:6]
    out_ref, result_ref, state_ref, gram_ref, out_sems, state_sems, sem = refs[6:]
    pairs = kernel_ref.shape[0] // PAIR
    size = PAIR * TILE
    fetches = slab_copies(state_hbm_ref, state_ref, state_sems)
    for copy in fetches:
        copy.start()

    def send(pair):
        rows = pl.ds(pair * size, size)
        return pltpu.make_async_copy(
            result_ref.at[pair], out_ref.at[:, :, rows, :], out_sems.at[pair]
        )

    total = jnp.sum(sums_ref[...], axis=0, keepdims=True)[:, 0:1] * (1.0 / TILE)
    like = -0.5 * (count / total) * like_ref[...]
    like = like - jnp.max(like, axis=1, keepdims=True)
    logw = (like - jnp.log(jnp.sum(jnp.exp(like), axis=1, keepdims=True))) * LOG2E

    def use(pair, moves):
        fetches[pair].wait()
        result_ref[pair] = transform(state_ref, pair, moves)
        send(pair).start()

    weights = jnp.exp2(logw + MASS)
    row, col, most = transports_scaled(kernel_ref, weights, mass_ref, use)
    sound = (row >= 2.0**-24) & (col >= 2.0**-30) & (most <= 2.0**30) & (row * col >= 2.0**-34)
    for pair in range(pairs):
        send(pair).wait()

    @pl.when(jnp.logical_not(sound))
    def _():
        for pair in range(pairs):
            again = []
            for region in range(pair * PAIR, (pair + 1) * PAIR):
                copy = pltpu.make_async_copy(gram_hbm_ref.at[region], gram_ref, sem)
                copy.start()
                copy.wait()
                again.append(transport_logs(gram_ref[...], logw[region : region + 1], scale))
            result_ref[pair] = transform(state_ref, pair, again)
            send(pair).start()
            send(pair).wait()


def finish(state, gram, kernel, mass, like, sums, count, scale):
    lon_dev, nvar, lat, members = state.shape
    pairs = lat // (PAIR * TILE)
    vmem = pl.BlockSpec(memory_space=pltpu.VMEM)
    hbm = pl.BlockSpec(memory_space=pltpu.HBM)
    return pl.pallas_call(
        functools.partial(finish_kernel, count, scale),
        in_specs=[hbm, hbm] + [vmem] * 4,
        out_specs=pl.BlockSpec(memory_space=pl.ANY),
        out_shape=jax.ShapeDtypeStruct(state.shape, state.dtype),
        scratch_shapes=[
            pltpu.VMEM((pairs, lon_dev, nvar, PAIR * TILE, members), state.dtype),
            pltpu.VMEM(state.shape, state.dtype),
            pltpu.VMEM((members, members), jnp.float32),
            pltpu.SemaphoreType.DMA((pairs,)),
            pltpu.SemaphoreType.DMA((pairs,)),
            pltpu.SemaphoreType.DMA,
        ],
        compiler_params=pltpu.CompilerParams(vmem_limit_bytes=24 * 2**20),
        name="finish",
    )(
        *[pltpu.with_memory_space_constraint(x, pltpu.HBM) for x in (state, gram)],
        kernel,
        mass,
        like,
        sums,
    )


def on_device(state, obs_index, obs_value, obs_var):
    nvar = state.shape[1]
    count = lax.axis_size("lon")
    odd = (lax.axis_index("lon") & 1).astype(jnp.int32).reshape(1)
    near_pairs = [(i, i ^ 1) for i in range(count)]
    far_pairs = [(i, (i + 1 if i % 2 else i - 1) % count) for i in range(count)]
    own_like, for_near, for_far, part = observe(odd, state, obs_index, obs_value, obs_var)
    far = lax.ppermute(for_far, "lon", far_pairs)
    near = lax.ppermute(for_near, "lon", near_pairs)
    start = near.shape[0] - TILE
    part = part[0] + jnp.sum(near[start : start + 3, :128].astype(jnp.float32), axis=0)
    sums = lax.all_to_all(
        jnp.broadcast_to(part, (count // 2 * TILE, 128)),
        "lon",
        0,
        0,
        axis_index_groups=[list(range(core, count, 2)) for core in range(2)],
        tiled=True,
    )
    offsets = range(REGION + 2 * HALO)
    line = [1.0 - max(0, HALO - p, p - (HALO + REGION - 1)) / (HALO + 1) for p in offsets]
    scale = LOG2E / EPS / (nvar * sum(line) ** 2)
    gram, like = own_gram(odd, state, near, own_like)
    gram, kernel, mass, like = prepare(odd, far, gram, like, scale)
    nobs = float(obs_index.shape[0] * count)
    return finish(state, gram, kernel, mass, like, sums, nobs, scale)


def solution(mesh):
    return jax.shard_map(
        on_device,
        mesh=mesh,
        in_specs=(
            P(("ens", "lon"), None, None, None),
            P(("ens", "lon")),
            P(("ens", "lon")),
            P(("ens", "lon")),
        ),
        out_specs=P(("ens", "lon"), None, None, None),
        check_vma=False,
    )
```

```python
import functools
import math

import jax
import jax.numpy as jnp
from jax import lax
from jax.experimental import pallas as pl
from jax.experimental.pallas import tpu as pltpu
from jax.sharding import PartitionSpec as P

REGION = 8
HALO = 4
SWEEPS = 4
EPS = 0.05
TILE = 8
PAIR = 2
LOG2E = 1.4426950408889634
ROWS = 32
LIFT, START, MASS = 20, -10, 60

HIGH = lax.Precision.HIGHEST


def line_weight(place):
    dist = jnp.maximum(0.0, jnp.maximum(HALO - place, place - (HALO + REGION - 1)))
    inside = (place >= 0) & (place < REGION + 2 * HALO)
    return jnp.where(inside, 1.0 - dist / (HALO + 1), 0.0)


def like_rows(rows):
    rows = rows.astype(jnp.float32)
    return rows[:TILE] + rows[TILE : 2 * TILE] + rows[2 * TILE : 3 * TILE]


def in_parts(values, extra):
    below = lax.broadcasted_iota(jnp.int32, values.shape, 0)
    extra_high = extra.astype(jnp.bfloat16).astype(jnp.float32)
    extra_middle = (extra - extra_high).astype(jnp.bfloat16).astype(jnp.float32)
    extra_low = extra - extra_high - extra_middle
    last = jnp.where(below == 0, extra_high, jnp.where(below == 1, extra_middle, extra_low))
    last = jnp.where(below < 3, last, 0.0)
    high = values.astype(jnp.bfloat16).astype(jnp.float32)
    middle = (values - high).astype(jnp.bfloat16).astype(jnp.float32)
    low = values - high - middle
    return jnp.concatenate([high, middle, low, last], axis=0).astype(jnp.bfloat16)


def observe_kernel(*refs):
    odd_ref, state_ref, rows_ref = refs[:3]
    own_ref, near_ref, far_ref, part_ref = refs[6:10]
    cells_ref, index_ref, value_ref, var_ref, sems = refs[10:]
    lon_dev, lat, members = cells_ref.shape
    nobs = index_ref.shape[1]
    edge = rows_ref.shape[0] // lon_dev * HALO
    last = rows_ref.shape[0] - edge
    far_at = pl.multiple_of(odd_ref[0] * last, 16)
    near_at = pl.multiple_of(last - far_at, 16)
    fetches = [
        (refs[3], index_ref),
        (refs[4], value_ref),
        (refs[5], var_ref),
        (state_ref.at[:, 0], cells_ref),
        (rows_ref.at[pl.ds(far_at, edge), :], far_ref.at[pl.ds(0, edge), :]),
        (rows_ref.at[pl.ds(near_at, edge), :], near_ref.at[pl.ds(0, edge), :]),
    ]
    copies = [
        pltpu.make_async_copy(src, dst, sems.at[i]) for i, (src, dst) in enumerate(fetches)
    ]
    for copy in copies:
        copy.start()
    for copy in copies[:3]:
        copy.wait()
    index = index_ref[...]
    sub = lax.broadcasted_iota(jnp.int32, (TILE, nobs), 0)
    table = jnp.where(
        sub == 0,
        index.astype(jnp.float32),
        jnp.where(sub == 1, value_ref[...], var_ref[...]),
    ).T
    index_col = table[:, 0:1].astype(jnp.int32)
    value = table[:, 1:2]
    var = table[:, 2:3]
    pick = index_col == lax.broadcasted_iota(jnp.int32, (nobs, lon_dev * lat), 1)
    pick = jnp.where(pick, 1.0, 0.0).astype(jnp.bfloat16)
    lon = (index // lat).astype(jnp.float32)
    along = index.astype(jnp.float32) - lon * lat
    blocks = own_ref.shape[0]
    block = lax.broadcasted_iota(jnp.int32, (blocks, nobs), 0).astype(jnp.float32)
    across = line_weight(along - REGION * block + HALO)
    side = jnp.where(odd_ref[0] == 1, float(REGION), float(-REGION))
    weights = [line_weight(lon + (HALO + shift)) * across for shift in (0.0, side, -side)]
    weights = jnp.concatenate(weights, axis=0)
    inverse = 1.0 / var
    copies[3].wait()
    rows = cells_ref[...].reshape(lon_dev * lat, members)
    seen = jnp.dot(pick, rows, preferred_element_type=jnp.float32)
    terms = (value - seen) ** 2 * inverse
    like = jnp.dot(weights, terms, precision=HIGH, preferred_element_type=jnp.float32)
    centre = jnp.sum(seen, axis=1, keepdims=True) * (1.0 / members)
    spread = jnp.sum((seen - centre) ** 2, axis=1, keepdims=True) * (1.0 / (members - 1))
    innovation = (value - centre) ** 2 / (var + spread)
    part = jnp.sum(innovation, axis=0, keepdims=True)
    part_ref[...] = jnp.broadcast_to(part, part_ref.shape)
    own_ref[...] = like[:blocks]
    near_ref[edge:, :] = in_parts(like[blocks : 2 * blocks], part)
    far_ref[edge:, :] = in_parts(like[2 * blocks :], jnp.zeros_like(part))
    for copy in copies[4:]:
        copy.wait()


def observe(odd, state, obs_index, obs_value, obs_var):
    lon_dev, nvar, lat, members = state.shape
    nobs = obs_index.size
    assert lat // REGION == TILE
    like = jax.ShapeDtypeStruct((lat // REGION, members), jnp.float32)
    payload = pltpu.VMEM((HALO * nvar * lat + 4 * TILE, members), state.dtype)
    part = jax.ShapeDtypeStruct((TILE, 128), jnp.float32)
    arrays = state, state.reshape(-1, members), obs_index[None], obs_value[None], obs_var[None]
    return pl.pallas_call(
        observe_kernel,
        in_specs=[pl.BlockSpec(memory_space=pltpu.SMEM)]
        + [pl.BlockSpec(memory_space=pltpu.HBM)] * len(arrays),
        out_specs=[pl.BlockSpec(memory_space=pltpu.VMEM)] * 4,
        out_shape=[like, payload, payload, part],
        scratch_shapes=[
            pltpu.VMEM((lon_dev, lat, members), state.dtype),
            pltpu.VMEM((1, nobs), jnp.int32),
            pltpu.VMEM((1, nobs), jnp.float32),
            pltpu.VMEM((1, nobs), jnp.float32),
            pltpu.SemaphoreType.DMA((6,)),
        ],
        compiler_params=pltpu.CompilerParams(vmem_limit_bytes=16 * 2**20),
        name="observe",
    )(odd, *[pltpu.with_memory_space_constraint(x, pltpu.HBM) for x in arrays])


def slab_of(ref, lat, at):
    size = PAIR * TILE
    planes = ref.shape[0] // lat
    rows = [ref[i * lat + at * size : i * lat + (at + 1) * size, :] for i in range(planes)]
    return jnp.stack(rows).astype(jnp.float32)


def pair_tiles(load, step, steps):
    here = load(step)
    none = jnp.zeros_like(here[:, :TILE])
    before = load(step - 1)[:, TILE:] if step else none
    after = load(step + 1)[:, :TILE] if step + 1 < steps else none
    return before, here[:, :TILE], here[:, TILE:], after


def halo_weights(to_left):
    steps = [jnp.float32(1.0) - jnp.float32(d) / jnp.float32(HALO + 1) for d in range(HALO, 0, -1)]
    return [jnp.where(to_left, x, y) for x, y in zip(steps, steps[::-1])]


def turn(tile):
    return tile.reshape(-1, tile.shape[-1]).astype(jnp.bfloat16).T


def gram_of(tiles, turned, weights):
    planes, _, members = tiles[0].shape
    depth = planes * TILE
    row = lax.broadcasted_iota(jnp.int32, (TILE, members), 0)
    upper = row < HALO
    rowf = row.astype(jnp.float32)
    edge = line_weight(jnp.where(upper, rowf + (HALO + REGION), rowf - HALO))
    lane = lax.broadcasted_iota(jnp.int32, (1, depth), 1) & (TILE - 1)
    take_next = jnp.where(lane < HALO, 1.0, 0.0).astype(jnp.bfloat16)
    take_prev = jnp.where(lane < HALO, 0.0, 1.0).astype(jnp.bfloat16)
    grams = []
    for at in (1, 2):
        margin = jnp.where(upper, tiles[at + 1], tiles[at - 1])
        main_rows, margin_rows = [], []
        for plane, weight in enumerate(weights):
            own = tiles[at][plane]
            main_rows.append(own if weight is None else own * weight)
            margin_rows.append(margin[plane] * (edge if weight is None else edge * weight))
        weighted = jnp.stack(main_rows + margin_rows)
        weighted = weighted.reshape(2 * depth, members).astype(jnp.bfloat16)
        margin = turned[at + 1] * take_next + turned[at - 1] * take_prev
        both = jnp.concatenate([turned[at], margin], axis=1)
        grams.append(jnp.dot(both, weighted, preferred_element_type=jnp.float32))
    return grams


def slab_copies(src_ref, dst_ref, sems, only=None):
    size = PAIR * TILE

    def slab(at):
        rows = pl.ds(pl.multiple_of(at * size, size), size)
        return pltpu.make_async_copy(
            src_ref.at[:, :, rows, :], dst_ref.at[:, :, rows, :], sems.at[at]
        )

    return slab(only) if only is not None else [slab(i) for i in range(src_ref.shape[2] // size)]


def own_gram_kernel(odd_ref, state_hbm_ref, near_ref, own_ref, *refs):
    gram_ref, like_ref, state_ref, sems = refs
    lon_dev, nvar, lat, members = state_ref.shape
    steps = lat // (PAIR * TILE)
    copies = slab_copies(state_hbm_ref, state_ref, sems)
    for copy in copies:
        copy.start()
    like_ref[...] = own_ref[...] + like_rows(near_ref[near_ref.shape[0] - 4 * TILE :, :])
    size = PAIR * TILE

    def load(step):
        own = state_ref[:, :, step * size : (step + 1) * size, :].astype(jnp.float32)
        own = own.reshape(lon_dev * nvar, size, members)
        return jnp.concatenate([own, slab_of(near_ref, lat, step)], axis=0)

    weights = [None] * (lon_dev * nvar)
    weights += [w for w in halo_weights(odd_ref[0] == 1) for _ in range(nvar)]
    for copy in copies:
        copy.wait()
    slabs = [load(step) for step in range(steps)]
    add_grams(slabs, weights, None, gram_ref)


def add_grams(slabs, weights, old_ref, new_ref, done=None):
    none = jnp.zeros_like(slabs[0][:, :TILE])
    tiles = [none]
    for slab in slabs:
        tiles += [slab[:, :TILE], slab[:, TILE:]]
    tiles.append(none)
    turned = [turn(tile) for tile in tiles[1:-1]]
    turned = [jnp.zeros_like(turned[0])] + turned + [jnp.zeros_like(turned[0])]
    for pair in range(len(slabs)):
        window = slice(pair * PAIR, pair * PAIR + PAIR + 2)
        grams = gram_of(tiles[window], turned[window], weights)
        for at, gram in enumerate(grams):
            region = pair * PAIR + at
            new_ref[region] = gram if old_ref is None else old_ref[region] + gram
        if done is not None:
            done(pair)


def own_gram(odd, state, near, own):
    _, _, lat, members = state.shape
    vmem = pl.BlockSpec(memory_space=pltpu.VMEM)
    return pl.pallas_call(
        own_gram_kernel,
        in_specs=[
            pl.BlockSpec(memory_space=pltpu.SMEM),
            pl.BlockSpec(memory_space=pltpu.HBM),
            vmem,
            vmem,
        ],
        out_specs=[vmem] * 2,
        out_shape=[
            jax.ShapeDtypeStruct((lat // REGION, members, members), jnp.float32),
            jax.ShapeDtypeStruct(own.shape, jnp.float32),
        ],
        scratch_shapes=[
            pltpu.VMEM(state.shape, state.dtype),
            pltpu.SemaphoreType.DMA((lat // (PAIR * TILE),)),
        ],
        compiler_params=pltpu.CompilerParams(vmem_limit_bytes=24 * 2**20),
        name="own_gram",
    )(odd, pltpu.with_memory_space_constraint(state, pltpu.HBM), near, own)


def halves(ref, region, rows):
    members = ref.shape[-1]
    return [ref[region, rows, at : at + 128] for at in range(0, members, 128)]


def diagonal(gram_ref, region):
    members = gram_ref.shape[-1]
    across = [None] * (members // 128)
    down = []
    for start in range(0, members, ROWS):
        lane = start // 128
        gram = gram_ref[region, pl.ds(start, ROWS), lane * 128 : lane * 128 + 128]
        i = lax.broadcasted_iota(jnp.int32, gram.shape, 0) + start
        j = lax.broadcasted_iota(jnp.int32, gram.shape, 1) + lane * 128
        kept = jnp.where(i == j, gram, 0.0)
        down.append(jnp.broadcast_to(jnp.sum(kept, axis=1, keepdims=True), gram.shape))
        part = jnp.sum(kept.reshape(ROWS // TILE, TILE, 128), axis=0)
        across[lane] = part if across[lane] is None else across[lane] + part
    return [jnp.sum(x, axis=0, keepdims=True) for x in across], down


def kernel_matrices(gram_ref, kernel_ref, mass_ref, scale):
    members = gram_ref.shape[-1]
    for region in range(gram_ref.shape[0]):
        across, down = diagonal(gram_ref, region)
        across = [0.5 * LIFT - x * scale for x in across]
        masses = [0.0 for _ in across]
        for i, start in enumerate(range(0, members, ROWS)):
            rows = pl.ds(start, ROWS)
            base = 0.5 * LIFT - down[i] * scale
            for lane, (gram, x) in enumerate(zip(halves(gram_ref, region, rows), across)):
                part = jnp.exp2(gram * (2.0 * scale) + base + x)
                kernel_ref[region, rows, lane * 128 : lane * 128 + 128] = part
                part = jnp.sum(part.reshape(ROWS // TILE, TILE, 128), axis=0)
                masses[lane] = masses[lane] + part
        masses = [jnp.sum(x, axis=0, keepdims=True) for x in masses]
        mass_ref[region] = jnp.concatenate(masses, axis=1)


def prepare_kernel(scale, *refs):
    odd_ref, halo_ref, old_ref, like_in_ref = refs[:4]
    gram_hbm_ref, kernel_ref, mass_ref, like_ref, gram_ref, sems = refs[4:]
    like_ref[...] = like_in_ref[...] + like_rows(halo_ref[halo_ref.shape[0] - 4 * TILE :, :])
    lat = gram_ref.shape[0] * REGION
    planes = halo_ref.shape[0] // lat
    weights = [w for w in halo_weights(odd_ref[0] == 0) for _ in range(planes // HALO)]
    slabs = [slab_of(halo_ref, lat, at) for at in range(lat // (PAIR * TILE))]

    def keep(pair):
        part = pl.ds(pair * PAIR, PAIR)
        return pltpu.make_async_copy(gram_ref.at[part], gram_hbm_ref.at[part], sems.at[pair])

    add_grams(slabs, weights, old_ref, gram_ref, lambda pair: keep(pair).start())
    kernel_matrices(gram_ref, kernel_ref, mass_ref, scale)
    for pair in range(len(slabs)):
        keep(pair).wait()


def prepare(odd, halo, gram, like, scale):
    vmem = pl.BlockSpec(memory_space=pltpu.VMEM)
    return pl.pallas_call(
        functools.partial(prepare_kernel, scale),
        in_specs=[pl.BlockSpec(memory_space=pltpu.SMEM)] + [vmem] * 3,
        out_specs=[pl.BlockSpec(memory_space=pltpu.HBM)] + [vmem] * 3,
        out_shape=[
            pltpu.HBM(gram.shape, jnp.float32),
            jax.ShapeDtypeStruct(gram.shape, jnp.float32),
            jax.ShapeDtypeStruct((gram.shape[0], 1, like.shape[1]), jnp.float32),
            jax.ShapeDtypeStruct(like.shape, jnp.float32),
        ],
        scratch_shapes=[
            pltpu.VMEM(gram.shape, jnp.float32),
            pltpu.SemaphoreType.DMA((gram.shape[0] // PAIR,)),
        ],
        compiler_params=pltpu.CompilerParams(vmem_limit_bytes=24 * 2**20),
        name="prepare",
    )(odd, halo, gram, like)


def fold(values, op):
    out = values[0]
    for value in values[1:]:
        out = op(out, value)
    return out


def transports_scaled(kernel_ref, weights, mass_ref, use):
    regions = range(kernel_ref.shape[0])
    members = kernel_ref.shape[-1]
    starts = range(0, members, ROWS)
    lanes = range(members // 128)
    share = 2.0**MASS / members

    def lane_parts(row):
        return [row[:, lane * 128 : lane * 128 + 128] for lane in lanes]

    def settle(totals, region):
        return [w / x for w, x in zip(lane_parts(weights[region : region + 1]), totals)]

    def masses_of(region, rows, factor):
        parts = [k * f for k, f in zip(halves(kernel_ref, region, rows), factor)]
        mass = jnp.sum(fold(parts, jnp.add), axis=1, keepdims=True)
        mass = jnp.broadcast_to(mass, (ROWS, 128))
        return parts, mass, pl.reciprocal(mass, approx=True)

    def sweep(_, carry):
        least_i, least_j, factors = carry
        next_i, next_j, next_factors = [], [], []
        for region, low_i, low_j, factor in zip(regions, least_i, least_j, factors):
            totals = [None for _ in lanes]
            for start in starts:
                rows = pl.ds(start, ROWS)
                _, mass, ratio = masses_of(region, rows, factor)
                low_j = jnp.minimum(low_j, mass)
                for lane, kernel in enumerate(halves(kernel_ref, region, rows)):
                    part = jnp.sum((kernel * ratio).reshape(ROWS // TILE, TILE, 128), axis=0)
                    totals[lane] = part if totals[lane] is None else totals[lane] + part
            totals = [jnp.sum(x, axis=0, keepdims=True) * share for x in totals]
            next_i.append(jnp.minimum(low_i, fold(totals, jnp.minimum)))
            next_j.append(low_j)
            next_factors.append(settle(totals, region))
        return next_i, next_j, next_factors

    masses = [lane_parts(mass_ref[region]) for region in regions]
    most = fold([fold(x, jnp.maximum) for x in masses], jnp.maximum)
    totals = [[x * 2.0**START for x in mass] for mass in masses]
    least_i = [fold(x, jnp.minimum) for x in totals]
    least_j = [jnp.full((ROWS, 128), 1e30, jnp.float32) for _ in regions]
    factors = [settle(x, region) for x, region in zip(totals, regions)]
    carry = lax.fori_loop(0, SWEEPS - 1, sweep, (least_i, least_j, factors))
    least_i, least_j, factors = carry
    moves, last_j = [], []
    for region, low_j, factor in zip(regions, least_j, factors):
        blocks = []
        for start in starts:
            parts, mass, ratio = masses_of(region, pl.ds(start, ROWS), factor)
            low_j = jnp.minimum(low_j, mass)
            blocks.append(jnp.concatenate([x * ratio for x in parts], axis=1).astype(jnp.bfloat16))
        moves.append(jnp.concatenate(blocks, axis=0))
        last_j.append(low_j)
        if len(moves) == PAIR:
            use(region // PAIR, moves)
            moves = []
    least_i = fold(least_i, jnp.minimum)
    return jnp.min(least_i), jnp.min(fold(last_j, jnp.minimum)), jnp.max(most)


def transport_logs(gram, logw, scale):
    members = gram.shape[-1]
    j = lax.broadcasted_iota(jnp.int32, gram.shape, 0)
    i = lax.broadcasted_iota(jnp.int32, gram.shape, 1)
    kept = jnp.where(i == j, gram, 0.0)
    down = jnp.sum(kept, axis=1, keepdims=True)
    across = jnp.sum(kept, axis=0, keepdims=True)
    cost = (down + across - 2.0 * gram) * scale
    pot_g = jnp.zeros((members, 1), jnp.float32)
    for sweep in range(SWEEPS):
        term = pot_g - cost
        top = jnp.max(term, axis=0, keepdims=True)
        pot_f = logw - top - jnp.log(jnp.sum(jnp.exp2(term - top), axis=0, keepdims=True)) * LOG2E
        term = pot_f - cost
        top = jnp.max(term, axis=1, keepdims=True)
        pot_g = -math.log2(members) - top
        pot_g = pot_g - jnp.log(jnp.sum(jnp.exp2(term - top), axis=1, keepdims=True)) * LOG2E
    return (members * jnp.exp2(pot_f + pot_g - cost)).astype(jnp.bfloat16)


def transform(state_ref, pair, moves):
    lon_dev, nvar, _, members = state_ref.shape
    size = PAIR * TILE
    own = state_ref[:, :, pair * size : (pair + 1) * size, :].astype(jnp.float32)
    parts = []
    for region, move in enumerate(moves):
        cells = own[:, :, region * TILE : (region + 1) * TILE].astype(jnp.bfloat16)
        cells = cells.reshape(lon_dev * nvar * TILE, members)
        moved = lax.dot_general(
            cells, move, (((1,), (1,)), ((), ())), preferred_element_type=jnp.float32
        )
        parts.append(moved.reshape(lon_dev, nvar, TILE, members))
    return jnp.concatenate(parts, axis=2).astype(jnp.bfloat16)


def finish_kernel(count, scale, *refs):
    state_hbm_ref, gram_hbm_ref, kernel_ref, mass_ref, like_ref, sums_ref = refs[:6]
    out_ref, result_ref, state_ref, gram_ref, out_sems, state_sems, sem = refs[6:]
    pairs = kernel_ref.shape[0] // PAIR
    size = PAIR * TILE
    fetches = slab_copies(state_hbm_ref, state_ref, state_sems)
    for copy in fetches:
        copy.start()

    def send(pair):
        rows = pl.ds(pair * size, size)
        return pltpu.make_async_copy(
            result_ref.at[pair], out_ref.at[:, :, rows, :], out_sems.at[pair]
        )

    total = jnp.sum(sums_ref[...], axis=0, keepdims=True)[:, 0:1]
    like = -0.5 * (count / total) * like_ref[...]
    like = like - jnp.max(like, axis=1, keepdims=True)
    logw = (like - jnp.log(jnp.sum(jnp.exp(like), axis=1, keepdims=True))) * LOG2E

    def use(pair, moves):
        fetches[pair].wait()
        result_ref[pair] = transform(state_ref, pair, moves)
        send(pair).start()

    weights = jnp.exp2(logw + MASS)
    row, col, most = transports_scaled(kernel_ref, weights, mass_ref, use)
    sound = (row >= 2.0**-24) & (col >= 2.0**-30) & (most <= 2.0**30) & (row * col >= 2.0**-34)
    for pair in range(pairs):
        send(pair).wait()

    @pl.when(jnp.logical_not(sound))
    def _():
        for pair in range(pairs):
            again = []
            for region in range(pair * PAIR, (pair + 1) * PAIR):
                copy = pltpu.make_async_copy(gram_hbm_ref.at[region], gram_ref, sem)
                copy.start()
                copy.wait()
                again.append(transport_logs(gram_ref[...], logw[region : region + 1], scale))
            result_ref[pair] = transform(state_ref, pair, again)
            send(pair).start()
            send(pair).wait()


def finish(state, gram, kernel, mass, like, sums, count, scale):
    lon_dev, nvar, lat, members = state.shape
    pairs = lat // (PAIR * TILE)
    vmem = pl.BlockSpec(memory_space=pltpu.VMEM)
    hbm = pl.BlockSpec(memory_space=pltpu.HBM)
    return pl.pallas_call(
        functools.partial(finish_kernel, count, scale),
        in_specs=[hbm, hbm] + [vmem] * 4,
        out_specs=pl.BlockSpec(memory_space=pl.ANY),
        out_shape=jax.ShapeDtypeStruct(state.shape, state.dtype),
        scratch_shapes=[
            pltpu.VMEM((pairs, lon_dev, nvar, PAIR * TILE, members), state.dtype),
            pltpu.VMEM(state.shape, state.dtype),
            pltpu.VMEM((members, members), jnp.float32),
            pltpu.SemaphoreType.DMA((pairs,)),
            pltpu.SemaphoreType.DMA((pairs,)),
            pltpu.SemaphoreType.DMA,
        ],
        compiler_params=pltpu.CompilerParams(vmem_limit_bytes=24 * 2**20),
        name="finish",
    )(
        *[pltpu.with_memory_space_constraint(x, pltpu.HBM) for x in (state, gram)],
        kernel,
        mass,
        like,
        sums,
    )


def on_device(state, obs_index, obs_value, obs_var):
    nvar = state.shape[1]
    count = lax.axis_size("lon")
    odd = (lax.axis_index("lon") & 1).astype(jnp.int32).reshape(1)
    near_pairs = [(i, i ^ 1) for i in range(count)]
    far_pairs = [(i, (i + 1 if i % 2 else i - 1) % count) for i in range(count)]
    own_like, for_near, for_far, part = observe(odd, state, obs_index, obs_value, obs_var)
    far = lax.ppermute(for_far, "lon", far_pairs)
    near = lax.ppermute(for_near, "lon", near_pairs)
    start = near.shape[0] - TILE
    part = part[0] + jnp.sum(near[start : start + 3, :128].astype(jnp.float32), axis=0)
    sums = lax.all_to_all(
        jnp.broadcast_to(part, (count // 2, 128)),
        "lon",
        0,
        0,
        axis_index_groups=[[i for i in range(count) if (i ^ i >> 1) & 1 == kind] for kind in range(2)],
        tiled=True,
    )
    offsets = range(REGION + 2 * HALO)
    line = [1.0 - max(0, HALO - p, p - (HALO + REGION - 1)) / (HALO + 1) for p in offsets]
    scale = LOG2E / EPS / (nvar * sum(line) ** 2)
    gram, like = own_gram(odd, state, near, own_like)
    gram, kernel, mass, like = prepare(odd, far, gram, like, scale)
    nobs = float(obs_index.shape[0] * count)
    return finish(state, gram, kernel, mass, like, sums, nobs, scale)


def solution(mesh):
    return jax.shard_map(
        on_device,
        mesh=mesh,
        in_specs=(
            P(("ens", "lon"), None, None, None),
            P(("ens", "lon")),
            P(("ens", "lon")),
            P(("ens", "lon")),
        ),
        out_specs=P(("ens", "lon"), None, None, None),
        check_vma=False,
    )
```

```python
import functools
import math

import jax
import jax.numpy as jnp
from jax import lax
from jax.experimental import pallas as pl
from jax.experimental.pallas import tpu as pltpu
from jax.sharding import PartitionSpec as P

REGION = 8
HALO = 4
SWEEPS = 4
EPS = 0.05
TILE = 8
PAIR = 2
LOG2E = 1.4426950408889634
ROWS = 32
LIFT, START, MASS = 20, -10, 60


def fold(values, op):
    out = values[0]
    for value in values[1:]:
        out = op(out, value)
    return out


def line_weight(place):
    dist = jnp.maximum(0.0, jnp.maximum(HALO - place, place - (HALO + REGION - 1)))
    inside = (place >= 0) & (place < REGION + 2 * HALO)
    return jnp.where(inside, 1.0 - dist / (HALO + 1), 0.0)


def like_rows(rows):
    rows = rows.astype(jnp.float32)
    return rows[:TILE] + rows[TILE : 2 * TILE] + rows[2 * TILE : 3 * TILE]


def in_parts(values, extra):
    below = lax.broadcasted_iota(jnp.int32, values.shape, 0)
    extra_high = extra.astype(jnp.bfloat16).astype(jnp.float32)
    extra_middle = (extra - extra_high).astype(jnp.bfloat16).astype(jnp.float32)
    extra_low = extra - extra_high - extra_middle
    last = jnp.where(below == 0, extra_high, jnp.where(below == 1, extra_middle, extra_low))
    last = jnp.where(below < 3, last, 0.0)
    high = values.astype(jnp.bfloat16).astype(jnp.float32)
    middle = (values - high).astype(jnp.bfloat16).astype(jnp.float32)
    low = values - high - middle
    return jnp.concatenate([high, middle, low, last], axis=0).astype(jnp.bfloat16)


def steps_inside(place):
    dist = jnp.maximum(0.0, jnp.maximum(HALO - place, place - (HALO + REGION - 1)))
    inside = (place >= 0) & (place < REGION + 2 * HALO)
    return jnp.where(inside, HALO + 1 - dist, 0.0)


def observe_kernel(*refs):
    odd_ref, state_ref, rows_ref = refs[:3]
    own_ref, near_ref, far_ref, part_ref = refs[6:10]
    cells_ref, index_ref, value_ref, var_ref, sems = refs[10:]
    lon_dev, lat, members = cells_ref.shape
    nobs = index_ref.shape[1]
    edge = rows_ref.shape[0] // lon_dev * HALO
    last = rows_ref.shape[0] - edge
    far_at = pl.multiple_of(odd_ref[0] * last, 16)
    near_at = pl.multiple_of(last - far_at, 16)
    fetches = [
        (refs[3], index_ref),
        (refs[4], value_ref),
        (refs[5], var_ref),
        (state_ref.at[:, 0], cells_ref),
        (rows_ref.at[pl.ds(far_at, edge), :], far_ref.at[pl.ds(0, edge), :]),
        (rows_ref.at[pl.ds(near_at, edge), :], near_ref.at[pl.ds(0, edge), :]),
    ]
    copies = [
        pltpu.make_async_copy(src, dst, sems.at[i]) for i, (src, dst) in enumerate(fetches)
    ]
    for copy in copies:
        copy.start()
    for copy in copies[:3]:
        copy.wait()
    index = index_ref[...]
    sub = lax.broadcasted_iota(jnp.int32, (TILE, nobs), 0)
    table = jnp.where(
        sub == 0,
        index.astype(jnp.float32),
        jnp.where(sub == 1, value_ref[...], var_ref[...]),
    ).T
    index_col = table[:, 0:1].astype(jnp.int32)
    value = table[:, 1:2]
    var = table[:, 2:3]
    pick = index_col == lax.broadcasted_iota(jnp.int32, (nobs, lon_dev * lat), 1)
    pick = jnp.where(pick, 1.0, 0.0).astype(jnp.bfloat16)
    lon = (index // lat).astype(jnp.float32)
    along = index.astype(jnp.float32) - lon * lat
    blocks = own_ref.shape[0]
    block = lax.broadcasted_iota(jnp.int32, (blocks, nobs), 0).astype(jnp.float32)
    across = steps_inside(along - REGION * block + HALO)
    side = jnp.where(odd_ref[0] == 1, float(REGION), float(-REGION))
    weights = [steps_inside(lon + (HALO + shift)) * across for shift in (0.0, side, -side)]
    weights = jnp.concatenate(weights, axis=0).astype(jnp.bfloat16)
    inverse = 1.0 / var
    copies[3].wait()
    rows = cells_ref[...].reshape(lon_dev * lat, members)
    seen = jnp.dot(pick, rows, preferred_element_type=jnp.float32)
    terms = (value - seen) ** 2 * inverse
    high = terms.astype(jnp.bfloat16)
    rest = terms - high.astype(jnp.float32)
    middle = rest.astype(jnp.bfloat16)
    low = (rest - middle.astype(jnp.float32)).astype(jnp.bfloat16)
    sums = [jnp.dot(weights, x, preferred_element_type=jnp.float32) for x in (low, middle, high)]
    like = fold(sums, jnp.add) * (1.0 / (HALO + 1) ** 2)
    centre = jnp.sum(seen, axis=1, keepdims=True) * (1.0 / members)
    spread = jnp.sum((seen - centre) ** 2, axis=1, keepdims=True) * (1.0 / (members - 1))
    innovation = (value - centre) ** 2 / (var + spread)
    part = jnp.sum(innovation, axis=0, keepdims=True)
    part_ref[...] = jnp.broadcast_to(part, part_ref.shape)
    own_ref[...] = like[:blocks]
    near_ref[edge:, :] = in_parts(like[blocks : 2 * blocks], part)
    far_ref[edge:, :] = in_parts(like[2 * blocks :], jnp.zeros_like(part))
    for copy in copies[4:]:
        copy.wait()


def observe(odd, state, obs_index, obs_value, obs_var):
    lon_dev, nvar, lat, members = state.shape
    nobs = obs_index.size
    assert lat // REGION == TILE
    like = jax.ShapeDtypeStruct((lat // REGION, members), jnp.float32)
    payload = pltpu.VMEM((HALO * nvar * lat + 4 * TILE, members), state.dtype)
    part = jax.ShapeDtypeStruct((TILE, 128), jnp.float32)
    arrays = state, state.reshape(-1, members), obs_index[None], obs_value[None], obs_var[None]
    return pl.pallas_call(
        observe_kernel,
        in_specs=[pl.BlockSpec(memory_space=pltpu.SMEM)]
        + [pl.BlockSpec(memory_space=pltpu.HBM)] * len(arrays),
        out_specs=[pl.BlockSpec(memory_space=pltpu.VMEM)] * 4,
        out_shape=[like, payload, payload, part],
        scratch_shapes=[
            pltpu.VMEM((lon_dev, lat, members), state.dtype),
            pltpu.VMEM((1, nobs), jnp.int32),
            pltpu.VMEM((1, nobs), jnp.float32),
            pltpu.VMEM((1, nobs), jnp.float32),
            pltpu.SemaphoreType.DMA((6,)),
        ],
        compiler_params=pltpu.CompilerParams(vmem_limit_bytes=16 * 2**20),
        name="observe",
    )(odd, *[pltpu.with_memory_space_constraint(x, pltpu.HBM) for x in arrays])


def slab_of(ref, lat, at):
    size = PAIR * TILE
    planes = ref.shape[0] // lat
    rows = [ref[i * lat + at * size : i * lat + (at + 1) * size, :] for i in range(planes)]
    return jnp.stack(rows).astype(jnp.float32)


def pair_tiles(load, step, steps):
    here = load(step)
    none = jnp.zeros_like(here[:, :TILE])
    before = load(step - 1)[:, TILE:] if step else none
    after = load(step + 1)[:, :TILE] if step + 1 < steps else none
    return before, here[:, :TILE], here[:, TILE:], after


def halo_weights(to_left):
    steps = [jnp.float32(1.0) - jnp.float32(d) / jnp.float32(HALO + 1) for d in range(HALO, 0, -1)]
    return [jnp.where(to_left, x, y) for x, y in zip(steps, steps[::-1])]


def turn(tile):
    return tile.reshape(-1, tile.shape[-1]).astype(jnp.bfloat16).T


def gram_of(tiles, turned, weights):
    planes, _, members = tiles[0].shape
    depth = planes * TILE
    row = lax.broadcasted_iota(jnp.int32, (TILE, members), 0)
    upper = row < HALO
    rowf = row.astype(jnp.float32)
    edge = line_weight(jnp.where(upper, rowf + (HALO + REGION), rowf - HALO))
    lane = lax.broadcasted_iota(jnp.int32, (1, depth), 1) & (TILE - 1)
    take_next = jnp.where(lane < HALO, 1.0, 0.0).astype(jnp.bfloat16)
    take_prev = jnp.where(lane < HALO, 0.0, 1.0).astype(jnp.bfloat16)
    grams = []
    for at in (1, 2):
        margin = jnp.where(upper, tiles[at + 1], tiles[at - 1])
        main_rows, margin_rows = [], []
        for plane, weight in enumerate(weights):
            own = tiles[at][plane]
            main_rows.append(own if weight is None else own * weight)
            margin_rows.append(margin[plane] * (edge if weight is None else edge * weight))
        weighted = jnp.stack(main_rows + margin_rows)
        weighted = weighted.reshape(2 * depth, members).astype(jnp.bfloat16)
        margin = turned[at + 1] * take_next + turned[at - 1] * take_prev
        both = jnp.concatenate([turned[at], margin], axis=1)
        grams.append(jnp.dot(both, weighted, preferred_element_type=jnp.float32))
    return grams


def slab_copies(src_ref, dst_ref, sems, only=None):
    size = PAIR * TILE

    def slab(at):
        rows = pl.ds(pl.multiple_of(at * size, size), size)
        return pltpu.make_async_copy(
            src_ref.at[:, :, rows, :], dst_ref.at[:, :, rows, :], sems.at[at]
        )

    return slab(only) if only is not None else [slab(i) for i in range(src_ref.shape[2] // size)]


def own_gram_kernel(odd_ref, state_hbm_ref, near_ref, own_ref, *refs):
    gram_ref, like_ref, state_ref, sems = refs
    lon_dev, nvar, lat, members = state_ref.shape
    steps = lat // (PAIR * TILE)
    copies = slab_copies(state_hbm_ref, state_ref, sems)
    for copy in copies:
        copy.start()
    like_ref[...] = own_ref[...] + like_rows(near_ref[near_ref.shape[0] - 4 * TILE :, :])
    size = PAIR * TILE

    def load(step):
        own = state_ref[:, :, step * size : (step + 1) * size, :].astype(jnp.float32)
        own = own.reshape(lon_dev * nvar, size, members)
        return jnp.concatenate([own, slab_of(near_ref, lat, step)], axis=0)

    weights = [None] * (lon_dev * nvar)
    weights += [w for w in halo_weights(odd_ref[0] == 1) for _ in range(nvar)]
    for copy in copies:
        copy.wait()
    slabs = [load(step) for step in range(steps)]
    add_grams(slabs, weights, None, gram_ref)


def add_grams(slabs, weights, old_ref, new_ref, done=None):
    none = jnp.zeros_like(slabs[0][:, :TILE])
    tiles = [none]
    for slab in slabs:
        tiles += [slab[:, :TILE], slab[:, TILE:]]
    tiles.append(none)
    turned = [turn(tile) for tile in tiles[1:-1]]
    turned = [jnp.zeros_like(turned[0])] + turned + [jnp.zeros_like(turned[0])]
    for pair in range(len(slabs)):
        window = slice(pair * PAIR, pair * PAIR + PAIR + 2)
        grams = gram_of(tiles[window], turned[window], weights)
        for at, gram in enumerate(grams):
            region = pair * PAIR + at
            new_ref[region] = gram if old_ref is None else old_ref[region] + gram
        if done is not None:
            done(pair)


def own_gram(odd, state, near, own):
    _, _, lat, members = state.shape
    vmem = pl.BlockSpec(memory_space=pltpu.VMEM)
    return pl.pallas_call(
        own_gram_kernel,
        in_specs=[
            pl.BlockSpec(memory_space=pltpu.SMEM),
            pl.BlockSpec(memory_space=pltpu.HBM),
            vmem,
            vmem,
        ],
        out_specs=[vmem] * 2,
        out_shape=[
            jax.ShapeDtypeStruct((lat // REGION, members, members), jnp.float32),
            jax.ShapeDtypeStruct(own.shape, jnp.float32),
        ],
        scratch_shapes=[
            pltpu.VMEM(state.shape, state.dtype),
            pltpu.SemaphoreType.DMA((lat // (PAIR * TILE),)),
        ],
        compiler_params=pltpu.CompilerParams(vmem_limit_bytes=24 * 2**20),
        name="own_gram",
    )(odd, pltpu.with_memory_space_constraint(state, pltpu.HBM), near, own)


def halves(ref, region, rows):
    members = ref.shape[-1]
    return [ref[region, rows, at : at + 128] for at in range(0, members, 128)]


def diagonal(gram_ref, region):
    members = gram_ref.shape[-1]
    across = [None] * (members // 128)
    down = []
    for start in range(0, members, ROWS):
        lane = start // 128
        gram = gram_ref[region, pl.ds(start, ROWS), lane * 128 : lane * 128 + 128]
        i = lax.broadcasted_iota(jnp.int32, gram.shape, 0) + start
        j = lax.broadcasted_iota(jnp.int32, gram.shape, 1) + lane * 128
        kept = jnp.where(i == j, gram, 0.0)
        down.append(jnp.broadcast_to(jnp.sum(kept, axis=1, keepdims=True), gram.shape))
        part = jnp.sum(kept.reshape(ROWS // TILE, TILE, 128), axis=0)
        across[lane] = part if across[lane] is None else across[lane] + part
    return [jnp.sum(x, axis=0, keepdims=True) for x in across], down


def kernel_matrices(gram_ref, kernel_ref, mass_ref, scale):
    members = gram_ref.shape[-1]
    for region in range(gram_ref.shape[0]):
        across, down = diagonal(gram_ref, region)
        across = [0.5 * LIFT - x * scale for x in across]
        masses = [0.0 for _ in across]
        for i, start in enumerate(range(0, members, ROWS)):
            rows = pl.ds(start, ROWS)
            base = 0.5 * LIFT - down[i] * scale
            for lane, (gram, x) in enumerate(zip(halves(gram_ref, region, rows), across)):
                part = jnp.exp2(gram * (2.0 * scale) + base + x)
                kernel_ref[region, rows, lane * 128 : lane * 128 + 128] = part
                part = jnp.sum(part.reshape(ROWS // TILE, TILE, 128), axis=0)
                masses[lane] = masses[lane] + part
        masses = [jnp.sum(x, axis=0, keepdims=True) for x in masses]
        mass_ref[region] = jnp.concatenate(masses, axis=1)


def prepare_kernel(scale, *refs):
    odd_ref, halo_ref, old_ref, like_in_ref = refs[:4]
    gram_hbm_ref, kernel_ref, mass_ref, like_ref, gram_ref, sems = refs[4:]
    like = like_in_ref[...] + like_rows(halo_ref[halo_ref.shape[0] - 4 * TILE :, :])
    like_ref[...] = like - jnp.min(like, axis=1, keepdims=True)
    lat = gram_ref.shape[0] * REGION
    planes = halo_ref.shape[0] // lat
    weights = [w for w in halo_weights(odd_ref[0] == 0) for _ in range(planes // HALO)]
    slabs = [slab_of(halo_ref, lat, at) for at in range(lat // (PAIR * TILE))]

    def keep(pair):
        part = pl.ds(pair * PAIR, PAIR)
        return pltpu.make_async_copy(gram_ref.at[part], gram_hbm_ref.at[part], sems.at[pair])

    add_grams(slabs, weights, old_ref, gram_ref, lambda pair: keep(pair).start())
    kernel_matrices(gram_ref, kernel_ref, mass_ref, scale)
    for pair in range(len(slabs)):
        keep(pair).wait()


def prepare(odd, halo, gram, like, scale):
    vmem = pl.BlockSpec(memory_space=pltpu.VMEM)
    return pl.pallas_call(
        functools.partial(prepare_kernel, scale),
        in_specs=[pl.BlockSpec(memory_space=pltpu.SMEM)] + [vmem] * 3,
        out_specs=[pl.BlockSpec(memory_space=pltpu.HBM)] + [vmem] * 3,
        out_shape=[
            pltpu.HBM(gram.shape, jnp.float32),
            jax.ShapeDtypeStruct(gram.shape, jnp.float32),
            jax.ShapeDtypeStruct((gram.shape[0], 1, like.shape[1]), jnp.float32),
            jax.ShapeDtypeStruct(like.shape, jnp.float32),
        ],
        scratch_shapes=[
            pltpu.VMEM(gram.shape, jnp.float32),
            pltpu.SemaphoreType.DMA((gram.shape[0] // PAIR,)),
        ],
        compiler_params=pltpu.CompilerParams(vmem_limit_bytes=24 * 2**20),
        name="prepare",
    )(odd, halo, gram, like)


def transports_scaled(kernel_ref, weights, mass_ref, use):
    regions = range(kernel_ref.shape[0])
    members = kernel_ref.shape[-1]
    starts = range(0, members, ROWS)
    lanes = range(members // 128)
    share = 2.0**MASS / members

    def lane_parts(row):
        return [row[:, lane * 128 : lane * 128 + 128] for lane in lanes]

    def settle(totals, region):
        return [w / x for w, x in zip(lane_parts(weights[region : region + 1]), totals)]

    def masses_of(region, rows, factor):
        parts = [k * f for k, f in zip(halves(kernel_ref, region, rows), factor)]
        mass = jnp.sum(fold(parts, jnp.add), axis=1, keepdims=True)
        mass = jnp.broadcast_to(mass, (ROWS, 128))
        return parts, mass, pl.reciprocal(mass, approx=True)

    def sweep(least_i, least_j, factors):
        next_i, next_j, next_factors = [], [], []
        for region, low_i, low_j, factor in zip(regions, least_i, least_j, factors):
            totals = [None for _ in lanes]
            for start in starts:
                rows = pl.ds(start, ROWS)
                _, mass, ratio = masses_of(region, rows, factor)
                low_j = jnp.minimum(low_j, mass)
                for lane, kernel in enumerate(halves(kernel_ref, region, rows)):
                    part = jnp.sum((kernel * ratio).reshape(ROWS // TILE, TILE, 128), axis=0)
                    totals[lane] = part if totals[lane] is None else totals[lane] + part
            totals = [jnp.sum(x, axis=0, keepdims=True) * share for x in totals]
            next_i.append(jnp.minimum(low_i, fold(totals, jnp.minimum)))
            next_j.append(low_j)
            next_factors.append(settle(totals, region))
        return next_i, next_j, next_factors

    masses = [lane_parts(mass_ref[region]) for region in regions]
    most = fold([fold(x, jnp.maximum) for x in masses], jnp.maximum)
    totals = [[x * 2.0**START for x in mass] for mass in masses]
    least_i = [fold(x, jnp.minimum) for x in totals]
    least_j = [jnp.full((ROWS, 128), 1e30, jnp.float32) for _ in regions]
    factors = [settle(x, region) for x, region in zip(totals, regions)]
    for _ in range(SWEEPS - 1):
        least_i, least_j, factors = sweep(least_i, least_j, factors)
    moves, last_j = [], []
    for region, low_j, factor in zip(regions, least_j, factors):
        blocks = []
        for start in starts:
            parts, mass, ratio = masses_of(region, pl.ds(start, ROWS), factor)
            low_j = jnp.minimum(low_j, mass)
            blocks.append(jnp.concatenate([x * ratio for x in parts], axis=1).astype(jnp.bfloat16))
        moves.append(jnp.concatenate(blocks, axis=0))
        last_j.append(low_j)
        if len(moves) == PAIR:
            use(region // PAIR, moves)
            moves = []
    least_i = fold(least_i, jnp.minimum)
    return jnp.min(least_i), jnp.min(fold(last_j, jnp.minimum)), jnp.max(most)


def transport_logs(gram, logw, scale):
    members = gram.shape[-1]
    j = lax.broadcasted_iota(jnp.int32, gram.shape, 0)
    i = lax.broadcasted_iota(jnp.int32, gram.shape, 1)
    kept = jnp.where(i == j, gram, 0.0)
    down = jnp.sum(kept, axis=1, keepdims=True)
    across = jnp.sum(kept, axis=0, keepdims=True)
    cost = (down + across - 2.0 * gram) * scale
    pot_g = jnp.zeros((members, 1), jnp.float32)
    for sweep in range(SWEEPS):
        term = pot_g - cost
        top = jnp.max(term, axis=0, keepdims=True)
        pot_f = logw - top - jnp.log(jnp.sum(jnp.exp2(term - top), axis=0, keepdims=True)) * LOG2E
        term = pot_f - cost
        top = jnp.max(term, axis=1, keepdims=True)
        pot_g = -math.log2(members) - top
        pot_g = pot_g - jnp.log(jnp.sum(jnp.exp2(term - top), axis=1, keepdims=True)) * LOG2E
    return (members * jnp.exp2(pot_f + pot_g - cost)).astype(jnp.bfloat16)


def transform(state_ref, pair, moves):
    lon_dev, nvar, _, members = state_ref.shape
    size = PAIR * TILE
    own = state_ref[:, :, pair * size : (pair + 1) * size, :].astype(jnp.float32)
    parts = []
    for region, move in enumerate(moves):
        cells = own[:, :, region * TILE : (region + 1) * TILE].astype(jnp.bfloat16)
        cells = cells.reshape(lon_dev * nvar * TILE, members)
        moved = lax.dot_general(
            cells, move, (((1,), (1,)), ((), ())), preferred_element_type=jnp.float32
        )
        parts.append(moved.reshape(lon_dev, nvar, TILE, members))
    return jnp.concatenate(parts, axis=2).astype(jnp.bfloat16)


def finish_kernel(count, scale, *refs):
    state_hbm_ref, gram_hbm_ref, kernel_ref, mass_ref, like_ref, sums_ref = refs[:6]
    out_ref, result_ref, state_ref, gram_ref, out_sems, state_sems, sem = refs[6:]
    pairs = kernel_ref.shape[0] // PAIR
    size = PAIR * TILE
    fetches = slab_copies(state_hbm_ref, state_ref, state_sems)
    for copy in fetches:
        copy.start()

    def send(pair):
        rows = pl.ds(pair * size, size)
        return pltpu.make_async_copy(
            result_ref.at[pair], out_ref.at[:, :, rows, :], out_sems.at[pair]
        )

    total = jnp.sum(sums_ref[...], axis=0, keepdims=True)[:, 0:1]
    like = -0.5 * (count / total) * like_ref[...]
    logw = (like - jnp.log(jnp.sum(jnp.exp(like), axis=1, keepdims=True))) * LOG2E

    def use(pair, moves):
        fetches[pair].wait()
        result_ref[pair] = transform(state_ref, pair, moves)
        send(pair).start()

    weights = jnp.exp2(logw + MASS)
    row, col, most = transports_scaled(kernel_ref, weights, mass_ref, use)
    sound = (row >= 2.0**-24) & (col >= 2.0**-30) & (most <= 2.0**30) & (row * col >= 2.0**-34)
    for pair in range(pairs):
        send(pair).wait()

    @pl.when(jnp.logical_not(sound))
    def _():
        for pair in range(pairs):
            again = []
            for region in range(pair * PAIR, (pair + 1) * PAIR):
                copy = pltpu.make_async_copy(gram_hbm_ref.at[region], gram_ref, sem)
                copy.start()
                copy.wait()
                again.append(transport_logs(gram_ref[...], logw[region : region + 1], scale))
            result_ref[pair] = transform(state_ref, pair, again)
            send(pair).start()
            send(pair).wait()


def finish(state, gram, kernel, mass, like, sums, count, scale):
    lon_dev, nvar, lat, members = state.shape
    pairs = lat // (PAIR * TILE)
    vmem = pl.BlockSpec(memory_space=pltpu.VMEM)
    hbm = pl.BlockSpec(memory_space=pltpu.HBM)
    return pl.pallas_call(
        functools.partial(finish_kernel, count, scale),
        in_specs=[hbm, hbm] + [vmem] * 4,
        out_specs=pl.BlockSpec(memory_space=pl.ANY),
        out_shape=jax.ShapeDtypeStruct(state.shape, state.dtype),
        scratch_shapes=[
            pltpu.VMEM((pairs, lon_dev, nvar, PAIR * TILE, members), state.dtype),
            pltpu.VMEM(state.shape, state.dtype),
            pltpu.VMEM((members, members), jnp.float32),
            pltpu.SemaphoreType.DMA((pairs,)),
            pltpu.SemaphoreType.DMA((pairs,)),
            pltpu.SemaphoreType.DMA,
        ],
        compiler_params=pltpu.CompilerParams(vmem_limit_bytes=24 * 2**20),
        name="finish",
    )(
        *[pltpu.with_memory_space_constraint(x, pltpu.HBM) for x in (state, gram)],
        kernel,
        mass,
        like,
        sums,
    )


def on_device(state, obs_index, obs_value, obs_var):
    nvar = state.shape[1]
    count = lax.axis_size("lon")
    odd = (lax.axis_index("lon") & 1).astype(jnp.int32).reshape(1)
    near_pairs = [(i, i ^ 1) for i in range(count)]
    far_pairs = [(i, (i + 1 if i % 2 else i - 1) % count) for i in range(count)]
    own_like, for_near, for_far, part = observe(odd, state, obs_index, obs_value, obs_var)
    far = lax.ppermute(for_far, "lon", far_pairs)
    near = lax.ppermute(for_near, "lon", near_pairs)
    start = near.shape[0] - TILE
    part = part[0] + jnp.sum(near[start : start + 3, :128].astype(jnp.float32), axis=0)
    sums = lax.all_to_all(
        jnp.broadcast_to(part, (count // 2, 128)),
        "lon",
        0,
        0,
        axis_index_groups=[[i for i in range(count) if (i ^ i >> 1) & 1 == kind] for kind in range(2)],
        tiled=True,
    )
    offsets = range(REGION + 2 * HALO)
    line = [1.0 - max(0, HALO - p, p - (HALO + REGION - 1)) / (HALO + 1) for p in offsets]
    scale = LOG2E / EPS / (nvar * sum(line) ** 2)
    gram, like = own_gram(odd, state, near, own_like)
    gram, kernel, mass, like = prepare(odd, far, gram, like, scale)
    nobs = float(obs_index.shape[0] * count)
    return finish(state, gram, kernel, mass, like, sums, nobs, scale)


def solution(mesh):
    return jax.shard_map(
        on_device,
        mesh=mesh,
        in_specs=(
            P(("ens", "lon"), None, None, None),
            P(("ens", "lon")),
            P(("ens", "lon")),
            P(("ens", "lon")),
        ),
        out_specs=P(("ens", "lon"), None, None, None),
        check_vma=False,
    )
```

```python
import functools
import math

import jax
import jax.numpy as jnp
from jax import lax
from jax.experimental import pallas as pl
from jax.experimental.pallas import tpu as pltpu
from jax.sharding import PartitionSpec as P

REGION = 8
HALO = 4
SWEEPS = 4
EPS = 0.05
TILE = 8
PAIR = 2
LOG2E = 1.4426950408889634
ROWS = 32
LIFT, START, MASS = 20, -10, 60


def fold(values, op):
    out = values[0]
    for value in values[1:]:
        out = op(out, value)
    return out


def line_weight(place):
    dist = jnp.maximum(0.0, jnp.maximum(HALO - place, place - (HALO + REGION - 1)))
    inside = (place >= 0) & (place < REGION + 2 * HALO)
    return jnp.where(inside, 1.0 - dist / (HALO + 1), 0.0)


def like_rows(rows):
    rows = rows.astype(jnp.float32)
    return rows[:TILE] + rows[TILE : 2 * TILE] + rows[2 * TILE : 3 * TILE]


def in_parts(values, extra):
    below = lax.broadcasted_iota(jnp.int32, values.shape, 0)
    extra_high = extra.astype(jnp.bfloat16).astype(jnp.float32)
    extra_middle = (extra - extra_high).astype(jnp.bfloat16).astype(jnp.float32)
    extra_low = extra - extra_high - extra_middle
    last = jnp.where(below == 0, extra_high, jnp.where(below == 1, extra_middle, extra_low))
    last = jnp.where(below < 3, last, 0.0)
    high = values.astype(jnp.bfloat16).astype(jnp.float32)
    middle = (values - high).astype(jnp.bfloat16).astype(jnp.float32)
    low = values - high - middle
    return jnp.concatenate([high, middle, low, last], axis=0).astype(jnp.bfloat16)


def steps_inside(place):
    dist = jnp.maximum(0.0, jnp.maximum(HALO - place, place - (HALO + REGION - 1)))
    inside = (place >= 0) & (place < REGION + 2 * HALO)
    return jnp.where(inside, HALO + 1 - dist, 0.0)


def observe_kernel(*refs):
    odd_ref, state_ref, rows_ref = refs[:3]
    own_ref, near_ref, far_ref, part_ref = refs[6:10]
    cells_ref, index_ref, value_ref, var_ref, sems = refs[10:]
    lon_dev, lat, members = cells_ref.shape
    nobs = index_ref.shape[1]
    edge = rows_ref.shape[0] // lon_dev * HALO
    last = rows_ref.shape[0] - edge
    far_at = pl.multiple_of(odd_ref[0] * last, 16)
    near_at = pl.multiple_of(last - far_at, 16)
    fetches = [
        (refs[3], index_ref),
        (refs[4], value_ref),
        (refs[5], var_ref),
        (state_ref.at[:, 0], cells_ref),
        (rows_ref.at[pl.ds(far_at, edge), :], far_ref.at[pl.ds(0, edge), :]),
        (rows_ref.at[pl.ds(near_at, edge), :], near_ref.at[pl.ds(0, edge), :]),
    ]
    copies = [
        pltpu.make_async_copy(src, dst, sems.at[i]) for i, (src, dst) in enumerate(fetches)
    ]
    for copy in copies:
        copy.start()
    for copy in copies[:3]:
        copy.wait()
    index = index_ref[...]
    sub = lax.broadcasted_iota(jnp.int32, (TILE, nobs), 0)
    table = jnp.where(
        sub == 0,
        index.astype(jnp.float32),
        jnp.where(sub == 1, value_ref[...], var_ref[...]),
    ).T
    index_col = table[:, 0:1].astype(jnp.int32)
    value = table[:, 1:2]
    var = table[:, 2:3]
    pick = index_col == lax.broadcasted_iota(jnp.int32, (nobs, lon_dev * lat), 1)
    pick = jnp.where(pick, 1.0, 0.0).astype(jnp.bfloat16)
    lon = (index // lat).astype(jnp.float32)
    along = index.astype(jnp.float32) - lon * lat
    blocks = own_ref.shape[0]
    block = lax.broadcasted_iota(jnp.int32, (blocks, nobs), 0).astype(jnp.float32)
    across = steps_inside(along - REGION * block + HALO)
    side = jnp.where(odd_ref[0] == 1, float(REGION), float(-REGION))
    weights = [steps_inside(lon + (HALO + shift)) * across for shift in (0.0, side, -side)]
    weights = jnp.concatenate(weights, axis=0).astype(jnp.bfloat16)
    inverse = 1.0 / var
    copies[3].wait()
    rows = cells_ref[...].reshape(lon_dev * lat, members)
    seen = jnp.dot(pick, rows, preferred_element_type=jnp.float32)
    terms = (value - seen) ** 2 * inverse
    high = terms.astype(jnp.bfloat16)
    rest = terms - high.astype(jnp.float32)
    middle = rest.astype(jnp.bfloat16)
    low = (rest - middle.astype(jnp.float32)).astype(jnp.bfloat16)
    sums = [jnp.dot(weights, x, preferred_element_type=jnp.float32) for x in (low, middle, high)]
    like = fold(sums, jnp.add) * (1.0 / (HALO + 1) ** 2)
    centre = jnp.sum(seen, axis=1, keepdims=True) * (1.0 / members)
    spread = jnp.sum((seen - centre) ** 2, axis=1, keepdims=True) * (1.0 / (members - 1))
    innovation = (value - centre) ** 2 / (var + spread)
    part = jnp.sum(innovation, axis=0, keepdims=True)
    part_ref[...] = jnp.broadcast_to(part, part_ref.shape)
    own_ref[...] = like[:blocks]
    near_ref[edge:, :] = in_parts(like[blocks : 2 * blocks], part)
    far_ref[edge:, :] = in_parts(like[2 * blocks :], jnp.zeros_like(part))
    for copy in copies[4:]:
        copy.wait()


def observe(odd, state, obs_index, obs_value, obs_var):
    lon_dev, nvar, lat, members = state.shape
    nobs = obs_index.size
    assert lat // REGION == TILE
    like = jax.ShapeDtypeStruct((lat // REGION, members), jnp.float32)
    payload = pltpu.VMEM((HALO * nvar * lat + 4 * TILE, members), state.dtype)
    part = jax.ShapeDtypeStruct((TILE, 128), jnp.float32)
    arrays = state, state.reshape(-1, members), obs_index[None], obs_value[None], obs_var[None]
    return pl.pallas_call(
        observe_kernel,
        in_specs=[pl.BlockSpec(memory_space=pltpu.SMEM)]
        + [pl.BlockSpec(memory_space=pltpu.HBM)] * len(arrays),
        out_specs=[pl.BlockSpec(memory_space=pltpu.VMEM)] * 4,
        out_shape=[like, payload, payload, part],
        scratch_shapes=[
            pltpu.VMEM((lon_dev, lat, members), state.dtype),
            pltpu.VMEM((1, nobs), jnp.int32),
            pltpu.VMEM((1, nobs), jnp.float32),
            pltpu.VMEM((1, nobs), jnp.float32),
            pltpu.SemaphoreType.DMA((6,)),
        ],
        compiler_params=pltpu.CompilerParams(vmem_limit_bytes=16 * 2**20),
        name="observe",
    )(odd, *[pltpu.with_memory_space_constraint(x, pltpu.HBM) for x in arrays])


def slab_of(ref, lat, at):
    size = PAIR * TILE
    planes = ref.shape[0] // lat
    rows = [ref[i * lat + at * size : i * lat + (at + 1) * size, :] for i in range(planes)]
    return jnp.stack(rows).astype(jnp.float32)


def pair_tiles(load, step, steps):
    here = load(step)
    none = jnp.zeros_like(here[:, :TILE])
    before = load(step - 1)[:, TILE:] if step else none
    after = load(step + 1)[:, :TILE] if step + 1 < steps else none
    return before, here[:, :TILE], here[:, TILE:], after


def halo_weights(to_left):
    steps = [jnp.float32(1.0) - jnp.float32(d) / jnp.float32(HALO + 1) for d in range(HALO, 0, -1)]
    return [jnp.where(to_left, x, y) for x, y in zip(steps, steps[::-1])]


def turn(tile):
    return tile.reshape(-1, tile.shape[-1]).astype(jnp.bfloat16).T


def gram_of(tiles, turned, weights):
    planes, _, members = tiles[0].shape
    depth = planes * TILE
    row = lax.broadcasted_iota(jnp.int32, (TILE, members), 0)
    upper = row < HALO
    rowf = row.astype(jnp.float32)
    edge = line_weight(jnp.where(upper, rowf + (HALO + REGION), rowf - HALO))
    lane = lax.broadcasted_iota(jnp.int32, (1, depth), 1) & (TILE - 1)
    take_next = jnp.where(lane < HALO, 1.0, 0.0).astype(jnp.bfloat16)
    take_prev = jnp.where(lane < HALO, 0.0, 1.0).astype(jnp.bfloat16)
    grams = []
    for at in (1, 2):
        margin = jnp.where(upper, tiles[at + 1], tiles[at - 1])
        main_rows, margin_rows = [], []
        for plane, weight in enumerate(weights):
            own = tiles[at][plane]
            main_rows.append(own if weight is None else own * weight)
            margin_rows.append(margin[plane] * (edge if weight is None else edge * weight))
        weighted = jnp.stack(main_rows + margin_rows)
        weighted = weighted.reshape(2 * depth, members).astype(jnp.bfloat16)
        margin = turned[at + 1] * take_next + turned[at - 1] * take_prev
        both = jnp.concatenate([turned[at], margin], axis=1)
        grams.append(jnp.dot(both, weighted, preferred_element_type=jnp.float32))
    return grams


def slab_copies(src_ref, dst_ref, sems, only=None):
    size = PAIR * TILE

    def slab(at):
        rows = pl.ds(pl.multiple_of(at * size, size), size)
        return pltpu.make_async_copy(
            src_ref.at[:, :, rows, :], dst_ref.at[:, :, rows, :], sems.at[at]
        )

    return slab(only) if only is not None else [slab(i) for i in range(src_ref.shape[2] // size)]


def own_gram_kernel(odd_ref, state_hbm_ref, near_ref, own_ref, *refs):
    gram_ref, like_ref, state_ref, sems = refs
    lon_dev, nvar, lat, members = state_ref.shape
    steps = lat // (PAIR * TILE)
    copies = slab_copies(state_hbm_ref, state_ref, sems)
    for copy in copies:
        copy.start()
    like_ref[...] = own_ref[...] + like_rows(near_ref[near_ref.shape[0] - 4 * TILE :, :])
    size = PAIR * TILE

    def load(step):
        own = state_ref[:, :, step * size : (step + 1) * size, :].astype(jnp.float32)
        own = own.reshape(lon_dev * nvar, size, members)
        return jnp.concatenate([own, slab_of(near_ref, lat, step)], axis=0)

    weights = [None] * (lon_dev * nvar)
    weights += [w for w in halo_weights(odd_ref[0] == 1) for _ in range(nvar)]
    for copy in copies:
        copy.wait()
    slabs = [load(step) for step in range(steps)]
    add_grams(slabs, weights, None, gram_ref)


def add_grams(slabs, weights, old_ref, new_ref):
    none = jnp.zeros_like(slabs[0][:, :TILE])
    tiles = [none]
    for slab in slabs:
        tiles += [slab[:, :TILE], slab[:, TILE:]]
    tiles.append(none)
    turned = [turn(tile) for tile in tiles[1:-1]]
    turned = [jnp.zeros_like(turned[0])] + turned + [jnp.zeros_like(turned[0])]
    for pair in range(len(slabs)):
        window = slice(pair * PAIR, pair * PAIR + PAIR + 2)
        grams = gram_of(tiles[window], turned[window], weights)
        for at, gram in enumerate(grams):
            region = pair * PAIR + at
            new_ref[region] = gram if old_ref is None else old_ref[region] + gram


def own_gram(odd, state, near, own):
    _, _, lat, members = state.shape
    vmem = pl.BlockSpec(memory_space=pltpu.VMEM)
    return pl.pallas_call(
        own_gram_kernel,
        in_specs=[
            pl.BlockSpec(memory_space=pltpu.SMEM),
            pl.BlockSpec(memory_space=pltpu.HBM),
            vmem,
            vmem,
        ],
        out_specs=[vmem] * 2,
        out_shape=[
            jax.ShapeDtypeStruct((lat // REGION, members, members), jnp.float32),
            jax.ShapeDtypeStruct(own.shape, jnp.float32),
        ],
        scratch_shapes=[
            pltpu.VMEM(state.shape, state.dtype),
            pltpu.SemaphoreType.DMA((lat // (PAIR * TILE),)),
        ],
        compiler_params=pltpu.CompilerParams(vmem_limit_bytes=24 * 2**20),
        name="own_gram",
    )(odd, pltpu.with_memory_space_constraint(state, pltpu.HBM), near, own)


def halves(ref, region, rows):
    members = ref.shape[-1]
    return [ref[region, rows, at : at + 128] for at in range(0, members, 128)]


def diagonal(gram_ref, region):
    members = gram_ref.shape[-1]
    across = [None] * (members // 128)
    down = []
    for start in range(0, members, ROWS):
        lane = start // 128
        gram = gram_ref[region, pl.ds(start, ROWS), lane * 128 : lane * 128 + 128]
        i = lax.broadcasted_iota(jnp.int32, gram.shape, 0) + start
        j = lax.broadcasted_iota(jnp.int32, gram.shape, 1) + lane * 128
        kept = jnp.where(i == j, gram, 0.0)
        down.append(jnp.broadcast_to(jnp.sum(kept, axis=1, keepdims=True), gram.shape))
        part = jnp.sum(kept.reshape(ROWS // TILE, TILE, 128), axis=0)
        across[lane] = part if across[lane] is None else across[lane] + part
    return [jnp.sum(x, axis=0, keepdims=True) for x in across], down


def kernel_matrices(gram_ref, kernel_ref, mass_ref, scale):
    members = gram_ref.shape[-1]
    for region in range(gram_ref.shape[0]):
        across, down = diagonal(gram_ref, region)
        across = [0.5 * LIFT - x * scale for x in across]
        masses = [0.0 for _ in across]
        for i, start in enumerate(range(0, members, ROWS)):
            rows = pl.ds(start, ROWS)
            base = 0.5 * LIFT - down[i] * scale
            for lane, (gram, x) in enumerate(zip(halves(gram_ref, region, rows), across)):
                part = jnp.exp2(gram * (2.0 * scale) + base + x)
                kernel_ref[region, rows, lane * 128 : lane * 128 + 128] = part
                part = jnp.sum(part.reshape(ROWS // TILE, TILE, 128), axis=0)
                masses[lane] = masses[lane] + part
        masses = [jnp.sum(x, axis=0, keepdims=True) for x in masses]
        mass_ref[region] = jnp.concatenate(masses, axis=1)


def transports_scaled(kernel_ref, weights, mass_ref, use):
    regions = range(kernel_ref.shape[0])
    members = kernel_ref.shape[-1]
    starts = range(0, members, ROWS)
    lanes = range(members // 128)
    share = 2.0**MASS / members

    def lane_parts(row):
        return [row[:, lane * 128 : lane * 128 + 128] for lane in lanes]

    def settle(totals, region):
        return [w / x for w, x in zip(lane_parts(weights[region : region + 1]), totals)]

    def masses_of(region, rows, factor):
        parts = [k * f for k, f in zip(halves(kernel_ref, region, rows), factor)]
        mass = jnp.sum(fold(parts, jnp.add), axis=1, keepdims=True)
        mass = jnp.broadcast_to(mass, (ROWS, 128))
        return parts, mass, pl.reciprocal(mass, approx=True)

    def sweep(least_i, least_j, factors):
        next_i, next_j, next_factors = [], [], []
        for region, low_i, low_j, factor in zip(regions, least_i, least_j, factors):
            totals = [None for _ in lanes]
            for start in starts:
                rows = pl.ds(start, ROWS)
                _, mass, ratio = masses_of(region, rows, factor)
                low_j = jnp.minimum(low_j, mass)
                for lane, kernel in enumerate(halves(kernel_ref, region, rows)):
                    part = jnp.sum((kernel * ratio).reshape(ROWS // TILE, TILE, 128), axis=0)
                    totals[lane] = part if totals[lane] is None else totals[lane] + part
            totals = [jnp.sum(x, axis=0, keepdims=True) * share for x in totals]
            next_i.append(jnp.minimum(low_i, fold(totals, jnp.minimum)))
            next_j.append(low_j)
            next_factors.append(settle(totals, region))
        return next_i, next_j, next_factors

    masses = [lane_parts(mass_ref[region]) for region in regions]
    most = fold([fold(x, jnp.maximum) for x in masses], jnp.maximum)
    totals = [[x * 2.0**START for x in mass] for mass in masses]
    least_i = [fold(x, jnp.minimum) for x in totals]
    least_j = [jnp.full((ROWS, 128), 1e30, jnp.float32) for _ in regions]
    factors = [settle(x, region) for x, region in zip(totals, regions)]
    for _ in range(SWEEPS - 1):
        least_i, least_j, factors = sweep(least_i, least_j, factors)
    moves, last_j = [], []
    for region, low_j, factor in zip(regions, least_j, factors):
        blocks = []
        for start in starts:
            parts, mass, ratio = masses_of(region, pl.ds(start, ROWS), factor)
            low_j = jnp.minimum(low_j, mass)
            blocks.append(jnp.concatenate([x * ratio for x in parts], axis=1).astype(jnp.bfloat16))
        moves.append(jnp.concatenate(blocks, axis=0))
        last_j.append(low_j)
        if len(moves) == PAIR:
            use(region // PAIR, moves)
            moves = []
    least_i = fold(least_i, jnp.minimum)
    return jnp.min(least_i), jnp.min(fold(last_j, jnp.minimum)), jnp.max(most)


def transport_logs(gram, logw, scale):
    members = gram.shape[-1]
    j = lax.broadcasted_iota(jnp.int32, gram.shape, 0)
    i = lax.broadcasted_iota(jnp.int32, gram.shape, 1)
    kept = jnp.where(i == j, gram, 0.0)
    down = jnp.sum(kept, axis=1, keepdims=True)
    across = jnp.sum(kept, axis=0, keepdims=True)
    cost = (down + across - 2.0 * gram) * scale
    pot_g = jnp.zeros((members, 1), jnp.float32)
    for sweep in range(SWEEPS):
        term = pot_g - cost
        top = jnp.max(term, axis=0, keepdims=True)
        pot_f = logw - top - jnp.log(jnp.sum(jnp.exp2(term - top), axis=0, keepdims=True)) * LOG2E
        term = pot_f - cost
        top = jnp.max(term, axis=1, keepdims=True)
        pot_g = -math.log2(members) - top
        pot_g = pot_g - jnp.log(jnp.sum(jnp.exp2(term - top), axis=1, keepdims=True)) * LOG2E
    return (members * jnp.exp2(pot_f + pot_g - cost)).astype(jnp.bfloat16)


def transform(state_ref, pair, moves):
    lon_dev, nvar, _, members = state_ref.shape
    size = PAIR * TILE
    own = state_ref[:, :, pair * size : (pair + 1) * size, :].astype(jnp.float32)
    parts = []
    for region, move in enumerate(moves):
        cells = own[:, :, region * TILE : (region + 1) * TILE].astype(jnp.bfloat16)
        cells = cells.reshape(lon_dev * nvar * TILE, members)
        moved = lax.dot_general(
            cells, move, (((1,), (1,)), ((), ())), preferred_element_type=jnp.float32
        )
        parts.append(moved.reshape(lon_dev, nvar, TILE, members))
    return jnp.concatenate(parts, axis=2).astype(jnp.bfloat16)


def analyse_kernel(count, scale, *refs):
    odd_ref, halo_ref, old_ref, state_hbm_ref, like_ref, sums_ref, out_ref = refs[:7]
    gram_ref, kernel_ref, mass_ref, result_ref, state_ref, out_sems, state_sems = refs[7:]
    regions, members, _ = gram_ref.shape
    pairs = regions // PAIR
    size = PAIR * TILE
    lat = regions * REGION
    fetches = slab_copies(state_hbm_ref, state_ref, state_sems)
    for copy in fetches:
        copy.start()

    def send(pair):
        rows = pl.ds(pair * size, size)
        return pltpu.make_async_copy(
            result_ref.at[pair], out_ref.at[:, :, rows, :], out_sems.at[pair]
        )

    misfit = like_ref[...] + like_rows(halo_ref[halo_ref.shape[0] - 4 * TILE :, :])
    misfit = misfit - jnp.min(misfit, axis=1, keepdims=True)
    factor = (-0.5 * LOG2E * count) / jnp.sum(sums_ref[...], axis=0, keepdims=True)
    like = misfit * jnp.concatenate([factor] * (members // 128), axis=1)
    weights = jnp.exp2(like + MASS)
    norm = jnp.sum(weights, axis=1, keepdims=True) * 2.0**-MASS
    weights = weights / norm

    planes = halo_ref.shape[0] // lat
    halo = [w for w in halo_weights(odd_ref[0] == 0) for _ in range(planes // HALO)]
    slabs = [slab_of(halo_ref, lat, at) for at in range(lat // size)]
    add_grams(slabs, halo, old_ref, gram_ref)
    kernel_matrices(gram_ref, kernel_ref, mass_ref, scale)

    def use(pair, moves):
        fetches[pair].wait()
        result_ref[pair] = transform(state_ref, pair, moves)
        send(pair).start()

    row, col, most = transports_scaled(kernel_ref, weights, mass_ref, use)
    sound = (row >= 2.0**-24) & (col >= 2.0**-30) & (most <= 2.0**30) & (row * col >= 2.0**-34)
    for pair in range(pairs):
        send(pair).wait()

    @pl.when(jnp.logical_not(sound))
    def _():
        logw = like - jnp.log(norm) * LOG2E
        for pair in range(pairs):
            again = [
                transport_logs(gram_ref[region], logw[region : region + 1], scale)
                for region in range(pair * PAIR, (pair + 1) * PAIR)
            ]
            result_ref[pair] = transform(state_ref, pair, again)
            send(pair).start()
            send(pair).wait()


def analyse(odd, halo, gram, state, like, sums, count, scale):
    lon_dev, nvar, lat, members = state.shape
    regions = lat // REGION
    pairs = regions // PAIR
    vmem = pl.BlockSpec(memory_space=pltpu.VMEM)
    return pl.pallas_call(
        functools.partial(analyse_kernel, count, scale),
        in_specs=[
            pl.BlockSpec(memory_space=pltpu.SMEM),
            vmem,
            vmem,
            pl.BlockSpec(memory_space=pltpu.HBM),
            vmem,
            vmem,
        ],
        out_specs=pl.BlockSpec(memory_space=pl.ANY),
        out_shape=jax.ShapeDtypeStruct(state.shape, state.dtype),
        scratch_shapes=[
            pltpu.VMEM(gram.shape, jnp.float32),
            pltpu.VMEM(gram.shape, jnp.float32),
            pltpu.VMEM((regions, 1, members), jnp.float32),
            pltpu.VMEM((pairs, lon_dev, nvar, PAIR * TILE, members), state.dtype),
            pltpu.VMEM(state.shape, state.dtype),
            pltpu.SemaphoreType.DMA((pairs,)),
            pltpu.SemaphoreType.DMA((pairs,)),
        ],
        compiler_params=pltpu.CompilerParams(vmem_limit_bytes=24 * 2**20),
        name="analyse",
    )(odd, halo, gram, pltpu.with_memory_space_constraint(state, pltpu.HBM), like, sums)


def on_device(state, obs_index, obs_value, obs_var):
    nvar = state.shape[1]
    count = lax.axis_size("lon")
    odd = (lax.axis_index("lon") & 1).astype(jnp.int32).reshape(1)
    near_pairs = [(i, i ^ 1) for i in range(count)]
    far_pairs = [(i, (i + 1 if i % 2 else i - 1) % count) for i in range(count)]
    own_like, for_near, for_far, part = observe(odd, state, obs_index, obs_value, obs_var)
    far = lax.ppermute(for_far, "lon", far_pairs)
    near = lax.ppermute(for_near, "lon", near_pairs)
    start = near.shape[0] - TILE
    part = part[0] + jnp.sum(near[start : start + 3, :128].astype(jnp.float32), axis=0)
    sums = lax.all_to_all(
        jnp.broadcast_to(part, (count // 2, 128)),
        "lon",
        0,
        0,
        axis_index_groups=[[i for i in range(count) if (i ^ i >> 1) & 1 == kind] for kind in range(2)],
        tiled=True,
    )
    offsets = range(REGION + 2 * HALO)
    line = [1.0 - max(0, HALO - p, p - (HALO + REGION - 1)) / (HALO + 1) for p in offsets]
    scale = LOG2E / EPS / (nvar * sum(line) ** 2)
    gram, like = own_gram(odd, state, near, own_like)
    nobs = float(obs_index.shape[0] * count)
    return analyse(odd, far, gram, state, like, sums, nobs, scale)


def solution(mesh):
    return jax.shard_map(
        on_device,
        mesh=mesh,
        in_specs=(
            P(("ens", "lon"), None, None, None),
            P(("ens", "lon")),
            P(("ens", "lon")),
            P(("ens", "lon")),
        ),
        out_specs=P(("ens", "lon"), None, None, None),
        check_vma=False,
    )
```

```python
import functools
import math

import jax
import jax.numpy as jnp
from jax import lax
from jax.experimental import pallas as pl
from jax.experimental.pallas import tpu as pltpu
from jax.sharding import PartitionSpec as P

REGION = 8
HALO = 4
SWEEPS = 4
EPS = 0.05
TILE = 8
PAIR = 2
LOG2E = 1.4426950408889634
ROWS = 32
LIFT, START, MASS = 20, -10, 60


def fold(values, op):
    out = values[0]
    for value in values[1:]:
        out = op(out, value)
    return out


def line_weight(place):
    dist = jnp.maximum(0.0, jnp.maximum(HALO - place, place - (HALO + REGION - 1)))
    inside = (place >= 0) & (place < REGION + 2 * HALO)
    return jnp.where(inside, 1.0 - dist / (HALO + 1), 0.0)


def like_rows(rows):
    rows = rows.astype(jnp.float32)
    return rows[:TILE] + rows[TILE : 2 * TILE] + rows[2 * TILE : 3 * TILE]


def in_parts(values, extra):
    below = lax.broadcasted_iota(jnp.int32, values.shape, 0)
    extra_high = extra.astype(jnp.bfloat16).astype(jnp.float32)
    extra_middle = (extra - extra_high).astype(jnp.bfloat16).astype(jnp.float32)
    extra_low = extra - extra_high - extra_middle
    last = jnp.where(below == 0, extra_high, jnp.where(below == 1, extra_middle, extra_low))
    last = jnp.where(below < 3, last, 0.0)
    high = values.astype(jnp.bfloat16).astype(jnp.float32)
    middle = (values - high).astype(jnp.bfloat16).astype(jnp.float32)
    low = values - high - middle
    return jnp.concatenate([high, middle, low, last], axis=0).astype(jnp.bfloat16)


def steps_inside(place):
    dist = jnp.maximum(0.0, jnp.maximum(HALO - place, place - (HALO + REGION - 1)))
    inside = (place >= 0) & (place < REGION + 2 * HALO)
    return jnp.where(inside, HALO + 1 - dist, 0.0)


def observe_kernel(*refs):
    odd_ref, state_ref, rows_ref = refs[:3]
    own_ref, near_ref, far_ref, part_ref = refs[6:10]
    cells_ref, index_ref, value_ref, var_ref, sems = refs[10:]
    lon_dev, lat, members = cells_ref.shape
    nobs = index_ref.shape[1]
    edge = rows_ref.shape[0] // lon_dev * HALO
    last = rows_ref.shape[0] - edge
    far_at = pl.multiple_of(odd_ref[0] * last, 16)
    near_at = pl.multiple_of(last - far_at, 16)
    fetches = [
        (refs[3], index_ref),
        (refs[4], value_ref),
        (refs[5], var_ref),
        (state_ref.at[:, 0], cells_ref),
        (rows_ref.at[pl.ds(far_at, edge), :], far_ref.at[pl.ds(0, edge), :]),
        (rows_ref.at[pl.ds(near_at, edge), :], near_ref.at[pl.ds(0, edge), :]),
    ]
    copies = [
        pltpu.make_async_copy(src, dst, sems.at[i]) for i, (src, dst) in enumerate(fetches)
    ]
    for copy in copies:
        copy.start()
    for copy in copies[:3]:
        copy.wait()
    index = index_ref[...]
    sub = lax.broadcasted_iota(jnp.int32, (TILE, nobs), 0)
    table = jnp.where(
        sub == 0,
        index.astype(jnp.float32),
        jnp.where(sub == 1, value_ref[...], var_ref[...]),
    ).T
    index_col = table[:, 0:1].astype(jnp.int32)
    value = table[:, 1:2]
    var = table[:, 2:3]
    pick = index_col == lax.broadcasted_iota(jnp.int32, (nobs, lon_dev * lat), 1)
    pick = jnp.where(pick, 1.0, 0.0).astype(jnp.bfloat16)
    lon = (index // lat).astype(jnp.float32)
    along = index.astype(jnp.float32) - lon * lat
    blocks = own_ref.shape[0]
    block = lax.broadcasted_iota(jnp.int32, (blocks, nobs), 0).astype(jnp.float32)
    across = steps_inside(along - REGION * block + HALO)
    side = jnp.where(odd_ref[0] == 1, float(REGION), float(-REGION))
    weights = [steps_inside(lon + (HALO + shift)) * across for shift in (0.0, side, -side)]
    weights = jnp.concatenate(weights, axis=0).astype(jnp.bfloat16)
    inverse = 1.0 / var
    copies[3].wait()
    rows = cells_ref[...].reshape(lon_dev * lat, members)
    seen = jnp.dot(pick, rows, preferred_element_type=jnp.float32)
    terms = (value - seen) ** 2 * inverse
    high = terms.astype(jnp.bfloat16)
    rest = terms - high.astype(jnp.float32)
    middle = rest.astype(jnp.bfloat16)
    low = (rest - middle.astype(jnp.float32)).astype(jnp.bfloat16)
    sums = [jnp.dot(weights, x, preferred_element_type=jnp.float32) for x in (low, middle, high)]
    like = fold(sums, jnp.add) * (1.0 / (HALO + 1) ** 2)
    centre = jnp.sum(seen, axis=1, keepdims=True) * (1.0 / members)
    spread = jnp.sum((seen - centre) ** 2, axis=1, keepdims=True) * (1.0 / (members - 1))
    innovation = (value - centre) ** 2 / (var + spread)
    part = jnp.sum(innovation, axis=0, keepdims=True)
    part_ref[...] = jnp.broadcast_to(part, part_ref.shape)
    own_ref[...] = like[:blocks]
    near_ref[edge:, :] = in_parts(like[blocks : 2 * blocks], part)
    far_ref[edge:, :] = in_parts(like[2 * blocks :], jnp.zeros_like(part))
    for copy in copies[4:]:
        copy.wait()


def observe(odd, state, obs_index, obs_value, obs_var):
    lon_dev, nvar, lat, members = state.shape
    nobs = obs_index.size
    assert lat // REGION == TILE
    like = jax.ShapeDtypeStruct((lat // REGION, members), jnp.float32)
    payload = pltpu.VMEM((HALO * nvar * lat + 4 * TILE, members), state.dtype)
    part = jax.ShapeDtypeStruct((TILE, 128), jnp.float32)
    arrays = state, state.reshape(-1, members), obs_index[None], obs_value[None], obs_var[None]
    return pl.pallas_call(
        observe_kernel,
        in_specs=[pl.BlockSpec(memory_space=pltpu.SMEM)]
        + [pl.BlockSpec(memory_space=pltpu.HBM)] * len(arrays),
        out_specs=[pl.BlockSpec(memory_space=pltpu.VMEM)] * 4,
        out_shape=[like, payload, payload, part],
        scratch_shapes=[
            pltpu.VMEM((lon_dev, lat, members), state.dtype),
            pltpu.VMEM((1, nobs), jnp.int32),
            pltpu.VMEM((1, nobs), jnp.float32),
            pltpu.VMEM((1, nobs), jnp.float32),
            pltpu.SemaphoreType.DMA((6,)),
        ],
        compiler_params=pltpu.CompilerParams(vmem_limit_bytes=16 * 2**20),
        name="observe",
    )(odd, *[pltpu.with_memory_space_constraint(x, pltpu.HBM) for x in arrays])


def slab_of(ref, lat, at):
    size = PAIR * TILE
    planes = ref.shape[0] // lat
    rows = [ref[i * lat + at * size : i * lat + (at + 1) * size, :] for i in range(planes)]
    return jnp.stack(rows).astype(jnp.float32)


def pair_tiles(load, step, steps):
    here = load(step)
    none = jnp.zeros_like(here[:, :TILE])
    before = load(step - 1)[:, TILE:] if step else none
    after = load(step + 1)[:, :TILE] if step + 1 < steps else none
    return before, here[:, :TILE], here[:, TILE:], after


def halo_weights(to_left):
    steps = [jnp.float32(1.0) - jnp.float32(d) / jnp.float32(HALO + 1) for d in range(HALO, 0, -1)]
    return [jnp.where(to_left, x, y) for x, y in zip(steps, steps[::-1])]


def turn(tile):
    return tile.reshape(-1, tile.shape[-1]).astype(jnp.bfloat16).T


def gram_of(tiles, turned, weights):
    planes, _, members = tiles[0].shape
    depth = planes * TILE
    row = lax.broadcasted_iota(jnp.int32, (TILE, members), 0)
    upper = row < HALO
    rowf = row.astype(jnp.float32)
    edge = line_weight(jnp.where(upper, rowf + (HALO + REGION), rowf - HALO))
    lane = lax.broadcasted_iota(jnp.int32, (1, depth), 1) & (TILE - 1)
    take_next = jnp.where(lane < HALO, 1.0, 0.0).astype(jnp.bfloat16)
    take_prev = jnp.where(lane < HALO, 0.0, 1.0).astype(jnp.bfloat16)
    grams = []
    for at in (1, 2):
        margin = jnp.where(upper, tiles[at + 1], tiles[at - 1])
        main_rows, margin_rows = [], []
        for plane, weight in enumerate(weights):
            own = tiles[at][plane]
            main_rows.append(own if weight is None else own * weight)
            margin_rows.append(margin[plane] * (edge if weight is None else edge * weight))
        weighted = jnp.stack(main_rows + margin_rows)
        weighted = weighted.reshape(2 * depth, members).astype(jnp.bfloat16)
        margin = turned[at + 1] * take_next + turned[at - 1] * take_prev
        both = jnp.concatenate([turned[at], margin], axis=1)
        grams.append(jnp.dot(both, weighted, preferred_element_type=jnp.float32))
    return grams


def slab_copies(src_ref, dst_ref, sems, only=None):
    size = PAIR * TILE

    def slab(at):
        rows = pl.ds(pl.multiple_of(at * size, size), size)
        return pltpu.make_async_copy(
            src_ref.at[:, :, rows, :], dst_ref.at[:, :, rows, :], sems.at[at]
        )

    return slab(only) if only is not None else [slab(i) for i in range(src_ref.shape[2] // size)]


def own_gram_kernel(odd_ref, state_hbm_ref, near_ref, own_ref, *refs):
    first_ref, last_hbm_ref, like_ref, state_ref, last_ref, sems, last_sems = refs
    lon_dev, nvar, lat, members = state_ref.shape
    kept = first_ref.shape[0]
    steps = lat // (PAIR * TILE)
    copies = slab_copies(state_hbm_ref, state_ref, sems)
    for copy in copies:
        copy.start()
    like_ref[...] = own_ref[...] + like_rows(near_ref[near_ref.shape[0] - 4 * TILE :, :])
    size = PAIR * TILE

    def load(step):
        own = state_ref[:, :, step * size : (step + 1) * size, :].astype(jnp.float32)
        own = own.reshape(lon_dev * nvar, size, members)
        return jnp.concatenate([own, slab_of(near_ref, lat, step)], axis=0)

    weights = [None] * (lon_dev * nvar)
    weights += [w for w in halo_weights(odd_ref[0] == 1) for _ in range(nvar)]
    for copy in copies:
        copy.wait()
    slabs = [load(step) for step in range(steps)]

    def put(region, gram):
        if region < kept:
            first_ref[region] = gram
        else:
            last_ref[region - kept] = gram
            keep(region - kept).start()

    def keep(at):
        return pltpu.make_async_copy(last_ref.at[at], last_hbm_ref.at[at], last_sems.at[at])

    add_grams(slabs, weights, put)
    for at in range(last_ref.shape[0]):
        keep(at).wait()


def add_grams(slabs, weights, put):
    none = jnp.zeros_like(slabs[0][:, :TILE])
    tiles = [none]
    for slab in slabs:
        tiles += [slab[:, :TILE], slab[:, TILE:]]
    tiles.append(none)
    turned = [turn(tile) for tile in tiles[1:-1]]
    turned = [jnp.zeros_like(turned[0])] + turned + [jnp.zeros_like(turned[0])]
    for pair in range(len(slabs)):
        window = slice(pair * PAIR, pair * PAIR + PAIR + 2)
        grams = gram_of(tiles[window], turned[window], weights)
        for at, gram in enumerate(grams):
            put(pair * PAIR + at, gram)


def own_gram(odd, state, near, own):
    _, _, lat, members = state.shape
    half = lat // REGION // 2
    vmem = pl.BlockSpec(memory_space=pltpu.VMEM)
    return pl.pallas_call(
        own_gram_kernel,
        in_specs=[
            pl.BlockSpec(memory_space=pltpu.SMEM),
            pl.BlockSpec(memory_space=pltpu.HBM),
            vmem,
            vmem,
        ],
        out_specs=[vmem, pl.BlockSpec(memory_space=pltpu.HBM), vmem],
        out_shape=[
            jax.ShapeDtypeStruct((half, members, members), jnp.float32),
            pltpu.HBM((half, members, members), jnp.float32),
            jax.ShapeDtypeStruct(own.shape, jnp.float32),
        ],
        scratch_shapes=[
            pltpu.VMEM(state.shape, state.dtype),
            pltpu.VMEM((half, members, members), jnp.float32),
            pltpu.SemaphoreType.DMA((lat // (PAIR * TILE),)),
            pltpu.SemaphoreType.DMA((half,)),
        ],
        compiler_params=pltpu.CompilerParams(vmem_limit_bytes=24 * 2**20),
        name="own_gram",
    )(odd, pltpu.with_memory_space_constraint(state, pltpu.HBM), near, own)


def halves(ref, region, rows):
    members = ref.shape[-1]
    return [ref[region, rows, at : at + 128] for at in range(0, members, 128)]


def diagonal(gram_ref, region):
    members = gram_ref.shape[-1]
    across = [None] * (members // 128)
    down = []
    for start in range(0, members, ROWS):
        lane = start // 128
        gram = gram_ref[region, pl.ds(start, ROWS), lane * 128 : lane * 128 + 128]
        i = lax.broadcasted_iota(jnp.int32, gram.shape, 0) + start
        j = lax.broadcasted_iota(jnp.int32, gram.shape, 1) + lane * 128
        kept = jnp.where(i == j, gram, 0.0)
        down.append(jnp.broadcast_to(jnp.sum(kept, axis=1, keepdims=True), gram.shape))
        part = jnp.sum(kept.reshape(ROWS // TILE, TILE, 128), axis=0)
        across[lane] = part if across[lane] is None else across[lane] + part
    return [jnp.sum(x, axis=0, keepdims=True) for x in across], down


def kernel_matrices(gram_ref, kernel_ref, mass_ref, scale):
    members = gram_ref.shape[-1]
    for region in range(gram_ref.shape[0]):
        across, down = diagonal(gram_ref, region)
        across = [0.5 * LIFT - x * scale for x in across]
        masses = [0.0 for _ in across]
        for i, start in enumerate(range(0, members, ROWS)):
            rows = pl.ds(start, ROWS)
            base = 0.5 * LIFT - down[i] * scale
            for lane, (gram, x) in enumerate(zip(halves(gram_ref, region, rows), across)):
                part = jnp.exp2(gram * (2.0 * scale) + base + x)
                kernel_ref[region, rows, lane * 128 : lane * 128 + 128] = part
                part = jnp.sum(part.reshape(ROWS // TILE, TILE, 128), axis=0)
                masses[lane] = masses[lane] + part
        masses = [jnp.sum(x, axis=0, keepdims=True) for x in masses]
        mass_ref[region] = jnp.concatenate(masses, axis=1)


def transports_scaled(kernel_ref, weights, mass_ref, use):
    regions = range(kernel_ref.shape[0])
    members = kernel_ref.shape[-1]
    starts = range(0, members, ROWS)
    lanes = range(members // 128)
    share = 2.0**MASS / members

    def lane_parts(row):
        return [row[:, lane * 128 : lane * 128 + 128] for lane in lanes]

    def settle(totals, region):
        return [w / x for w, x in zip(lane_parts(weights[region : region + 1]), totals)]

    def masses_of(region, rows, factor):
        parts = [k * f for k, f in zip(halves(kernel_ref, region, rows), factor)]
        mass = jnp.sum(fold(parts, jnp.add), axis=1, keepdims=True)
        mass = jnp.broadcast_to(mass, (ROWS, 128))
        return parts, mass, pl.reciprocal(mass, approx=True)

    def sweep(least_i, least_j, factors):
        next_i, next_j, next_factors = [], [], []
        for region, low_i, low_j, factor in zip(regions, least_i, least_j, factors):
            totals = [None for _ in lanes]
            for start in starts:
                rows = pl.ds(start, ROWS)
                _, mass, ratio = masses_of(region, rows, factor)
                low_j = jnp.minimum(low_j, mass)
                for lane, kernel in enumerate(halves(kernel_ref, region, rows)):
                    part = jnp.sum((kernel * ratio).reshape(ROWS // TILE, TILE, 128), axis=0)
                    totals[lane] = part if totals[lane] is None else totals[lane] + part
            totals = [jnp.sum(x, axis=0, keepdims=True) * share for x in totals]
            next_i.append(jnp.minimum(low_i, fold(totals, jnp.minimum)))
            next_j.append(low_j)
            next_factors.append(settle(totals, region))
        return next_i, next_j, next_factors

    masses = [lane_parts(mass_ref[region]) for region in regions]
    most = fold([fold(x, jnp.maximum) for x in masses], jnp.maximum)
    totals = [[x * 2.0**START for x in mass] for mass in masses]
    least_i = [fold(x, jnp.minimum) for x in totals]
    least_j = [jnp.full((ROWS, 128), 1e30, jnp.float32) for _ in regions]
    factors = [settle(x, region) for x, region in zip(totals, regions)]
    for _ in range(SWEEPS - 1):
        least_i, least_j, factors = sweep(least_i, least_j, factors)
    moves, last_j = [], []
    for region, low_j, factor in zip(regions, least_j, factors):
        blocks = []
        for start in starts:
            parts, mass, ratio = masses_of(region, pl.ds(start, ROWS), factor)
            low_j = jnp.minimum(low_j, mass)
            blocks.append(jnp.concatenate([x * ratio for x in parts], axis=1).astype(jnp.bfloat16))
        moves.append(jnp.concatenate(blocks, axis=0))
        last_j.append(low_j)
        if len(moves) == PAIR:
            use(region // PAIR, moves)
            moves = []
    least_i = fold(least_i, jnp.minimum)
    return jnp.min(least_i), jnp.min(fold(last_j, jnp.minimum)), jnp.max(most)


def transport_logs(gram, logw, scale):
    members = gram.shape[-1]
    j = lax.broadcasted_iota(jnp.int32, gram.shape, 0)
    i = lax.broadcasted_iota(jnp.int32, gram.shape, 1)
    kept = jnp.where(i == j, gram, 0.0)
    down = jnp.sum(kept, axis=1, keepdims=True)
    across = jnp.sum(kept, axis=0, keepdims=True)
    cost = (down + across - 2.0 * gram) * scale
    pot_g = jnp.zeros((members, 1), jnp.float32)
    for sweep in range(SWEEPS):
        term = pot_g - cost
        top = jnp.max(term, axis=0, keepdims=True)
        pot_f = logw - top - jnp.log(jnp.sum(jnp.exp2(term - top), axis=0, keepdims=True)) * LOG2E
        term = pot_f - cost
        top = jnp.max(term, axis=1, keepdims=True)
        pot_g = -math.log2(members) - top
        pot_g = pot_g - jnp.log(jnp.sum(jnp.exp2(term - top), axis=1, keepdims=True)) * LOG2E
    return (members * jnp.exp2(pot_f + pot_g - cost)).astype(jnp.bfloat16)


def transform(state_ref, pair, moves):
    lon_dev, nvar, _, members = state_ref.shape
    size = PAIR * TILE
    own = state_ref[:, :, pair * size : (pair + 1) * size, :].astype(jnp.float32)
    parts = []
    for region, move in enumerate(moves):
        cells = own[:, :, region * TILE : (region + 1) * TILE].astype(jnp.bfloat16)
        cells = cells.reshape(lon_dev * nvar * TILE, members)
        moved = lax.dot_general(
            cells, move, (((1,), (1,)), ((), ())), preferred_element_type=jnp.float32
        )
        parts.append(moved.reshape(lon_dev, nvar, TILE, members))
    return jnp.concatenate(parts, axis=2).astype(jnp.bfloat16)


def analyse_kernel(count, scale, *refs):
    odd_ref, halo_ref, first_ref, last_hbm_ref, state_hbm_ref, like_ref, sums_ref = refs[:7]
    out_ref, gram_ref, kernel_ref, mass_ref, result_ref, state_ref, last_ref = refs[7:14]
    out_sems, state_sems, last_sems = refs[14:]
    kept = first_ref.shape[0]
    olds = [
        pltpu.make_async_copy(last_hbm_ref.at[at], last_ref.at[at], last_sems.at[at])
        for at in range(last_ref.shape[0])
    ]
    for copy in olds:
        copy.start()
    regions, members, _ = gram_ref.shape
    pairs = regions // PAIR
    size = PAIR * TILE
    lat = regions * REGION
    fetches = slab_copies(state_hbm_ref, state_ref, state_sems)
    for copy in fetches:
        copy.start()

    def send(pair):
        rows = pl.ds(pair * size, size)
        return pltpu.make_async_copy(
            result_ref.at[pair], out_ref.at[:, :, rows, :], out_sems.at[pair]
        )

    misfit = like_ref[...] + like_rows(halo_ref[halo_ref.shape[0] - 4 * TILE :, :])
    misfit = misfit - jnp.min(misfit, axis=1, keepdims=True)
    factor = (-0.5 * LOG2E * count) / jnp.sum(sums_ref[...], axis=0, keepdims=True)
    like = misfit * jnp.concatenate([factor] * (members // 128), axis=1)
    weights = jnp.exp2(like + MASS)
    norm = jnp.sum(weights, axis=1, keepdims=True) * 2.0**-MASS
    weights = weights / norm

    planes = halo_ref.shape[0] // lat
    halo = [w for w in halo_weights(odd_ref[0] == 0) for _ in range(planes // HALO)]
    slabs = [slab_of(halo_ref, lat, at) for at in range(lat // size)]

    def put(region, gram):
        if region < kept:
            gram_ref[region] = first_ref[region] + gram
        else:
            olds[region - kept].wait()
            gram_ref[region] = last_ref[region - kept] + gram

    add_grams(slabs, halo, put)
    kernel_matrices(gram_ref, kernel_ref, mass_ref, scale)

    def use(pair, moves):
        fetches[pair].wait()
        result_ref[pair] = transform(state_ref, pair, moves)
        send(pair).start()

    row, col, most = transports_scaled(kernel_ref, weights, mass_ref, use)
    sound = (row >= 2.0**-24) & (col >= 2.0**-30) & (most <= 2.0**30) & (row * col >= 2.0**-34)
    for pair in range(pairs):
        send(pair).wait()

    @pl.when(jnp.logical_not(sound))
    def _():
        logw = like - jnp.log(norm) * LOG2E
        for pair in range(pairs):
            again = [
                transport_logs(gram_ref[region], logw[region : region + 1], scale)
                for region in range(pair * PAIR, (pair + 1) * PAIR)
            ]
            result_ref[pair] = transform(state_ref, pair, again)
            send(pair).start()
            send(pair).wait()


def analyse(odd, halo, first, last, state, like, sums, count, scale):
    lon_dev, nvar, lat, members = state.shape
    regions = lat // REGION
    pairs = regions // PAIR
    vmem = pl.BlockSpec(memory_space=pltpu.VMEM)
    return pl.pallas_call(
        functools.partial(analyse_kernel, count, scale),
        in_specs=[
            pl.BlockSpec(memory_space=pltpu.SMEM),
            vmem,
            vmem,
            pl.BlockSpec(memory_space=pltpu.HBM),
            pl.BlockSpec(memory_space=pltpu.HBM),
            vmem,
            vmem,
        ],
        out_specs=pl.BlockSpec(memory_space=pl.ANY),
        out_shape=jax.ShapeDtypeStruct(state.shape, state.dtype),
        scratch_shapes=[
            pltpu.VMEM((regions, members, members), jnp.float32),
            pltpu.VMEM((regions, members, members), jnp.float32),
            pltpu.VMEM((regions, 1, members), jnp.float32),
            pltpu.VMEM((pairs, lon_dev, nvar, PAIR * TILE, members), state.dtype),
            pltpu.VMEM(state.shape, state.dtype),
            pltpu.VMEM(last.shape, jnp.float32),
            pltpu.SemaphoreType.DMA((pairs,)),
            pltpu.SemaphoreType.DMA((pairs,)),
            pltpu.SemaphoreType.DMA((last.shape[0],)),
        ],
        compiler_params=pltpu.CompilerParams(vmem_limit_bytes=24 * 2**20),
        name="analyse",
    )(
        odd,
        halo,
        first,
        *[pltpu.with_memory_space_constraint(x, pltpu.HBM) for x in (last, state)],
        like,
        sums,
    )


def on_device(state, obs_index, obs_value, obs_var):
    nvar = state.shape[1]
    count = lax.axis_size("lon")
    odd = (lax.axis_index("lon") & 1).astype(jnp.int32).reshape(1)
    near_pairs = [(i, i ^ 1) for i in range(count)]
    far_pairs = [(i, (i + 1 if i % 2 else i - 1) % count) for i in range(count)]
    own_like, for_near, for_far, part = observe(odd, state, obs_index, obs_value, obs_var)
    far = lax.ppermute(for_far, "lon", far_pairs)
    near = lax.ppermute(for_near, "lon", near_pairs)
    start = near.shape[0] - TILE
    part = part[0] + jnp.sum(near[start : start + 3, :128].astype(jnp.float32), axis=0)
    sums = lax.all_to_all(
        jnp.broadcast_to(part, (count // 2, 128)),
        "lon",
        0,
        0,
        axis_index_groups=[[i for i in range(count) if (i ^ i >> 1) & 1 == kind] for kind in range(2)],
        tiled=True,
    )
    offsets = range(REGION + 2 * HALO)
    line = [1.0 - max(0, HALO - p, p - (HALO + REGION - 1)) / (HALO + 1) for p in offsets]
    scale = LOG2E / EPS / (nvar * sum(line) ** 2)
    first, last, like = own_gram(odd, state, near, own_like)
    nobs = float(obs_index.shape[0] * count)
    return analyse(odd, far, first, last, state, like, sums, nobs, scale)


def solution(mesh):
    return jax.shard_map(
        on_device,
        mesh=mesh,
        in_specs=(
            P(("ens", "lon"), None, None, None),
            P(("ens", "lon")),
            P(("ens", "lon")),
            P(("ens", "lon")),
        ),
        out_specs=P(("ens", "lon"), None, None, None),
        check_vma=False,
    )
```

```python
import functools
import math

import jax
import jax.numpy as jnp
from jax import lax
from jax.experimental import pallas as pl
from jax.experimental.pallas import tpu as pltpu
from jax.sharding import PartitionSpec as P

REGION = 8
HALO = 4
SWEEPS = 4
EPS = 0.05
TILE = 8
PAIR = 2
LOG2E = 1.4426950408889634
ROWS = 32
LIFT, START, MASS = 20, -10, 60


def fold(values, op):
    out = values[0]
    for value in values[1:]:
        out = op(out, value)
    return out


def line_weight(place):
    dist = jnp.maximum(0.0, jnp.maximum(HALO - place, place - (HALO + REGION - 1)))
    inside = (place >= 0) & (place < REGION + 2 * HALO)
    return jnp.where(inside, 1.0 - dist / (HALO + 1), 0.0)


def like_rows(rows):
    rows = rows.astype(jnp.float32)
    return rows[:TILE] + rows[TILE : 2 * TILE] + rows[2 * TILE : 3 * TILE]


def in_parts(values, extra):
    below = lax.broadcasted_iota(jnp.int32, values.shape, 0)
    extra_high = extra.astype(jnp.bfloat16).astype(jnp.float32)
    extra_middle = (extra - extra_high).astype(jnp.bfloat16).astype(jnp.float32)
    extra_low = extra - extra_high - extra_middle
    last = jnp.where(below == 0, extra_high, jnp.where(below == 1, extra_middle, extra_low))
    last = jnp.where(below < 3, last, 0.0)
    high = values.astype(jnp.bfloat16).astype(jnp.float32)
    middle = (values - high).astype(jnp.bfloat16).astype(jnp.float32)
    low = values - high - middle
    return jnp.concatenate([high, middle, low, last], axis=0).astype(jnp.bfloat16)


def steps_inside(place):
    dist = jnp.maximum(0.0, jnp.maximum(HALO - place, place - (HALO + REGION - 1)))
    inside = (place >= 0) & (place < REGION + 2 * HALO)
    return jnp.where(inside, HALO + 1 - dist, 0.0)


def observe_kernel(*refs):
    odd_ref, state_ref, rows_ref = refs[:3]
    own_ref, near_ref, far_ref, part_ref = refs[6:10]
    cells_ref, index_ref, value_ref, var_ref, sems = refs[10:]
    lon_dev, lat, members = cells_ref.shape
    nobs = index_ref.shape[1]
    edge = rows_ref.shape[0] // lon_dev * HALO
    last = rows_ref.shape[0] - edge
    far_at = pl.multiple_of(odd_ref[0] * last, 16)
    near_at = pl.multiple_of(last - far_at, 16)
    fetches = [
        (refs[3], index_ref),
        (refs[4], value_ref),
        (refs[5], var_ref),
        (state_ref.at[:, 0], cells_ref),
        (rows_ref.at[pl.ds(far_at, edge), :], far_ref.at[pl.ds(0, edge), :]),
        (rows_ref.at[pl.ds(near_at, edge), :], near_ref.at[pl.ds(0, edge), :]),
    ]
    copies = [
        pltpu.make_async_copy(src, dst, sems.at[i]) for i, (src, dst) in enumerate(fetches)
    ]
    for copy in copies:
        copy.start()
    for copy in copies[:3]:
        copy.wait()
    index = index_ref[...]
    sub = lax.broadcasted_iota(jnp.int32, (TILE, nobs), 0)
    table = jnp.where(
        sub == 0,
        index.astype(jnp.float32),
        jnp.where(sub == 1, value_ref[...], var_ref[...]),
    ).T
    index_col = table[:, 0:1].astype(jnp.int32)
    value = table[:, 1:2]
    var = table[:, 2:3]
    pick = index_col == lax.broadcasted_iota(jnp.int32, (nobs, lon_dev * lat), 1)
    pick = jnp.where(pick, 1.0, 0.0).astype(jnp.bfloat16)
    lon = (index // lat).astype(jnp.float32)
    along = index.astype(jnp.float32) - lon * lat
    blocks = own_ref.shape[0]
    block = lax.broadcasted_iota(jnp.int32, (blocks, nobs), 0).astype(jnp.float32)
    across = steps_inside(along - REGION * block + HALO)
    side = jnp.where(odd_ref[0] == 1, float(REGION), float(-REGION))
    weights = [steps_inside(lon + (HALO + shift)) * across for shift in (0.0, side, -side)]
    weights = jnp.concatenate(weights, axis=0).astype(jnp.bfloat16)
    inverse = 1.0 / var
    copies[3].wait()
    rows = cells_ref[...].reshape(lon_dev * lat, members)
    seen = jnp.dot(pick, rows, preferred_element_type=jnp.float32)
    terms = (value - seen) ** 2 * inverse
    high = terms.astype(jnp.bfloat16)
    rest = terms - high.astype(jnp.float32)
    middle = rest.astype(jnp.bfloat16)
    low = (rest - middle.astype(jnp.float32)).astype(jnp.bfloat16)
    sums = [jnp.dot(weights, x, preferred_element_type=jnp.float32) for x in (low, middle, high)]
    like = fold(sums, jnp.add) * (1.0 / (HALO + 1) ** 2)
    centre = jnp.sum(seen, axis=1, keepdims=True) * (1.0 / members)
    spread = jnp.sum((seen - centre) ** 2, axis=1, keepdims=True) * (1.0 / (members - 1))
    innovation = (value - centre) ** 2 / (var + spread)
    part = jnp.sum(innovation, axis=0, keepdims=True)
    part_ref[...] = jnp.broadcast_to(part, part_ref.shape)
    own_ref[...] = like[:blocks]
    near_ref[edge:, :] = in_parts(like[blocks : 2 * blocks], part)
    far_ref[edge:, :] = in_parts(like[2 * blocks :], jnp.zeros_like(part))
    for copy in copies[4:]:
        copy.wait()


def observe(odd, state, obs_index, obs_value, obs_var):
    lon_dev, nvar, lat, members = state.shape
    nobs = obs_index.size
    assert lat // REGION == TILE
    like = jax.ShapeDtypeStruct((lat // REGION, members), jnp.float32)
    payload = pltpu.VMEM((HALO * nvar * lat + 4 * TILE, members), state.dtype)
    part = jax.ShapeDtypeStruct((TILE, 128), jnp.float32)
    arrays = state, state.reshape(-1, members), obs_index[None], obs_value[None], obs_var[None]
    return pl.pallas_call(
        observe_kernel,
        in_specs=[pl.BlockSpec(memory_space=pltpu.SMEM)]
        + [pl.BlockSpec(memory_space=pltpu.HBM)] * len(arrays),
        out_specs=[pl.BlockSpec(memory_space=pltpu.VMEM)] * 4,
        out_shape=[like, payload, payload, part],
        scratch_shapes=[
            pltpu.VMEM((lon_dev, lat, members), state.dtype),
            pltpu.VMEM((1, nobs), jnp.int32),
            pltpu.VMEM((1, nobs), jnp.float32),
            pltpu.VMEM((1, nobs), jnp.float32),
            pltpu.SemaphoreType.DMA((6,)),
        ],
        compiler_params=pltpu.CompilerParams(vmem_limit_bytes=16 * 2**20),
        name="observe",
    )(odd, *[pltpu.with_memory_space_constraint(x, pltpu.HBM) for x in arrays])


def slab_of(ref, lat, at):
    size = PAIR * TILE
    planes = ref.shape[0] // lat
    rows = [ref[i * lat + at * size : i * lat + (at + 1) * size, :] for i in range(planes)]
    return jnp.stack(rows).astype(jnp.float32)


def pair_tiles(load, step, steps):
    here = load(step)
    none = jnp.zeros_like(here[:, :TILE])
    before = load(step - 1)[:, TILE:] if step else none
    after = load(step + 1)[:, :TILE] if step + 1 < steps else none
    return before, here[:, :TILE], here[:, TILE:], after


def halo_weights(to_left):
    steps = [jnp.float32(1.0) - jnp.float32(d) / jnp.float32(HALO + 1) for d in range(HALO, 0, -1)]
    return [jnp.where(to_left, x, y) for x, y in zip(steps, steps[::-1])]


def turn(tile):
    return tile.reshape(-1, tile.shape[-1]).astype(jnp.bfloat16).T


def gram_of(tiles, turned, weights):
    planes, _, members = tiles[0].shape
    depth = planes * TILE
    row = lax.broadcasted_iota(jnp.int32, (TILE, members), 0)
    upper = row < HALO
    rowf = row.astype(jnp.float32)
    edge = line_weight(jnp.where(upper, rowf + (HALO + REGION), rowf - HALO))
    lane = lax.broadcasted_iota(jnp.int32, (1, depth), 1) & (TILE - 1)
    take_next = jnp.where(lane < HALO, 1.0, 0.0).astype(jnp.bfloat16)
    take_prev = jnp.where(lane < HALO, 0.0, 1.0).astype(jnp.bfloat16)
    grams = []
    for at in (1, 2):
        margin = jnp.where(upper, tiles[at + 1], tiles[at - 1])
        main_rows, margin_rows = [], []
        for plane, weight in enumerate(weights):
            own = tiles[at][plane]
            main_rows.append(own if weight is None else own * weight)
            margin_rows.append(margin[plane] * (edge if weight is None else edge * weight))
        weighted = jnp.stack(main_rows + margin_rows)
        weighted = weighted.reshape(2 * depth, members).astype(jnp.bfloat16)
        margin = turned[at + 1] * take_next + turned[at - 1] * take_prev
        both = jnp.concatenate([turned[at], margin], axis=1)
        grams.append(jnp.dot(both, weighted, preferred_element_type=jnp.float32))
    return grams


def slab_copies(src_ref, dst_ref, sems, only=None):
    size = PAIR * TILE

    def slab(at):
        rows = pl.ds(pl.multiple_of(at * size, size), size)
        return pltpu.make_async_copy(
            src_ref.at[:, :, rows, :], dst_ref.at[:, :, rows, :], sems.at[at]
        )

    return slab(only) if only is not None else [slab(i) for i in range(src_ref.shape[2] // size)]


def own_gram_kernel(odd_ref, state_hbm_ref, near_ref, own_ref, *refs):
    first_ref, last_hbm_ref, like_ref, state_ref, last_ref, sems, last_sem = refs
    lon_dev, nvar, lat, members = state_ref.shape
    kept = first_ref.shape[0]
    steps = lat // (PAIR * TILE)
    copies = slab_copies(state_hbm_ref, state_ref, sems)
    for copy in copies:
        copy.start()
    like_ref[...] = own_ref[...] + like_rows(near_ref[near_ref.shape[0] - 4 * TILE :, :])
    size = PAIR * TILE

    def load(step):
        own = state_ref[:, :, step * size : (step + 1) * size, :].astype(jnp.float32)
        own = own.reshape(lon_dev * nvar, size, members)
        return jnp.concatenate([own, slab_of(near_ref, lat, step)], axis=0)

    weights = [None] * (lon_dev * nvar)
    weights += [w for w in halo_weights(odd_ref[0] == 1) for _ in range(nvar)]
    for copy in copies:
        copy.wait()
    slabs = [load(step) for step in range(steps)]

    def put(region, gram):
        if region < kept:
            first_ref[region] = gram
        else:
            last_ref[region - kept] = gram

    add_grams(slabs, weights, put)
    keep = pltpu.make_async_copy(last_ref, last_hbm_ref, last_sem)
    keep.start()
    keep.wait()


def add_grams(slabs, weights, put):
    none = jnp.zeros_like(slabs[0][:, :TILE])
    tiles = [none]
    for slab in slabs:
        tiles += [slab[:, :TILE], slab[:, TILE:]]
    tiles.append(none)
    turned = [turn(tile) for tile in tiles[1:-1]]
    turned = [jnp.zeros_like(turned[0])] + turned + [jnp.zeros_like(turned[0])]
    for pair in range(len(slabs)):
        window = slice(pair * PAIR, pair * PAIR + PAIR + 2)
        grams = gram_of(tiles[window], turned[window], weights)
        for at, gram in enumerate(grams):
            put(pair * PAIR + at, gram)


def own_gram(odd, state, near, own):
    _, _, lat, members = state.shape
    kept = lat // REGION - PAIR
    vmem = pl.BlockSpec(memory_space=pltpu.VMEM)
    return pl.pallas_call(
        own_gram_kernel,
        in_specs=[
            pl.BlockSpec(memory_space=pltpu.SMEM),
            pl.BlockSpec(memory_space=pltpu.HBM),
            vmem,
            vmem,
        ],
        out_specs=[vmem, pl.BlockSpec(memory_space=pltpu.HBM), vmem],
        out_shape=[
            jax.ShapeDtypeStruct((kept, members, members), jnp.float32),
            pltpu.HBM((PAIR, members, members), jnp.float32),
            jax.ShapeDtypeStruct(own.shape, jnp.float32),
        ],
        scratch_shapes=[
            pltpu.VMEM(state.shape, state.dtype),
            pltpu.VMEM((PAIR, members, members), jnp.float32),
            pltpu.SemaphoreType.DMA((lat // (PAIR * TILE),)),
            pltpu.SemaphoreType.DMA,
        ],
        compiler_params=pltpu.CompilerParams(vmem_limit_bytes=24 * 2**20),
        name="own_gram",
    )(odd, pltpu.with_memory_space_constraint(state, pltpu.HBM), near, own)


def halves(ref, region, rows):
    members = ref.shape[-1]
    return [ref[region, rows, at : at + 128] for at in range(0, members, 128)]


def diagonal(gram_ref, region):
    members = gram_ref.shape[-1]
    across = [None] * (members // 128)
    down = []
    for start in range(0, members, ROWS):
        lane = start // 128
        gram = gram_ref[region, pl.ds(start, ROWS), lane * 128 : lane * 128 + 128]
        i = lax.broadcasted_iota(jnp.int32, gram.shape, 0) + start
        j = lax.broadcasted_iota(jnp.int32, gram.shape, 1) + lane * 128
        kept = jnp.where(i == j, gram, 0.0)
        down.append(jnp.broadcast_to(jnp.sum(kept, axis=1, keepdims=True), gram.shape))
        part = jnp.sum(kept.reshape(ROWS // TILE, TILE, 128), axis=0)
        across[lane] = part if across[lane] is None else across[lane] + part
    return [jnp.sum(x, axis=0, keepdims=True) for x in across], down


def kernel_matrices(regions, gram_ref, kernel_ref, mass_ref, scale):
    members = gram_ref.shape[-1]
    for region in regions:
        across, down = diagonal(gram_ref, region)
        across = [0.5 * LIFT - x * scale for x in across]
        masses = [0.0 for _ in across]
        for i, start in enumerate(range(0, members, ROWS)):
            rows = pl.ds(start, ROWS)
            base = 0.5 * LIFT - down[i] * scale
            for lane, (gram, x) in enumerate(zip(halves(gram_ref, region, rows), across)):
                part = jnp.exp2(gram * (2.0 * scale) + base + x)
                kernel_ref[region, rows, lane * 128 : lane * 128 + 128] = part
                part = jnp.sum(part.reshape(ROWS // TILE, TILE, 128), axis=0)
                masses[lane] = masses[lane] + part
        masses = [jnp.sum(x, axis=0, keepdims=True) for x in masses]
        mass_ref[region] = jnp.concatenate(masses, axis=1)


def transports_scaled(kernel_ref, weights, mass_ref, use):
    regions = range(kernel_ref.shape[0])
    members = kernel_ref.shape[-1]
    starts = range(0, members, ROWS)
    lanes = range(members // 128)
    share = 2.0**MASS / members

    def lane_parts(row):
        return [row[:, lane * 128 : lane * 128 + 128] for lane in lanes]

    def settle(totals, region):
        return [w / x for w, x in zip(lane_parts(weights[region : region + 1]), totals)]

    def masses_of(region, rows, factor):
        parts = [k * f for k, f in zip(halves(kernel_ref, region, rows), factor)]
        mass = jnp.sum(fold(parts, jnp.add), axis=1, keepdims=True)
        mass = jnp.broadcast_to(mass, (ROWS, 128))
        return parts, mass, pl.reciprocal(mass, approx=True)

    def sweep(least_i, least_j, factors):
        next_i, next_j, next_factors = [], [], []
        for region, low_i, low_j, factor in zip(regions, least_i, least_j, factors):
            totals = [None for _ in lanes]
            for start in starts:
                rows = pl.ds(start, ROWS)
                _, mass, ratio = masses_of(region, rows, factor)
                low_j = jnp.minimum(low_j, mass)
                for lane, kernel in enumerate(halves(kernel_ref, region, rows)):
                    part = jnp.sum((kernel * ratio).reshape(ROWS // TILE, TILE, 128), axis=0)
                    totals[lane] = part if totals[lane] is None else totals[lane] + part
            totals = [jnp.sum(x, axis=0, keepdims=True) * share for x in totals]
            next_i.append(jnp.minimum(low_i, fold(totals, jnp.minimum)))
            next_j.append(low_j)
            next_factors.append(settle(totals, region))
        return next_i, next_j, next_factors

    masses = [lane_parts(mass_ref[region]) for region in regions]
    most = fold([fold(x, jnp.maximum) for x in masses], jnp.maximum)
    totals = [[x * 2.0**START for x in mass] for mass in masses]
    least_i = [fold(x, jnp.minimum) for x in totals]
    least_j = [jnp.full((ROWS, 128), 1e30, jnp.float32) for _ in regions]
    factors = [settle(x, region) for x, region in zip(totals, regions)]
    for _ in range(SWEEPS - 1):
        least_i, least_j, factors = sweep(least_i, least_j, factors)
    moves, last_j = [], []
    for region, low_j, factor in zip(regions, least_j, factors):
        blocks = []
        for start in starts:
            parts, mass, ratio = masses_of(region, pl.ds(start, ROWS), factor)
            low_j = jnp.minimum(low_j, mass)
            blocks.append(jnp.concatenate([x * ratio for x in parts], axis=1).astype(jnp.bfloat16))
        moves.append(jnp.concatenate(blocks, axis=0))
        last_j.append(low_j)
        if len(moves) == PAIR:
            use(region // PAIR, moves)
            moves = []
    least_i = fold(least_i, jnp.minimum)
    return jnp.min(least_i), jnp.min(fold(last_j, jnp.minimum)), jnp.max(most)


def transport_logs(gram, logw, scale):
    members = gram.shape[-1]
    j = lax.broadcasted_iota(jnp.int32, gram.shape, 0)
    i = lax.broadcasted_iota(jnp.int32, gram.shape, 1)
    kept = jnp.where(i == j, gram, 0.0)
    down = jnp.sum(kept, axis=1, keepdims=True)
    across = jnp.sum(kept, axis=0, keepdims=True)
    cost = (down + across - 2.0 * gram) * scale
    pot_g = jnp.zeros((members, 1), jnp.float32)
    for sweep in range(SWEEPS):
        term = pot_g - cost
        top = jnp.max(term, axis=0, keepdims=True)
        pot_f = logw - top - jnp.log(jnp.sum(jnp.exp2(term - top), axis=0, keepdims=True)) * LOG2E
        term = pot_f - cost
        top = jnp.max(term, axis=1, keepdims=True)
        pot_g = -math.log2(members) - top
        pot_g = pot_g - jnp.log(jnp.sum(jnp.exp2(term - top), axis=1, keepdims=True)) * LOG2E
    return (members * jnp.exp2(pot_f + pot_g - cost)).astype(jnp.bfloat16)


def transform(state_ref, pair, moves):
    lon_dev, nvar, _, members = state_ref.shape
    size = PAIR * TILE
    own = state_ref[:, :, pair * size : (pair + 1) * size, :].astype(jnp.float32)
    parts = []
    for region, move in enumerate(moves):
        cells = own[:, :, region * TILE : (region + 1) * TILE].astype(jnp.bfloat16)
        cells = cells.reshape(lon_dev * nvar * TILE, members)
        moved = lax.dot_general(
            cells, move, (((1,), (1,)), ((), ())), preferred_element_type=jnp.float32
        )
        parts.append(moved.reshape(lon_dev, nvar, TILE, members))
    return jnp.concatenate(parts, axis=2).astype(jnp.bfloat16)


def analyse_kernel(count, scale, *refs):
    odd_ref, halo_ref, first_ref, last_hbm_ref, state_hbm_ref, like_ref, sums_ref = refs[:7]
    out_ref, gram_ref, kernel_ref, mass_ref, result_ref, state_ref, last_ref = refs[7:14]
    out_sems, state_sems, last_sem = refs[14:]
    kept = first_ref.shape[0]
    fetch_last = pltpu.make_async_copy(last_hbm_ref, last_ref, last_sem)
    fetch_last.start()
    regions, members, _ = gram_ref.shape
    pairs = regions // PAIR
    size = PAIR * TILE
    lat = regions * REGION
    fetches = slab_copies(state_hbm_ref, state_ref, state_sems)
    for copy in fetches:
        copy.start()

    def send(pair):
        rows = pl.ds(pair * size, size)
        return pltpu.make_async_copy(
            result_ref.at[pair], out_ref.at[:, :, rows, :], out_sems.at[pair]
        )

    misfit = like_ref[...] + like_rows(halo_ref[halo_ref.shape[0] - 4 * TILE :, :])
    misfit = misfit - jnp.min(misfit, axis=1, keepdims=True)
    factor = (-0.5 * LOG2E * count) / jnp.sum(sums_ref[...], axis=0, keepdims=True)
    like = misfit * jnp.concatenate([factor] * (members // 128), axis=1)
    weights = jnp.exp2(like + MASS)
    norm = jnp.sum(weights, axis=1, keepdims=True) * 2.0**-MASS
    weights = weights / norm

    planes = halo_ref.shape[0] // lat
    halo = [w for w in halo_weights(odd_ref[0] == 0) for _ in range(planes // HALO)]
    slabs = [slab_of(halo_ref, lat, at) for at in range(lat // size)]

    def put(region, gram):
        if region < kept:
            gram_ref[region] = first_ref[region] + gram
        else:
            if region == kept:
                kernel_matrices(range(kept), gram_ref, kernel_ref, mass_ref, scale)
                fetch_last.wait()
            gram_ref[region] = last_ref[region - kept] + gram

    add_grams(slabs, halo, put)
    kernel_matrices(range(kept, regions), gram_ref, kernel_ref, mass_ref, scale)

    def use(pair, moves):
        fetches[pair].wait()
        result_ref[pair] = transform(state_ref, pair, moves)
        send(pair).start()

    row, col, most = transports_scaled(kernel_ref, weights, mass_ref, use)
    sound = (row >= 2.0**-24) & (col >= 2.0**-30) & (most <= 2.0**30) & (row * col >= 2.0**-34)
    for pair in range(pairs):
        send(pair).wait()

    @pl.when(jnp.logical_not(sound))
    def _():
        logw = like - jnp.log(norm) * LOG2E
        for pair in range(pairs):
            again = [
                transport_logs(gram_ref[region], logw[region : region + 1], scale)
                for region in range(pair * PAIR, (pair + 1) * PAIR)
            ]
            result_ref[pair] = transform(state_ref, pair, again)
            send(pair).start()
            send(pair).wait()


def analyse(odd, halo, first, last, state, like, sums, count, scale):
    lon_dev, nvar, lat, members = state.shape
    regions = lat // REGION
    pairs = regions // PAIR
    vmem = pl.BlockSpec(memory_space=pltpu.VMEM)
    return pl.pallas_call(
        functools.partial(analyse_kernel, count, scale),
        in_specs=[
            pl.BlockSpec(memory_space=pltpu.SMEM),
            vmem,
            vmem,
            pl.BlockSpec(memory_space=pltpu.HBM),
            pl.BlockSpec(memory_space=pltpu.HBM),
            vmem,
            vmem,
        ],
        out_specs=pl.BlockSpec(memory_space=pl.ANY),
        out_shape=jax.ShapeDtypeStruct(state.shape, state.dtype),
        scratch_shapes=[
            pltpu.VMEM((regions, members, members), jnp.float32),
            pltpu.VMEM((regions, members, members), jnp.float32),
            pltpu.VMEM((regions, 1, members), jnp.float32),
            pltpu.VMEM((pairs, lon_dev, nvar, PAIR * TILE, members), state.dtype),
            pltpu.VMEM(state.shape, state.dtype),
            pltpu.VMEM(last.shape, jnp.float32),
            pltpu.SemaphoreType.DMA((pairs,)),
            pltpu.SemaphoreType.DMA((pairs,)),
            pltpu.SemaphoreType.DMA,
        ],
        compiler_params=pltpu.CompilerParams(vmem_limit_bytes=24 * 2**20),
        name="analyse",
    )(
        odd,
        halo,
        first,
        *[pltpu.with_memory_space_constraint(x, pltpu.HBM) for x in (last, state)],
        like,
        sums,
    )


def on_device(state, obs_index, obs_value, obs_var):
    nvar = state.shape[1]
    count = lax.axis_size("lon")
    odd = (lax.axis_index("lon") & 1).astype(jnp.int32).reshape(1)
    near_pairs = [(i, i ^ 1) for i in range(count)]
    far_pairs = [(i, (i + 1 if i % 2 else i - 1) % count) for i in range(count)]
    own_like, for_near, for_far, part = observe(odd, state, obs_index, obs_value, obs_var)
    far = lax.ppermute(for_far, "lon", far_pairs)
    near = lax.ppermute(for_near, "lon", near_pairs)
    start = near.shape[0] - TILE
    part = part[0] + jnp.sum(near[start : start + 3, :128].astype(jnp.float32), axis=0)
    sums = lax.all_to_all(
        jnp.broadcast_to(part, (count // 2, 128)),
        "lon",
        0,
        0,
        axis_index_groups=[[i for i in range(count) if (i ^ i >> 1) & 1 == kind] for kind in range(2)],
        tiled=True,
    )
    offsets = range(REGION + 2 * HALO)
    line = [1.0 - max(0, HALO - p, p - (HALO + REGION - 1)) / (HALO + 1) for p in offsets]
    scale = LOG2E / EPS / (nvar * sum(line) ** 2)
    first, last, like = own_gram(odd, state, near, own_like)
    nobs = float(obs_index.shape[0] * count)
    return analyse(odd, far, first, last, state, like, sums, nobs, scale)


def solution(mesh):
    return jax.shard_map(
        on_device,
        mesh=mesh,
        in_specs=(
            P(("ens", "lon"), None, None, None),
            P(("ens", "lon")),
            P(("ens", "lon")),
            P(("ens", "lon")),
        ),
        out_specs=P(("ens", "lon"), None, None, None),
        check_vma=False,
    )
```

```python
import functools
import math

import jax
import jax.numpy as jnp
from jax import lax
from jax.experimental import pallas as pl
from jax.experimental.pallas import tpu as pltpu
from jax.sharding import PartitionSpec as P

REGION = 8
HALO = 4
SWEEPS = 4
EPS = 0.05
TILE = 8
PAIR = 2
LOG2E = 1.4426950408889634
ROWS = 32
LIFT, START, MASS = 20, -10, 60


def fold(values, op):
    out = values[0]
    for value in values[1:]:
        out = op(out, value)
    return out


def line_weight(place):
    dist = jnp.maximum(0.0, jnp.maximum(HALO - place, place - (HALO + REGION - 1)))
    inside = (place >= 0) & (place < REGION + 2 * HALO)
    return jnp.where(inside, 1.0 - dist / (HALO + 1), 0.0)


def like_rows(rows):
    rows = rows.astype(jnp.float32)
    return rows[:TILE] + rows[TILE : 2 * TILE] + rows[2 * TILE : 3 * TILE]


def in_parts(values, extra):
    below = lax.broadcasted_iota(jnp.int32, values.shape, 0)
    extra_high = extra.astype(jnp.bfloat16).astype(jnp.float32)
    extra_middle = (extra - extra_high).astype(jnp.bfloat16).astype(jnp.float32)
    extra_low = extra - extra_high - extra_middle
    last = jnp.where(below == 0, extra_high, jnp.where(below == 1, extra_middle, extra_low))
    last = jnp.where(below < 3, last, 0.0)
    high = values.astype(jnp.bfloat16).astype(jnp.float32)
    middle = (values - high).astype(jnp.bfloat16).astype(jnp.float32)
    low = values - high - middle
    return jnp.concatenate([high, middle, low, last], axis=0).astype(jnp.bfloat16)


def steps_inside(place):
    dist = jnp.maximum(0.0, jnp.maximum(HALO - place, place - (HALO + REGION - 1)))
    inside = (place >= 0) & (place < REGION + 2 * HALO)
    return jnp.where(inside, HALO + 1 - dist, 0.0)


def observe_kernel(*refs):
    odd_ref, state_ref, rows_ref = refs[:3]
    own_ref, near_ref, far_ref, part_ref = refs[6:10]
    cells_ref, index_ref, value_ref, var_ref, sems = refs[10:]
    lon_dev, lat, members = cells_ref.shape
    nobs = index_ref.shape[1]
    edge = rows_ref.shape[0] // lon_dev * HALO
    last = rows_ref.shape[0] - edge
    far_at = pl.multiple_of(odd_ref[0] * last, 16)
    near_at = pl.multiple_of(last - far_at, 16)
    fetches = [
        (refs[3], index_ref),
        (refs[4], value_ref),
        (refs[5], var_ref),
        (state_ref.at[:, 0], cells_ref),
        (rows_ref.at[pl.ds(far_at, edge), :], far_ref.at[pl.ds(0, edge), :]),
        (rows_ref.at[pl.ds(near_at, edge), :], near_ref.at[pl.ds(0, edge), :]),
    ]
    copies = [
        pltpu.make_async_copy(src, dst, sems.at[i]) for i, (src, dst) in enumerate(fetches)
    ]
    for copy in copies:
        copy.start()
    for copy in copies[:3]:
        copy.wait()
    index = index_ref[...]
    sub = lax.broadcasted_iota(jnp.int32, (TILE, nobs), 0)
    table = jnp.where(
        sub == 0,
        index.astype(jnp.float32),
        jnp.where(sub == 1, value_ref[...], var_ref[...]),
    ).T
    index_col = table[:, 0:1].astype(jnp.int32)
    value = table[:, 1:2]
    var = table[:, 2:3]
    pick = index_col == lax.broadcasted_iota(jnp.int32, (nobs, lon_dev * lat), 1)
    pick = jnp.where(pick, 1.0, 0.0).astype(jnp.bfloat16)
    lon = (index // lat).astype(jnp.float32)
    along = index.astype(jnp.float32) - lon * lat
    blocks = own_ref.shape[0]
    block = lax.broadcasted_iota(jnp.int32, (blocks, nobs), 0).astype(jnp.float32)
    across = steps_inside(along - REGION * block + HALO)
    side = jnp.where(odd_ref[0] == 1, float(REGION), float(-REGION))
    weights = [steps_inside(lon + (HALO + shift)) * across for shift in (0.0, side, -side)]
    weights = jnp.concatenate(weights, axis=0).astype(jnp.bfloat16)
    inverse = 1.0 / var
    copies[3].wait()
    rows = cells_ref[...].reshape(lon_dev * lat, members)
    seen = jnp.dot(pick, rows, preferred_element_type=jnp.float32)
    terms = (value - seen) ** 2 * inverse
    high = terms.astype(jnp.bfloat16)
    rest = terms - high.astype(jnp.float32)
    middle = rest.astype(jnp.bfloat16)
    low = (rest - middle.astype(jnp.float32)).astype(jnp.bfloat16)
    sums = [jnp.dot(weights, x, preferred_element_type=jnp.float32) for x in (low, middle, high)]
    like = fold(sums, jnp.add) * (1.0 / (HALO + 1) ** 2)
    centre = jnp.sum(seen, axis=1, keepdims=True) * (1.0 / members)
    spread = jnp.sum((seen - centre) ** 2, axis=1, keepdims=True) * (1.0 / (members - 1))
    innovation = (value - centre) ** 2 / (var + spread)
    part = jnp.sum(innovation, axis=0, keepdims=True)
    part_ref[...] = jnp.broadcast_to(part, part_ref.shape)
    own_ref[...] = like[:blocks]
    near_ref[edge:, :] = in_parts(like[blocks : 2 * blocks], part)
    far_ref[edge:, :] = in_parts(like[2 * blocks :], jnp.zeros_like(part))
    for copy in copies[4:]:
        copy.wait()


def observe(odd, state, obs_index, obs_value, obs_var):
    lon_dev, nvar, lat, members = state.shape
    nobs = obs_index.size
    assert lat // REGION == TILE
    like = jax.ShapeDtypeStruct((lat // REGION, members), jnp.float32)
    payload = pltpu.VMEM((HALO * nvar * lat + 4 * TILE, members), state.dtype)
    part = jax.ShapeDtypeStruct((TILE, 128), jnp.float32)
    arrays = state, state.reshape(-1, members), obs_index[None], obs_value[None], obs_var[None]
    return pl.pallas_call(
        observe_kernel,
        in_specs=[pl.BlockSpec(memory_space=pltpu.SMEM)]
        + [pl.BlockSpec(memory_space=pltpu.HBM)] * len(arrays),
        out_specs=[pl.BlockSpec(memory_space=pltpu.VMEM)] * 4,
        out_shape=[like, payload, payload, part],
        scratch_shapes=[
            pltpu.VMEM((lon_dev, lat, members), state.dtype),
            pltpu.VMEM((1, nobs), jnp.int32),
            pltpu.VMEM((1, nobs), jnp.float32),
            pltpu.VMEM((1, nobs), jnp.float32),
            pltpu.SemaphoreType.DMA((6,)),
        ],
        compiler_params=pltpu.CompilerParams(vmem_limit_bytes=16 * 2**20),
        name="observe",
    )(odd, *[pltpu.with_memory_space_constraint(x, pltpu.HBM) for x in arrays])


def slab_of(ref, lat, at):
    size = PAIR * TILE
    planes = ref.shape[0] // lat
    rows = [ref[i * lat + at * size : i * lat + (at + 1) * size, :] for i in range(planes)]
    return jnp.stack(rows).astype(jnp.float32)


def pair_tiles(load, step, steps):
    here = load(step)
    none = jnp.zeros_like(here[:, :TILE])
    before = load(step - 1)[:, TILE:] if step else none
    after = load(step + 1)[:, :TILE] if step + 1 < steps else none
    return before, here[:, :TILE], here[:, TILE:], after


def halo_weights(to_left):
    steps = [jnp.float32(1.0) - jnp.float32(d) / jnp.float32(HALO + 1) for d in range(HALO, 0, -1)]
    return [jnp.where(to_left, x, y) for x, y in zip(steps, steps[::-1])]


def turn(tile):
    return tile.reshape(-1, tile.shape[-1]).astype(jnp.bfloat16).T


def gram_of(tiles, turned, weights):
    planes, _, members = tiles[0].shape
    depth = planes * TILE
    row = lax.broadcasted_iota(jnp.int32, (TILE, members), 0)
    upper = row < HALO
    rowf = row.astype(jnp.float32)
    edge = line_weight(jnp.where(upper, rowf + (HALO + REGION), rowf - HALO))
    lane = lax.broadcasted_iota(jnp.int32, (1, depth), 1) & (TILE - 1)
    take_next = jnp.where(lane < HALO, 1.0, 0.0).astype(jnp.bfloat16)
    take_prev = jnp.where(lane < HALO, 0.0, 1.0).astype(jnp.bfloat16)
    grams = []
    for at in (1, 2):
        margin = jnp.where(upper, tiles[at + 1], tiles[at - 1])
        main_rows, margin_rows = [], []
        for plane, weight in enumerate(weights):
            own = tiles[at][plane]
            main_rows.append(own if weight is None else own * weight)
            margin_rows.append(margin[plane] * (edge if weight is None else edge * weight))
        weighted = jnp.stack(main_rows + margin_rows)
        weighted = weighted.reshape(2 * depth, members).astype(jnp.bfloat16)
        margin = turned[at + 1] * take_next + turned[at - 1] * take_prev
        both = jnp.concatenate([turned[at], margin], axis=1)
        grams.append(jnp.dot(both, weighted, preferred_element_type=jnp.float32))
    return grams


def slab_copies(src_ref, dst_ref, sems, only=None):
    size = PAIR * TILE

    def slab(at):
        rows = pl.ds(pl.multiple_of(at * size, size), size)
        return pltpu.make_async_copy(
            src_ref.at[:, :, rows, :], dst_ref.at[:, :, rows, :], sems.at[at]
        )

    return slab(only) if only is not None else [slab(i) for i in range(src_ref.shape[2] // size)]


def own_gram_kernel(odd_ref, state_hbm_ref, near_ref, own_ref, *refs):
    first_ref, last_hbm_ref, like_ref, state_ref, last_ref, sems, last_sem = refs
    lon_dev, nvar, lat, members = state_ref.shape
    kept = first_ref.shape[0]
    steps = lat // (PAIR * TILE)
    copies = slab_copies(state_hbm_ref, state_ref, sems)
    for copy in copies:
        copy.start()
    like_ref[...] = own_ref[...] + like_rows(near_ref[near_ref.shape[0] - 4 * TILE :, :])
    size = PAIR * TILE

    def load(step):
        own = state_ref[:, :, step * size : (step + 1) * size, :].astype(jnp.float32)
        own = own.reshape(lon_dev * nvar, size, members)
        return jnp.concatenate([own, slab_of(near_ref, lat, step)], axis=0)

    weights = [None] * (lon_dev * nvar)
    weights += [w for w in halo_weights(odd_ref[0] == 1) for _ in range(nvar)]
    for copy in copies:
        copy.wait()
    slabs = [load(step) for step in range(steps)]

    def put(region, gram):
        if region < kept:
            first_ref[region] = gram
        else:
            last_ref[region - kept] = gram

    add_grams(slabs, weights, put)
    keep = pltpu.make_async_copy(last_ref, last_hbm_ref, last_sem)
    keep.start()
    keep.wait()


def add_grams(slabs, weights, put):
    none = jnp.zeros_like(slabs[0][:, :TILE])
    tiles = [none]
    for slab in slabs:
        tiles += [slab[:, :TILE], slab[:, TILE:]]
    tiles.append(none)
    turned = [turn(tile) for tile in tiles[1:-1]]
    turned = [jnp.zeros_like(turned[0])] + turned + [jnp.zeros_like(turned[0])]
    for pair in range(len(slabs)):
        window = slice(pair * PAIR, pair * PAIR + PAIR + 2)
        grams = gram_of(tiles[window], turned[window], weights)
        for at, gram in enumerate(grams):
            put(pair * PAIR + at, gram)


def own_gram(odd, state, near, own):
    _, _, lat, members = state.shape
    kept = lat // REGION - PAIR
    vmem = pl.BlockSpec(memory_space=pltpu.VMEM)
    return pl.pallas_call(
        own_gram_kernel,
        in_specs=[
            pl.BlockSpec(memory_space=pltpu.SMEM),
            pl.BlockSpec(memory_space=pltpu.HBM),
            vmem,
            vmem,
        ],
        out_specs=[vmem, pl.BlockSpec(memory_space=pltpu.HBM), vmem],
        out_shape=[
            jax.ShapeDtypeStruct((kept, members, members), jnp.float32),
            pltpu.HBM((PAIR, members, members), jnp.float32),
            jax.ShapeDtypeStruct(own.shape, jnp.float32),
        ],
        scratch_shapes=[
            pltpu.VMEM(state.shape, state.dtype),
            pltpu.VMEM((PAIR, members, members), jnp.float32),
            pltpu.SemaphoreType.DMA((lat // (PAIR * TILE),)),
            pltpu.SemaphoreType.DMA,
        ],
        compiler_params=pltpu.CompilerParams(vmem_limit_bytes=24 * 2**20),
        name="own_gram",
    )(odd, pltpu.with_memory_space_constraint(state, pltpu.HBM), near, own)


def halves(ref, region, rows):
    members = ref.shape[-1]
    return [ref[region, rows, at : at + 128] for at in range(0, members, 128)]


def diagonal(gram_ref, region):
    members = gram_ref.shape[-1]
    across = [None] * (members // 128)
    down = []
    for start in range(0, members, ROWS):
        lane = start // 128
        gram = gram_ref[region, pl.ds(start, ROWS), lane * 128 : lane * 128 + 128]
        i = lax.broadcasted_iota(jnp.int32, gram.shape, 0) + start
        j = lax.broadcasted_iota(jnp.int32, gram.shape, 1) + lane * 128
        kept = jnp.where(i == j, gram, 0.0)
        down.append(jnp.broadcast_to(jnp.sum(kept, axis=1, keepdims=True), gram.shape))
        part = jnp.sum(kept.reshape(ROWS // TILE, TILE, 128), axis=0)
        across[lane] = part if across[lane] is None else across[lane] + part
    return [jnp.sum(x, axis=0, keepdims=True) for x in across], down


def kernel_matrices(regions, gram_ref, kernel_ref, mass_ref, scale):
    members = gram_ref.shape[-1]
    for region in regions:
        across, down = diagonal(gram_ref, region)
        across = [0.5 * LIFT - x * scale for x in across]
        masses = [0.0 for _ in across]
        for i, start in enumerate(range(0, members, ROWS)):
            rows = pl.ds(start, ROWS)
            base = 0.5 * LIFT - down[i] * scale
            for lane, (gram, x) in enumerate(zip(halves(gram_ref, region, rows), across)):
                part = jnp.exp2(gram * (2.0 * scale) + base + x)
                kernel_ref[region, rows, lane * 128 : lane * 128 + 128] = part
                part = jnp.sum(part.reshape(ROWS // TILE, TILE, 128), axis=0)
                masses[lane] = masses[lane] + part
        masses = [jnp.sum(x, axis=0, keepdims=True) for x in masses]
        mass_ref[region] = jnp.concatenate(masses, axis=1)


def transports_scaled(kernel_ref, weights, mass_ref, use):
    regions = range(kernel_ref.shape[0])
    members = kernel_ref.shape[-1]
    starts = range(0, members, ROWS)
    lanes = range(members // 128)
    share = 2.0**MASS / members

    def lane_parts(row):
        return [row[:, lane * 128 : lane * 128 + 128] for lane in lanes]

    def settle(totals, region):
        return [w / x for w, x in zip(lane_parts(weights[region : region + 1]), totals)]

    def masses_of(region, rows, factor):
        parts = [k * f for k, f in zip(halves(kernel_ref, region, rows), factor)]
        mass = jnp.sum(fold(parts, jnp.add), axis=1, keepdims=True)
        mass = jnp.broadcast_to(mass, (ROWS, 128))
        return parts, mass, pl.reciprocal(mass, approx=True)

    def sweep(least_i, least_j, factors):
        next_i, next_j, next_factors = [], [], []
        for region, low_i, low_j, factor in zip(regions, least_i, least_j, factors):
            totals = [None for _ in lanes]
            for start in starts:
                rows = pl.ds(start, ROWS)
                _, mass, ratio = masses_of(region, rows, factor)
                low_j = jnp.minimum(low_j, mass)
                for lane, kernel in enumerate(halves(kernel_ref, region, rows)):
                    part = jnp.sum((kernel * ratio).reshape(ROWS // TILE, TILE, 128), axis=0)
                    totals[lane] = part if totals[lane] is None else totals[lane] + part
            totals = [jnp.sum(x, axis=0, keepdims=True) * share for x in totals]
            next_i.append(jnp.minimum(low_i, fold(totals, jnp.minimum)))
            next_j.append(low_j)
            next_factors.append(settle(totals, region))
        return next_i, next_j, next_factors

    masses = [lane_parts(mass_ref[region]) for region in regions]
    most = fold([fold(x, jnp.maximum) for x in masses], jnp.maximum)
    totals = [[x * 2.0**START for x in mass] for mass in masses]
    least_i = [fold(x, jnp.minimum) for x in totals]
    least_j = [jnp.full((ROWS, 128), 1e30, jnp.float32) for _ in regions]
    factors = [settle(x, region) for x, region in zip(totals, regions)]
    for _ in range(SWEEPS - 1):
        least_i, least_j, factors = sweep(least_i, least_j, factors)
    moves, last_j = [], []
    for region, low_j, factor in zip(regions, least_j, factors):
        blocks = []
        for start in starts:
            parts, mass, ratio = masses_of(region, pl.ds(start, ROWS), factor)
            low_j = jnp.minimum(low_j, mass)
            blocks.append(jnp.concatenate([x * ratio for x in parts], axis=1).astype(jnp.bfloat16))
        moves.append(jnp.concatenate(blocks, axis=0))
        last_j.append(low_j)
        if len(moves) == PAIR:
            use(region // PAIR, moves)
            moves = []
    least_i = fold(least_i, jnp.minimum)
    return jnp.min(least_i), jnp.min(fold(last_j, jnp.minimum)), jnp.max(most)


def transport_logs(gram, logw, scale):
    members = gram.shape[-1]
    j = lax.broadcasted_iota(jnp.int32, gram.shape, 0)
    i = lax.broadcasted_iota(jnp.int32, gram.shape, 1)
    kept = jnp.where(i == j, gram, 0.0)
    down = jnp.sum(kept, axis=1, keepdims=True)
    across = jnp.sum(kept, axis=0, keepdims=True)
    cost = (down + across - 2.0 * gram) * scale
    pot_g = jnp.zeros((members, 1), jnp.float32)
    for sweep in range(SWEEPS):
        term = pot_g - cost
        top = jnp.max(term, axis=0, keepdims=True)
        pot_f = logw - top - jnp.log(jnp.sum(jnp.exp2(term - top), axis=0, keepdims=True)) * LOG2E
        term = pot_f - cost
        top = jnp.max(term, axis=1, keepdims=True)
        pot_g = -math.log2(members) - top
        pot_g = pot_g - jnp.log(jnp.sum(jnp.exp2(term - top), axis=1, keepdims=True)) * LOG2E
    return (members * jnp.exp2(pot_f + pot_g - cost)).astype(jnp.bfloat16)


def transform(state_ref, pair, moves):
    lon_dev, nvar, _, members = state_ref.shape
    size = PAIR * TILE
    own = state_ref[:, :, pair * size : (pair + 1) * size, :].astype(jnp.float32)
    parts = []
    for region, move in enumerate(moves):
        cells = own[:, :, region * TILE : (region + 1) * TILE].astype(jnp.bfloat16)
        cells = cells.reshape(lon_dev * nvar * TILE, members)
        moved = lax.dot_general(
            cells, move, (((1,), (1,)), ((), ())), preferred_element_type=jnp.float32
        )
        parts.append(moved.reshape(lon_dev, nvar, TILE, members))
    return jnp.concatenate(parts, axis=2).astype(jnp.bfloat16)


def analyse_kernel(count, scale, *refs):
    odd_ref, halo_ref, first_ref, last_hbm_ref, state_hbm_ref, like_ref, sums_ref = refs[:7]
    out_ref, gram_ref, kernel_ref, mass_ref, result_ref, state_ref, last_ref = refs[7:14]
    out_sems, state_sems, last_sem = refs[14:]
    kept = first_ref.shape[0]
    fetch_last = pltpu.make_async_copy(last_hbm_ref, last_ref, last_sem)
    fetch_last.start()
    regions, members, _ = gram_ref.shape
    pairs = regions // PAIR
    size = PAIR * TILE
    lat = regions * REGION
    fetches = slab_copies(state_hbm_ref, state_ref, state_sems)
    for copy in fetches:
        copy.start()

    def send(pair):
        rows = pl.ds(pair * size, size)
        return pltpu.make_async_copy(
            result_ref.at[pair], out_ref.at[:, :, rows, :], out_sems.at[pair]
        )

    misfit = like_ref[...] + like_rows(halo_ref[halo_ref.shape[0] - 4 * TILE :, :])
    misfit = misfit - jnp.min(misfit, axis=1, keepdims=True)
    factor = (-0.5 * LOG2E * count) / jnp.sum(sums_ref[...], axis=0, keepdims=True)
    like = misfit * jnp.concatenate([factor] * (members // 128), axis=1)
    weights = jnp.exp2(like + MASS)
    norm = jnp.sum(weights, axis=1, keepdims=True) * 2.0**-MASS
    weights = weights / norm

    planes = halo_ref.shape[0] // lat
    halo = [w for w in halo_weights(odd_ref[0] == 0) for _ in range(planes // HALO)]
    slabs = [slab_of(halo_ref, lat, at) for at in range(lat // size)]

    def put(region, gram):
        if region < kept:
            gram_ref[region] = first_ref[region] + gram
        else:
            if region == kept:
                kernel_matrices(range(kept), gram_ref, kernel_ref, mass_ref, scale)
                fetch_last.wait()
                for copy in fetches:
                    copy.wait()
            gram_ref[region] = last_ref[region - kept] + gram

    add_grams(slabs, halo, put)
    kernel_matrices(range(kept, regions), gram_ref, kernel_ref, mass_ref, scale)

    def use(pair, moves):
        result_ref[pair] = transform(state_ref, pair, moves)
        send(pair).start()

    row, col, most = transports_scaled(kernel_ref, weights, mass_ref, use)
    sound = (row >= 2.0**-24) & (col >= 2.0**-30) & (most <= 2.0**30) & (row * col >= 2.0**-34)
    for pair in range(pairs):
        send(pair).wait()

    @pl.when(jnp.logical_not(sound))
    def _():
        logw = like - jnp.log(norm) * LOG2E
        for pair in range(pairs):
            again = [
                transport_logs(gram_ref[region], logw[region : region + 1], scale)
                for region in range(pair * PAIR, (pair + 1) * PAIR)
            ]
            result_ref[pair] = transform(state_ref, pair, again)
            send(pair).start()
            send(pair).wait()


def analyse(odd, halo, first, last, state, like, sums, count, scale):
    lon_dev, nvar, lat, members = state.shape
    regions = lat // REGION
    pairs = regions // PAIR
    vmem = pl.BlockSpec(memory_space=pltpu.VMEM)
    return pl.pallas_call(
        functools.partial(analyse_kernel, count, scale),
        in_specs=[
            pl.BlockSpec(memory_space=pltpu.SMEM),
            vmem,
            vmem,
            pl.BlockSpec(memory_space=pltpu.HBM),
            pl.BlockSpec(memory_space=pltpu.HBM),
            vmem,
            vmem,
        ],
        out_specs=pl.BlockSpec(memory_space=pl.ANY),
        out_shape=jax.ShapeDtypeStruct(state.shape, state.dtype),
        scratch_shapes=[
            pltpu.VMEM((regions, members, members), jnp.float32),
            pltpu.VMEM((regions, members, members), jnp.float32),
            pltpu.VMEM((regions, 1, members), jnp.float32),
            pltpu.VMEM((pairs, lon_dev, nvar, PAIR * TILE, members), state.dtype),
            pltpu.VMEM(state.shape, state.dtype),
            pltpu.VMEM(last.shape, jnp.float32),
            pltpu.SemaphoreType.DMA((pairs,)),
            pltpu.SemaphoreType.DMA((pairs,)),
            pltpu.SemaphoreType.DMA,
        ],
        compiler_params=pltpu.CompilerParams(vmem_limit_bytes=24 * 2**20),
        name="analyse",
    )(
        odd,
        halo,
        first,
        *[pltpu.with_memory_space_constraint(x, pltpu.HBM) for x in (last, state)],
        like,
        sums,
    )


def on_device(state, obs_index, obs_value, obs_var):
    nvar = state.shape[1]
    count = lax.axis_size("lon")
    odd = (lax.axis_index("lon") & 1).astype(jnp.int32).reshape(1)
    near_pairs = [(i, i ^ 1) for i in range(count)]
    far_pairs = [(i, (i + 1 if i % 2 else i - 1) % count) for i in range(count)]
    own_like, for_near, for_far, part = observe(odd, state, obs_index, obs_value, obs_var)
    far = lax.ppermute(for_far, "lon", far_pairs)
    near = lax.ppermute(for_near, "lon", near_pairs)
    start = near.shape[0] - TILE
    part = part[0] + jnp.sum(near[start : start + 3, :128].astype(jnp.float32), axis=0)
    sums = lax.all_to_all(
        jnp.broadcast_to(part, (count // 2, 128)),
        "lon",
        0,
        0,
        axis_index_groups=[[i for i in range(count) if (i ^ i >> 1) & 1 == kind] for kind in range(2)],
        tiled=True,
    )
    offsets = range(REGION + 2 * HALO)
    line = [1.0 - max(0, HALO - p, p - (HALO + REGION - 1)) / (HALO + 1) for p in offsets]
    scale = LOG2E / EPS / (nvar * sum(line) ** 2)
    first, last, like = own_gram(odd, state, near, own_like)
    nobs = float(obs_index.shape[0] * count)
    return analyse(odd, far, first, last, state, like, sums, nobs, scale)


def solution(mesh):
    return jax.shard_map(
        on_device,
        mesh=mesh,
        in_specs=(
            P(("ens", "lon"), None, None, None),
            P(("ens", "lon")),
            P(("ens", "lon")),
            P(("ens", "lon")),
        ),
        out_specs=P(("ens", "lon"), None, None, None),
        check_vma=False,
    )
```

```python
import functools
import math

import jax
import jax.numpy as jnp
from jax import lax
from jax.experimental import pallas as pl
from jax.experimental.pallas import tpu as pltpu
from jax.sharding import PartitionSpec as P

REGION = 8
HALO = 4
SWEEPS = 4
EPS = 0.05
TILE = 8
PAIR = 2
LOG2E = 1.4426950408889634
ROWS = 32
LIFT, START, MASS = 20, -10, 60


def fold(values, op):
    out = values[0]
    for value in values[1:]:
        out = op(out, value)
    return out


def line_weight(place):
    dist = jnp.maximum(0.0, jnp.maximum(HALO - place, place - (HALO + REGION - 1)))
    inside = (place >= 0) & (place < REGION + 2 * HALO)
    return jnp.where(inside, 1.0 - dist / (HALO + 1), 0.0)


def like_rows(rows):
    rows = rows.astype(jnp.float32)
    return rows[:TILE] + rows[TILE : 2 * TILE] + rows[2 * TILE : 3 * TILE]


def in_parts(values, extra):
    below = lax.broadcasted_iota(jnp.int32, values.shape, 0)
    extra_high = extra.astype(jnp.bfloat16).astype(jnp.float32)
    extra_middle = (extra - extra_high).astype(jnp.bfloat16).astype(jnp.float32)
    extra_low = extra - extra_high - extra_middle
    last = jnp.where(below == 0, extra_high, jnp.where(below == 1, extra_middle, extra_low))
    last = jnp.where(below < 3, last, 0.0)
    high = values.astype(jnp.bfloat16).astype(jnp.float32)
    middle = (values - high).astype(jnp.bfloat16).astype(jnp.float32)
    low = values - high - middle
    return jnp.concatenate([high, middle, low, last], axis=0).astype(jnp.bfloat16)


def steps_inside(place):
    dist = jnp.maximum(0.0, jnp.maximum(HALO - place, place - (HALO + REGION - 1)))
    inside = (place >= 0) & (place < REGION + 2 * HALO)
    return jnp.where(inside, HALO + 1 - dist, 0.0)


def observe_kernel(*refs):
    odd_ref, state_ref, rows_ref = refs[:3]
    own_ref, near_ref, far_ref, part_ref = refs[6:10]
    cells_ref, index_ref, value_ref, var_ref, sems = refs[10:]
    lon_dev, lat, members = cells_ref.shape
    nobs = index_ref.shape[1]
    edge = rows_ref.shape[0] // lon_dev * HALO
    last = rows_ref.shape[0] - edge
    far_at = pl.multiple_of(odd_ref[0] * last, 16)
    near_at = pl.multiple_of(last - far_at, 16)
    fetches = [
        (refs[3], index_ref),
        (refs[4], value_ref),
        (refs[5], var_ref),
        (state_ref.at[:, 0], cells_ref),
        (rows_ref.at[pl.ds(far_at, edge), :], far_ref.at[pl.ds(0, edge), :]),
        (rows_ref.at[pl.ds(near_at, edge), :], near_ref.at[pl.ds(0, edge), :]),
    ]
    copies = [
        pltpu.make_async_copy(src, dst, sems.at[i]) for i, (src, dst) in enumerate(fetches)
    ]
    for copy in copies:
        copy.start()
    for copy in copies[:3]:
        copy.wait()
    index = index_ref[...]
    sub = lax.broadcasted_iota(jnp.int32, (TILE, nobs), 0)
    table = jnp.where(
        sub == 0,
        index.astype(jnp.float32),
        jnp.where(sub == 1, value_ref[...], var_ref[...]),
    ).T
    index_col = table[:, 0:1].astype(jnp.int32)
    value = table[:, 1:2]
    var = table[:, 2:3]
    pick = index_col == lax.broadcasted_iota(jnp.int32, (nobs, lon_dev * lat), 1)
    pick = jnp.where(pick, 1.0, 0.0).astype(jnp.bfloat16)
    lon = (index // lat).astype(jnp.float32)
    along = index.astype(jnp.float32) - lon * lat
    blocks = own_ref.shape[0]
    block = lax.broadcasted_iota(jnp.int32, (blocks, nobs), 0).astype(jnp.float32)
    across = steps_inside(along - REGION * block + HALO)
    side = jnp.where(odd_ref[0] == 1, float(REGION), float(-REGION))
    weights = [steps_inside(lon + (HALO + shift)) * across for shift in (0.0, side, -side)]
    weights = jnp.concatenate(weights, axis=0).astype(jnp.bfloat16)
    inverse = 1.0 / var
    copies[3].wait()
    rows = cells_ref[...].reshape(lon_dev * lat, members)
    seen = jnp.dot(pick, rows, preferred_element_type=jnp.float32)
    terms = (value - seen) ** 2 * inverse
    high = terms.astype(jnp.bfloat16)
    rest = terms - high.astype(jnp.float32)
    middle = rest.astype(jnp.bfloat16)
    low = (rest - middle.astype(jnp.float32)).astype(jnp.bfloat16)
    sums = [jnp.dot(weights, x, preferred_element_type=jnp.float32) for x in (low, middle, high)]
    like = fold(sums, jnp.add) * (1.0 / (HALO + 1) ** 2)
    centre = jnp.sum(seen, axis=1, keepdims=True) * (1.0 / members)
    spread = jnp.sum((seen - centre) ** 2, axis=1, keepdims=True) * (1.0 / (members - 1))
    innovation = (value - centre) ** 2 / (var + spread)
    part = jnp.sum(innovation, axis=0, keepdims=True)
    part_ref[...] = jnp.broadcast_to(part, part_ref.shape)
    own_ref[...] = like[:blocks]
    near_ref[edge:, :] = in_parts(like[blocks : 2 * blocks], part)
    far_ref[edge:, :] = in_parts(like[2 * blocks :], jnp.zeros_like(part))
    for copy in copies[4:]:
        copy.wait()


def observe(odd, state, obs_index, obs_value, obs_var):
    lon_dev, nvar, lat, members = state.shape
    nobs = obs_index.size
    assert lat // REGION == TILE
    like = jax.ShapeDtypeStruct((lat // REGION, members), jnp.float32)
    payload = pltpu.VMEM((HALO * nvar * lat + 4 * TILE, members), state.dtype)
    part = jax.ShapeDtypeStruct((TILE, 128), jnp.float32)
    arrays = state, state.reshape(-1, members), obs_index[None], obs_value[None], obs_var[None]
    return pl.pallas_call(
        observe_kernel,
        in_specs=[pl.BlockSpec(memory_space=pltpu.SMEM)]
        + [pl.BlockSpec(memory_space=pltpu.HBM)] * len(arrays),
        out_specs=[pl.BlockSpec(memory_space=pltpu.VMEM)] * 4,
        out_shape=[like, payload, payload, part],
        scratch_shapes=[
            pltpu.VMEM((lon_dev, lat, members), state.dtype),
            pltpu.VMEM((1, nobs), jnp.int32),
            pltpu.VMEM((1, nobs), jnp.float32),
            pltpu.VMEM((1, nobs), jnp.float32),
            pltpu.SemaphoreType.DMA((6,)),
        ],
        compiler_params=pltpu.CompilerParams(vmem_limit_bytes=16 * 2**20),
        name="observe",
    )(odd, *[pltpu.with_memory_space_constraint(x, pltpu.HBM) for x in arrays])


def slab_of(ref, lat, at):
    size = PAIR * TILE
    planes = ref.shape[0] // lat
    rows = [ref[i * lat + at * size : i * lat + (at + 1) * size, :] for i in range(planes)]
    return jnp.stack(rows).astype(jnp.float32)


def pair_tiles(load, step, steps):
    here = load(step)
    none = jnp.zeros_like(here[:, :TILE])
    before = load(step - 1)[:, TILE:] if step else none
    after = load(step + 1)[:, :TILE] if step + 1 < steps else none
    return before, here[:, :TILE], here[:, TILE:], after


def halo_weights(to_left):
    steps = [jnp.float32(1.0) - jnp.float32(d) / jnp.float32(HALO + 1) for d in range(HALO, 0, -1)]
    return [jnp.where(to_left, x, y) for x, y in zip(steps, steps[::-1])]


def turn(tile):
    return tile.reshape(-1, tile.shape[-1]).astype(jnp.bfloat16).T


def gram_of(tiles, turned, weights):
    planes, _, members = tiles[0].shape
    depth = planes * TILE
    row = lax.broadcasted_iota(jnp.int32, (TILE, members), 0)
    upper = row < HALO
    rowf = row.astype(jnp.float32)
    edge = line_weight(jnp.where(upper, rowf + (HALO + REGION), rowf - HALO))
    lane = lax.broadcasted_iota(jnp.int32, (1, depth), 1) & (TILE - 1)
    take_next = jnp.where(lane < HALO, 1.0, 0.0).astype(jnp.bfloat16)
    take_prev = jnp.where(lane < HALO, 0.0, 1.0).astype(jnp.bfloat16)
    grams = []
    for at in (1, 2):
        margin = jnp.where(upper, tiles[at + 1], tiles[at - 1])
        main_rows, margin_rows = [], []
        for plane, weight in enumerate(weights):
            own = tiles[at][plane]
            main_rows.append(own if weight is None else own * weight)
            margin_rows.append(margin[plane] * (edge if weight is None else edge * weight))
        weighted = jnp.stack(main_rows + margin_rows)
        weighted = weighted.reshape(2 * depth, members).astype(jnp.bfloat16)
        margin = turned[at + 1] * take_next + turned[at - 1] * take_prev
        both = jnp.concatenate([turned[at], margin], axis=1)
        grams.append(jnp.dot(both, weighted, preferred_element_type=jnp.float32))
    return grams


def slab_copies(src_ref, dst_ref, sems, only=None):
    size = PAIR * TILE

    def slab(at):
        rows = pl.ds(pl.multiple_of(at * size, size), size)
        return pltpu.make_async_copy(
            src_ref.at[:, :, rows, :], dst_ref.at[:, :, rows, :], sems.at[at]
        )

    return slab(only) if only is not None else [slab(i) for i in range(src_ref.shape[2] // size)]


def own_gram_kernel(odd_ref, state_hbm_ref, near_ref, own_ref, *refs):
    first_ref, last_hbm_ref, like_ref, state_ref, last_ref, sems, last_sem = refs
    lon_dev, nvar, lat, members = state_ref.shape
    kept = first_ref.shape[0]
    steps = lat // (PAIR * TILE)
    copies = slab_copies(state_hbm_ref, state_ref, sems)
    for copy in copies:
        copy.start()
    like_ref[...] = own_ref[...] + like_rows(near_ref[near_ref.shape[0] - 4 * TILE :, :])
    size = PAIR * TILE

    def load(step):
        own = state_ref[:, :, step * size : (step + 1) * size, :].astype(jnp.float32)
        own = own.reshape(lon_dev * nvar, size, members)
        return jnp.concatenate([own, slab_of(near_ref, lat, step)], axis=0)

    weights = [None] * (lon_dev * nvar)
    weights += [w for w in halo_weights(odd_ref[0] == 1) for _ in range(nvar)]
    for copy in copies:
        copy.wait()
    slabs = [load(step) for step in range(steps)]

    def put(region, gram):
        if region < kept:
            first_ref[region] = gram
        else:
            last_ref[region - kept] = gram

    add_grams(slabs, weights, put)
    keep = pltpu.make_async_copy(last_ref, last_hbm_ref, last_sem)
    keep.start()
    keep.wait()


def add_grams(slabs, weights, put):
    none = jnp.zeros_like(slabs[0][:, :TILE])
    tiles = [none]
    for slab in slabs:
        tiles += [slab[:, :TILE], slab[:, TILE:]]
    tiles.append(none)
    turned = [turn(tile) for tile in tiles[1:-1]]
    turned = [jnp.zeros_like(turned[0])] + turned + [jnp.zeros_like(turned[0])]
    for pair in range(len(slabs)):
        window = slice(pair * PAIR, pair * PAIR + PAIR + 2)
        grams = gram_of(tiles[window], turned[window], weights)
        for at, gram in enumerate(grams):
            put(pair * PAIR + at, gram)


def own_gram(odd, state, near, own):
    _, _, lat, members = state.shape
    kept = lat // REGION - PAIR
    vmem = pl.BlockSpec(memory_space=pltpu.VMEM)
    return pl.pallas_call(
        own_gram_kernel,
        in_specs=[
            pl.BlockSpec(memory_space=pltpu.SMEM),
            pl.BlockSpec(memory_space=pltpu.HBM),
            vmem,
            vmem,
        ],
        out_specs=[vmem, pl.BlockSpec(memory_space=pltpu.HBM), vmem],
        out_shape=[
            jax.ShapeDtypeStruct((kept, members, members), jnp.float32),
            pltpu.HBM((PAIR, members, members), jnp.float32),
            jax.ShapeDtypeStruct(own.shape, jnp.float32),
        ],
        scratch_shapes=[
            pltpu.VMEM(state.shape, state.dtype),
            pltpu.VMEM((PAIR, members, members), jnp.float32),
            pltpu.SemaphoreType.DMA((lat // (PAIR * TILE),)),
            pltpu.SemaphoreType.DMA,
        ],
        compiler_params=pltpu.CompilerParams(vmem_limit_bytes=24 * 2**20),
        name="own_gram",
    )(odd, pltpu.with_memory_space_constraint(state, pltpu.HBM), near, own)


def halves(ref, region, rows):
    members = ref.shape[-1]
    return [ref[region, rows, at : at + 128] for at in range(0, members, 128)]


def diagonal(gram_ref, region):
    members = gram_ref.shape[-1]
    across = [None] * (members // 128)
    down = []
    for start in range(0, members, ROWS):
        lane = start // 128
        gram = gram_ref[region, pl.ds(start, ROWS), lane * 128 : lane * 128 + 128]
        i = lax.broadcasted_iota(jnp.int32, gram.shape, 0) + start
        j = lax.broadcasted_iota(jnp.int32, gram.shape, 1) + lane * 128
        kept = jnp.where(i == j, gram, 0.0)
        down.append(jnp.broadcast_to(jnp.sum(kept, axis=1, keepdims=True), gram.shape))
        part = jnp.sum(kept.reshape(ROWS // TILE, TILE, 128), axis=0)
        across[lane] = part if across[lane] is None else across[lane] + part
    return [jnp.sum(x, axis=0, keepdims=True) for x in across], down


def kernel_matrices(regions, gram_ref, kernel_ref, mass_ref, scale):
    members = gram_ref.shape[-1]
    for region in regions:
        across, down = diagonal(gram_ref, region)
        across = [0.5 * LIFT - x * scale for x in across]
        masses = [0.0 for _ in across]
        for i, start in enumerate(range(0, members, ROWS)):
            rows = pl.ds(start, ROWS)
            base = 0.5 * LIFT - down[i] * scale
            for lane, (gram, x) in enumerate(zip(halves(gram_ref, region, rows), across)):
                part = jnp.exp2(gram * (2.0 * scale) + base + x)
                kernel_ref[region, rows, lane * 128 : lane * 128 + 128] = part
                part = jnp.sum(part.reshape(ROWS // TILE, TILE, 128), axis=0)
                masses[lane] = masses[lane] + part
        masses = [jnp.sum(x, axis=0, keepdims=True) for x in masses]
        mass_ref[region] = jnp.concatenate(masses, axis=1)


def transports_scaled(kernel_ref, weights, mass_ref, use):
    regions = range(kernel_ref.shape[0])
    members = kernel_ref.shape[-1]
    starts = range(0, members, ROWS)
    lanes = range(members // 128)
    share = 2.0**MASS / members

    def lane_parts(row):
        return [row[:, lane * 128 : lane * 128 + 128] for lane in lanes]

    def settle(totals, region):
        return [w / x for w, x in zip(lane_parts(weights[region : region + 1]), totals)]

    def masses_of(region, rows, factor):
        parts = [k * f for k, f in zip(halves(kernel_ref, region, rows), factor)]
        mass = jnp.sum(fold(parts, jnp.add), axis=1, keepdims=True)
        mass = jnp.broadcast_to(mass, (ROWS, 128))
        return parts, mass, pl.reciprocal(mass, approx=True)

    def sweep(least_i, least_j, factors):
        next_i, next_j, next_factors = [], [], []
        for region, low_i, low_j, factor in zip(regions, least_i, least_j, factors):
            totals = [None for _ in lanes]
            for start in starts:
                rows = pl.ds(start, ROWS)
                _, mass, ratio = masses_of(region, rows, factor)
                low_j = jnp.minimum(low_j, mass)
                for lane, kernel in enumerate(halves(kernel_ref, region, rows)):
                    part = jnp.sum((kernel * ratio).reshape(ROWS // TILE, TILE, 128), axis=0)
                    totals[lane] = part if totals[lane] is None else totals[lane] + part
            totals = [jnp.sum(x, axis=0, keepdims=True) * share for x in totals]
            next_i.append(jnp.minimum(low_i, fold(totals, jnp.minimum)))
            next_j.append(low_j)
            next_factors.append(settle(totals, region))
        return next_i, next_j, next_factors

    masses = [lane_parts(mass_ref[region]) for region in regions]
    most = fold([fold(x, jnp.maximum) for x in masses], jnp.maximum)
    totals = [[x * 2.0**START for x in mass] for mass in masses]
    least_i = [fold(x, jnp.minimum) for x in totals]
    least_j = [jnp.full((ROWS, 128), 1e30, jnp.float32) for _ in regions]
    factors = [settle(x, region) for x, region in zip(totals, regions)]
    for _ in range(SWEEPS - 1):
        least_i, least_j, factors = sweep(least_i, least_j, factors)
    moves, last_j = [], []
    for region, low_j, factor in zip(regions, least_j, factors):
        blocks = []
        for start in starts:
            parts, mass, ratio = masses_of(region, pl.ds(start, ROWS), factor)
            low_j = jnp.minimum(low_j, mass)
            blocks.append(jnp.concatenate([x * ratio for x in parts], axis=1).astype(jnp.bfloat16))
        moves.append(jnp.concatenate(blocks, axis=0))
        last_j.append(low_j)
        if len(moves) == PAIR:
            use(region // PAIR, moves)
            moves = []
    least_i = fold(least_i, jnp.minimum)
    return jnp.min(least_i), jnp.min(fold(last_j, jnp.minimum)), jnp.max(most)


def transport_logs(gram, logw, scale):
    members = gram.shape[-1]
    j = lax.broadcasted_iota(jnp.int32, gram.shape, 0)
    i = lax.broadcasted_iota(jnp.int32, gram.shape, 1)
    kept = jnp.where(i == j, gram, 0.0)
    down = jnp.sum(kept, axis=1, keepdims=True)
    across = jnp.sum(kept, axis=0, keepdims=True)
    cost = (down + across - 2.0 * gram) * scale
    pot_g = jnp.zeros((members, 1), jnp.float32)
    for sweep in range(SWEEPS):
        term = pot_g - cost
        top = jnp.max(term, axis=0, keepdims=True)
        pot_f = logw - top - jnp.log(jnp.sum(jnp.exp2(term - top), axis=0, keepdims=True)) * LOG2E
        term = pot_f - cost
        top = jnp.max(term, axis=1, keepdims=True)
        pot_g = -math.log2(members) - top
        pot_g = pot_g - jnp.log(jnp.sum(jnp.exp2(term - top), axis=1, keepdims=True)) * LOG2E
    return (members * jnp.exp2(pot_f + pot_g - cost)).astype(jnp.bfloat16)


def transform(state_ref, pair, moves):
    lon_dev, nvar, _, members = state_ref.shape
    size = PAIR * TILE
    own = state_ref[:, :, pair * size : (pair + 1) * size, :].astype(jnp.float32)
    parts = []
    for region, move in enumerate(moves):
        cells = own[:, :, region * TILE : (region + 1) * TILE].astype(jnp.bfloat16)
        cells = cells.reshape(lon_dev * nvar * TILE, members)
        moved = lax.dot_general(
            cells, move, (((1,), (1,)), ((), ())), preferred_element_type=jnp.float32
        )
        parts.append(moved.reshape(lon_dev, nvar, TILE, members))
    return jnp.concatenate(parts, axis=2).astype(jnp.bfloat16)


def analyse_kernel(count, scale, *refs):
    odd_ref, halo_ref, first_ref, last_hbm_ref, state_hbm_ref, like_ref, sums_ref = refs[:7]
    out_ref, gram_ref, kernel_ref, mass_ref, result_ref, state_ref, last_ref = refs[7:14]
    out_sems, state_sems, last_sem = refs[14:]
    kept = first_ref.shape[0]
    fetch_last = pltpu.make_async_copy(last_hbm_ref, last_ref, last_sem)
    fetch_last.start()
    regions, members, _ = gram_ref.shape
    pairs = regions // PAIR
    size = PAIR * TILE
    lat = regions * REGION
    fetches = slab_copies(state_hbm_ref, state_ref, state_sems)
    for copy in fetches:
        copy.start()

    def send(pair):
        rows = pl.ds(pair * size, size)
        return pltpu.make_async_copy(
            result_ref.at[pair], out_ref.at[:, :, rows, :], out_sems.at[pair]
        )

    misfit = like_ref[...] + like_rows(halo_ref[halo_ref.shape[0] - 4 * TILE :, :])
    misfit = misfit - jnp.min(misfit, axis=1, keepdims=True)
    factor = (-0.5 * LOG2E * count) / jnp.sum(sums_ref[...], axis=0, keepdims=True)
    like = misfit * jnp.concatenate([factor] * (members // 128), axis=1)
    weights = jnp.exp2(like + MASS)
    norm = jnp.sum(weights, axis=1, keepdims=True) * 2.0**-MASS
    weights = weights / norm

    planes = halo_ref.shape[0] // lat
    halo = [w for w in halo_weights(odd_ref[0] == 0) for _ in range(planes // HALO)]
    slabs = [slab_of(halo_ref, lat, at) for at in range(lat // size)]

    def put(region, gram):
        if region < kept:
            gram_ref[region] = first_ref[region] + gram
        else:
            if region == kept:
                kernel_matrices(range(kept), gram_ref, kernel_ref, mass_ref, scale)
                fetch_last.wait()
            gram_ref[region] = last_ref[region - kept] + gram

    add_grams(slabs, halo, put)
    kernel_matrices(range(kept, regions), gram_ref, kernel_ref, mass_ref, scale)

    def use(pair, moves):
        if pair == 0:
            for copy in fetches:
                copy.wait()
        result_ref[pair] = transform(state_ref, pair, moves)
        send(pair).start()

    row, col, most = transports_scaled(kernel_ref, weights, mass_ref, use)
    sound = (row >= 2.0**-24) & (col >= 2.0**-30) & (most <= 2.0**30) & (row * col >= 2.0**-34)
    for pair in range(pairs):
        send(pair).wait()

    @pl.when(jnp.logical_not(sound))
    def _():
        logw = like - jnp.log(norm) * LOG2E
        for pair in range(pairs):
            again = [
                transport_logs(gram_ref[region], logw[region : region + 1], scale)
                for region in range(pair * PAIR, (pair + 1) * PAIR)
            ]
            result_ref[pair] = transform(state_ref, pair, again)
            send(pair).start()
            send(pair).wait()


def analyse(odd, halo, first, last, state, like, sums, count, scale):
    lon_dev, nvar, lat, members = state.shape
    regions = lat // REGION
    pairs = regions // PAIR
    vmem = pl.BlockSpec(memory_space=pltpu.VMEM)
    return pl.pallas_call(
        functools.partial(analyse_kernel, count, scale),
        in_specs=[
            pl.BlockSpec(memory_space=pltpu.SMEM),
            vmem,
            vmem,
            pl.BlockSpec(memory_space=pltpu.HBM),
            pl.BlockSpec(memory_space=pltpu.HBM),
            vmem,
            vmem,
        ],
        out_specs=pl.BlockSpec(memory_space=pl.ANY),
        out_shape=jax.ShapeDtypeStruct(state.shape, state.dtype),
        scratch_shapes=[
            pltpu.VMEM((regions, members, members), jnp.float32),
            pltpu.VMEM((regions, members, members), jnp.float32),
            pltpu.VMEM((regions, 1, members), jnp.float32),
            pltpu.VMEM((pairs, lon_dev, nvar, PAIR * TILE, members), state.dtype),
            pltpu.VMEM(state.shape, state.dtype),
            pltpu.VMEM(last.shape, jnp.float32),
            pltpu.SemaphoreType.DMA((pairs,)),
            pltpu.SemaphoreType.DMA((pairs,)),
            pltpu.SemaphoreType.DMA,
        ],
        compiler_params=pltpu.CompilerParams(vmem_limit_bytes=24 * 2**20),
        name="analyse",
    )(
        odd,
        halo,
        first,
        *[pltpu.with_memory_space_constraint(x, pltpu.HBM) for x in (last, state)],
        like,
        sums,
    )


def on_device(state, obs_index, obs_value, obs_var):
    nvar = state.shape[1]
    count = lax.axis_size("lon")
    odd = (lax.axis_index("lon") & 1).astype(jnp.int32).reshape(1)
    near_pairs = [(i, i ^ 1) for i in range(count)]
    far_pairs = [(i, (i + 1 if i % 2 else i - 1) % count) for i in range(count)]
    own_like, for_near, for_far, part = observe(odd, state, obs_index, obs_value, obs_var)
    far = lax.ppermute(for_far, "lon", far_pairs)
    near = lax.ppermute(for_near, "lon", near_pairs)
    start = near.shape[0] - TILE
    part = part[0] + jnp.sum(near[start : start + 3, :128].astype(jnp.float32), axis=0)
    sums = lax.all_to_all(
        jnp.broadcast_to(part, (count // 2, 128)),
        "lon",
        0,
        0,
        axis_index_groups=[[i for i in range(count) if (i ^ i >> 1) & 1 == kind] for kind in range(2)],
        tiled=True,
    )
    offsets = range(REGION + 2 * HALO)
    line = [1.0 - max(0, HALO - p, p - (HALO + REGION - 1)) / (HALO + 1) for p in offsets]
    scale = LOG2E / EPS / (nvar * sum(line) ** 2)
    first, last, like = own_gram(odd, state, near, own_like)
    nobs = float(obs_index.shape[0] * count)
    return analyse(odd, far, first, last, state, like, sums, nobs, scale)


def solution(mesh):
    return jax.shard_map(
        on_device,
        mesh=mesh,
        in_specs=(
            P(("ens", "lon"), None, None, None),
            P(("ens", "lon")),
            P(("ens", "lon")),
            P(("ens", "lon")),
        ),
        out_specs=P(("ens", "lon"), None, None, None),
        check_vma=False,
    )
```

```python
import functools
import math

import jax
import jax.numpy as jnp
from jax import lax
from jax.experimental import pallas as pl
from jax.experimental.pallas import tpu as pltpu
from jax.sharding import PartitionSpec as P

REGION = 8
HALO = 4
SWEEPS = 4
EPS = 0.05
TILE = 8
PAIR = 2
LOG2E = 1.4426950408889634
ROWS = 32
LIFT, START, MASS = 20, -10, 60


def fold(values, op):
    out = values[0]
    for value in values[1:]:
        out = op(out, value)
    return out


def line_weight(place):
    dist = jnp.maximum(0.0, jnp.maximum(HALO - place, place - (HALO + REGION - 1)))
    inside = (place >= 0) & (place < REGION + 2 * HALO)
    return jnp.where(inside, 1.0 - dist / (HALO + 1), 0.0)


def like_rows(rows):
    rows = rows.astype(jnp.float32)
    return rows[:TILE] + rows[TILE : 2 * TILE] + rows[2 * TILE : 3 * TILE]


def in_parts(values, extra):
    below = lax.broadcasted_iota(jnp.int32, values.shape, 0)
    extra_high = extra.astype(jnp.bfloat16).astype(jnp.float32)
    extra_middle = (extra - extra_high).astype(jnp.bfloat16).astype(jnp.float32)
    extra_low = extra - extra_high - extra_middle
    last = jnp.where(below == 0, extra_high, jnp.where(below == 1, extra_middle, extra_low))
    last = jnp.where(below < 3, last, 0.0)
    high = values.astype(jnp.bfloat16).astype(jnp.float32)
    middle = (values - high).astype(jnp.bfloat16).astype(jnp.float32)
    low = values - high - middle
    return jnp.concatenate([high, middle, low, last], axis=0).astype(jnp.bfloat16)


def steps_inside(place):
    dist = jnp.maximum(0.0, jnp.maximum(HALO - place, place - (HALO + REGION - 1)))
    inside = (place >= 0) & (place < REGION + 2 * HALO)
    return jnp.where(inside, HALO + 1 - dist, 0.0)


def observe_kernel(*refs):
    odd_ref, state_ref, rows_ref = refs[:3]
    own_ref, near_ref, far_ref, part_ref = refs[6:10]
    cells_ref, index_ref, value_ref, var_ref, sems = refs[10:]
    lon_dev, lat, members = cells_ref.shape
    nobs = index_ref.shape[1]
    edge = rows_ref.shape[0] // lon_dev * HALO
    last = rows_ref.shape[0] - edge
    far_at = pl.multiple_of(odd_ref[0] * last, 16)
    near_at = pl.multiple_of(last - far_at, 16)
    fetches = [
        (refs[3], index_ref),
        (refs[4], value_ref),
        (refs[5], var_ref),
        (state_ref.at[:, 0], cells_ref),
        (rows_ref.at[pl.ds(far_at, edge), :], far_ref.at[pl.ds(0, edge), :]),
        (rows_ref.at[pl.ds(near_at, edge), :], near_ref.at[pl.ds(0, edge), :]),
    ]
    copies = [
        pltpu.make_async_copy(src, dst, sems.at[i]) for i, (src, dst) in enumerate(fetches)
    ]
    for copy in copies:
        copy.start()
    for copy in copies[:3]:
        copy.wait()
    index = index_ref[...]
    sub = lax.broadcasted_iota(jnp.int32, (TILE, nobs), 0)
    table = jnp.where(
        sub == 0,
        index.astype(jnp.float32),
        jnp.where(sub == 1, value_ref[...], var_ref[...]),
    ).T
    index_col = table[:, 0:1].astype(jnp.int32)
    value = table[:, 1:2]
    var = table[:, 2:3]
    pick = index_col == lax.broadcasted_iota(jnp.int32, (nobs, lon_dev * lat), 1)
    pick = jnp.where(pick, 1.0, 0.0).astype(jnp.bfloat16)
    lon = (index // lat).astype(jnp.float32)
    along = index.astype(jnp.float32) - lon * lat
    blocks = own_ref.shape[0]
    block = lax.broadcasted_iota(jnp.int32, (blocks, nobs), 0).astype(jnp.float32)
    across = steps_inside(along - REGION * block + HALO)
    side = jnp.where(odd_ref[0] == 1, float(REGION), float(-REGION))
    weights = [steps_inside(lon + (HALO + shift)) * across for shift in (0.0, side, -side)]
    weights = jnp.concatenate(weights, axis=0).astype(jnp.bfloat16)
    inverse = 1.0 / var
    copies[3].wait()
    rows = cells_ref[...].reshape(lon_dev * lat, members)
    seen = jnp.dot(pick, rows, preferred_element_type=jnp.float32)
    terms = (value - seen) ** 2 * inverse
    high = terms.astype(jnp.bfloat16)
    rest = terms - high.astype(jnp.float32)
    middle = rest.astype(jnp.bfloat16)
    low = (rest - middle.astype(jnp.float32)).astype(jnp.bfloat16)
    sums = [jnp.dot(weights, x, preferred_element_type=jnp.float32) for x in (low, middle, high)]
    like = fold(sums, jnp.add) * (1.0 / (HALO + 1) ** 2)
    centre = jnp.sum(seen, axis=1, keepdims=True) * (1.0 / members)
    spread = jnp.sum((seen - centre) ** 2, axis=1, keepdims=True) * (1.0 / (members - 1))
    innovation = (value - centre) ** 2 / (var + spread)
    part = jnp.sum(innovation, axis=0, keepdims=True)
    part_ref[...] = jnp.broadcast_to(part, part_ref.shape)
    own_ref[...] = like[:blocks]
    near_ref[edge:, :] = in_parts(like[blocks : 2 * blocks], part)
    far_ref[edge:, :] = in_parts(like[2 * blocks :], jnp.zeros_like(part))
    for copy in copies[4:]:
        copy.wait()


def observe(odd, state, obs_index, obs_value, obs_var):
    lon_dev, nvar, lat, members = state.shape
    nobs = obs_index.size
    assert lat // REGION == TILE
    like = jax.ShapeDtypeStruct((lat // REGION, members), jnp.float32)
    payload = pltpu.VMEM((HALO * nvar * lat + 4 * TILE, members), state.dtype)
    part = jax.ShapeDtypeStruct((TILE, 128), jnp.float32)
    arrays = state, state.reshape(-1, members), obs_index[None], obs_value[None], obs_var[None]
    return pl.pallas_call(
        observe_kernel,
        in_specs=[pl.BlockSpec(memory_space=pltpu.SMEM)]
        + [pl.BlockSpec(memory_space=pltpu.HBM)] * len(arrays),
        out_specs=[pl.BlockSpec(memory_space=pltpu.VMEM)] * 4,
        out_shape=[like, payload, payload, part],
        scratch_shapes=[
            pltpu.VMEM((lon_dev, lat, members), state.dtype),
            pltpu.VMEM((1, nobs), jnp.int32),
            pltpu.VMEM((1, nobs), jnp.float32),
            pltpu.VMEM((1, nobs), jnp.float32),
            pltpu.SemaphoreType.DMA((6,)),
        ],
        compiler_params=pltpu.CompilerParams(vmem_limit_bytes=16 * 2**20),
        name="observe",
    )(odd, *[pltpu.with_memory_space_constraint(x, pltpu.HBM) for x in arrays])


def slab_of(ref, lat, at):
    size = PAIR * TILE
    planes = ref.shape[0] // lat
    rows = [ref[i * lat + at * size : i * lat + (at + 1) * size, :] for i in range(planes)]
    return jnp.stack(rows).astype(jnp.float32)


def pair_tiles(load, step, steps):
    here = load(step)
    none = jnp.zeros_like(here[:, :TILE])
    before = load(step - 1)[:, TILE:] if step else none
    after = load(step + 1)[:, :TILE] if step + 1 < steps else none
    return before, here[:, :TILE], here[:, TILE:], after


def halo_weights(to_left):
    steps = [jnp.float32(1.0) - jnp.float32(d) / jnp.float32(HALO + 1) for d in range(HALO, 0, -1)]
    return [jnp.where(to_left, x, y) for x, y in zip(steps, steps[::-1])]


def turn(tile):
    return tile.reshape(-1, tile.shape[-1]).astype(jnp.bfloat16).T


def gram_of(tiles, turned, weights):
    planes, _, members = tiles[0].shape
    depth = planes * TILE
    row = lax.broadcasted_iota(jnp.int32, (TILE, members), 0)
    upper = row < HALO
    rowf = row.astype(jnp.float32)
    edge = line_weight(jnp.where(upper, rowf + (HALO + REGION), rowf - HALO))
    lane = lax.broadcasted_iota(jnp.int32, (1, depth), 1) & (TILE - 1)
    take_next = jnp.where(lane < HALO, 1.0, 0.0).astype(jnp.bfloat16)
    take_prev = jnp.where(lane < HALO, 0.0, 1.0).astype(jnp.bfloat16)
    grams = []
    for at in (1, 2):
        margin = jnp.where(upper, tiles[at + 1], tiles[at - 1])
        main_rows, margin_rows = [], []
        for plane, weight in enumerate(weights):
            own = tiles[at][plane]
            main_rows.append(own if weight is None else own * weight)
            margin_rows.append(margin[plane] * (edge if weight is None else edge * weight))
        weighted = jnp.stack(main_rows + margin_rows)
        weighted = weighted.reshape(2 * depth, members).astype(jnp.bfloat16)
        margin = turned[at + 1] * take_next + turned[at - 1] * take_prev
        both = jnp.concatenate([turned[at], margin], axis=1)
        grams.append(jnp.dot(both, weighted, preferred_element_type=jnp.float32))
    return grams


def slab_copies(src_ref, dst_ref, sems, only=None):
    size = PAIR * TILE

    def slab(at):
        rows = pl.ds(pl.multiple_of(at * size, size), size)
        return pltpu.make_async_copy(
            src_ref.at[:, :, rows, :], dst_ref.at[:, :, rows, :], sems.at[at]
        )

    return slab(only) if only is not None else [slab(i) for i in range(src_ref.shape[2] // size)]


def own_gram_kernel(odd_ref, state_hbm_ref, near_ref, own_ref, *refs):
    first_ref, last_hbm_ref, like_ref, state_ref, last_ref, sems, last_sem = refs
    lon_dev, nvar, lat, members = state_ref.shape
    kept = first_ref.shape[0]
    steps = lat // (PAIR * TILE)
    copies = slab_copies(state_hbm_ref, state_ref, sems)
    for copy in copies:
        copy.start()
    like_ref[...] = own_ref[...] + like_rows(near_ref[near_ref.shape[0] - 4 * TILE :, :])
    size = PAIR * TILE

    def load(step):
        own = state_ref[:, :, step * size : (step + 1) * size, :].astype(jnp.float32)
        own = own.reshape(lon_dev * nvar, size, members)
        return jnp.concatenate([own, slab_of(near_ref, lat, step)], axis=0)

    weights = [None] * (lon_dev * nvar)
    weights += [w for w in halo_weights(odd_ref[0] == 1) for _ in range(nvar)]
    for copy in copies:
        copy.wait()
    slabs = [load(step) for step in range(steps)]

    def put(region, gram):
        if region < kept:
            first_ref[region] = gram
        else:
            last_ref[region - kept] = gram

    add_grams(slabs, weights, put)
    keep = pltpu.make_async_copy(last_ref, last_hbm_ref, last_sem)
    keep.start()
    keep.wait()


def add_grams(slabs, weights, put):
    none = jnp.zeros_like(slabs[0][:, :TILE])
    tiles = [none]
    for slab in slabs:
        tiles += [slab[:, :TILE], slab[:, TILE:]]
    tiles.append(none)
    turned = [turn(tile) for tile in tiles[1:-1]]
    turned = [jnp.zeros_like(turned[0])] + turned + [jnp.zeros_like(turned[0])]
    for pair in range(len(slabs)):
        window = slice(pair * PAIR, pair * PAIR + PAIR + 2)
        grams = gram_of(tiles[window], turned[window], weights)
        for at, gram in enumerate(grams):
            put(pair * PAIR + at, gram)


def own_gram(odd, state, near, own):
    _, _, lat, members = state.shape
    kept = lat // REGION - PAIR
    vmem = pl.BlockSpec(memory_space=pltpu.VMEM)
    return pl.pallas_call(
        own_gram_kernel,
        in_specs=[
            pl.BlockSpec(memory_space=pltpu.SMEM),
            pl.BlockSpec(memory_space=pltpu.HBM),
            vmem,
            vmem,
        ],
        out_specs=[vmem, pl.BlockSpec(memory_space=pltpu.HBM), vmem],
        out_shape=[
            jax.ShapeDtypeStruct((kept, members, members), jnp.float32),
            pltpu.HBM((PAIR, members, members), jnp.float32),
            jax.ShapeDtypeStruct(own.shape, jnp.float32),
        ],
        scratch_shapes=[
            pltpu.VMEM(state.shape, state.dtype),
            pltpu.VMEM((PAIR, members, members), jnp.float32),
            pltpu.SemaphoreType.DMA((lat // (PAIR * TILE),)),
            pltpu.SemaphoreType.DMA,
        ],
        compiler_params=pltpu.CompilerParams(vmem_limit_bytes=24 * 2**20),
        name="own_gram",
    )(odd, pltpu.with_memory_space_constraint(state, pltpu.HBM), near, own)


def halves(ref, region, rows):
    members = ref.shape[-1]
    return [ref[region, rows, at : at + 128] for at in range(0, members, 128)]


def diagonal(gram_ref, region):
    members = gram_ref.shape[-1]
    across = [None] * (members // 128)
    down = []
    for start in range(0, members, ROWS):
        lane = start // 128
        gram = gram_ref[region, pl.ds(start, ROWS), lane * 128 : lane * 128 + 128]
        i = lax.broadcasted_iota(jnp.int32, gram.shape, 0) + start
        j = lax.broadcasted_iota(jnp.int32, gram.shape, 1) + lane * 128
        kept = jnp.where(i == j, gram, 0.0)
        down.append(jnp.broadcast_to(jnp.sum(kept, axis=1, keepdims=True), gram.shape))
        part = jnp.sum(kept.reshape(ROWS // TILE, TILE, 128), axis=0)
        across[lane] = part if across[lane] is None else across[lane] + part
    return [jnp.sum(x, axis=0, keepdims=True) for x in across], down


def kernel_matrices(regions, gram_ref, kernel_ref, mass_ref, scale):
    members = gram_ref.shape[-1]
    for region in regions:
        across, down = diagonal(gram_ref, region)
        across = [0.5 * LIFT - x * scale for x in across]
        masses = [0.0 for _ in across]
        for i, start in enumerate(range(0, members, ROWS)):
            rows = pl.ds(start, ROWS)
            base = 0.5 * LIFT - down[i] * scale
            for lane, (gram, x) in enumerate(zip(halves(gram_ref, region, rows), across)):
                part = jnp.exp2(gram * (2.0 * scale) + base + x)
                kernel_ref[region, rows, lane * 128 : lane * 128 + 128] = part
                part = jnp.sum(part.reshape(ROWS // TILE, TILE, 128), axis=0)
                masses[lane] = masses[lane] + part
        masses = [jnp.sum(x, axis=0, keepdims=True) for x in masses]
        mass_ref[region] = jnp.concatenate(masses, axis=1)


def transports_scaled(kernel_ref, weights, mass_ref, use):
    regions = range(kernel_ref.shape[0])
    members = kernel_ref.shape[-1]
    starts = range(0, members, ROWS)
    lanes = range(members // 128)
    share = 2.0**MASS / members

    def lane_parts(row):
        return [row[:, lane * 128 : lane * 128 + 128] for lane in lanes]

    def settle(totals, region):
        return [w / x for w, x in zip(lane_parts(weights[region : region + 1]), totals)]

    def masses_of(region, rows, factor):
        parts = [k * f for k, f in zip(halves(kernel_ref, region, rows), factor)]
        mass = jnp.sum(fold(parts, jnp.add), axis=1, keepdims=True)
        mass = jnp.broadcast_to(mass, (ROWS, 128))
        return parts, mass, pl.reciprocal(mass, approx=True)

    def sweep(least_i, least_j, factors):
        next_i, next_j, next_factors = [], [], []
        for region, low_i, low_j, factor in zip(regions, least_i, least_j, factors):
            totals = [None for _ in lanes]
            for start in starts:
                rows = pl.ds(start, ROWS)
                _, mass, ratio = masses_of(region, rows, factor)
                low_j = jnp.minimum(low_j, mass)
                for lane, kernel in enumerate(halves(kernel_ref, region, rows)):
                    part = jnp.sum((kernel * ratio).reshape(ROWS // TILE, TILE, 128), axis=0)
                    totals[lane] = part if totals[lane] is None else totals[lane] + part
            totals = [jnp.sum(x, axis=0, keepdims=True) * share for x in totals]
            next_i.append(jnp.minimum(low_i, fold(totals, jnp.minimum)))
            next_j.append(low_j)
            next_factors.append(settle(totals, region))
        return next_i, next_j, next_factors

    masses = [lane_parts(mass_ref[region]) for region in regions]
    most = fold([fold(x, jnp.maximum) for x in masses], jnp.maximum)
    totals = [[x * 2.0**START for x in mass] for mass in masses]
    least_i = [fold(x, jnp.minimum) for x in totals]
    least_j = [jnp.full((ROWS, 128), 1e30, jnp.float32) for _ in regions]
    factors = [settle(x, region) for x, region in zip(totals, regions)]
    for _ in range(SWEEPS - 1):
        least_i, least_j, factors = sweep(least_i, least_j, factors)
    moves, last_j = [], []
    for region, low_j, factor in zip(regions, least_j, factors):
        blocks = []
        for start in starts:
            parts, mass, ratio = masses_of(region, pl.ds(start, ROWS), factor)
            low_j = jnp.minimum(low_j, mass)
            blocks.append(jnp.concatenate([x * ratio for x in parts], axis=1).astype(jnp.bfloat16))
        moves.append(jnp.concatenate(blocks, axis=0))
        last_j.append(low_j)
        if len(moves) == PAIR:
            use(region // PAIR, moves)
            moves = []
    least_i = fold(least_i, jnp.minimum)
    return jnp.min(least_i), jnp.min(fold(last_j, jnp.minimum)), jnp.max(most)


def transport_logs(gram, logw, scale):
    members = gram.shape[-1]
    j = lax.broadcasted_iota(jnp.int32, gram.shape, 0)
    i = lax.broadcasted_iota(jnp.int32, gram.shape, 1)
    kept = jnp.where(i == j, gram, 0.0)
    down = jnp.sum(kept, axis=1, keepdims=True)
    across = jnp.sum(kept, axis=0, keepdims=True)
    cost = (down + across - 2.0 * gram) * scale
    pot_g = jnp.zeros((members, 1), jnp.float32)
    for sweep in range(SWEEPS):
        term = pot_g - cost
        top = jnp.max(term, axis=0, keepdims=True)
        pot_f = logw - top - jnp.log(jnp.sum(jnp.exp2(term - top), axis=0, keepdims=True)) * LOG2E
        term = pot_f - cost
        top = jnp.max(term, axis=1, keepdims=True)
        pot_g = -math.log2(members) - top
        pot_g = pot_g - jnp.log(jnp.sum(jnp.exp2(term - top), axis=1, keepdims=True)) * LOG2E
    return (members * jnp.exp2(pot_f + pot_g - cost)).astype(jnp.bfloat16)


def transform(state_ref, pair, moves):
    lon_dev, nvar, _, members = state_ref.shape
    size = PAIR * TILE
    own = state_ref[:, :, pair * size : (pair + 1) * size, :].astype(jnp.float32)
    parts = []
    for region, move in enumerate(moves):
        cells = own[:, :, region * TILE : (region + 1) * TILE].astype(jnp.bfloat16)
        cells = cells.reshape(lon_dev * nvar * TILE, members)
        moved = lax.dot_general(
            cells, move, (((1,), (1,)), ((), ())), preferred_element_type=jnp.float32
        )
        parts.append(moved.reshape(lon_dev, nvar, TILE, members))
    return jnp.concatenate(parts, axis=2).astype(jnp.bfloat16)


def analyse_kernel(count, scale, *refs):
    odd_ref, halo_ref, first_ref, last_hbm_ref, state_hbm_ref, like_ref, sums_ref = refs[:7]
    out_ref, gram_ref, kernel_ref, mass_ref, result_ref, state_ref, last_ref = refs[7:14]
    out_sems, state_sems, last_sem = refs[14:]
    kept = first_ref.shape[0]
    fetch_last = pltpu.make_async_copy(last_hbm_ref, last_ref, last_sem)
    fetch_last.start()
    regions, members, _ = gram_ref.shape
    pairs = regions // PAIR
    size = PAIR * TILE
    lat = regions * REGION
    fetches = slab_copies(state_hbm_ref, state_ref, state_sems)
    for copy in fetches:
        copy.start()

    def send(pair):
        rows = pl.ds(pair * size, size)
        return pltpu.make_async_copy(
            result_ref.at[pair], out_ref.at[:, :, rows, :], out_sems.at[pair]
        )

    misfit = like_ref[...] + like_rows(halo_ref[halo_ref.shape[0] - 4 * TILE :, :])
    misfit = misfit - jnp.min(misfit, axis=1, keepdims=True)
    factor = (-0.5 * LOG2E * count) / jnp.sum(sums_ref[...], axis=0, keepdims=True)
    like = misfit * jnp.concatenate([factor] * (members // 128), axis=1)
    weights = jnp.exp2(like + MASS)
    norm = jnp.sum(weights, axis=1, keepdims=True) * 2.0**-MASS
    weights = weights / norm

    planes = halo_ref.shape[0] // lat
    halo = [w for w in halo_weights(odd_ref[0] == 0) for _ in range(planes // HALO)]
    slabs = [slab_of(halo_ref, lat, at) for at in range(lat // size)]

    def put(region, gram):
        if region < kept:
            gram_ref[region] = first_ref[region] + gram
        else:
            if region == kept:
                kernel_matrices(range(kept), gram_ref, kernel_ref, mass_ref, scale)
                fetch_last.wait()
            gram_ref[region] = last_ref[region - kept] + gram

    add_grams(slabs, halo, put)
    kernel_matrices(range(kept, regions), gram_ref, kernel_ref, mass_ref, scale)

    def use(pair, moves):
        if pair == 0:
            for copy in fetches:
                copy.wait()
        result_ref[pair] = transform(state_ref, pair, moves)
        if pair % 2 or pair == pairs - 1:
            for at in range(pair - pair % 2, pair + 1):
                send(at).start()

    row, col, most = transports_scaled(kernel_ref, weights, mass_ref, use)
    sound = (row >= 2.0**-24) & (col >= 2.0**-30) & (most <= 2.0**30) & (row * col >= 2.0**-34)
    for pair in range(pairs):
        send(pair).wait()

    @pl.when(jnp.logical_not(sound))
    def _():
        logw = like - jnp.log(norm) * LOG2E
        for pair in range(pairs):
            again = [
                transport_logs(gram_ref[region], logw[region : region + 1], scale)
                for region in range(pair * PAIR, (pair + 1) * PAIR)
            ]
            result_ref[pair] = transform(state_ref, pair, again)
            send(pair).start()
            send(pair).wait()


def analyse(odd, halo, first, last, state, like, sums, count, scale):
    lon_dev, nvar, lat, members = state.shape
    regions = lat // REGION
    pairs = regions // PAIR
    vmem = pl.BlockSpec(memory_space=pltpu.VMEM)
    return pl.pallas_call(
        functools.partial(analyse_kernel, count, scale),
        in_specs=[
            pl.BlockSpec(memory_space=pltpu.SMEM),
            vmem,
            vmem,
            pl.BlockSpec(memory_space=pltpu.HBM),
            pl.BlockSpec(memory_space=pltpu.HBM),
            vmem,
            vmem,
        ],
        out_specs=pl.BlockSpec(memory_space=pl.ANY),
        out_shape=jax.ShapeDtypeStruct(state.shape, state.dtype),
        scratch_shapes=[
            pltpu.VMEM((regions, members, members), jnp.float32),
            pltpu.VMEM((regions, members, members), jnp.float32),
            pltpu.VMEM((regions, 1, members), jnp.float32),
            pltpu.VMEM((pairs, lon_dev, nvar, PAIR * TILE, members), state.dtype),
            pltpu.VMEM(state.shape, state.dtype),
            pltpu.VMEM(last.shape, jnp.float32),
            pltpu.SemaphoreType.DMA((pairs,)),
            pltpu.SemaphoreType.DMA((pairs,)),
            pltpu.SemaphoreType.DMA,
        ],
        compiler_params=pltpu.CompilerParams(vmem_limit_bytes=24 * 2**20),
        name="analyse",
    )(
        odd,
        halo,
        first,
        *[pltpu.with_memory_space_constraint(x, pltpu.HBM) for x in (last, state)],
        like,
        sums,
    )


def on_device(state, obs_index, obs_value, obs_var):
    nvar = state.shape[1]
    count = lax.axis_size("lon")
    odd = (lax.axis_index("lon") & 1).astype(jnp.int32).reshape(1)
    near_pairs = [(i, i ^ 1) for i in range(count)]
    far_pairs = [(i, (i + 1 if i % 2 else i - 1) % count) for i in range(count)]
    own_like, for_near, for_far, part = observe(odd, state, obs_index, obs_value, obs_var)
    far = lax.ppermute(for_far, "lon", far_pairs)
    near = lax.ppermute(for_near, "lon", near_pairs)
    start = near.shape[0] - TILE
    part = part[0] + jnp.sum(near[start : start + 3, :128].astype(jnp.float32), axis=0)
    sums = lax.all_to_all(
        jnp.broadcast_to(part, (count // 2, 128)),
        "lon",
        0,
        0,
        axis_index_groups=[[i for i in range(count) if (i ^ i >> 1) & 1 == kind] for kind in range(2)],
        tiled=True,
    )
    offsets = range(REGION + 2 * HALO)
    line = [1.0 - max(0, HALO - p, p - (HALO + REGION - 1)) / (HALO + 1) for p in offsets]
    scale = LOG2E / EPS / (nvar * sum(line) ** 2)
    first, last, like = own_gram(odd, state, near, own_like)
    nobs = float(obs_index.shape[0] * count)
    return analyse(odd, far, first, last, state, like, sums, nobs, scale)


def solution(mesh):
    return jax.shard_map(
        on_device,
        mesh=mesh,
        in_specs=(
            P(("ens", "lon"), None, None, None),
            P(("ens", "lon")),
            P(("ens", "lon")),
            P(("ens", "lon")),
        ),
        out_specs=P(("ens", "lon"), None, None, None),
        check_vma=False,
    )
```

```python
import functools
import math

import jax
import jax.numpy as jnp
from jax import lax
from jax.experimental import pallas as pl
from jax.experimental.pallas import tpu as pltpu
from jax.sharding import PartitionSpec as P

REGION = 8
HALO = 4
SWEEPS = 4
EPS = 0.05
TILE = 8
PAIR = 2
LOG2E = 1.4426950408889634
ROWS = 32
LIFT, START, MASS = 20, -10, 60


def fold(values, op):
    out = values[0]
    for value in values[1:]:
        out = op(out, value)
    return out


def line_weight(place):
    dist = jnp.maximum(0.0, jnp.maximum(HALO - place, place - (HALO + REGION - 1)))
    inside = (place >= 0) & (place < REGION + 2 * HALO)
    return jnp.where(inside, 1.0 - dist / (HALO + 1), 0.0)


def like_rows(rows):
    rows = rows.astype(jnp.float32)
    return rows[:TILE] + rows[TILE : 2 * TILE] + rows[2 * TILE : 3 * TILE]


def in_parts(values, extra):
    below = lax.broadcasted_iota(jnp.int32, values.shape, 0)
    extra_high = extra.astype(jnp.bfloat16).astype(jnp.float32)
    extra_middle = (extra - extra_high).astype(jnp.bfloat16).astype(jnp.float32)
    extra_low = extra - extra_high - extra_middle
    last = jnp.where(below == 0, extra_high, jnp.where(below == 1, extra_middle, extra_low))
    last = jnp.where(below < 3, last, 0.0)
    high = values.astype(jnp.bfloat16).astype(jnp.float32)
    middle = (values - high).astype(jnp.bfloat16).astype(jnp.float32)
    low = values - high - middle
    return jnp.concatenate([high, middle, low, last], axis=0).astype(jnp.bfloat16)


def steps_inside(place):
    dist = jnp.maximum(0.0, jnp.maximum(HALO - place, place - (HALO + REGION - 1)))
    inside = (place >= 0) & (place < REGION + 2 * HALO)
    return jnp.where(inside, HALO + 1 - dist, 0.0)


def observe_kernel(*refs):
    odd_ref, state_ref, rows_ref = refs[:3]
    own_ref, near_ref, far_ref, part_ref = refs[6:10]
    cells_ref, index_ref, value_ref, var_ref, sems = refs[10:]
    lon_dev, lat, members = cells_ref.shape
    nobs = index_ref.shape[1]
    edge = rows_ref.shape[0] // lon_dev * HALO
    last = rows_ref.shape[0] - edge
    far_at = pl.multiple_of(odd_ref[0] * last, 16)
    near_at = pl.multiple_of(last - far_at, 16)
    fetches = [
        (refs[3], index_ref),
        (refs[4], value_ref),
        (refs[5], var_ref),
        (state_ref.at[:, 0], cells_ref),
        (rows_ref.at[pl.ds(far_at, edge), :], far_ref.at[pl.ds(0, edge), :]),
        (rows_ref.at[pl.ds(near_at, edge), :], near_ref.at[pl.ds(0, edge), :]),
    ]
    copies = [
        pltpu.make_async_copy(src, dst, sems.at[i]) for i, (src, dst) in enumerate(fetches)
    ]
    for copy in copies:
        copy.start()
    for copy in copies[:3]:
        copy.wait()
    index = index_ref[...]
    sub = lax.broadcasted_iota(jnp.int32, (TILE, nobs), 0)
    table = jnp.where(
        sub == 0,
        index.astype(jnp.float32),
        jnp.where(sub == 1, value_ref[...], var_ref[...]),
    ).T
    index_col = table[:, 0:1].astype(jnp.int32)
    value = table[:, 1:2]
    var = table[:, 2:3]
    pick = index_col == lax.broadcasted_iota(jnp.int32, (nobs, lon_dev * lat), 1)
    pick = jnp.where(pick, 1.0, 0.0).astype(jnp.bfloat16)
    lon = (index // lat).astype(jnp.float32)
    along = index.astype(jnp.float32) - lon * lat
    blocks = own_ref.shape[0]
    block = lax.broadcasted_iota(jnp.int32, (blocks, nobs), 0).astype(jnp.float32)
    across = steps_inside(along - REGION * block + HALO)
    side = jnp.where(odd_ref[0] == 1, float(REGION), float(-REGION))
    weights = [steps_inside(lon + (HALO + shift)) * across for shift in (0.0, side, -side)]
    weights = jnp.concatenate(weights, axis=0).astype(jnp.bfloat16)
    inverse = 1.0 / var
    copies[3].wait()
    rows = cells_ref[...].reshape(lon_dev * lat, members)
    seen = jnp.dot(pick, rows, preferred_element_type=jnp.float32)
    terms = (value - seen) ** 2 * inverse
    high = terms.astype(jnp.bfloat16)
    rest = terms - high.astype(jnp.float32)
    middle = rest.astype(jnp.bfloat16)
    low = (rest - middle.astype(jnp.float32)).astype(jnp.bfloat16)
    sums = [jnp.dot(weights, x, preferred_element_type=jnp.float32) for x in (low, middle, high)]
    like = fold(sums, jnp.add) * (1.0 / (HALO + 1) ** 2)
    centre = jnp.sum(seen, axis=1, keepdims=True) * (1.0 / members)
    spread = jnp.sum((seen - centre) ** 2, axis=1, keepdims=True) * (1.0 / (members - 1))
    innovation = (value - centre) ** 2 / (var + spread)
    part = jnp.sum(innovation, axis=0, keepdims=True)
    part_ref[...] = jnp.broadcast_to(part, part_ref.shape)
    own_ref[...] = like[:blocks]
    near_ref[edge:, :] = in_parts(like[blocks : 2 * blocks], part)
    far_ref[edge:, :] = in_parts(like[2 * blocks :], jnp.zeros_like(part))
    for copy in copies[4:]:
        copy.wait()


def observe(odd, state, obs_index, obs_value, obs_var):
    lon_dev, nvar, lat, members = state.shape
    nobs = obs_index.size
    assert lat // REGION == TILE
    like = jax.ShapeDtypeStruct((lat // REGION, members), jnp.float32)
    payload = pltpu.VMEM((HALO * nvar * lat + 4 * TILE, members), state.dtype)
    part = jax.ShapeDtypeStruct((TILE, 128), jnp.float32)
    arrays = state, state.reshape(-1, members), obs_index[None], obs_value[None], obs_var[None]
    return pl.pallas_call(
        observe_kernel,
        in_specs=[pl.BlockSpec(memory_space=pltpu.SMEM)]
        + [pl.BlockSpec(memory_space=pltpu.HBM)] * len(arrays),
        out_specs=[pl.BlockSpec(memory_space=pltpu.VMEM)] * 4,
        out_shape=[like, payload, payload, part],
        scratch_shapes=[
            pltpu.VMEM((lon_dev, lat, members), state.dtype),
            pltpu.VMEM((1, nobs), jnp.int32),
            pltpu.VMEM((1, nobs), jnp.float32),
            pltpu.VMEM((1, nobs), jnp.float32),
            pltpu.SemaphoreType.DMA((6,)),
        ],
        compiler_params=pltpu.CompilerParams(vmem_limit_bytes=16 * 2**20),
        name="observe",
    )(odd, *[pltpu.with_memory_space_constraint(x, pltpu.HBM) for x in arrays])


def slab_of(ref, lat, at):
    size = PAIR * TILE
    planes = ref.shape[0] // lat
    rows = [ref[i * lat + at * size : i * lat + (at + 1) * size, :] for i in range(planes)]
    return jnp.stack(rows).astype(jnp.float32)


def pair_tiles(load, step, steps):
    here = load(step)
    none = jnp.zeros_like(here[:, :TILE])
    before = load(step - 1)[:, TILE:] if step else none
    after = load(step + 1)[:, :TILE] if step + 1 < steps else none
    return before, here[:, :TILE], here[:, TILE:], after


def halo_weights(to_left):
    steps = [jnp.float32(1.0) - jnp.float32(d) / jnp.float32(HALO + 1) for d in range(HALO, 0, -1)]
    return [jnp.where(to_left, x, y) for x, y in zip(steps, steps[::-1])]


def turn(tile):
    return tile.reshape(-1, tile.shape[-1]).astype(jnp.bfloat16).T


def gram_of(tiles, turned, weights):
    planes, _, members = tiles[0].shape
    depth = planes * TILE
    row = lax.broadcasted_iota(jnp.int32, (TILE, members), 0)
    upper = row < HALO
    rowf = row.astype(jnp.float32)
    edge = line_weight(jnp.where(upper, rowf + (HALO + REGION), rowf - HALO))
    lane = lax.broadcasted_iota(jnp.int32, (1, depth), 1) & (TILE - 1)
    take_next = jnp.where(lane < HALO, 1.0, 0.0).astype(jnp.bfloat16)
    take_prev = jnp.where(lane < HALO, 0.0, 1.0).astype(jnp.bfloat16)
    grams = []
    for at in (1, 2):
        margin = jnp.where(upper, tiles[at + 1], tiles[at - 1])
        main_rows, margin_rows = [], []
        for plane, weight in enumerate(weights):
            own = tiles[at][plane]
            main_rows.append(own if weight is None else own * weight)
            margin_rows.append(margin[plane] * (edge if weight is None else edge * weight))
        weighted = jnp.stack(main_rows + margin_rows)
        weighted = weighted.reshape(2 * depth, members).astype(jnp.bfloat16)
        margin = turned[at + 1] * take_next + turned[at - 1] * take_prev
        both = jnp.concatenate([turned[at], margin], axis=1)
        grams.append(jnp.dot(both, weighted, preferred_element_type=jnp.float32))
    return grams


def slab_copies(src_ref, dst_ref, sems, only=None):
    size = PAIR * TILE

    def slab(at):
        rows = pl.ds(pl.multiple_of(at * size, size), size)
        return pltpu.make_async_copy(
            src_ref.at[:, :, rows, :], dst_ref.at[:, :, rows, :], sems.at[at]
        )

    return slab(only) if only is not None else [slab(i) for i in range(src_ref.shape[2] // size)]


def own_gram_kernel(odd_ref, state_hbm_ref, near_ref, own_ref, *refs):
    first_ref, last_hbm_ref, like_ref, state_ref, last_ref, sems, last_sem = refs
    lon_dev, nvar, lat, members = state_ref.shape
    kept = first_ref.shape[0]
    steps = lat // (PAIR * TILE)
    copies = slab_copies(state_hbm_ref, state_ref, sems)
    for copy in copies:
        copy.start()
    like_ref[...] = own_ref[...] + like_rows(near_ref[near_ref.shape[0] - 4 * TILE :, :])
    size = PAIR * TILE

    def load(step):
        own = state_ref[:, :, step * size : (step + 1) * size, :].astype(jnp.float32)
        own = own.reshape(lon_dev * nvar, size, members)
        return jnp.concatenate([own, slab_of(near_ref, lat, step)], axis=0)

    weights = [None] * (lon_dev * nvar)
    weights += [w for w in halo_weights(odd_ref[0] == 1) for _ in range(nvar)]
    for copy in copies:
        copy.wait()
    slabs = [load(step) for step in range(steps)]

    def put(region, gram):
        if region < kept:
            first_ref[region] = gram
        else:
            last_ref[region - kept] = gram

    add_grams(slabs, weights, put)
    keep = pltpu.make_async_copy(last_ref, last_hbm_ref, last_sem)
    keep.start()
    keep.wait()


def add_grams(slabs, weights, put):
    none = jnp.zeros_like(slabs[0][:, :TILE])
    tiles = [none]
    for slab in slabs:
        tiles += [slab[:, :TILE], slab[:, TILE:]]
    tiles.append(none)
    turned = [turn(tile) for tile in tiles[1:-1]]
    turned = [jnp.zeros_like(turned[0])] + turned + [jnp.zeros_like(turned[0])]
    for pair in range(len(slabs)):
        window = slice(pair * PAIR, pair * PAIR + PAIR + 2)
        grams = gram_of(tiles[window], turned[window], weights)
        for at, gram in enumerate(grams):
            put(pair * PAIR + at, gram)


def own_gram(odd, state, near, own):
    _, _, lat, members = state.shape
    kept = lat // REGION - PAIR
    vmem = pl.BlockSpec(memory_space=pltpu.VMEM)
    return pl.pallas_call(
        own_gram_kernel,
        in_specs=[
            pl.BlockSpec(memory_space=pltpu.SMEM),
            pl.BlockSpec(memory_space=pltpu.HBM),
            vmem,
            vmem,
        ],
        out_specs=[vmem, pl.BlockSpec(memory_space=pltpu.HBM), vmem],
        out_shape=[
            jax.ShapeDtypeStruct((kept, members, members), jnp.float32),
            pltpu.HBM((PAIR, members, members), jnp.float32),
            jax.ShapeDtypeStruct(own.shape, jnp.float32),
        ],
        scratch_shapes=[
            pltpu.VMEM(state.shape, state.dtype),
            pltpu.VMEM((PAIR, members, members), jnp.float32),
            pltpu.SemaphoreType.DMA((lat // (PAIR * TILE),)),
            pltpu.SemaphoreType.DMA,
        ],
        compiler_params=pltpu.CompilerParams(vmem_limit_bytes=24 * 2**20),
        name="own_gram",
    )(odd, pltpu.with_memory_space_constraint(state, pltpu.HBM), near, own)


def halves(ref, region, rows):
    members = ref.shape[-1]
    return [ref[region, rows, at : at + 128] for at in range(0, members, 128)]


def diagonal(gram_ref, region):
    members = gram_ref.shape[-1]
    across = [None] * (members // 128)
    down = []
    for start in range(0, members, ROWS):
        lane = start // 128
        gram = gram_ref[region, pl.ds(start, ROWS), lane * 128 : lane * 128 + 128]
        i = lax.broadcasted_iota(jnp.int32, gram.shape, 0) + start
        j = lax.broadcasted_iota(jnp.int32, gram.shape, 1) + lane * 128
        kept = jnp.where(i == j, gram, 0.0)
        down.append(jnp.broadcast_to(jnp.sum(kept, axis=1, keepdims=True), gram.shape))
        part = jnp.sum(kept.reshape(ROWS // TILE, TILE, 128), axis=0)
        across[lane] = part if across[lane] is None else across[lane] + part
    return [jnp.sum(x, axis=0, keepdims=True) for x in across], down


def kernel_matrices(regions, gram_ref, kernel_ref, mass_ref, scale):
    members = gram_ref.shape[-1]
    for region in regions:
        across, down = diagonal(gram_ref, region)
        across = [0.5 * LIFT - x * scale for x in across]
        masses = [0.0 for _ in across]
        for i, start in enumerate(range(0, members, ROWS)):
            rows = pl.ds(start, ROWS)
            base = 0.5 * LIFT - down[i] * scale
            for lane, (gram, x) in enumerate(zip(halves(gram_ref, region, rows), across)):
                part = jnp.exp2(gram * (2.0 * scale) + base + x)
                kernel_ref[region, rows, lane * 128 : lane * 128 + 128] = part
                part = jnp.sum(part.reshape(ROWS // TILE, TILE, 128), axis=0)
                masses[lane] = masses[lane] + part
        masses = [jnp.sum(x, axis=0, keepdims=True) for x in masses]
        mass_ref[region] = jnp.concatenate(masses, axis=1)


def transports_scaled(kernel_ref, weights, mass_ref, use):
    regions = range(kernel_ref.shape[0])
    members = kernel_ref.shape[-1]
    starts = range(0, members, ROWS)
    lanes = range(members // 128)
    share = 2.0**MASS / members

    def lane_parts(row):
        return [row[:, lane * 128 : lane * 128 + 128] for lane in lanes]

    def settle(totals, region):
        return [w / x for w, x in zip(lane_parts(weights[region : region + 1]), totals)]

    def masses_of(region, rows, factor):
        parts = [k * f for k, f in zip(halves(kernel_ref, region, rows), factor)]
        mass = jnp.sum(fold(parts, jnp.add), axis=1, keepdims=True)
        mass = jnp.broadcast_to(mass, (ROWS, 128))
        return parts, mass, pl.reciprocal(mass, approx=True)

    def sweep(least_i, least_j, factors):
        next_i, next_j, next_factors = [], [], []
        for region, low_i, low_j, factor in zip(regions, least_i, least_j, factors):
            totals = [None for _ in lanes]
            for start in starts:
                rows = pl.ds(start, ROWS)
                _, mass, ratio = masses_of(region, rows, factor)
                low_j = jnp.minimum(low_j, mass)
                for lane, kernel in enumerate(halves(kernel_ref, region, rows)):
                    part = jnp.sum((kernel * ratio).reshape(ROWS // TILE, TILE, 128), axis=0)
                    totals[lane] = part if totals[lane] is None else totals[lane] + part
            totals = [jnp.sum(x, axis=0, keepdims=True) * share for x in totals]
            next_i.append(jnp.minimum(low_i, fold(totals, jnp.minimum)))
            next_j.append(low_j)
            next_factors.append(settle(totals, region))
        return next_i, next_j, next_factors

    masses = [lane_parts(mass_ref[region]) for region in regions]
    most = fold([fold(x, jnp.maximum) for x in masses], jnp.maximum)
    totals = [[x * 2.0**START for x in mass] for mass in masses]
    least_i = [fold(x, jnp.minimum) for x in totals]
    least_j = [jnp.full((ROWS, 128), 1e30, jnp.float32) for _ in regions]
    factors = [settle(x, region) for x, region in zip(totals, regions)]
    for _ in range(SWEEPS - 1):
        least_i, least_j, factors = sweep(least_i, least_j, factors)
    moves, last_j = [], []
    for region, low_j, factor in zip(regions, least_j, factors):
        blocks = []
        for start in starts:
            parts, mass, ratio = masses_of(region, pl.ds(start, ROWS), factor)
            low_j = jnp.minimum(low_j, mass)
            blocks.append(jnp.concatenate([x * ratio for x in parts], axis=1).astype(jnp.bfloat16))
        moves.append(jnp.concatenate(blocks, axis=0))
        last_j.append(low_j)
        if len(moves) == PAIR:
            use(region // PAIR, moves)
            moves = []
    least_i = fold(least_i, jnp.minimum)
    return jnp.min(least_i), jnp.min(fold(last_j, jnp.minimum)), jnp.max(most)


def transport_logs(gram, logw, scale):
    members = gram.shape[-1]
    j = lax.broadcasted_iota(jnp.int32, gram.shape, 0)
    i = lax.broadcasted_iota(jnp.int32, gram.shape, 1)
    kept = jnp.where(i == j, gram, 0.0)
    down = jnp.sum(kept, axis=1, keepdims=True)
    across = jnp.sum(kept, axis=0, keepdims=True)
    cost = (down + across - 2.0 * gram) * scale
    pot_g = jnp.zeros((members, 1), jnp.float32)
    for sweep in range(SWEEPS):
        term = pot_g - cost
        top = jnp.max(term, axis=0, keepdims=True)
        pot_f = logw - top - jnp.log(jnp.sum(jnp.exp2(term - top), axis=0, keepdims=True)) * LOG2E
        term = pot_f - cost
        top = jnp.max(term, axis=1, keepdims=True)
        pot_g = -math.log2(members) - top
        pot_g = pot_g - jnp.log(jnp.sum(jnp.exp2(term - top), axis=1, keepdims=True)) * LOG2E
    return (members * jnp.exp2(pot_f + pot_g - cost)).astype(jnp.bfloat16)


def transform(state_ref, pair, moves):
    lon_dev, nvar, _, members = state_ref.shape
    size = PAIR * TILE
    own = state_ref[:, :, pair * size : (pair + 1) * size, :].astype(jnp.float32)
    parts = []
    for region, move in enumerate(moves):
        cells = own[:, :, region * TILE : (region + 1) * TILE].astype(jnp.bfloat16)
        cells = cells.reshape(lon_dev * nvar * TILE, members)
        moved = lax.dot_general(
            cells, move, (((1,), (1,)), ((), ())), preferred_element_type=jnp.float32
        )
        parts.append(moved.reshape(lon_dev, nvar, TILE, members))
    return jnp.concatenate(parts, axis=2).astype(jnp.bfloat16)


def analyse_kernel(count, scale, *refs):
    odd_ref, halo_ref, first_ref, last_hbm_ref, state_hbm_ref, like_ref, sums_ref = refs[:7]
    out_ref, gram_ref, kernel_ref, mass_ref, result_ref, state_ref, last_ref = refs[7:14]
    out_sems, state_sems, last_sem = refs[14:]
    kept = first_ref.shape[0]
    fetch_last = pltpu.make_async_copy(last_hbm_ref, last_ref, last_sem)
    fetch_last.start()
    regions, members, _ = gram_ref.shape
    pairs = regions // PAIR
    size = PAIR * TILE
    lat = regions * REGION
    fetches = slab_copies(state_hbm_ref, state_ref, state_sems)
    for copy in fetches:
        copy.start()

    def send(pair):
        rows = pl.ds(pair * size, size)
        return pltpu.make_async_copy(
            result_ref.at[pair], out_ref.at[:, :, rows, :], out_sems.at[pair]
        )

    misfit = like_ref[...] + like_rows(halo_ref[halo_ref.shape[0] - 4 * TILE :, :])
    misfit = misfit - jnp.min(misfit, axis=1, keepdims=True)
    factor = (-0.5 * LOG2E * count) / jnp.sum(sums_ref[...], axis=0, keepdims=True)
    like = misfit * jnp.concatenate([factor] * (members // 128), axis=1)
    weights = jnp.exp2(like + MASS)
    norm = jnp.sum(weights, axis=1, keepdims=True) * 2.0**-MASS
    weights = weights / norm

    planes = halo_ref.shape[0] // lat
    halo = [w for w in halo_weights(odd_ref[0] == 0) for _ in range(planes // HALO)]
    slabs = [slab_of(halo_ref, lat, at) for at in range(lat // size)]

    def put(region, gram):
        if region < kept:
            gram_ref[region] = first_ref[region] + gram
        else:
            if region == kept:
                fetch_last.wait()
            gram_ref[region] = last_ref[region - kept] + gram

    add_grams(slabs, halo, put)
    kernel_matrices(range(regions), gram_ref, kernel_ref, mass_ref, scale)

    def use(pair, moves):
        if pair == 0:
            for copy in fetches:
                copy.wait()
        result_ref[pair] = transform(state_ref, pair, moves)
        send(pair).start()

    row, col, most = transports_scaled(kernel_ref, weights, mass_ref, use)
    sound = (row >= 2.0**-24) & (col >= 2.0**-30) & (most <= 2.0**30) & (row * col >= 2.0**-34)
    for pair in range(pairs):
        send(pair).wait()

    @pl.when(jnp.logical_not(sound))
    def _():
        logw = like - jnp.log(norm) * LOG2E
        for pair in range(pairs):
            again = [
                transport_logs(gram_ref[region], logw[region : region + 1], scale)
                for region in range(pair * PAIR, (pair + 1) * PAIR)
            ]
            result_ref[pair] = transform(state_ref, pair, again)
            send(pair).start()
            send(pair).wait()


def analyse(odd, halo, first, last, state, like, sums, count, scale):
    lon_dev, nvar, lat, members = state.shape
    regions = lat // REGION
    pairs = regions // PAIR
    vmem = pl.BlockSpec(memory_space=pltpu.VMEM)
    return pl.pallas_call(
        functools.partial(analyse_kernel, count, scale),
        in_specs=[
            pl.BlockSpec(memory_space=pltpu.SMEM),
            vmem,
            vmem,
            pl.BlockSpec(memory_space=pltpu.HBM),
            pl.BlockSpec(memory_space=pltpu.HBM),
            vmem,
            vmem,
        ],
        out_specs=pl.BlockSpec(memory_space=pl.ANY),
        out_shape=jax.ShapeDtypeStruct(state.shape, state.dtype),
        scratch_shapes=[
            pltpu.VMEM((regions, members, members), jnp.float32),
            pltpu.VMEM((regions, members, members), jnp.float32),
            pltpu.VMEM((regions, 1, members), jnp.float32),
            pltpu.VMEM((pairs, lon_dev, nvar, PAIR * TILE, members), state.dtype),
            pltpu.VMEM(state.shape, state.dtype),
            pltpu.VMEM(last.shape, jnp.float32),
            pltpu.SemaphoreType.DMA((pairs,)),
            pltpu.SemaphoreType.DMA((pairs,)),
            pltpu.SemaphoreType.DMA,
        ],
        compiler_params=pltpu.CompilerParams(vmem_limit_bytes=24 * 2**20),
        name="analyse",
    )(
        odd,
        halo,
        first,
        *[pltpu.with_memory_space_constraint(x, pltpu.HBM) for x in (last, state)],
        like,
        sums,
    )


def on_device(state, obs_index, obs_value, obs_var):
    nvar = state.shape[1]
    count = lax.axis_size("lon")
    odd = (lax.axis_index("lon") & 1).astype(jnp.int32).reshape(1)
    near_pairs = [(i, i ^ 1) for i in range(count)]
    far_pairs = [(i, (i + 1 if i % 2 else i - 1) % count) for i in range(count)]
    own_like, for_near, for_far, part = observe(odd, state, obs_index, obs_value, obs_var)
    far = lax.ppermute(for_far, "lon", far_pairs)
    near = lax.ppermute(for_near, "lon", near_pairs)
    start = near.shape[0] - TILE
    part = part[0] + jnp.sum(near[start : start + 3, :128].astype(jnp.float32), axis=0)
    sums = lax.all_to_all(
        jnp.broadcast_to(part, (count // 2, 128)),
        "lon",
        0,
        0,
        axis_index_groups=[[i for i in range(count) if (i ^ i >> 1) & 1 == kind] for kind in range(2)],
        tiled=True,
    )
    offsets = range(REGION + 2 * HALO)
    line = [1.0 - max(0, HALO - p, p - (HALO + REGION - 1)) / (HALO + 1) for p in offsets]
    scale = LOG2E / EPS / (nvar * sum(line) ** 2)
    first, last, like = own_gram(odd, state, near, own_like)
    nobs = float(obs_index.shape[0] * count)
    return analyse(odd, far, first, last, state, like, sums, nobs, scale)


def solution(mesh):
    return jax.shard_map(
        on_device,
        mesh=mesh,
        in_specs=(
            P(("ens", "lon"), None, None, None),
            P(("ens", "lon")),
            P(("ens", "lon")),
            P(("ens", "lon")),
        ),
        out_specs=P(("ens", "lon"), None, None, None),
        check_vma=False,
    )
```

```python
import functools
import math

import jax
import jax.numpy as jnp
from jax import lax
from jax.experimental import pallas as pl
from jax.experimental.pallas import tpu as pltpu
from jax.sharding import PartitionSpec as P

REGION = 8
HALO = 4
SWEEPS = 4
EPS = 0.05
TILE = 8
PAIR = 2
LOG2E = 1.4426950408889634
ROWS = 64
LIFT, START, MASS = 20, -10, 60


def fold(values, op):
    out = values[0]
    for value in values[1:]:
        out = op(out, value)
    return out


def line_weight(place):
    dist = jnp.maximum(0.0, jnp.maximum(HALO - place, place - (HALO + REGION - 1)))
    inside = (place >= 0) & (place < REGION + 2 * HALO)
    return jnp.where(inside, 1.0 - dist / (HALO + 1), 0.0)


def like_rows(rows):
    rows = rows.astype(jnp.float32)
    return rows[:TILE] + rows[TILE : 2 * TILE] + rows[2 * TILE : 3 * TILE]


def in_parts(values, extra):
    below = lax.broadcasted_iota(jnp.int32, values.shape, 0)
    extra_high = extra.astype(jnp.bfloat16).astype(jnp.float32)
    extra_middle = (extra - extra_high).astype(jnp.bfloat16).astype(jnp.float32)
    extra_low = extra - extra_high - extra_middle
    last = jnp.where(below == 0, extra_high, jnp.where(below == 1, extra_middle, extra_low))
    last = jnp.where(below < 3, last, 0.0)
    high = values.astype(jnp.bfloat16).astype(jnp.float32)
    middle = (values - high).astype(jnp.bfloat16).astype(jnp.float32)
    low = values - high - middle
    return jnp.concatenate([high, middle, low, last], axis=0).astype(jnp.bfloat16)


def steps_inside(place):
    dist = jnp.maximum(0.0, jnp.maximum(HALO - place, place - (HALO + REGION - 1)))
    inside = (place >= 0) & (place < REGION + 2 * HALO)
    return jnp.where(inside, HALO + 1 - dist, 0.0)


def observe_kernel(*refs):
    odd_ref, state_ref, rows_ref = refs[:3]
    own_ref, near_ref, far_ref, part_ref = refs[6:10]
    cells_ref, index_ref, value_ref, var_ref, sems = refs[10:]
    lon_dev, lat, members = cells_ref.shape
    nobs = index_ref.shape[1]
    edge = rows_ref.shape[0] // lon_dev * HALO
    last = rows_ref.shape[0] - edge
    far_at = pl.multiple_of(odd_ref[0] * last, 16)
    near_at = pl.multiple_of(last - far_at, 16)
    fetches = [
        (refs[3], index_ref),
        (refs[4], value_ref),
        (refs[5], var_ref),
        (state_ref.at[:, 0], cells_ref),
        (rows_ref.at[pl.ds(far_at, edge), :], far_ref.at[pl.ds(0, edge), :]),
        (rows_ref.at[pl.ds(near_at, edge), :], near_ref.at[pl.ds(0, edge), :]),
    ]
    copies = [
        pltpu.make_async_copy(src, dst, sems.at[i]) for i, (src, dst) in enumerate(fetches)
    ]
    for copy in copies:
        copy.start()
    for copy in copies[:3]:
        copy.wait()
    index = index_ref[...]
    sub = lax.broadcasted_iota(jnp.int32, (TILE, nobs), 0)
    table = jnp.where(
        sub == 0,
        index.astype(jnp.float32),
        jnp.where(sub == 1, value_ref[...], var_ref[...]),
    ).T
    index_col = table[:, 0:1].astype(jnp.int32)
    value = table[:, 1:2]
    var = table[:, 2:3]
    pick = index_col == lax.broadcasted_iota(jnp.int32, (nobs, lon_dev * lat), 1)
    pick = jnp.where(pick, 1.0, 0.0).astype(jnp.bfloat16)
    lon = (index // lat).astype(jnp.float32)
    along = index.astype(jnp.float32) - lon * lat
    blocks = own_ref.shape[0]
    block = lax.broadcasted_iota(jnp.int32, (blocks, nobs), 0).astype(jnp.float32)
    across = steps_inside(along - REGION * block + HALO)
    side = jnp.where(odd_ref[0] == 1, float(REGION), float(-REGION))
    weights = [steps_inside(lon + (HALO + shift)) * across for shift in (0.0, side, -side)]
    weights = jnp.concatenate(weights, axis=0).astype(jnp.bfloat16)
    inverse = 1.0 / var
    copies[3].wait()
    rows = cells_ref[...].reshape(lon_dev * lat, members)
    seen = jnp.dot(pick, rows, preferred_element_type=jnp.float32)
    terms = (value - seen) ** 2 * inverse
    high = terms.astype(jnp.bfloat16)
    rest = terms - high.astype(jnp.float32)
    middle = rest.astype(jnp.bfloat16)
    low = (rest - middle.astype(jnp.float32)).astype(jnp.bfloat16)
    sums = [jnp.dot(weights, x, preferred_element_type=jnp.float32) for x in (low, middle, high)]
    like = fold(sums, jnp.add) * (1.0 / (HALO + 1) ** 2)
    centre = jnp.sum(seen, axis=1, keepdims=True) * (1.0 / members)
    spread = jnp.sum((seen - centre) ** 2, axis=1, keepdims=True) * (1.0 / (members - 1))
    innovation = (value - centre) ** 2 / (var + spread)
    part = jnp.sum(innovation, axis=0, keepdims=True)
    part_ref[...] = jnp.broadcast_to(part, part_ref.shape)
    own_ref[...] = like[:blocks]
    near_ref[edge:, :] = in_parts(like[blocks : 2 * blocks], part)
    far_ref[edge:, :] = in_parts(like[2 * blocks :], jnp.zeros_like(part))
    for copy in copies[4:]:
        copy.wait()


def observe(odd, state, obs_index, obs_value, obs_var):
    lon_dev, nvar, lat, members = state.shape
    nobs = obs_index.size
    assert lat // REGION == TILE
    like = jax.ShapeDtypeStruct((lat // REGION, members), jnp.float32)
    payload = pltpu.VMEM((HALO * nvar * lat + 4 * TILE, members), state.dtype)
    part = jax.ShapeDtypeStruct((TILE, 128), jnp.float32)
    arrays = state, state.reshape(-1, members), obs_index[None], obs_value[None], obs_var[None]
    return pl.pallas_call(
        observe_kernel,
        in_specs=[pl.BlockSpec(memory_space=pltpu.SMEM)]
        + [pl.BlockSpec(memory_space=pltpu.HBM)] * len(arrays),
        out_specs=[pl.BlockSpec(memory_space=pltpu.VMEM)] * 4,
        out_shape=[like, payload, payload, part],
        scratch_shapes=[
            pltpu.VMEM((lon_dev, lat, members), state.dtype),
            pltpu.VMEM((1, nobs), jnp.int32),
            pltpu.VMEM((1, nobs), jnp.float32),
            pltpu.VMEM((1, nobs), jnp.float32),
            pltpu.SemaphoreType.DMA((6,)),
        ],
        compiler_params=pltpu.CompilerParams(vmem_limit_bytes=16 * 2**20),
        name="observe",
    )(odd, *[pltpu.with_memory_space_constraint(x, pltpu.HBM) for x in arrays])


def slab_of(ref, lat, at):
    size = PAIR * TILE
    planes = ref.shape[0] // lat
    rows = [ref[i * lat + at * size : i * lat + (at + 1) * size, :] for i in range(planes)]
    return jnp.stack(rows).astype(jnp.float32)


def pair_tiles(load, step, steps):
    here = load(step)
    none = jnp.zeros_like(here[:, :TILE])
    before = load(step - 1)[:, TILE:] if step else none
    after = load(step + 1)[:, :TILE] if step + 1 < steps else none
    return before, here[:, :TILE], here[:, TILE:], after


def halo_weights(to_left):
    steps = [jnp.float32(1.0) - jnp.float32(d) / jnp.float32(HALO + 1) for d in range(HALO, 0, -1)]
    return [jnp.where(to_left, x, y) for x, y in zip(steps, steps[::-1])]


def turn(tile):
    return tile.reshape(-1, tile.shape[-1]).astype(jnp.bfloat16).T


def gram_of(tiles, turned, weights):
    planes, _, members = tiles[0].shape
    depth = planes * TILE
    row = lax.broadcasted_iota(jnp.int32, (TILE, members), 0)
    upper = row < HALO
    rowf = row.astype(jnp.float32)
    edge = line_weight(jnp.where(upper, rowf + (HALO + REGION), rowf - HALO))
    lane = lax.broadcasted_iota(jnp.int32, (1, depth), 1) & (TILE - 1)
    take_next = jnp.where(lane < HALO, 1.0, 0.0).astype(jnp.bfloat16)
    take_prev = jnp.where(lane < HALO, 0.0, 1.0).astype(jnp.bfloat16)
    grams = []
    for at in (1, 2):
        margin = jnp.where(upper, tiles[at + 1], tiles[at - 1])
        main_rows, margin_rows = [], []
        for plane, weight in enumerate(weights):
            own = tiles[at][plane]
            main_rows.append(own if weight is None else own * weight)
            margin_rows.append(margin[plane] * (edge if weight is None else edge * weight))
        weighted = jnp.stack(main_rows + margin_rows)
        weighted = weighted.reshape(2 * depth, members).astype(jnp.bfloat16)
        margin = turned[at + 1] * take_next + turned[at - 1] * take_prev
        both = jnp.concatenate([turned[at], margin], axis=1)
        grams.append(jnp.dot(both, weighted, preferred_element_type=jnp.float32))
    return grams


def slab_copies(src_ref, dst_ref, sems, only=None):
    size = PAIR * TILE

    def slab(at):
        rows = pl.ds(pl.multiple_of(at * size, size), size)
        return pltpu.make_async_copy(
            src_ref.at[:, :, rows, :], dst_ref.at[:, :, rows, :], sems.at[at]
        )

    return slab(only) if only is not None else [slab(i) for i in range(src_ref.shape[2] // size)]


def own_gram_kernel(odd_ref, state_hbm_ref, near_ref, own_ref, *refs):
    first_ref, last_hbm_ref, like_ref, state_ref, last_ref, sems, last_sem = refs
    lon_dev, nvar, lat, members = state_ref.shape
    kept = first_ref.shape[0]
    steps = lat // (PAIR * TILE)
    copies = slab_copies(state_hbm_ref, state_ref, sems)
    for copy in copies:
        copy.start()
    like_ref[...] = own_ref[...] + like_rows(near_ref[near_ref.shape[0] - 4 * TILE :, :])
    size = PAIR * TILE

    def load(step):
        own = state_ref[:, :, step * size : (step + 1) * size, :].astype(jnp.float32)
        own = own.reshape(lon_dev * nvar, size, members)
        return jnp.concatenate([own, slab_of(near_ref, lat, step)], axis=0)

    weights = [None] * (lon_dev * nvar)
    weights += [w for w in halo_weights(odd_ref[0] == 1) for _ in range(nvar)]
    for copy in copies:
        copy.wait()
    slabs = [load(step) for step in range(steps)]

    def put(region, gram):
        if region < kept:
            first_ref[region] = gram
        else:
            last_ref[region - kept] = gram

    add_grams(slabs, weights, put)
    keep = pltpu.make_async_copy(last_ref, last_hbm_ref, last_sem)
    keep.start()
    keep.wait()


def add_grams(slabs, weights, put):
    none = jnp.zeros_like(slabs[0][:, :TILE])
    tiles = [none]
    for slab in slabs:
        tiles += [slab[:, :TILE], slab[:, TILE:]]
    tiles.append(none)
    turned = [turn(tile) for tile in tiles[1:-1]]
    turned = [jnp.zeros_like(turned[0])] + turned + [jnp.zeros_like(turned[0])]
    for pair in range(len(slabs)):
        window = slice(pair * PAIR, pair * PAIR + PAIR + 2)
        grams = gram_of(tiles[window], turned[window], weights)
        for at, gram in enumerate(grams):
            put(pair * PAIR + at, gram)


def own_gram(odd, state, near, own):
    _, _, lat, members = state.shape
    kept = lat // REGION - PAIR
    vmem = pl.BlockSpec(memory_space=pltpu.VMEM)
    return pl.pallas_call(
        own_gram_kernel,
        in_specs=[
            pl.BlockSpec(memory_space=pltpu.SMEM),
            pl.BlockSpec(memory_space=pltpu.HBM),
            vmem,
            vmem,
        ],
        out_specs=[vmem, pl.BlockSpec(memory_space=pltpu.HBM), vmem],
        out_shape=[
            jax.ShapeDtypeStruct((kept, members, members), jnp.float32),
            pltpu.HBM((PAIR, members, members), jnp.float32),
            jax.ShapeDtypeStruct(own.shape, jnp.float32),
        ],
        scratch_shapes=[
            pltpu.VMEM(state.shape, state.dtype),
            pltpu.VMEM((PAIR, members, members), jnp.float32),
            pltpu.SemaphoreType.DMA((lat // (PAIR * TILE),)),
            pltpu.SemaphoreType.DMA,
        ],
        compiler_params=pltpu.CompilerParams(vmem_limit_bytes=24 * 2**20),
        name="own_gram",
    )(odd, pltpu.with_memory_space_constraint(state, pltpu.HBM), near, own)


def halves(ref, region, rows):
    members = ref.shape[-1]
    return [ref[region, rows, at : at + 128] for at in range(0, members, 128)]


def diagonal(gram_ref, region):
    members = gram_ref.shape[-1]
    across = [None] * (members // 128)
    down = []
    for start in range(0, members, ROWS):
        lane = start // 128
        gram = gram_ref[region, pl.ds(start, ROWS), lane * 128 : lane * 128 + 128]
        i = lax.broadcasted_iota(jnp.int32, gram.shape, 0) + start
        j = lax.broadcasted_iota(jnp.int32, gram.shape, 1) + lane * 128
        kept = jnp.where(i == j, gram, 0.0)
        down.append(jnp.broadcast_to(jnp.sum(kept, axis=1, keepdims=True), gram.shape))
        part = jnp.sum(kept.reshape(ROWS // TILE, TILE, 128), axis=0)
        across[lane] = part if across[lane] is None else across[lane] + part
    return [jnp.sum(x, axis=0, keepdims=True) for x in across], down


def kernel_matrices(regions, gram_ref, kernel_ref, mass_ref, scale):
    members = gram_ref.shape[-1]
    for region in regions:
        across, down = diagonal(gram_ref, region)
        across = [0.5 * LIFT - x * scale for x in across]
        masses = [0.0 for _ in across]
        for i, start in enumerate(range(0, members, ROWS)):
            rows = pl.ds(start, ROWS)
            base = 0.5 * LIFT - down[i] * scale
            for lane, (gram, x) in enumerate(zip(halves(gram_ref, region, rows), across)):
                part = jnp.exp2(gram * (2.0 * scale) + base + x)
                kernel_ref[region, rows, lane * 128 : lane * 128 + 128] = part
                part = jnp.sum(part.reshape(ROWS // TILE, TILE, 128), axis=0)
                masses[lane] = masses[lane] + part
        masses = [jnp.sum(x, axis=0, keepdims=True) for x in masses]
        mass_ref[region] = jnp.concatenate(masses, axis=1)


def transports_scaled(kernel_ref, weights, mass_ref, use):
    regions = range(kernel_ref.shape[0])
    members = kernel_ref.shape[-1]
    starts = range(0, members, ROWS)
    lanes = range(members // 128)
    share = 2.0**MASS / members

    def lane_parts(row):
        return [row[:, lane * 128 : lane * 128 + 128] for lane in lanes]

    def settle(totals, region):
        return [w / x for w, x in zip(lane_parts(weights[region : region + 1]), totals)]

    def masses_of(region, rows, factor):
        parts = [k * f for k, f in zip(halves(kernel_ref, region, rows), factor)]
        mass = jnp.sum(fold(parts, jnp.add), axis=1, keepdims=True)
        mass = jnp.broadcast_to(mass, (ROWS, 128))
        return parts, mass, pl.reciprocal(mass, approx=True)

    def sweep(least_i, least_j, factors):
        next_i, next_j, next_factors = [], [], []
        for region, low_i, low_j, factor in zip(regions, least_i, least_j, factors):
            totals = [None for _ in lanes]
            for start in starts:
                rows = pl.ds(start, ROWS)
                _, mass, ratio = masses_of(region, rows, factor)
                low_j = jnp.minimum(low_j, mass)
                for lane, kernel in enumerate(halves(kernel_ref, region, rows)):
                    part = jnp.sum((kernel * ratio).reshape(ROWS // TILE, TILE, 128), axis=0)
                    totals[lane] = part if totals[lane] is None else totals[lane] + part
            totals = [jnp.sum(x, axis=0, keepdims=True) * share for x in totals]
            next_i.append(jnp.minimum(low_i, fold(totals, jnp.minimum)))
            next_j.append(low_j)
            next_factors.append(settle(totals, region))
        return next_i, next_j, next_factors

    masses = [lane_parts(mass_ref[region]) for region in regions]
    most = fold([fold(x, jnp.maximum) for x in masses], jnp.maximum)
    totals = [[x * 2.0**START for x in mass] for mass in masses]
    least_i = [fold(x, jnp.minimum) for x in totals]
    least_j = [jnp.full((ROWS, 128), 1e30, jnp.float32) for _ in regions]
    factors = [settle(x, region) for x, region in zip(totals, regions)]
    for _ in range(SWEEPS - 1):
        least_i, least_j, factors = sweep(least_i, least_j, factors)
    moves, last_j = [], []
    for region, low_j, factor in zip(regions, least_j, factors):
        blocks = []
        for start in starts:
            parts, mass, ratio = masses_of(region, pl.ds(start, ROWS), factor)
            low_j = jnp.minimum(low_j, mass)
            blocks.append(jnp.concatenate([x * ratio for x in parts], axis=1).astype(jnp.bfloat16))
        moves.append(jnp.concatenate(blocks, axis=0))
        last_j.append(low_j)
        if len(moves) == PAIR:
            use(region // PAIR, moves)
            moves = []
    least_i = fold(least_i, jnp.minimum)
    return jnp.min(least_i), jnp.min(fold(last_j, jnp.minimum)), jnp.max(most)


def transport_logs(gram, logw, scale):
    members = gram.shape[-1]
    j = lax.broadcasted_iota(jnp.int32, gram.shape, 0)
    i = lax.broadcasted_iota(jnp.int32, gram.shape, 1)
    kept = jnp.where(i == j, gram, 0.0)
    down = jnp.sum(kept, axis=1, keepdims=True)
    across = jnp.sum(kept, axis=0, keepdims=True)
    cost = (down + across - 2.0 * gram) * scale
    pot_g = jnp.zeros((members, 1), jnp.float32)
    for sweep in range(SWEEPS):
        term = pot_g - cost
        top = jnp.max(term, axis=0, keepdims=True)
        pot_f = logw - top - jnp.log(jnp.sum(jnp.exp2(term - top), axis=0, keepdims=True)) * LOG2E
        term = pot_f - cost
        top = jnp.max(term, axis=1, keepdims=True)
        pot_g = -math.log2(members) - top
        pot_g = pot_g - jnp.log(jnp.sum(jnp.exp2(term - top), axis=1, keepdims=True)) * LOG2E
    return (members * jnp.exp2(pot_f + pot_g - cost)).astype(jnp.bfloat16)


def transform(state_ref, pair, moves):
    lon_dev, nvar, _, members = state_ref.shape
    size = PAIR * TILE
    own = state_ref[:, :, pair * size : (pair + 1) * size, :].astype(jnp.float32)
    parts = []
    for region, move in enumerate(moves):
        cells = own[:, :, region * TILE : (region + 1) * TILE].astype(jnp.bfloat16)
        cells = cells.reshape(lon_dev * nvar * TILE, members)
        moved = lax.dot_general(
            cells, move, (((1,), (1,)), ((), ())), preferred_element_type=jnp.float32
        )
        parts.append(moved.reshape(lon_dev, nvar, TILE, members))
    return jnp.concatenate(parts, axis=2).astype(jnp.bfloat16)


def analyse_kernel(count, scale, *refs):
    odd_ref, halo_ref, first_ref, last_hbm_ref, state_hbm_ref, like_ref, sums_ref = refs[:7]
    out_ref, gram_ref, kernel_ref, mass_ref, result_ref, state_ref, last_ref = refs[7:14]
    out_sems, state_sems, last_sem = refs[14:]
    kept = first_ref.shape[0]
    fetch_last = pltpu.make_async_copy(last_hbm_ref, last_ref, last_sem)
    fetch_last.start()
    regions, members, _ = gram_ref.shape
    pairs = regions // PAIR
    size = PAIR * TILE
    lat = regions * REGION
    fetches = slab_copies(state_hbm_ref, state_ref, state_sems)
    for copy in fetches:
        copy.start()

    def send(pair):
        rows = pl.ds(pair * size, size)
        return pltpu.make_async_copy(
            result_ref.at[pair], out_ref.at[:, :, rows, :], out_sems.at[pair]
        )

    misfit = like_ref[...] + like_rows(halo_ref[halo_ref.shape[0] - 4 * TILE :, :])
    misfit = misfit - jnp.min(misfit, axis=1, keepdims=True)
    factor = (-0.5 * LOG2E * count) / jnp.sum(sums_ref[...], axis=0, keepdims=True)
    like = misfit * jnp.concatenate([factor] * (members // 128), axis=1)
    weights = jnp.exp2(like + MASS)
    norm = jnp.sum(weights, axis=1, keepdims=True) * 2.0**-MASS
    weights = weights / norm

    planes = halo_ref.shape[0] // lat
    halo = [w for w in halo_weights(odd_ref[0] == 0) for _ in range(planes // HALO)]
    slabs = [slab_of(halo_ref, lat, at) for at in range(lat // size)]

    def put(region, gram):
        if region < kept:
            gram_ref[region] = first_ref[region] + gram
        else:
            if region == kept:
                kernel_matrices(range(kept), gram_ref, kernel_ref, mass_ref, scale)
                fetch_last.wait()
            gram_ref[region] = last_ref[region - kept] + gram

    add_grams(slabs, halo, put)
    kernel_matrices(range(kept, regions), gram_ref, kernel_ref, mass_ref, scale)

    def use(pair, moves):
        if pair == 0:
            for copy in fetches:
                copy.wait()
        result_ref[pair] = transform(state_ref, pair, moves)
        send(pair).start()

    row, col, most = transports_scaled(kernel_ref, weights, mass_ref, use)
    sound = (row >= 2.0**-24) & (col >= 2.0**-30) & (most <= 2.0**30) & (row * col >= 2.0**-34)
    for pair in range(pairs):
        send(pair).wait()

    @pl.when(jnp.logical_not(sound))
    def _():
        logw = like - jnp.log(norm) * LOG2E
        for pair in range(pairs):
            again = [
                transport_logs(gram_ref[region], logw[region : region + 1], scale)
                for region in range(pair * PAIR, (pair + 1) * PAIR)
            ]
            result_ref[pair] = transform(state_ref, pair, again)
            send(pair).start()
            send(pair).wait()


def analyse(odd, halo, first, last, state, like, sums, count, scale):
    lon_dev, nvar, lat, members = state.shape
    regions = lat // REGION
    pairs = regions // PAIR
    vmem = pl.BlockSpec(memory_space=pltpu.VMEM)
    return pl.pallas_call(
        functools.partial(analyse_kernel, count, scale),
        in_specs=[
            pl.BlockSpec(memory_space=pltpu.SMEM),
            vmem,
            vmem,
            pl.BlockSpec(memory_space=pltpu.HBM),
            pl.BlockSpec(memory_space=pltpu.HBM),
            vmem,
            vmem,
        ],
        out_specs=pl.BlockSpec(memory_space=pl.ANY),
        out_shape=jax.ShapeDtypeStruct(state.shape, state.dtype),
        scratch_shapes=[
            pltpu.VMEM((regions, members, members), jnp.float32),
            pltpu.VMEM((regions, members, members), jnp.float32),
            pltpu.VMEM((regions, 1, members), jnp.float32),
            pltpu.VMEM((pairs, lon_dev, nvar, PAIR * TILE, members), state.dtype),
            pltpu.VMEM(state.shape, state.dtype),
            pltpu.VMEM(last.shape, jnp.float32),
            pltpu.SemaphoreType.DMA((pairs,)),
            pltpu.SemaphoreType.DMA((pairs,)),
            pltpu.SemaphoreType.DMA,
        ],
        compiler_params=pltpu.CompilerParams(vmem_limit_bytes=24 * 2**20),
        name="analyse",
    )(
        odd,
        halo,
        first,
        *[pltpu.with_memory_space_constraint(x, pltpu.HBM) for x in (last, state)],
        like,
        sums,
    )


def on_device(state, obs_index, obs_value, obs_var):
    nvar = state.shape[1]
    count = lax.axis_size("lon")
    odd = (lax.axis_index("lon") & 1).astype(jnp.int32).reshape(1)
    near_pairs = [(i, i ^ 1) for i in range(count)]
    far_pairs = [(i, (i + 1 if i % 2 else i - 1) % count) for i in range(count)]
    own_like, for_near, for_far, part = observe(odd, state, obs_index, obs_value, obs_var)
    far = lax.ppermute(for_far, "lon", far_pairs)
    near = lax.ppermute(for_near, "lon", near_pairs)
    start = near.shape[0] - TILE
    part = part[0] + jnp.sum(near[start : start + 3, :128].astype(jnp.float32), axis=0)
    sums = lax.all_to_all(
        jnp.broadcast_to(part, (count // 2, 128)),
        "lon",
        0,
        0,
        axis_index_groups=[[i for i in range(count) if (i ^ i >> 1) & 1 == kind] for kind in range(2)],
        tiled=True,
    )
    offsets = range(REGION + 2 * HALO)
    line = [1.0 - max(0, HALO - p, p - (HALO + REGION - 1)) / (HALO + 1) for p in offsets]
    scale = LOG2E / EPS / (nvar * sum(line) ** 2)
    first, last, like = own_gram(odd, state, near, own_like)
    nobs = float(obs_index.shape[0] * count)
    return analyse(odd, far, first, last, state, like, sums, nobs, scale)


def solution(mesh):
    return jax.shard_map(
        on_device,
        mesh=mesh,
        in_specs=(
            P(("ens", "lon"), None, None, None),
            P(("ens", "lon")),
            P(("ens", "lon")),
            P(("ens", "lon")),
        ),
        out_specs=P(("ens", "lon"), None, None, None),
        check_vma=False,
    )
```
